32 devices in a mesh: dp: 8 (over z, x), rep: 4 (over y, core).
Axes of the slice: x: 2, y: 2, z: 4, core: 2. Of those that a mesh axis runs over, the one named last changes fastest.
Arguments:
- input_160: bfloat16 [128, 10, 10, 1024], P(('dp', 'rep')), may hold values from -6 to 6
- input_224: bfloat16 [64, 14, 14, 1024], P(('dp', 'rep')), may hold values from -6 to 6
- input_288: bfloat16 [64, 18, 18, 1024], P(('dp', 'rep')), may hold values from -6 to 6
- cotangent_160: bfloat16 [128, 5, 5, 2048], P(('dp', 'rep')), may hold values from -6 to 6
- cotangent_224: bfloat16 [64, 7, 7, 2048], P(('dp', 'rep')), may hold values from -6 to 6
- cotangent_288: bfloat16 [64, 9, 9, 2048], P(('dp', 'rep')), may hold values from -6 to 6
- live_counts: int32 [32, 3], P(('dp', 'rep')), may hold values from 1 to 4, as said below
- conv_a1: bfloat16 [1024, 512], P(None, 'dp'), may hold values from -0.1875 to 0.1875
- norm_a1: bfloat16 [2, 512], P(None, 'dp')
- conv_a2: bfloat16 [3, 3, 512, 512], P(None, None, None, 'dp'), may hold values from -0.09375 to 0.09375
- norm_a2: bfloat16 [2, 512], P(None, 'dp')
- conv_a3: bfloat16 [512, 2048], P(None, 'dp'), may hold values from -0.25 to 0.25
- norm_a3: bfloat16 [2, 2048], P(None, 'dp')
- conv_as: bfloat16 [1024, 2048], P(None, 'dp'), may hold values from -0.1875 to 0.1875
- norm_as: bfloat16 [2, 2048], P(None, 'dp')
- conv_b1: bfloat16 [2048, 512], P(None, 'dp'), may hold values from -0.125 to 0.125
- norm_b1: bfloat16 [2, 512], P(None, 'dp')
- conv_b2: bfloat16 [3, 3, 512, 512], P(None, None, None, 'dp'), may hold values from -0.09375 to 0.09375
- norm_b2: bfloat16 [2, 512], P(None, 'dp')
- conv_b3: bfloat16 [512, 2048], P(None, 'dp'), may hold values from -0.25 to 0.25
- norm_b3: bfloat16 [2, 2048], P(None, 'dp')
Outputs:
- output_160: bfloat16 [128, 5, 5, 2048], P(('dp', 'rep'))
- output_224: bfloat16 [64, 7, 7, 2048], P(('dp', 'rep'))
- output_288: bfloat16 [64, 9, 9, 2048], P(('dp', 'rep'))
- grad_input_160: bfloat16 [128, 10, 10, 1024], P(('dp', 'rep'))
- grad_input_224: bfloat16 [64, 14, 14, 1024], P(('dp', 'rep'))
- grad_input_288: bfloat16 [64, 18, 18, 1024], P(('dp', 'rep'))
- grad_conv_a1: float32 [1024, 512], P(None, 'dp')
- grad_norm_a1: float32 [2, 512], P(None, 'dp')
- grad_conv_a2: float32 [3, 3, 512, 512], P(None, None, None, 'dp')
- grad_norm_a2: float32 [2, 512], P(None, 'dp')
- grad_conv_a3: float32 [512, 2048], P(None, 'dp')
- grad_norm_a3: float32 [2, 2048], P(None, 'dp')
- grad_conv_as: float32 [1024, 2048], P(None, 'dp')
- grad_norm_as: float32 [2, 2048], P(None, 'dp')
- grad_conv_b1: float32 [2048, 512], P(None, 'dp')
- grad_norm_b1: float32 [2, 512], P(None, 'dp')
- grad_conv_b2: float32 [3, 3, 512, 512], P(None, None, None, 'dp')
- grad_norm_b2: float32 [2, 512], P(None, 'dp')
- grad_conv_b3: float32 [512, 2048], P(None, 'dp')
- grad_norm_b3: float32 [2, 2048], P(None, 'dp')
- lars_conv_a1: float32 [1024, 512], P(None, 'dp')
- lars_conv_a2: float32 [3, 3, 512, 512], P(None, None, None, 'dp')
- lars_conv_a3: float32 [512, 2048], P(None, 'dp')
- lars_conv_as: float32 [1024, 2048], P(None, 'dp')
- lars_conv_b1: float32 [2048, 512], P(None, 'dp')
- lars_conv_b2: float32 [3, 3, 512, 512], P(None, None, None, 'dp')
- lars_conv_b3: float32 [512, 2048], P(None, 'dp')
- norm_sums: float32 [2, 7], replicated
The draws below stay inside these ranges and needn't reach their ends.
Inputs may be any that keep to these rules, and one draw needn't show every extreme that they name: `live_counts`: column k of a device is at least 1 and at most that group's slots on one device (4, 2, 2); in each column some device is full and some holds one image.
All inputs are finite; a program needn't handle non-finite values.
Results may differ from the reference program's by a relative error of at most 0.019.
Values may be sent and summed in bfloat16 or wider, within the bound.
A program may use at most 144 MiB of HBM per device.

```python
import jax
import jax.numpy as jnp
from jax import lax

C_IN = 1024
MID = 512
C_OUT = 2048
SIDE160 = 10
SIDE224 = 14
SIDE288 = 18
SLOTS_PIXEL160 = 4
SLOTS_PIXEL224 = 2
SLOTS_PIXEL288 = 2
IMG160 = 128
IMG224 = 64
IMG288 = 64
N_DP = 8
N_REP = 4


def norm_rows(key, width, gain_floor, gain_ceiling, shift_scale):
    gain_key, shift_key = jax.random.split(key)
    gain_row = jax.random.uniform(gain_key, (1, width), jnp.float32, gain_floor, gain_ceiling)
    shift_row = shift_scale * jax.random.normal(shift_key, (1, width), jnp.float32)
    return jnp.concatenate([gain_row, shift_row], axis=0).astype(jnp.bfloat16)


def draw_norm_a1(key, part):
    key = jax.random.fold_in(key, 11)
    return norm_rows(key, MID, 0.5, 1.5, 0.5)


def draw_norm_a2(key, part):
    key = jax.random.fold_in(key, 12)
    return norm_rows(key, MID, 0.5, 1.5, 0.5)


def draw_norm_a3(key, part):
    key = jax.random.fold_in(key, 13)
    return norm_rows(key, C_OUT, 0.5, 1.5, 0.5)


def draw_norm_as(key, part):
    key = jax.random.fold_in(key, 14)
    return norm_rows(key, C_OUT, 0.5, 1.5, 0.5)


def draw_norm_b1(key, part):
    key = jax.random.fold_in(key, 15)
    return norm_rows(key, MID, 0.5, 1.5, 0.5)


def draw_norm_b2(key, part):
    key = jax.random.fold_in(key, 16)
    return norm_rows(key, MID, 0.5, 1.5, 0.5)


def draw_norm_b3(key, part):
    key = jax.random.fold_in(key, 17)
    return norm_rows(key, C_OUT, 0.5, 1.5, 0.5)


def draw_live_counts(key, part):
    key = jax.random.fold_in(key, 5)
    devices = N_DP * N_REP
    columns = []
    group_slot_counts = (SLOTS_PIXEL160, SLOTS_PIXEL224, SLOTS_PIXEL288)
    for column_number in range(3):
        group_slot_count = group_slot_counts[column_number]
        column_key = jax.random.fold_in(key, column_number)
        picked = jax.random.randint(jax.random.fold_in(column_key, 1), (devices,), 1, group_slot_count + 1)
        shuffle = jax.random.permutation(jax.random.fold_in(column_key, 2), devices)
        picked = picked.at[shuffle[0]].set(group_slot_count).at[shuffle[1]].set(1)
        columns.append(picked)
    return jnp.stack(columns, axis=1).astype(jnp.int32)


def block_levels(own_key, extent, cuts, least, top_value):
    level, own = 1.0, jax.random.fold_in(own_key, 6)
    for dim, shards_of in cuts:
        draws = jnp.exp(jax.random.uniform(jax.random.fold_in(own, dim), (shards_of,), jnp.float32, least / len(cuts), top_value / len(cuts)))
        level = level * jnp.repeat(draws, extent[dim] // shards_of).reshape([-1 if axis == dim else 1 for axis in range(len(extent))])
    return level


def gaussian(key, shape, scale, bound, pieces=(), kind=jnp.bfloat16):
    gain = block_levels(key, shape, pieces, -0.22, 0.18) if pieces else 1.0
    drawn = jax.random.normal(key, shape, jnp.float32) * scale * gain
    return jnp.minimum(jnp.maximum(drawn, -bound), bound).astype(kind)


def setup_inputs(seed: int = 0) -> dict:
    keys = jax.random.split(jax.random.key(seed), 22)
    return {
        "input_160": gaussian(keys[0], (IMG160, SIDE160, SIDE160, C_IN), 1.0, 6.0, ((0, 32),)),
        "input_224": gaussian(keys[1], (IMG224, SIDE224, SIDE224, C_IN), 1.0, 6.0, ((0, 32),)),
        "input_288": gaussian(keys[2], (IMG288, SIDE288, SIDE288, C_IN), 1.0, 6.0, ((0, 32),)),
        "cotangent_160": gaussian(keys[3], (IMG160, SIDE160 // 2, SIDE160 // 2, C_OUT), 1.0, 6.0, ((0, 32),)),
        "cotangent_224": gaussian(keys[4], (IMG224, SIDE224 // 2, SIDE224 // 2, C_OUT), 1.0, 6.0, ((0, 32),)),
        "cotangent_288": gaussian(keys[5], (IMG288, SIDE288 // 2, SIDE288 // 2, C_OUT), 1.0, 6.0, ((0, 32),)),
        "live_counts": draw_live_counts(jax.random.fold_in(keys[21], 71), 0),
        "conv_a1": gaussian(keys[7], (C_IN, MID), C_IN ** -0.5, 0.1875, ((1, 8),)),
        "norm_a1": draw_norm_a1(jax.random.fold_in(keys[21], 71), 0),
        "conv_a2": gaussian(keys[9], (3, 3, MID, MID), (9 * MID) ** -0.5, 0.09375, ((3, 8),)),
        "norm_a2": draw_norm_a2(jax.random.fold_in(keys[21], 71), 0),
        "conv_a3": gaussian(keys[11], (MID, C_OUT), MID ** -0.5, 0.25, ((1, 8),)),
        "norm_a3": draw_norm_a3(jax.random.fold_in(keys[21], 71), 0),
        "conv_as": gaussian(keys[13], (C_IN, C_OUT), C_IN ** -0.5, 0.1875, ((1, 8),)),
        "norm_as": draw_norm_as(jax.random.fold_in(keys[21], 71), 0),
        "conv_b1": gaussian(keys[15], (C_OUT, MID), C_OUT ** -0.5, 0.125, ((1, 8),)),
        "norm_b1": draw_norm_b1(jax.random.fold_in(keys[21], 71), 0),
        "conv_b2": gaussian(keys[17], (3, 3, MID, MID), (9 * MID) ** -0.5, 0.09375, ((3, 8),)),
        "norm_b2": draw_norm_b2(jax.random.fold_in(keys[21], 71), 0),
        "conv_b3": gaussian(keys[19], (MID, C_OUT), MID ** -0.5, 0.25, ((1, 8),)),
        "norm_b3": draw_norm_b3(jax.random.fold_in(keys[21], 71), 0),
    }


EPSILON = 1e-05
DECAY_RATE = 5e-05

@jax.custom_vjp
def low(v):
    return lax.optimization_barrier(v.astype(jnp.bfloat16)).astype(jnp.float32)

@jax.custom_vjp
def low_back(v):
    return v

def low_keep(v):
    return (low(v), None)

def low_pass(kept, grad):
    return (grad,)

def back_keep(v):
    return (v, None)

def back_low(kept, grad):
    return (low(grad),)
low.defvjp(low_keep, low_pass)
low_back.defvjp(back_keep, back_low)

def pointwise(inputs, weight):
    return jnp.einsum('nhwc,cd->nhwd', inputs, weight, precision=lax.Precision.HIGHEST)

def spatial(inputs, kernel, stride):
    return lax.conv_general_dilated(inputs, kernel, (stride, stride), ((1, 1), (1, 1)), dimension_numbers=('NHWC', 'HWIO', 'NHWC'), precision=lax.Precision.HIGHEST)

def batch_norm(values, live_masks, norm_param, totals):
    results = []
    for group_member in range(3):
        pixel_count = totals[group_member] * values[group_member].shape[1] * values[group_member].shape[2]
        weighted = values[group_member] * live_masks[group_member]
        mean_value = lax.optimization_barrier(jnp.sum(weighted, axis=(0, 1, 2))) / pixel_count
        square_mean = lax.optimization_barrier(jnp.sum(weighted * values[group_member], axis=(0, 1, 2))) / pixel_count
        inv_std = lax.rsqrt(square_mean - mean_value * mean_value + EPSILON)
        results.append((values[group_member] - mean_value) * inv_std * norm_param[0] + norm_param[1])
    return results

def forward(images, params, live_masks, totals):
    conv_a1, norm_a1, conv_a2, norm_a2, conv_a3, norm_a3, conv_as, norm_as, conv_b1, norm_b1, conv_b2, norm_b2, conv_b3, norm_b3 = params
    masked = [images[group_member] * live_masks[group_member] for group_member in range(3)]
    hidden = [low_back(pointwise(masked[group_member], conv_a1)) for group_member in range(3)]
    activated = [low(jax.nn.silu(normed)) for normed in batch_norm(hidden, live_masks, norm_a1, totals)]
    hidden = [low_back(spatial(activated[group_member], conv_a2, 2)) for group_member in range(3)]
    activated = [low(jax.nn.silu(normed)) for normed in batch_norm(hidden, live_masks, norm_a2, totals)]
    main_path = [low_back(pointwise(activated[group_member], conv_a3)) for group_member in range(3)]
    short_path = [low_back(pointwise(masked[group_member][:, ::2, ::2, :], conv_as)) for group_member in range(3)]
    main_path = batch_norm(main_path, live_masks, norm_a3, totals)
    short_path = batch_norm(short_path, live_masks, norm_as, totals)
    out_a = [low(jax.nn.silu(main_path[group_member] + short_path[group_member]) * live_masks[group_member]) for group_member in range(3)]
    hidden = [low_back(pointwise(out_a[group_member], conv_b1)) for group_member in range(3)]
    activated = [low(jax.nn.silu(normed)) for normed in batch_norm(hidden, live_masks, norm_b1, totals)]
    hidden = [low_back(spatial(activated[group_member], conv_b2, 1)) for group_member in range(3)]
    activated = [low(jax.nn.silu(normed)) for normed in batch_norm(hidden, live_masks, norm_b2, totals)]
    main_path = [low_back(pointwise(activated[group_member], conv_b3)) for group_member in range(3)]
    main_path = batch_norm(main_path, live_masks, norm_b3, totals)
    return [jax.nn.silu(main_path[group_member] + out_a[group_member]) * live_masks[group_member] for group_member in range(3)]

def reference(input_160, input_224, input_288, cotangent_160, cotangent_224, cotangent_288, live_counts, conv_a1, norm_a1, conv_a2, norm_a2, conv_a3, norm_a3, conv_as, norm_as, conv_b1, norm_b1, conv_b2, norm_b2, conv_b3, norm_b3):
    group_slot_counts = (SLOTS_PIXEL160, SLOTS_PIXEL224, SLOTS_PIXEL288)
    live_masks = []
    totals = []
    for group_member in range(3):
        group_slot_count = group_slot_counts[group_member]
        slot_ids = jnp.arange(group_slot_count * N_DP * N_REP, dtype=jnp.int32)
        live_here = live_counts[slot_ids // group_slot_count, group_member]
        live_masks.append((slot_ids % group_slot_count < live_here).astype(jnp.float32).reshape(-1, 1, 1, 1))
        totals.append(jnp.sum(live_counts[:, group_member]).astype(jnp.float32))
    images = [input_160.astype(jnp.float32), input_224.astype(jnp.float32), input_288.astype(jnp.float32)]
    raw_params = (conv_a1, norm_a1, conv_a2, norm_a2, conv_a3, norm_a3, conv_as, norm_as, conv_b1, norm_b1, conv_b2, norm_b2, conv_b3, norm_b3)
    params = [weight.astype(jnp.float32) for weight in raw_params]

    def bound_forward(images, params):
        return forward(images, params, live_masks, totals)
    outputs, pullback = jax.vjp(bound_forward, images, params)
    cotangents = [cotangent_160.astype(jnp.float32), cotangent_224.astype(jnp.float32), cotangent_288.astype(jnp.float32)]
    grad_images, grad_params = pullback(cotangents)
    conv_values = [params[2 * layer_id] for layer_id in range(7)]
    conv_grads = [grad_params[2 * layer_id] for layer_id in range(7)]
    weight_squares = jnp.stack([jnp.sum(weight * weight) for weight in conv_values])
    grad_squares = jnp.stack([jnp.sum(gradient * gradient) for gradient in conv_grads])
    weight_norm = jnp.sqrt(weight_squares)
    grad_norm = jnp.sqrt(grad_squares)
    trust_ratio = weight_norm / (grad_norm + DECAY_RATE * weight_norm)
    scaled = [trust_ratio[layer_id] * (conv_grads[layer_id] + DECAY_RATE * conv_values[layer_id]) for layer_id in range(7)]
    return (outputs[0].astype(jnp.bfloat16), outputs[1].astype(jnp.bfloat16), outputs[2].astype(jnp.bfloat16), grad_images[0].astype(jnp.bfloat16), grad_images[1].astype(jnp.bfloat16), grad_images[2].astype(jnp.bfloat16), grad_params[0], grad_params[1], grad_params[2], grad_params[3], grad_params[4], grad_params[5], grad_params[6], grad_params[7], grad_params[8], grad_params[9], grad_params[10], grad_params[11], grad_params[12], grad_params[13], scaled[0], scaled[1], scaled[2], scaled[3], scaled[4], scaled[5], scaled[6], jnp.stack([weight_squares, grad_squares]))
```

```python
import functools

import jax
import jax.numpy as jnp
import numpy as np
from jax import lax
from jax.experimental import pallas as pl
from jax.experimental.pallas import tpu as pltpu
from jax.sharding import PartitionSpec as P

DP, REP = "dp", "rep"
EPSILON = 1e-05
DECAY_RATE = 5e-05


def silu_slope(values):
    sigmoid = jax.nn.sigmoid(values)
    return sigmoid * (1.0 + values * (1.0 - sigmoid))


def pointwise(inputs, weight):
    return jnp.tensordot(inputs, weight, 1, preferred_element_type=jnp.float32)


def pointwise_back(upstream, weight):
    return jnp.tensordot(upstream, weight, ((3,), (1,)), preferred_element_type=jnp.float32)


def weight_term(inputs, upstream):
    return jnp.tensordot(inputs, upstream, ((0, 1, 2),) * 2, preferred_element_type=jnp.float32)


def summed_terms(inputs, upstream):
    running = weight_term(inputs[0], upstream[0])
    for group_member in (1, 2):
        running = running + weight_term(inputs[group_member], upstream[group_member])
    return running


def patches(inputs, stride):
    padded = jnp.pad(inputs, ((0, 0), (1, 1), (1, 1), (0, 0)))
    extent = inputs.shape[1]
    pieces = []
    for offset_row in range(3):
        for offset_col in range(3):
            pieces.append(
                padded[
                    :,
                    offset_row : offset_row + extent : stride,
                    offset_col : offset_col + extent : stride,
                    :,
                ]
            )
    return jnp.concatenate(pieces, axis=3)


def fold_patches(upstream, stride, side_in):
    channels = upstream.shape[3] // 9
    padded = jnp.zeros((upstream.shape[0], side_in + 2, side_in + 2, channels), jnp.float32)
    for offset_row in range(3):
        for offset_col in range(3):
            start_at = (offset_row * 3 + offset_col) * channels
            padded = padded.at[
                :,
                offset_row : offset_row + side_in : stride,
                offset_col : offset_col + side_in : stride,
                :,
            ].add(upstream[..., start_at : start_at + channels])
    return padded[:, 1 : side_in + 1, 1 : side_in + 1, :]


def batch_norm(values, live_masks, norm_param, totals):
    gain_row = norm_param[0].astype(jnp.float32)
    shift_row = norm_param[1].astype(jnp.float32)
    firsts = []
    seconds = []
    for group_member in range(3):
        weighted = values[group_member] * live_masks[group_member]
        firsts.append(jnp.sum(weighted, axis=(0, 1, 2)))
        seconds.append(jnp.sum(weighted * values[group_member], axis=(0, 1, 2)))
    summed = lax.psum(
        (firsts[0], seconds[0], firsts[1], seconds[1], firsts[2], seconds[2]), (DP, REP)
    )
    normed = []
    means = []
    scales = []
    for group_member in range(3):
        pixel_count = (
            totals[group_member] * values[group_member].shape[1] * values[group_member].shape[2]
        )
        mean_value = summed[2 * group_member] / pixel_count
        inv_std = lax.rsqrt(
            summed[2 * group_member + 1] / pixel_count - mean_value * mean_value + EPSILON
        )
        normed.append((values[group_member] - mean_value) * inv_std * gain_row + shift_row)
        means.append(mean_value)
        scales.append(inv_std)
    return (normed, means, scales)


def norm_back(upstream, values, live_masks, norm_param, means, scales, totals):
    gain_row = norm_param[0].astype(jnp.float32)
    normals = []
    firsts = []
    seconds = []
    for group_member in range(3):
        normal = (values[group_member] - means[group_member]) * scales[group_member]
        weighted = upstream[group_member] * live_masks[group_member]
        normals.append(normal)
        firsts.append(jnp.sum(weighted, axis=(0, 1, 2)))
        seconds.append(jnp.sum(weighted * normal, axis=(0, 1, 2)))
    summed = lax.psum(
        (firsts[0], seconds[0], firsts[1], seconds[1], firsts[2], seconds[2]), (DP, REP)
    )
    results = []
    for group_member in range(3):
        pixel_count = (
            totals[group_member] * values[group_member].shape[1] * values[group_member].shape[2]
        )
        centered = (
            upstream[group_member]
            - summed[2 * group_member] / pixel_count
            - normals[group_member] * (summed[2 * group_member + 1] / pixel_count)
        )
        results.append(
            (live_masks[group_member] * gain_row * scales[group_member] * centered).astype(
                jnp.bfloat16
            )
        )
    param_grad = jnp.stack([summed[1] + summed[3] + summed[5], summed[0] + summed[2] + summed[4]])
    return (results, param_grad)


def own_columns(full, local_width):
    return lax.dynamic_slice_in_dim(full, lax.axis_index(DP) * local_width, local_width, 1)


def plain_on_device(
    input_160,
    input_224,
    input_288,
    cotangent_160,
    cotangent_224,
    cotangent_288,
    live_counts,
    conv_a1,
    norm_a1,
    conv_a2,
    norm_a2,
    conv_a3,
    norm_a3,
    conv_as,
    norm_as,
    conv_b1,
    norm_b1,
    conv_b2,
    norm_b2,
    conv_b3,
    norm_b3,
):
    inputs = (input_160, input_224, input_288)
    cotangents = (cotangent_160, cotangent_224, cotangent_288)
    live_masks = []
    masked = []
    for group_member in range(3):
        group_slot_count = inputs[group_member].shape[0]
        live_flags = (
            (jnp.arange(group_slot_count) < live_counts[0, group_member])
            .astype(jnp.float32)
            .reshape(group_slot_count, 1, 1, 1)
        )
        live_masks.append(live_flags)
        masked.append(inputs[group_member] * live_flags.astype(jnp.bfloat16))
    totals = lax.psum(live_counts[0].astype(jnp.float32), (DP, REP))
    local_weights = (conv_a1, conv_a2, conv_a3, conv_as, conv_b1, conv_b2, conv_b3)
    squares_list = []
    for weight in local_weights:
        squares_list.append(jnp.sum(jnp.square(weight.astype(jnp.float32))))
    weight_squares = jnp.stack(squares_list)
    gathered_a = (
        lax.all_gather(conv_a1, DP, axis=1, tiled=True),
        lax.all_gather(norm_a1, DP, axis=1, tiled=True),
        lax.all_gather(conv_a2, DP, axis=3, tiled=True),
        lax.all_gather(norm_a2, DP, axis=1, tiled=True),
        lax.all_gather(conv_a3, DP, axis=1, tiled=True),
        lax.all_gather(norm_a3, DP, axis=1, tiled=True),
        lax.all_gather(conv_as, DP, axis=1, tiled=True),
        lax.all_gather(norm_as, DP, axis=1, tiled=True),
    )
    full_a1, param_a1, full_a2, param_a2, full_a3, param_a3, full_as, param_as = gathered_a
    mid_width = full_a2.shape[3]
    out_width = full_a3.shape[1]
    hidden_a1 = [pointwise(masked[group_member], full_a1) for group_member in range(3)]
    normed_a1, means_a1, scales_a1 = batch_norm(hidden_a1, live_masks, param_a1, totals)
    act_a1 = [
        jax.nn.silu(normed_a1[group_member]).astype(jnp.bfloat16) for group_member in range(3)
    ]
    kernel_a2 = full_a2.reshape(9 * mid_width, mid_width)
    hidden_a2 = [
        pointwise(patches(act_a1[group_member], 2), kernel_a2) for group_member in range(3)
    ]
    normed_a2, means_a2, scales_a2 = batch_norm(hidden_a2, live_masks, param_a2, totals)
    act_a2 = [
        jax.nn.silu(normed_a2[group_member]).astype(jnp.bfloat16) for group_member in range(3)
    ]
    strided = [masked[group_member][:, ::2, ::2, :] for group_member in range(3)]
    joined = [
        jnp.concatenate(
            [pointwise(act_a2[group_member], full_a3), pointwise(strided[group_member], full_as)],
            axis=3,
        )
        for group_member in range(3)
    ]
    param_joined = jnp.concatenate([param_a3, param_as], axis=1)
    normed_j, means_j, scales_j = batch_norm(joined, live_masks, param_joined, totals)
    sum_a = [
        normed_j[group_member][..., :out_width] + normed_j[group_member][..., out_width:]
        for group_member in range(3)
    ]
    out_a = [
        (jax.nn.silu(sum_a[group_member]) * live_masks[group_member]).astype(jnp.bfloat16)
        for group_member in range(3)
    ]
    gathered_b = (
        lax.all_gather(conv_b1, DP, axis=1, tiled=True),
        lax.all_gather(norm_b1, DP, axis=1, tiled=True),
        lax.all_gather(conv_b2, DP, axis=3, tiled=True),
        lax.all_gather(norm_b2, DP, axis=1, tiled=True),
        lax.all_gather(conv_b3, DP, axis=1, tiled=True),
        lax.all_gather(norm_b3, DP, axis=1, tiled=True),
    )
    full_b1, param_b1, full_b2, param_b2, full_b3, param_b3 = gathered_b
    hidden_b1 = [pointwise(out_a[group_member], full_b1) for group_member in range(3)]
    normed_b1, means_b1, scales_b1 = batch_norm(hidden_b1, live_masks, param_b1, totals)
    act_b1 = [
        jax.nn.silu(normed_b1[group_member]).astype(jnp.bfloat16) for group_member in range(3)
    ]
    kernel_b2 = full_b2.reshape(9 * mid_width, mid_width)
    hidden_b2 = [
        pointwise(patches(act_b1[group_member], 1), kernel_b2) for group_member in range(3)
    ]
    normed_b2, means_b2, scales_b2 = batch_norm(hidden_b2, live_masks, param_b2, totals)
    act_b2 = [
        jax.nn.silu(normed_b2[group_member]).astype(jnp.bfloat16) for group_member in range(3)
    ]
    hidden_b3 = [pointwise(act_b2[group_member], full_b3) for group_member in range(3)]
    normed_b3, means_b3, scales_b3 = batch_norm(hidden_b3, live_masks, param_b3, totals)
    sum_b = [
        normed_b3[group_member] + out_a[group_member].astype(jnp.float32)
        for group_member in range(3)
    ]
    outputs = [
        (jax.nn.silu(sum_b[group_member]) * live_masks[group_member]).astype(jnp.bfloat16)
        for group_member in range(3)
    ]
    back_b = (
        lax.all_gather(conv_b1, DP, axis=1, tiled=True),
        lax.all_gather(norm_b1, DP, axis=1, tiled=True),
        lax.all_gather(conv_b2, DP, axis=3, tiled=True),
        lax.all_gather(norm_b2, DP, axis=1, tiled=True),
        lax.all_gather(conv_b3, DP, axis=1, tiled=True),
        lax.all_gather(norm_b3, DP, axis=1, tiled=True),
    )
    full_b1, param_b1, full_b2, param_b2, full_b3, param_b3 = back_b
    kernel_b2 = full_b2.reshape(9 * mid_width, mid_width)
    grad_sum_b = [
        cotangents[group_member].astype(jnp.float32)
        * live_masks[group_member]
        * silu_slope(sum_b[group_member])
        for group_member in range(3)
    ]
    grad_h_b3, pgrad_b3 = norm_back(
        grad_sum_b, hidden_b3, live_masks, param_b3, means_b3, scales_b3, totals
    )
    term_b3 = summed_terms(act_b2, grad_h_b3)
    grad_act = [
        pointwise_back(grad_h_b3[group_member], full_b3) * silu_slope(normed_b2[group_member])
        for group_member in range(3)
    ]
    grad_h_b2, pgrad_b2 = norm_back(
        grad_act, hidden_b2, live_masks, param_b2, means_b2, scales_b2, totals
    )
    term_b2 = summed_terms(
        [patches(act_b1[group_member], 1) for group_member in range(3)], grad_h_b2
    ).reshape(3, 3, mid_width, mid_width)
    grad_act = [
        fold_patches(
            pointwise_back(grad_h_b2[group_member], kernel_b2), 1, act_b1[group_member].shape[1]
        )
        * silu_slope(normed_b1[group_member])
        for group_member in range(3)
    ]
    grad_h_b1, pgrad_b1 = norm_back(
        grad_act, hidden_b1, live_masks, param_b1, means_b1, scales_b1, totals
    )
    term_b1 = summed_terms(out_a, grad_h_b1)
    grad_out_a = [
        grad_sum_b[group_member] + pointwise_back(grad_h_b1[group_member], full_b1)
        for group_member in range(3)
    ]
    shard_b = (
        lax.psum_scatter(term_b1, DP, scatter_dimension=1, tiled=True),
        lax.psum_scatter(term_b2, DP, scatter_dimension=3, tiled=True),
        lax.psum_scatter(term_b3, DP, scatter_dimension=1, tiled=True),
    )
    grads_b = (
        lax.psum(shard_b[0].astype(jnp.bfloat16), REP).astype(jnp.float32),
        lax.psum(shard_b[1].astype(jnp.bfloat16), REP).astype(jnp.float32),
        lax.psum(shard_b[2].astype(jnp.bfloat16), REP).astype(jnp.float32),
    )
    back_a = (
        lax.all_gather(conv_a1, DP, axis=1, tiled=True),
        lax.all_gather(norm_a1, DP, axis=1, tiled=True),
        lax.all_gather(conv_a2, DP, axis=3, tiled=True),
        lax.all_gather(norm_a2, DP, axis=1, tiled=True),
        lax.all_gather(conv_a3, DP, axis=1, tiled=True),
        lax.all_gather(norm_a3, DP, axis=1, tiled=True),
        lax.all_gather(conv_as, DP, axis=1, tiled=True),
        lax.all_gather(norm_as, DP, axis=1, tiled=True),
    )
    full_a1, param_a1, full_a2, param_a2, full_a3, param_a3, full_as, param_as = back_a
    kernel_a2 = full_a2.reshape(9 * mid_width, mid_width)
    param_joined = jnp.concatenate([param_a3, param_as], axis=1)
    grad_sum_a = [
        grad_out_a[group_member] * live_masks[group_member] * silu_slope(sum_a[group_member])
        for group_member in range(3)
    ]
    grad_joined = [
        jnp.concatenate([grad_sum_a[group_member], grad_sum_a[group_member]], axis=3)
        for group_member in range(3)
    ]
    grad_h_j, pgrad_j = norm_back(
        grad_joined, joined, live_masks, param_joined, means_j, scales_j, totals
    )
    grad_h_a3 = [grad_h_j[group_member][..., :out_width] for group_member in range(3)]
    grad_h_as = [grad_h_j[group_member][..., out_width:] for group_member in range(3)]
    term_a3 = summed_terms(act_a2, grad_h_a3)
    term_as = summed_terms(strided, grad_h_as)
    grad_act = [
        pointwise_back(grad_h_a3[group_member], full_a3) * silu_slope(normed_a2[group_member])
        for group_member in range(3)
    ]
    grad_h_a2, pgrad_a2 = norm_back(
        grad_act, hidden_a2, live_masks, param_a2, means_a2, scales_a2, totals
    )
    term_a2 = summed_terms(
        [patches(act_a1[group_member], 2) for group_member in range(3)], grad_h_a2
    ).reshape(3, 3, mid_width, mid_width)
    grad_act = [
        fold_patches(
            pointwise_back(grad_h_a2[group_member], kernel_a2), 2, act_a1[group_member].shape[1]
        )
        * silu_slope(normed_a1[group_member])
        for group_member in range(3)
    ]
    grad_h_a1, pgrad_a1 = norm_back(
        grad_act, hidden_a1, live_masks, param_a1, means_a1, scales_a1, totals
    )
    term_a1 = summed_terms(masked, grad_h_a1)
    grad_inputs = [
        pointwise_back(grad_h_a1[group_member], full_a1)
        .at[:, ::2, ::2, :]
        .add(pointwise_back(grad_h_as[group_member], full_as))
        .astype(jnp.bfloat16)
        for group_member in range(3)
    ]
    shard_a = (
        lax.psum_scatter(term_a1, DP, scatter_dimension=1, tiled=True),
        lax.psum_scatter(term_a2, DP, scatter_dimension=3, tiled=True),
        lax.psum_scatter(term_a3, DP, scatter_dimension=1, tiled=True),
        lax.psum_scatter(term_as, DP, scatter_dimension=1, tiled=True),
    )
    grads_a = (
        lax.psum(shard_a[0].astype(jnp.bfloat16), REP).astype(jnp.float32),
        lax.psum(shard_a[1].astype(jnp.bfloat16), REP).astype(jnp.float32),
        lax.psum(shard_a[2].astype(jnp.bfloat16), REP).astype(jnp.float32),
        lax.psum(shard_a[3].astype(jnp.bfloat16), REP).astype(jnp.float32),
    )
    mid_local = norm_a1.shape[1]
    out_local = norm_a3.shape[1]
    norm_grad_a1 = own_columns(pgrad_a1, mid_local)
    norm_grad_a2 = own_columns(pgrad_a2, mid_local)
    norm_grad_a3 = own_columns(pgrad_j[:, :out_width], out_local)
    norm_grad_as = own_columns(pgrad_j[:, out_width:], out_local)
    norm_grad_b1 = own_columns(pgrad_b1, mid_local)
    norm_grad_b2 = own_columns(pgrad_b2, mid_local)
    norm_grad_b3 = own_columns(pgrad_b3, out_local)
    gradients = (grads_a[0], grads_a[1], grads_a[2], grads_a[3], grads_b[0], grads_b[1], grads_b[2])
    grad_list = []
    for gradient in gradients:
        grad_list.append(jnp.sum(gradient * gradient))
    grad_squares = jnp.stack(grad_list)
    weight_totals, grad_totals = lax.psum((weight_squares, grad_squares), DP)
    weight_norm = jnp.sqrt(weight_totals)
    grad_norm = jnp.sqrt(grad_totals)
    trust_ratio = weight_norm / (grad_norm + DECAY_RATE * weight_norm)
    scaled = [
        trust_ratio[layer_id]
        * (gradients[layer_id] + DECAY_RATE * local_weights[layer_id].astype(jnp.float32))
        for layer_id in range(7)
    ]
    return (
        outputs[0],
        outputs[1],
        outputs[2],
        grad_inputs[0],
        grad_inputs[1],
        grad_inputs[2],
        gradients[0],
        norm_grad_a1,
        gradients[1],
        norm_grad_a2,
        gradients[2],
        norm_grad_a3,
        gradients[3],
        norm_grad_as,
        gradients[4],
        norm_grad_b1,
        gradients[5],
        norm_grad_b2,
        gradients[6],
        norm_grad_b3,
        scaled[0],
        scaled[1],
        scaled[2],
        scaled[3],
        scaled[4],
        scaled[5],
        scaled[6],
        jnp.stack([weight_totals, grad_totals]),
    )


MESH = pl.DeviceIdType.MESH
ANY = pl.BlockSpec(memory_space=pl.ANY)


def position():
    dp, rep = lax.axis_index(DP), lax.axis_index(REP)
    return dp // 2, lax.rem(dp, 2), rep // 2, lax.rem(rep, 2)


def device_at(z, x, y, core):
    return (z * 2 + x, y * 2 + core)


def greet(depth):
    z, x, y, core = position()
    barrier = pltpu.get_barrier_semaphore()
    peers = [(z, x, y, 1 - core), (z, x, 1 - y, core), (z, x, 1 - y, 1 - core)]
    peers += [(z, 1 - x, y, core), (z, 1 - x, y, 1 - core), (z, 1 - x, 1 - y, core), (z, 1 - x, 1 - y, 1 - core)]
    peers += [(lax.rem(z + step, depth), x, y, core) for step in range(1, depth)]
    for peer in peers:
        pl.semaphore_signal(barrier, inc=1, device_id=device_at(*peer), device_id_type=MESH)
    pl.semaphore_wait(barrier, len(peers))


def remote(src, dst, send, recv, peer):
    return pltpu.make_async_remote_copy(
        src_ref=src, dst_ref=dst, send_sem=send, recv_sem=recv, device_id=device_at(*peer), device_id_type=MESH
    )


def chunk_rows(rows, both, y, core):
    if both:
        return pl.ds(pl.multiple_of(core * (rows // 2), rows // 2), rows // 2)
    return pl.ds(pl.multiple_of(core * (rows // 2) + y * (rows // 4), rows // 4), rows // 4)


def core_rows(rows, core):
    return pl.ds(pl.multiple_of(core * (rows // 2), rows // 2), rows // 2)


class Gather:
    AHEAD = 3

    def __init__(self, shards, fulls, sems, depth):
        self.shards, self.fulls, self.depth = shards, fulls, depth
        (self.local_sem, self.z_send, self.z_recv, self.x_send, self.x_recv) = sems[:5]
        (self.y_send, self.y_recv, self.c_send, self.c_recv) = sems[5:]
        self.z, self.x, self.y, self.core = position()
        self.count, self.now = len(GATHER_CHUNKS), 0

    @staticmethod
    def scratch(depth):
        dma, count = pltpu.SemaphoreType.DMA, len(GATHER_CHUNKS)
        return [dma((count,))] + [dma((count, depth - 1))] * 2 + [dma((count,))] * 6

    def part(self, k):
        tensor, lead, leads, both, column, columns = GATHER_CHUNKS[k]
        rows = chunk_rows(self.shards[tensor].shape[1], both, self.y, self.core)
        return self.fulls[tensor], pl.ds(lead, leads), rows, pl.ds(column, columns)

    def place(self, k):
        full, lead, rows, cols = self.part(k)
        shard = self.shards[GATHER_CHUNKS[k][0]]
        return pltpu.make_async_copy(
            shard.at[lead, rows, cols], full.at[self.z, self.x, lead, rows, cols], self.local_sem.at[k]
        )

    def z_copies(self, k):
        full, lead, rows, cols = self.part(k)
        here = full.at[self.z, self.x, lead, rows, cols]
        return [
            remote(
                here,
                here,
                self.z_send.at[k, step - 1],
                self.z_recv.at[k, step - 1],
                (lax.rem(self.z + step, self.depth), self.x, self.y, self.core),
            )
            for step in range(1, self.depth)
        ]

    def x_copy(self, k):
        full, lead, rows, cols = self.part(k)
        here = full.at[:, self.x, lead, rows, cols]
        return remote(here, here, self.x_send.at[k], self.x_recv.at[k], (self.z, 1 - self.x, self.y, self.core))

    def y_copy(self, k):
        full, lead, rows, cols = self.part(k)
        here = full.at[:, :, lead, rows, cols]
        return remote(here, here, self.y_send.at[k], self.y_recv.at[k], (self.z, self.x, 1 - self.y, self.core))

    def c_copy(self, k):
        full, lead, _, cols = self.part(k)
        here = full.at[:, :, lead, core_rows(full.shape[3], self.core), cols]
        return remote(here, here, self.c_send.at[k], self.c_recv.at[k], (self.z, self.x, self.y, 1 - self.core))

    def place_all(self):
        for k in range(self.count):
            self.place(k).start()

    def launch(self, k):
        if k < self.count:
            self.place(k).wait()
            for copy in self.z_copies(k):
                copy.start()

    def begin(self):
        for k in range(self.AHEAD):
            self.launch(k)

    def tick(self):
        now, count = self.now, self.count
        self.now += 1
        if now < count:
            for copy in self.z_copies(now):
                copy.wait_recv()
            self.x_copy(now).start()
            self.launch(now + self.AHEAD)
        k = now - 1
        if 0 <= k < count:
            self.x_copy(k).wait_recv()
            (self.c_copy if GATHER_CHUNKS[k][3] else self.y_copy)(k).start()
        k = now - 2
        if 0 <= k < count and not GATHER_CHUNKS[k][3]:
            self.y_copy(k).wait_recv()
            self.c_copy(k).start()
        k = now - 3
        if 0 <= k < count:
            self.c_copy(k).wait_recv()

    def pump(self, ticks=1):
        for _ in range(ticks):
            if self.now < self.count + 3:
                self.tick()

    def ready(self, tensor):
        last = max(k for k, chunk in enumerate(GATHER_CHUNKS) if chunk[0] == tensor)
        while self.now <= last + 3:
            self.tick()

    def close(self):
        for k in range(self.count):
            for copy in self.z_copies(k):
                copy.wait_send()
            self.x_copy(k).wait_send()
            if not GATHER_CHUNKS[k][3]:
                self.y_copy(k).wait_send()
            self.c_copy(k).wait_send()


def taps(tensor):
    pieces = []
    for lead in (0, 3, 6):
        pieces += [(tensor, lead, 1, True, 0, 512), (tensor, lead + 1, 2, False, 0, 512)]
    return pieces


CHUNKS = (
    [(0, 0, 1, False, column, 512) for column in (0, 512)],
    taps(1),
    [(2, lead, 1, False, 0, 256) for lead in (0, 1)],
    [(3, lead, 1, lead == 0, 0, 256) for lead in range(4)],
    [(4, 0, 1, column % 1024 == 0, column, 512) for column in (0, 512, 1024, 1536)],
    taps(5),
    [(6, lead, 1, False, 0, 256) for lead in (0, 1)],
)
GATHER_CHUNKS = [chunk for tensor in (0, 1, 3, 2, 4, 5, 6) for chunk in CHUNKS[tensor]]
REDUCE_CHUNKS = [chunk for tensor in (6, 5, 4, 2, 3, 1, 0) for chunk in CHUNKS[tensor]]


def add_blocks(extents, body):
    total = 1
    for extent in extents:
        total *= extent

    def step(flat, carry):
        index = []
        for extent in reversed(extents):
            index.append(lax.rem(flat, extent))
            flat = flat // extent
        body(*reversed(index))
        return carry

    lax.fori_loop(0, total, step, 0)


def add_to(target, source):
    target[...] = (target[...].astype(jnp.float32) + source[...].astype(jnp.float32)).astype(jnp.bfloat16)


class Reduce:
    def __init__(self, held, outs, c_hbm, y_hbm, refs, depth):
        self.held, self.outs, self.c_hbm, self.y_hbm, self.depth = held, outs, c_hbm, y_hbm, depth
        self.count = len(REDUCE_CHUNKS)
        refs = list(refs)

        def take(count):
            taken = refs[:count]
            del refs[:count]
            return taken

        self.from_x, self.from_z, self.swap = take(self.count), take(self.count), take(self.count)
        self.final = take(self.count)
        self.c_tall, self.c_wide, self.y_tall, self.y_wide, self.squares = take(5)
        self.c_sem, self.y_sem, self.x_sem, self.z_sem, self.s_sem, self.f_sem, self.q_sem, self.local_sem = take(8)
        self.z, self.x, self.y, self.core = position()
        self.now = self.enabled = 0

    @staticmethod
    def sizes(shapes):
        for tensor, _, leads, both, _, columns in REDUCE_CHUNKS:
            rows = shapes[tensor][3]
            yield leads, rows, columns, rows // 2 if both else rows // 4, both

    @staticmethod
    def scratch(shapes, depth):
        dma, count = pltpu.SemaphoreType.DMA, len(REDUCE_CHUNKS)
        buffer = lambda *shape: pltpu.VMEM(shape, jnp.bfloat16)
        sizes = list(Reduce.sizes(shapes))
        return (
            [buffer(depth, leads, part, columns) for leads, _, columns, part, _ in sizes]
            + [buffer(depth - 1, leads, part, columns) for leads, _, columns, part, _ in sizes]
            + [buffer(leads, part, columns) if both else buffer(16, 128) for leads, _, columns, part, both in sizes]
            + [buffer(leads, rows, columns) for leads, rows, columns, _, _ in sizes]
            + [buffer(2, depth, 2, 1, shapes[2][3] // 2, shapes[2][4]), buffer(2, depth, 2, 2, shapes[0][3] // 2, 512)]
            + [buffer(2, depth, 2, 1, shapes[2][3] // 4, shapes[2][4]), buffer(2, depth, 2, 2, shapes[0][3] // 4, 512)]
            + [pltpu.VMEM((2 * depth + 3, 8, 128), jnp.float32)]
            + [dma((2, count))] * 3
            + [dma((2, count, depth - 1)), dma((2, count)), dma((2, count, 3)), dma((2, depth)), dma((3, count))]
        )

    def piece(self, k):
        tensor, lead, leads, both, column, columns = REDUCE_CHUNKS[k]
        held = self.held[tensor]
        rows = held.shape[3]
        return held, rows, pl.ds(lead, leads), pl.ds(column, columns), chunk_rows(rows, both, self.y, self.core)

    def extents(self, k):
        return REDUCE_CHUNKS[k][2], REDUCE_CHUNKS[k][1]

    def slot(self, k, tall, wide):
        tensor, _, leads = REDUCE_CHUNKS[k][:3]
        buffer = tall if tensor in (2, 3, 6) else wide
        return buffer.at[k % 2, :, :, pl.ds(0, leads)]

    def c_copy(self, k):
        held, rows, lead, cols, _ = self.piece(k)
        return remote(
            held.at[:, :, lead, core_rows(rows, 1 - self.core), cols],
            self.c_hbm[REDUCE_CHUNKS[k][0]].at[:, :, lead, :, cols],
            self.c_sem.at[0, k],
            self.c_sem.at[1, k],
            (self.z, self.x, self.y, 1 - self.core),
        )

    def c_load(self, k):
        _, _, lead, cols, _ = self.piece(k)
        return pltpu.make_async_copy(
            self.c_hbm[REDUCE_CHUNKS[k][0]].at[:, :, lead, :, cols],
            self.slot(k, self.c_tall, self.c_wide),
            self.local_sem.at[0, k],
        )

    def y_copy(self, k):
        held, rows, lead, cols, _ = self.piece(k)
        return remote(
            held.at[:, :, lead, chunk_rows(rows, False, 1 - self.y, self.core), cols],
            self.y_hbm[REDUCE_CHUNKS[k][0]].at[:, :, lead, :, cols],
            self.y_sem.at[0, k],
            self.y_sem.at[1, k],
            (self.z, self.x, 1 - self.y, self.core),
        )

    def y_load(self, k):
        _, _, lead, cols, _ = self.piece(k)
        return pltpu.make_async_copy(
            self.y_hbm[REDUCE_CHUNKS[k][0]].at[:, :, lead, :, cols],
            self.slot(k, self.y_tall, self.y_wide),
            self.local_sem.at[1, k],
        )

    def x_copy(self, k):
        held, _, lead, cols, rows = self.piece(k)
        return remote(
            held.at[:, 1 - self.x, lead, rows, cols],
            self.from_x[k],
            self.x_sem.at[0, k],
            self.x_sem.at[1, k],
            (self.z, 1 - self.x, self.y, self.core),
        )

    def z_copies(self, k):
        held, _, lead, cols, rows = self.piece(k)
        copies = []
        for step in range(1, self.depth):
            there = lax.rem(self.z + step, self.depth)
            copies.append(
                remote(
                    held.at[there, self.x, lead, rows, cols],
                    self.from_z[k].at[step - 1],
                    self.z_sem.at[0, k, step - 1],
                    self.z_sem.at[1, k, step - 1],
                    (there, self.x, self.y, self.core),
                )
            )
        return copies

    def s_copy(self, k):
        rows = self.piece(k)[4]
        return remote(
            self.final[k].at[:, rows],
            self.swap[k],
            self.s_sem.at[0, k],
            self.s_sem.at[1, k],
            (self.z, self.x, 1 - self.y, self.core),
        )

    def f_copies(self, k):
        here = self.final[k].at[:, self.piece(k)[4]]
        peers = [(self.z, self.x, self.y, 1 - self.core)]
        if not REDUCE_CHUNKS[k][3]:
            peers += [(self.z, self.x, 1 - self.y, self.core), (self.z, self.x, 1 - self.y, 1 - self.core)]
        return [
            remote(here, here, self.f_sem.at[0, k, i], self.f_sem.at[1, k, i], peer) for i, peer in enumerate(peers)
        ]

    def store(self, k):
        tensor = REDUCE_CHUNKS[k][0]
        _, _, lead, cols, _ = self.piece(k)
        return pltpu.make_async_copy(self.final[k], self.outs[tensor].at[lead, :, cols], self.local_sem.at[2, k])

    def add_c(self, k):
        held, rows, _, cols, _ = self.piece(k)
        leads, lead = self.extents(k)
        half, slot = core_rows(rows, self.core), self.slot(k, self.c_tall, self.c_wide)
        add_blocks(
            (self.depth, 2, leads), lambda z, x, i: add_to(held.at[z, x, lead + i, half, cols], slot.at[z, x, i])
        )

    def add_y(self, k):
        held, _, _, cols, rows = self.piece(k)
        leads, lead = self.extents(k)
        slot = self.slot(k, self.y_tall, self.y_wide)
        add_blocks(
            (self.depth, 2, leads), lambda z, x, i: add_to(held.at[z, x, lead + i, rows, cols], slot.at[z, x, i])
        )

    def add_x(self, k):
        held, _, _, cols, rows = self.piece(k)
        leads, lead = self.extents(k)
        add_blocks(
            (self.depth, leads), lambda z, i: add_to(held.at[z, self.x, lead + i, rows, cols], self.from_x[k].at[z, i])
        )

    def add_z(self, k):
        held, _, _, cols, rows = self.piece(k)
        leads, lead = self.extents(k)

        def body(i):
            total = held[self.z, self.x, lead + i, rows, cols].astype(jnp.float32)
            for step in range(1, self.depth):
                total = total + self.from_z[k][step - 1, i].astype(jnp.float32)
            self.final[k][i, rows] = total.astype(jnp.bfloat16)

        add_blocks((leads,), body)

    def add_s(self, k):
        rows = self.piece(k)[4]
        add_blocks((self.extents(k)[0],), lambda i: add_to(self.final[k].at[i, rows], self.swap[k].at[i]))

    def add_squares(self, k):
        leads = self.extents(k)[0]
        lanes = lax.broadcasted_iota(jnp.int32, (8, 128), 1)
        subs = lax.broadcasted_iota(jnp.int32, (8, 128), 0)
        where = (subs == 1) & (lanes == REDUCE_CHUNKS[k][0])

        def body(i):
            block = self.final[k][i].astype(jnp.float32)
            total = jnp.sum(jnp.sum(block * block, axis=0, keepdims=True), axis=1, keepdims=True)
            self.squares[2 * self.depth + 2] += jnp.where(where, total, 0.0)

        add_blocks((leads,), body)

    STAGES = 9

    def stage(self, k, number):
        both = REDUCE_CHUNKS[k][3]
        if number == 0:
            self.c_copy(k).start()
        elif number == 1:
            self.c_copy(k).wait_recv()
            self.c_load(k).start()
        elif number == 2:
            self.c_load(k).wait()
            self.add_c(k)
            (self.x_copy if both else self.y_copy)(k).start()
        elif number == 3 and not both:
            self.y_copy(k).wait_recv()
            self.y_load(k).start()
        elif number == 4 and not both:
            self.y_load(k).wait()
            self.add_y(k)
            self.x_copy(k).start()
        elif number == 5:
            self.x_copy(k).wait_recv()
            self.add_x(k)
            for copy in self.z_copies(k):
                copy.start()
        elif number == 6:
            for copy in self.z_copies(k):
                copy.wait_recv()
            self.add_z(k)
            for copy in [self.s_copy(k)] if both else self.f_copies(k):
                copy.start()
        elif number == 7 and both:
            self.s_copy(k).wait_recv()
            self.s_copy(k).wait_send()
            self.add_s(k)
            for copy in self.f_copies(k):
                copy.start()
        elif number == 8:
            for copy in self.f_copies(k):
                copy.wait_recv()
            self.store(k).start()
            self.add_squares(k)

    def enable(self, tensor, leads_done=None):
        while self.enabled < self.count:
            chunk = REDUCE_CHUNKS[self.enabled]
            if chunk[0] != tensor or (leads_done is not None and chunk[1] + chunk[2] > leads_done):
                break
            self.enabled += 1

    def pump(self, ticks=1):
        for _ in range(ticks):
            if self.now < self.enabled or (self.enabled == self.count and self.now < self.count + self.STAGES):
                for number in reversed(range(self.STAGES)):
                    k = self.now - number
                    if 0 <= k < self.count:
                        self.stage(k, number)
                self.now += 1

    def finish(self, weight_squares, sums_out):
        while self.now < self.count + self.STAGES:
            self.pump()
        squares, depth = self.squares, self.depth
        subs = lax.broadcasted_iota(jnp.int32, (8, 128), 0)
        mine = squares.at[self.z * 2 + self.x]
        mine[...] = squares[2 * depth + 2] + jnp.where(subs == 0, weight_squares[...], 0.0)
        copies = [
            remote(
                mine,
                mine,
                self.q_sem.at[0, step],
                self.q_sem.at[1, step],
                (lax.rem(self.z + step, depth), self.x, self.y, self.core),
            )
            for step in range(1, depth)
        ]
        for copy in copies:
            copy.start()
        for copy in copies:
            copy.wait_recv()
        own = squares[self.x]
        for deep in range(1, depth):
            own = own + squares[deep * 2 + self.x]
        column = squares.at[2 * depth + self.x]
        column[...] = own
        across = remote(
            column, column, self.q_sem.at[0, 0], self.q_sem.at[1, 0], (self.z, 1 - self.x, self.y, self.core)
        )
        across.start()
        across.wait_recv()
        sums_out[...] = squares[2 * depth] + squares[2 * depth + 1]
        across.wait_send()
        for copy in copies:
            copy.wait_send()
        for k in range(self.count):
            self.c_copy(k).wait_send()
            if not REDUCE_CHUNKS[k][3]:
                self.y_copy(k).wait_send()
            self.x_copy(k).wait_send()
            for copy in self.z_copies(k) + self.f_copies(k):
                copy.wait_send()
            self.store(k).wait()


class NearFar:
    def __init__(self, refs, depth):
        self.near, self.far, self.total, self.near_send, self.near_recv, self.far_send, self.far_recv = refs
        self.depth = depth
        self.z, self.x, self.y, self.core = position()
        self.mine = self.x * 4 + self.y * 2 + self.core
        self.pay = self.near.at[self.mine]
        self.sent = []

    @staticmethod
    def scratch(width, depth):
        dma = pltpu.SemaphoreType.DMA
        return [
            pltpu.VMEM((8, 8, width), jnp.float32),
            pltpu.VMEM((depth, 8, width), jnp.float32),
            pltpu.VMEM((8, width), jnp.float32),
            dma((7,)),
            dma((7,)),
            dma((depth - 1,)),
            dma((depth - 1,)),
        ]

    def near_copies(self):
        copies = []
        for offset in range(1, 8):
            x = 1 - self.x if offset & 4 else self.x
            y = 1 - self.y if offset & 2 else self.y
            core = 1 - self.core if offset & 1 else self.core
            here = self.near.at[self.mine]
            copies.append(
                remote(here, here, self.near_send.at[offset - 1], self.near_recv.at[offset - 1], (self.z, x, y, core))
            )
        return copies

    def far_copies(self):
        here = self.far.at[self.z]
        return [
            remote(
                here,
                here,
                self.far_send.at[step - 1],
                self.far_recv.at[step - 1],
                (lax.rem(self.z + step, self.depth), self.x, self.y, self.core),
            )
            for step in range(1, self.depth)
        ]

    def begin(self):
        for copy in self.near_copies():
            copy.start()

    def stages(self):
        def middle():
            for copy in self.near_copies():
                copy.wait_recv()
            total = self.near[0]
            for slot in range(1, 8):
                total = total + self.near[slot]
            self.far[self.z] = total
            for copy in self.far_copies():
                copy.start()

        def last():
            for copy in self.far_copies():
                copy.wait_recv()
            total = self.far[0]
            for slot in range(1, self.depth):
                total = total + self.far[slot]
            self.total[...] = total

        return [middle, last]

    def close(self):
        for copy in self.near_copies() + self.far_copies():
            copy.wait_send()


class Split:
    def __init__(self, refs, depth):
        (self.pay, self.half, self.quad, self.deep, self.total, self.c_send, self.c_recv) = refs[:7]
        (self.q_send, self.q_recv, self.z_send, self.z_recv, self.g_send, self.g_recv) = refs[7:]
        self.depth = depth
        self.z, self.x, self.y, self.core = position()
        self.width = self.pay.shape[1]
        self.mine = self.x * 2 + self.y

    @staticmethod
    def scratch(width, depth):
        dma = pltpu.SemaphoreType.DMA
        return [
            pltpu.VMEM((8, width), jnp.float32),
            pltpu.VMEM((8, width // 2), jnp.float32),
            pltpu.VMEM((4, 8, width // 8), jnp.float32),
            pltpu.VMEM((depth, 8, width // 8), jnp.float32),
            pltpu.VMEM((8, width), jnp.float32),
            dma((2,)),
            dma((2,)),
            dma((3,)),
            dma((3,)),
            dma((depth - 1,)),
            dma((depth - 1,)),
            dma((3,)),
            dma((3,)),
        ]

    def half_of(self, core):
        return pl.ds(pl.multiple_of(core * (self.width // 2), 128), self.width // 2)

    def eighth_of(self, slot):
        start = self.core * (self.width // 2) + slot * (self.width // 8)
        return pl.ds(pl.multiple_of(start, 128), self.width // 8)

    def core_copy(self):
        return remote(
            self.pay.at[:, self.half_of(1 - self.core)],
            self.half,
            self.c_send.at[0],
            self.c_recv.at[0],
            (self.z, self.x, self.y, 1 - self.core),
        )

    def around(self):
        for offset in range(1, 4):
            x = 1 - self.x if offset & 2 else self.x
            y = 1 - self.y if offset & 1 else self.y
            yield offset - 1, x, y

    def quad_copies(self):
        return [
            remote(
                self.pay.at[:, self.eighth_of(x * 2 + y)],
                self.quad.at[self.mine],
                self.q_send.at[i],
                self.q_recv.at[i],
                (self.z, x, y, self.core),
            )
            for i, x, y in self.around()
        ]

    def deep_copies(self):
        here = self.deep.at[self.z]
        return [
            remote(
                here,
                here,
                self.z_send.at[step - 1],
                self.z_recv.at[step - 1],
                (lax.rem(self.z + step, self.depth), self.x, self.y, self.core),
            )
            for step in range(1, self.depth)
        ]

    def gather_copies(self):
        here = self.total.at[:, self.eighth_of(self.mine)]
        return [
            remote(here, here, self.g_send.at[i], self.g_recv.at[i], (self.z, x, y, self.core))
            for i, x, y in self.around()
        ]

    def last_copy(self):
        here = self.total.at[:, self.half_of(self.core)]
        return remote(here, here, self.c_send.at[1], self.c_recv.at[1], (self.z, self.x, self.y, 1 - self.core))

    def begin(self):
        self.core_copy().start()

    def stages(self):
        def first():
            self.core_copy().wait_recv()
            half = self.half_of(self.core)
            self.pay[:, half] = self.pay[:, half] + self.half[...]
            for copy in self.quad_copies():
                copy.start()
            self.quad[self.mine] = self.pay[:, self.eighth_of(self.mine)]

        def second():
            for copy in self.quad_copies():
                copy.wait_recv()
            self.deep[self.z] = (self.quad[0] + self.quad[1]) + (self.quad[2] + self.quad[3])
            for copy in self.deep_copies():
                copy.start()

        def third():
            for copy in self.deep_copies():
                copy.wait_recv()
            total = self.deep[0]
            for slot in range(1, self.depth):
                total = total + self.deep[slot]
            self.total[:, self.eighth_of(self.mine)] = total
            for copy in self.gather_copies():
                copy.start()

        def fourth():
            for copy in self.gather_copies():
                copy.wait_recv()
            self.last_copy().start()

        def fifth():
            self.last_copy().wait_recv()
            for copy in self.gather_copies() + [self.last_copy()]:
                copy.wait_send()

        return [first, second, third, fourth, fifth]

    def close(self):
        self.core_copy().wait_send()
        for copy in self.quad_copies() + self.deep_copies():
            copy.wait_send()


def interleave(stages, works):
    done = 0
    for i, stage in enumerate(stages):
        upto = (len(works) * (i + 1)) // len(stages)
        for work in works[done:upto]:
            work()
        done = upto
        stage()


HAT_A1, HAT_A2, HAT_A3, HAT_AS, HAT_B1, HAT_B2, HAT_B3, PATCH_A, PATCH_B, ACT_A2, ACT_B2, OUT_A = SAVED = range(12)
NORMS_MID, NORMS_OUT, SUM_A1, SUM_A2, SUM_A3, SUM_AS, SUM_B1, SUM_B2, SUM_B3, SUM_J = range(10)


def columns(j):
    return pl.ds(pl.multiple_of(j * 128, 128), 128)


def dot(a, b):
    return lax.dot_general(a, b, (((1,), (0,)), ((), ())), preferred_element_type=jnp.float32)


def dot_nt(a, b):
    return lax.dot_general(a, b, (((1,), (1,)), ((), ())), preferred_element_type=jnp.float32)


def sigmoid(v):
    return 0.5 * jnp.tanh(0.5 * v) + 0.5


def slope(v):
    s = sigmoid(v)
    return s * (1.0 + v * (1.0 - s))


class Plan:
    def __init__(self, shapes):
        self.sides = [shape[1] // 2 for shape in shapes]
        self.slots = [shape[0] for shape in shapes]
        self.valid = [side * side * slots for side, slots in zip(self.sides, self.slots)]
        sizes = [-(-valid // 8) * 8 for valid in self.valid]
        sizes[2] += -sum(sizes) % 128
        self.starts = [0, sizes[0], sizes[0] + sizes[1]]
        self.sizes = sizes
        self.rows = sum(sizes)

    def spans(self):
        return [slice(start, start + size) for start, size in zip(self.starts, self.sizes)]

    def shifts(self):
        out = np.zeros((9, self.rows, self.rows), np.float32)
        for side, slots, start in zip(self.sides, self.slots, self.starts):
            at = lambda i, j, n: start + (i * side + j) * slots + n
            for di in (-1, 0, 1):
                for dj in (-1, 0, 1):
                    for i in range(max(0, -di), min(side, side - di)):
                        for j in range(max(0, -dj), min(side, side - dj)):
                            for n in range(slots):
                                out[(di + 1) * 3 + dj + 1, at(i, j, n), at(i + di, j + dj, n)] = 1.0
        return out.astype(jnp.bfloat16)


def put_sums(plan, pairs, mask, pay, base, width):
    def body(j, carry):
        firsts, seconds = [0.0] * 3, [0.0] * 3
        for first, second in pairs(j):
            for g, span in enumerate(plan.spans()):
                live = first[span] * mask[span, :]
                firsts[g] = firsts[g] + jnp.sum(live, axis=0, keepdims=True)
                seconds[g] = seconds[g] + jnp.sum(live * second[span], axis=0, keepdims=True)
        zero = jnp.zeros((1, 128), jnp.float32)
        pay[:, columns(base + j)] = jnp.concatenate(firsts + seconds + [zero, zero], axis=0)
        return carry

    lax.fori_loop(0, width // 128, body, 0)


def put_scales(total, inverse, over, width, factor=1.0):
    def body(j, carry):
        at = columns(j)
        per = over[0:3, :] * factor
        means = total[0:3, at] * per
        variance = total[3:6, at] * per - means * means
        scales = lax.rsqrt(variance + EPSILON)
        zero = jnp.zeros((5, 128), jnp.float32)
        total[:, at] = jnp.concatenate([means, zero], axis=0)
        inverse[:, at] = jnp.concatenate([scales, zero], axis=0)
        return carry

    lax.fori_loop(0, width // 128, body, 0)


def by_group(plan, of):
    return jnp.concatenate([of(g, span) for g, span in enumerate(plan.spans())], axis=0)


def forward_names(depth):
    return (
        (NORMS_MID, NearFar.scratch(512, depth)),
        (NORMS_OUT, Split.scratch(2048, depth)),
        (SUM_A1, NearFar.scratch(512, depth)),
        (SUM_A2, NearFar.scratch(512, depth)),
        (SUM_AS, Split.scratch(2048, depth)),
        (SUM_A3, Split.scratch(2048, depth)),
        (SUM_B1, NearFar.scratch(512, depth)),
        (SUM_B2, NearFar.scratch(512, depth)),
        (SUM_B3, Split.scratch(2048, depth)),
    )


def forward_kernel(plan, depth, *refs):
    refs = list(refs)

    def take(count):
        taken = refs[:count]
        del refs[:count]
        return taken

    x_hbm, shift_hbm, mask, counts, norm_mid, norm_out = take(6)
    shards = take(7)
    out, inv_mid, inv_out, par_mid, par_out, over = take(6)
    weights_hbm = take(7)
    saved_hbm = dict(zip(SAVED, take(len(SAVED))))
    sums = {}
    for name, scratch in forward_names(depth):
        sums[name] = (NearFar if len(scratch) == 7 else Split)(take(len(scratch)), depth)
    x, shift = take(2)
    w_a1, w_a2, w_a3, w_as, w_b1, w_b2, w_b3 = weights = take(7)
    saved = dict(zip(SAVED, take(len(SAVED))))
    hid_a1, hid_mid, hid_out, hid_as, act = take(5)
    load_sem, save_sem, full_sem = take(3)
    gather = Gather(shards, weights, take(9), depth)

    loads = [
        pltpu.make_async_copy(src, dst, load_sem.at[i])
        for i, (src, dst) in enumerate(zip([x_hbm, shift_hbm], [x, shift]))
    ]
    gather.place_all()
    for copy in loads:
        copy.start()

    def keep(i):
        return pltpu.make_async_copy(weights[i], weights_hbm[i], full_sem.at[i])

    def ready(i):
        gather.ready(i)
        keep(i).start()

    def pump():
        gather.pump()

    def save(name):
        pltpu.make_async_copy(saved[name], saved_hbm[name], save_sem.at[SAVED.index(name)]).start()

    greet(depth)
    gather.begin()
    sums[NORMS_MID].pay[...] = norm_mid[...]
    sums[NORMS_MID].begin()
    sums[NORMS_OUT].pay[...] = norm_out[...]
    sums[NORMS_OUT].begin()
    norms_mid_stages = sums[NORMS_MID].stages()
    norms_out_stages = sums[NORMS_OUT].stages()
    rows = plan.rows

    loads[0].wait()
    norms_mid_stages[0]()
    norms_out_stages[0]()
    ready(0)

    def conv_a1(p, carry):
        hid_a1[p] = dot_nt(x[p], w_a1[...].reshape(512, -1))
        return carry

    lax.fori_loop(0, 2, conv_a1, 0)
    norms_mid_stages[1]()
    norms_out_stages[1]()
    pump()
    lax.fori_loop(2, 4, conv_a1, 0)
    par_mid[...] = sums[NORMS_MID].total[...]
    norms_out_stages[2]()

    total = sums[SUM_A1]
    put_sums(
        plan, lambda j: [(hid_a1[p, :, columns(j)],) * 2 for p in range(4)], mask, total.pay, 0, 512
    )
    total.pay[6:7, 0:128] = counts[...]
    total.begin()
    pump()
    total.stages()[0]()
    norms_out_stages[3]()
    pump()
    total.stages()[1]()
    norms_out_stages[4]()
    par_out[...] = sums[NORMS_OUT].total[...]

    pixels = total.total[6:7, 0:128]
    lanes = lax.broadcasted_iota(jnp.int32, (1, 128), 1)
    inverse_counts = [
        jnp.broadcast_to(1.0 / jnp.sum(jnp.where(lanes == g, pixels, 0.0), axis=1, keepdims=True), (1, 128))
        for g in range(3)
    ]
    over[...] = jnp.concatenate(inverse_counts + [jnp.zeros((5, 128), jnp.float32)], axis=0)
    put_scales(total.total, inv_mid.at[0], over, 512, 0.25)

    def normalized(hidden, total, inverse, hat, params, row, j):
        at = columns(j)
        xhat = by_group(plan, lambda g, span: (hidden[span] - total[g : g + 1, at]) * inverse[g : g + 1, at])
        hat[:, at] = xhat.astype(jnp.bfloat16)
        return xhat * params[row : row + 1, at] + params[row + 1 : row + 2, at]

    def activate(hidden_of, total, inverse, hat, params, row, target):
        def body(j, carry):
            v = normalized(hidden_of(j), total, inverse, hat, params, row, j)
            target[:, columns(j)] = (v * sigmoid(v)).astype(jnp.bfloat16)
            return carry

        lax.fori_loop(0, 4, body, 0)

    def activate_a1(p, carry):
        activate(
            lambda j: hid_a1[p, :, columns(j)],
            total.total,
            inv_mid.at[0],
            saved[HAT_A1].at[p],
            par_mid,
            0,
            act.at[p],
        )
        return carry

    lax.fori_loop(0, 2, activate_a1, 0)
    pump()
    lax.fori_loop(2, 4, activate_a1, 0)
    save(HAT_A1)

    loads[1].wait()
    patch = saved[PATCH_A]
    for tap in range(9):
        a, b = tap // 3, tap % 3
        plane = (0 if a == 1 else 2) + (0 if b == 1 else 1)
        matrix = (0 if a == 0 else 1) * 3 + (0 if b == 0 else 1)
        if matrix == 4:
            patch[tap] = act[plane]
        else:
            patch[tap] = dot(shift[matrix], act[plane]).astype(jnp.bfloat16)
        if tap == 4:
            pump()
    save(PATCH_A)
    ready(1)

    def spatial(patch, weight):
        hid_mid[...] = dot_nt(patch[0], weight[:, :, 0].reshape(512, 512))

        def body(tap, carry):
            hid_mid[...] += dot_nt(patch[tap], weight[:, :, tap].reshape(512, 512))
            return carry

        lax.fori_loop(1, 9, body, 0)

    spatial(patch, w_a2)

    def conv_as(d, carry):
        at = pl.ds(pl.multiple_of(d * 256, 256), 256)
        hid_as[:, at] = dot(x[0], w_as[d // 2, lax.rem(d, 2)].reshape(1024, 256))
        return carry

    def shortcut():
        ready(3)
        lax.fori_loop(0, 8, conv_as, 0)
        put_sums(plan, lambda j: [(hid_as[:, columns(j)],) * 2], mask, sums[SUM_AS].pay, 0, 2048)
        sums[SUM_AS].begin()

    as_stages = sums[SUM_AS].stages()

    def mid_sums(total, name_index, works):
        put_sums(plan, lambda j: [(hid_mid[:, columns(j)],) * 2], mask, total.pay, 0, 512)
        total.begin()
        interleave(total.stages(), works)
        put_scales(total.total, inv_mid.at[name_index], over, 512)

    mid_sums(sums[SUM_A2], 1, [pump, pump])
    activate(
        lambda j: hid_mid[:, columns(j)], sums[SUM_A2].total, inv_mid.at[1], saved[HAT_A2], par_mid, 2, saved[ACT_A2]
    )
    save(HAT_A2)
    save(ACT_A2)

    def expand(act_ref, weight):
        def body(d, carry):
            at = pl.ds(pl.multiple_of(d * 256, 256), 256)
            hid_out[:, at] = dot(act_ref[...], weight[d // 2, lax.rem(d, 2)].reshape(512, 256))
            return carry

        lax.fori_loop(0, 8, body, 0)

    def out_sums(total, name_index, works):
        put_sums(plan, lambda j: [(hid_out[:, columns(j)],) * 2], mask, total.pay, 0, 2048)
        total.begin()
        interleave(total.stages(), works)
        put_scales(total.total, inv_out.at[name_index], over, 2048)

    shortcut()
    as_stages[0]()
    ready(2)
    as_stages[1]()
    expand(saved[ACT_A2], w_a3)
    as_stages[2]()
    out_sums(sums[SUM_A3], 0, [as_stages[3], pump, as_stages[4], pump, pump])
    put_scales(sums[SUM_AS].total, inv_out.at[1], over, 2048)

    def join(j, carry):
        at = columns(j)
        v = normalized(hid_out[:, at], sums[SUM_A3].total, inv_out.at[0], saved[HAT_A3], par_out, 0, j)
        v = v + normalized(hid_as[:, at], sums[SUM_AS].total, inv_out.at[1], saved[HAT_AS], par_out, 2, j)
        saved[OUT_A][:, at] = (v * sigmoid(v) * mask[...]).astype(jnp.bfloat16)
        return carry

    lax.fori_loop(0, 16, join, 0)
    for name in (HAT_A3, HAT_AS, OUT_A):
        save(name)

    ready(4)
    hid_mid[...] = dot_nt(saved[OUT_A][...], w_b1[...].reshape(512, -1))
    mid_sums(sums[SUM_B1], 2, [pump, pump])
    activate(
        lambda j: hid_mid[:, columns(j)], sums[SUM_B1].total, inv_mid.at[2], saved[HAT_B1], par_mid, 4, act.at[0]
    )
    save(HAT_B1)

    def patches(tap, carry):
        saved[PATCH_B][tap] = dot(shift[tap], act[0]).astype(jnp.bfloat16)
        return carry

    lax.fori_loop(0, 9, patches, 0)
    save(PATCH_B)
    ready(5)
    spatial(saved[PATCH_B], w_b2)
    mid_sums(sums[SUM_B2], 3, [pump, pump])
    activate(
        lambda j: hid_mid[:, columns(j)], sums[SUM_B2].total, inv_mid.at[3], saved[HAT_B2], par_mid, 6, saved[ACT_B2]
    )
    save(HAT_B2)
    save(ACT_B2)
    ready(6)
    expand(saved[ACT_B2], w_b3)
    out_sums(sums[SUM_B3], 2, [])

    def finish(j, carry):
        at = columns(j)
        v = normalized(hid_out[:, at], sums[SUM_B3].total, inv_out.at[2], saved[HAT_B3], par_out, 4, j)
        v = v + saved[OUT_A][:, at].astype(jnp.float32)
        out[:, at] = (v * sigmoid(v) * mask[...]).astype(jnp.bfloat16)
        return carry

    lax.fori_loop(0, 16, finish, 0)
    save(HAT_B3)
    for total in sums.values():
        total.close()
    for i, name in enumerate(SAVED):
        pltpu.make_async_copy(saved[name], saved_hbm[name], save_sem.at[i]).wait()
    gather.close()
    for i in range(7):
        keep(i).wait()


def saved_shapes(rows):
    bf16 = jnp.bfloat16
    return (
        ((4, rows, 512), bf16),
        ((rows, 512), bf16),
        ((rows, 2048), bf16),
        ((rows, 2048), bf16),
        ((rows, 512), bf16),
        ((rows, 512), bf16),
        ((rows, 2048), bf16),
        ((9, rows, 512), bf16),
        ((9, rows, 512), bf16),
        ((rows, 512), bf16),
        ((rows, 512), bf16),
        ((rows, 2048), bf16),
    )


WHOLE = pl.BlockSpec(memory_space=pltpu.VMEM)
VMEM_LIMIT = 62 * 1024 * 1024


def run_forward(plan, depth, x, shifts, mask, counts, norm_mid, norm_out, shards):
    rows, f32, bf16 = plan.rows, jnp.float32, jnp.bfloat16
    dma = pltpu.SemaphoreType.DMA
    scratch = []
    for _, pieces in forward_names(depth):
        scratch += pieces
    scratch += [pltpu.VMEM(x.shape, bf16), pltpu.VMEM(shifts.shape, bf16)]
    fulls = [jax.ShapeDtypeStruct((depth, 2, *shard.shape), bf16) for shard in shards]
    scratch += [pltpu.VMEM(full.shape, bf16) for full in fulls]
    scratch += [pltpu.VMEM(shape, kind) for shape, kind in saved_shapes(rows)]
    scratch += [
        pltpu.VMEM((4, rows, 512), f32),
        pltpu.VMEM((rows, 512), f32),
        pltpu.VMEM((rows, 2048), f32),
        pltpu.VMEM((rows, 2048), f32),
        pltpu.VMEM((4, rows, 512), bf16),
        dma((2,)),
        dma((len(SAVED),)),
        dma((7,)),
    ]
    scratch += Gather.scratch(depth)
    small = [
        jax.ShapeDtypeStruct((rows, 2048), bf16),
        jax.ShapeDtypeStruct((4, 8, 512), f32),
        jax.ShapeDtypeStruct((3, 8, 2048), f32),
        jax.ShapeDtypeStruct((8, 512), f32),
        jax.ShapeDtypeStruct((8, 2048), f32),
        jax.ShapeDtypeStruct((8, 128), f32),
    ]
    return pl.pallas_call(
        functools.partial(forward_kernel, plan, depth),
        out_shape=small + fulls + [jax.ShapeDtypeStruct(shape, kind) for shape, kind in saved_shapes(rows)],
        in_specs=[ANY, ANY] + [WHOLE] * 4 + [ANY] * 7,
        out_specs=[WHOLE] * 6 + [ANY] * 7 + [ANY] * len(SAVED),
        scratch_shapes=scratch,
        compiler_params=pltpu.CompilerParams(collective_id=0, has_side_effects=True, vmem_limit_bytes=VMEM_LIMIT),
    )(x, shifts, mask, counts, norm_mid, norm_out, *shards)


def backward_names(depth):
    return (
        (SUM_B3, Split.scratch(2048, depth)),
        (SUM_B2, NearFar.scratch(512, depth)),
        (SUM_B1, NearFar.scratch(512, depth)),
        (SUM_J, Split.scratch(4096, depth)),
        (SUM_A2, NearFar.scratch(512, depth)),
        (SUM_A1, NearFar.scratch(512, depth)),
    )


def backward_kernel(plan, depth, *refs):
    refs = list(refs)

    def take(count):
        taken = refs[:count]
        del refs[:count]
        return taken

    x_hbm, shift_hbm, cot_hbm, mask, weight_squares, inv_mid, inv_out, par_mid, par_out, over = take(10)
    saved_hbm = dict(zip(SAVED, take(len(SAVED))))
    weights_hbm = take(7)
    dx_hbm, pgrad_mid, pgrad_b3, pgrad_j, squares_out = take(5)
    gradients_hbm, c_hbm, y_hbm = take(7), take(7), take(7)
    sums = {}
    for name, scratch in backward_names(depth):
        sums[name] = (NearFar if len(scratch) == 7 else Split)(take(len(scratch)), depth)
    x, shift, cot = take(3)
    w_a1, w_a2, w_a3, w_as, w_b1, w_b2, w_b3 = weights = take(7)
    kept = [name for name in SAVED if name != PATCH_B]
    saved = dict(zip(kept, take(len(kept))))
    saved[PATCH_B] = saved[PATCH_A]
    dz, dact, dh_mid, flip = take(4)
    load_sem, saved_sem, dx_sem = take(3)
    dh_a, dh_b = cot, saved[HAT_B3]
    planes = [saved[HAT_AS].at[:, pl.ds(plane * 512, 512)] for plane in range(4)]
    reduce = Reduce(weights, gradients_hbm, c_hbm, y_hbm, refs, depth)
    reduce.squares[2 * depth + 2] = jnp.zeros((8, 128), jnp.float32)

    def pump():
        reduce.pump()

    def loading(name):
        return pltpu.make_async_copy(saved_hbm[name], saved[name], saved_sem.at[SAVED.index(name)])

    loads = [
        pltpu.make_async_copy(src, dst, load_sem.at[i])
        for i, (src, dst) in enumerate(zip([x_hbm, shift_hbm, cot_hbm, *weights_hbm], [x, shift, cot, *weights]))
    ]
    first = (HAT_B3, OUT_A)
    for name in first:
        loading(name).start()
    loads[2].start()
    order = (HAT_B2, ACT_B2, HAT_B1, PATCH_B, HAT_A3, HAT_AS, HAT_A2, ACT_A2, HAT_A1)
    loads[9].start()
    for name in order[:4]:
        loading(name).start()
    for i in (1, 8, 7):
        loads[i].start()
    for name in order[4:]:
        loading(name).start()
    for i in (5, 6, 4, 0, 3):
        loads[i].start()

    greet(depth)

    def quarter(d):
        return pl.ds(pl.multiple_of(d * 256, 256), 256)

    def affine(hat, params, row, at):
        return hat[:, at].astype(jnp.float32) * params[row : row + 1, at] + params[row + 1 : row + 2, at]

    def norm_back(dz_of, hat, total, base, inverse, params, row, target, blocks):
        def body(j, carry):
            at = columns(j)
            sums_at = columns(base + j)
            gain = params[row : row + 1, at]
            value, xhat = dz_of(j), hat[:, at].astype(jnp.float32)

            def of(g, span):
                first = total[g : g + 1, sums_at] * over_of(g)
                second = total[3 + g : 4 + g, sums_at] * over_of(g)
                return (gain * inverse[g : g + 1, at]) * (value[span] - first - xhat[span] * second)

            target[:, at] = (by_group(plan, of) * mask[...]).astype(jnp.bfloat16)
            return carry

        lax.fori_loop(0, blocks, body, 0)

    scale = [1.0]

    def over_of(g):
        return over[g : g + 1, :] * scale[0]

    for name in first:
        loading(name).wait()
    loads[2].wait()

    def out_pairs(j):
        at = columns(j)
        v = affine(saved[HAT_B3], par_out, 4, at) + saved[OUT_A][:, at].astype(jnp.float32)
        value = cot[:, at].astype(jnp.float32) * mask[...] * slope(v)
        dz[:, at] = value
        return [(value, saved[HAT_B3][:, at].astype(jnp.float32))]

    total = sums[SUM_B3]
    put_sums(plan, out_pairs, mask, total.pay, 0, 2048)
    total.begin()
    for i in (9, 1, 8, 7):
        loads[i].wait()
    for name in order[:4]:
        loading(name).wait()
    flip[0:512] = saved[ACT_B2][...].T
    interleave(total.stages(), [])
    pgrad_b3[...] = total.total[...]
    norm_back(lambda j: dz[:, columns(j)], saved[HAT_B3], total.total, 0, inv_out.at[2], par_out, 4, dh_a, 16)

    def contract(dh, weight):
        dact[...] = dot_nt(dh[:, 0:256], weight[0, 0].reshape(512, 256))

        def body(d, carry):
            dact[...] += dot_nt(dh[:, quarter(d)], weight[d // 2, lax.rem(d, 2)].reshape(512, 256))
            return carry

        lax.fori_loop(1, 8, body, 0)

    def expand_term(lhs, dh, weight, first_slot, last_slot):
        def body(d, carry):
            shape = weight.shape[2:]
            weight[d // 2, lax.rem(d, 2)] = dot(lhs, dh[:, quarter(d)]).astype(jnp.bfloat16).reshape(shape)
            return carry

        lax.fori_loop(first_slot, last_slot, body, 0)

    def mid_pairs(hat, row):
        def pairs(j):
            at = columns(j)
            value = dact[:, at] * slope(affine(saved[hat], par_mid, row, at))
            dact[:, at] = value
            return [(value, saved[hat][:, at].astype(jnp.float32))]

        return pairs

    def mid_norm(name, hat, index, row, works):
        total = sums[name]
        put_sums(plan, mid_pairs(hat, row), mask, total.pay, 0, 512)
        total.begin()
        interleave(total.stages(), works)
        pgrad_mid[index] = total.total[...]
        norm_back(lambda j: dact[:, columns(j)], saved[hat], total.total, 0, inv_mid.at[index], par_mid, row, dh_mid, 4)

    contract(dh_a, w_b3)

    def third_term(part):
        def work():
            expand_term(flip[0:512, :], dh_a, w_b3, 4 * part, 4 * part + 4)
            if part:
                reduce.enable(6)
                pump()

        return work

    mid_norm(SUM_B2, HAT_B2, 3, 6, [third_term(0), third_term(1)])

    def spread(tap, carry):
        part = dot(
            dot(shift[8 - tap], dh_mid[...]).astype(jnp.bfloat16), w_b2[:, :, tap].reshape(512, 512)
        )
        dact[...] = part + jnp.where(tap == 0, 0.0, dact[...])
        return carry

    lax.fori_loop(0, 3, spread, 0)
    pump()
    lax.fori_loop(3, 6, spread, 0)
    pump()
    lax.fori_loop(6, 9, spread, 0)
    flip[0:512] = dh_mid[...].T

    def spatial_term(weight, patch, first_tap, last_tap, tensor):
        def work():
            def body(tap, carry):
                weight[:, :, tap] = dot(flip[0:512, :], patch[tap]).astype(jnp.bfloat16).reshape(depth, 2, 64, 512)
                return carry

            lax.fori_loop(first_tap, last_tap, body, 0)
            reduce.enable(tensor, last_tap)
            pump()

        return work

    mid_norm(
        SUM_B1,
        HAT_B1,
        2,
        4,
        [spatial_term(w_b2, saved[PATCH_B], 0, 3, 5), spatial_term(w_b2, saved[PATCH_B], 3, 6, 5)],
    )
    spatial_term(w_b2, saved[PATCH_B], 6, 9, 5)()
    loading(PATCH_A).start()

    def residual(d, carry):
        at = quarter(d)
        dz[:, at] = dz[:, at] + dot(dh_mid[...], w_b1[:, :, 0, :, at].reshape(512, 256))
        return carry

    lax.fori_loop(0, 4, residual, 0)
    pump()
    lax.fori_loop(4, 8, residual, 0)
    pump()
    for name in order[4:]:
        loading(name).wait()

    def join_pairs(j):
        at = columns(j)
        v = affine(saved[HAT_A3], par_out, 0, at) + affine(saved[HAT_AS], par_out, 2, at)
        value = dz[:, at] * mask[...] * slope(v)
        dz[:, at] = value
        return [(value, saved[HAT_A3][:, at].astype(jnp.float32))]

    total = sums[SUM_J]
    put_sums(plan, join_pairs, mask, total.pay, 0, 2048)
    put_sums(
        plan, lambda j: [(dz[:, columns(j)], saved[HAT_AS][:, columns(j)].astype(jnp.float32))], mask, total.pay, 16, 2048
    )
    total.begin()
    flip[0:512] = dh_mid[...].T

    def first_term(part):
        def work():
            def body(d, carry):
                at = quarter(d)
                value = dot(flip[0:512, :], saved[OUT_A][:, at]).astype(jnp.bfloat16)
                w_b1[:, :, 0, :, at] = value.reshape(depth, 2, 64, 256)
                return carry

            lax.fori_loop(2 * part, 2 * part + 2, body, 0)
            if part == 3:
                reduce.enable(4)
            pump()

        return work

    interleave(total.stages(), [first_term(part) for part in range(4)])
    pgrad_j[...] = total.total[...]
    norm_back(lambda j: dz[:, columns(j)], saved[HAT_A3], total.total, 0, inv_out.at[0], par_out, 0, dh_a, 16)
    pump()
    norm_back(lambda j: dz[:, columns(j)], saved[HAT_AS], total.total, 16, inv_out.at[1], par_out, 2, dh_b, 16)
    for i in (5, 6, 4, 0, 3):
        loads[i].wait()

    pump()
    contract(dh_a, w_a3)
    pump()
    flip[0:512] = saved[ACT_A2][...].T

    def third_term_a():
        expand_term(flip[0:512, :], dh_a, w_a3, 0, 8)
        reduce.enable(2)
        pump()

    def shortcut():
        even = dz.at[:, 0:1024]
        even[...] = dot_nt(dh_b[:, 0:256], w_as[0, 0].reshape(1024, 256))

        def body(d, carry):
            even[...] += dot_nt(dh_b[:, quarter(d)], w_as[d // 2, lax.rem(d, 2)].reshape(1024, 256))
            return carry

        lax.fori_loop(1, 8, body, 0)

        def keep(j, carry):
            value = even[:, columns(j)]
            high = value.astype(jnp.bfloat16)
            saved[OUT_A][:, columns(j)] = high
            saved[OUT_A][:, columns(8 + j)] = (value - high.astype(jnp.float32)).astype(jnp.bfloat16)
            return carry

        lax.fori_loop(0, 8, keep, 0)

    mid_norm(SUM_A2, HAT_A2, 1, 2, [third_term_a, shortcut])

    loading(PATCH_A).wait()
    flip[...] = x[0].T
    expand_term(flip[...], dh_b, w_as, 0, 8)
    reduce.enable(3)
    for plane in range(4):
        at = slice(plane * 512, plane * 512 + 512)
        begun = False
        for tap in range(9):
            a, b = tap // 3, tap % 3
            if plane != (0 if a == 1 else 2) + (0 if b == 1 else 1):
                continue
            matrix = (2 if a == 0 else 1) * 3 + (2 if b == 0 else 1)
            moved = dh_mid[...] if matrix == 4 else dot(shift[matrix], dh_mid[...]).astype(jnp.bfloat16)
            part = dot(moved, w_a2[:, :, tap].reshape(512, 512))
            if begun:
                dz[:, at] += part
            else:
                dz[:, at] = part
            begun = True
        pump()

    def plane_pairs(j):
        at = columns(j)
        pairs = []
        for plane in range(4):
            wide = columns(4 * plane + j)
            xhat = saved[HAT_A1][plane, :, at].astype(jnp.float32)
            v = xhat * par_mid[0:1, at] + par_mid[1:2, at]
            value = dz[:, wide] * slope(v)
            dz[:, wide] = value
            pairs.append((value, xhat))
        return pairs

    total = sums[SUM_A1]
    put_sums(plan, plane_pairs, mask, total.pay, 0, 512)
    total.begin()
    flip[0:512] = dh_mid[...].T
    stages = total.stages()
    spatial_term(w_a2, saved[PATCH_A], 0, 3, 1)()
    stages[0]()
    spatial_term(w_a2, saved[PATCH_A], 3, 6, 1)()
    stages[1]()
    spatial_term(w_a2, saved[PATCH_A], 6, 9, 1)()
    pgrad_mid[0] = total.total[...]
    scale[0] = 0.25
    for plane in range(4):
        norm_back(
            lambda j, plane=plane: dz[:, columns(4 * plane + j)],
            saved[HAT_A1].at[plane],
            total.total,
            0,
            inv_mid.at[0],
            par_mid,
            0,
            planes[plane],
            4,
        )

    def input_gradient(p):
        target = (dh_a if p < 2 else dh_b).at[:, pl.ds((p % 2) * 1024, 1024)]
        value = dot(planes[p][...], w_a1[...].reshape(512, -1))
        if p == 0:
            value = value + saved[OUT_A][:, 0:1024].astype(jnp.float32)
            value = value + saved[OUT_A][:, 1024:2048].astype(jnp.float32)
        target[...] = value.astype(jnp.bfloat16)
        copy = pltpu.make_async_copy(target, dx_hbm.at[p], dx_sem.at[p])
        copy.start()
        return copy

    copies = []
    for p in range(4):
        copies.append(input_gradient(p))
        pump()

    def last_term(c, carry):
        at = quarter(c)
        total = jnp.zeros((512, 256), jnp.float32)
        for p in range(4):
            total = total + lax.dot_general(
                planes[p][...], x[p, :, at], (((0,), (0,)), ((), ())), preferred_element_type=jnp.float32
            )
        w_a1[:, :, 0, :, at] = total.astype(jnp.bfloat16).reshape(depth, 2, 64, 256)
        return carry

    lax.fori_loop(0, 4, last_term, 0)
    reduce.enable(0)
    reduce.finish(weight_squares, squares_out)
    for copy in copies:
        copy.wait()
    for total in sums.values():
        total.close()


def run_backward(plan, depth, x, shifts, cot, mask, weight_squares, small, saved, fulls):
    rows, f32, bf16 = plan.rows, jnp.float32, jnp.bfloat16
    dma = pltpu.SemaphoreType.DMA
    scratch = []
    for _, pieces in backward_names(depth):
        scratch += pieces
    scratch += [pltpu.VMEM(value.shape, bf16) for value in (x, shifts, cot)]
    scratch += [pltpu.VMEM(full.shape, bf16) for full in fulls]
    scratch += [pltpu.VMEM(shape, kind) for name, (shape, kind) in zip(SAVED, saved_shapes(rows)) if name != PATCH_B]
    scratch += [
        pltpu.VMEM((rows, 2048), f32),
        pltpu.VMEM((rows, 512), f32),
        pltpu.VMEM((rows, 512), bf16),
        pltpu.VMEM((1024, rows), bf16),
        dma((10,)),
        dma((len(SAVED),)),
        dma((4,)),
    ]
    shapes = [full.shape for full in fulls]
    scratch += Reduce.scratch(shapes, depth)

    def part(shape, over):
        return jax.ShapeDtypeStruct((*shape[:3], shape[3] // over, shape[4]), bf16)

    outs = pl.pallas_call(
        functools.partial(backward_kernel, plan, depth),
        out_shape=[
            jax.ShapeDtypeStruct(x.shape, bf16),
            jax.ShapeDtypeStruct((4, 8, 512), f32),
            jax.ShapeDtypeStruct((8, 2048), f32),
            jax.ShapeDtypeStruct((8, 4096), f32),
            jax.ShapeDtypeStruct((8, 128), f32),
        ]
        + [jax.ShapeDtypeStruct(shape[2:], bf16) for shape in shapes]
        + [part(shape, 2) for shape in shapes]
        + [part(shape, 4) for shape in shapes],
        in_specs=[ANY] * 3 + [WHOLE] * 7 + [ANY] * len(SAVED) + [ANY] * 7,
        out_specs=[ANY] + [WHOLE] * 4 + [ANY] * 21,
        scratch_shapes=scratch,
        compiler_params=pltpu.CompilerParams(collective_id=1, has_side_effects=True, vmem_limit_bytes=VMEM_LIMIT),
    )(x, shifts, cot, mask, weight_squares, *small, *saved, *fulls)
    return outs[:12]


def on_device(
    input_160,
    input_224,
    input_288,
    cotangent_160,
    cotangent_224,
    cotangent_288,
    live_counts,
    conv_a1,
    norm_a1,
    conv_a2,
    norm_a2,
    conv_a3,
    norm_a3,
    conv_as,
    norm_as,
    conv_b1,
    norm_b1,
    conv_b2,
    norm_b2,
    conv_b3,
    norm_b3,
):
    if conv_a1.shape[1] % 64 or conv_a3.shape[1] % 128 or lax.axis_size(REP) != 4:
        return plain_on_device(
            input_160,
            input_224,
            input_288,
            cotangent_160,
            cotangent_224,
            cotangent_288,
            live_counts,
            conv_a1,
            norm_a1,
            conv_a2,
            norm_a2,
            conv_a3,
            norm_a3,
            conv_as,
            norm_as,
            conv_b1,
            norm_b1,
            conv_b2,
            norm_b2,
            conv_b3,
            norm_b3,
        )
    depth = lax.axis_size(DP) // 2
    inputs = (input_160, input_224, input_288)
    plan = Plan([value.shape for value in inputs])
    shards = (
        conv_a1.T[None],
        jnp.transpose(conv_a2, (0, 1, 3, 2)).reshape(9, conv_a2.shape[3], conv_a2.shape[2]),
        conv_a3.reshape(2, -1, conv_a3.shape[1]),
        conv_as.reshape(4, -1, conv_as.shape[1]),
        conv_b1.T[None],
        jnp.transpose(conv_b2, (0, 1, 3, 2)).reshape(9, conv_b2.shape[3], conv_b2.shape[2]),
        conv_b3.reshape(2, -1, conv_b3.shape[1]),
    )
    local_weights = (conv_a1, conv_a2, conv_a3, conv_as, conv_b1, conv_b2, conv_b3)

    planes, cotangents, masks, live_pixels = [], [], [], []
    for g, (value, cotangent) in enumerate(
        zip(inputs, (cotangent_160, cotangent_224, cotangent_288))
    ):
        side, slots, fill = plan.sides[g], plan.slots[g], plan.sizes[g] - plan.valid[g]
        split = jnp.transpose(value, (1, 2, 0, 3)).reshape(side, 2, side, 2, slots, -1)
        split = jnp.transpose(split, (1, 3, 0, 2, 4, 5)).reshape(4, plan.valid[g], -1)
        planes.append(jnp.pad(split, ((0, 0), (0, fill), (0, 0))))
        cotangents.append(
            jnp.pad(jnp.transpose(cotangent, (1, 2, 0, 3)).reshape(plan.valid[g], -1), ((0, fill), (0, 0)))
        )
        row = jnp.arange(plan.sizes[g])
        live = (lax.rem(row, slots) < live_counts[0, g]) & (row < plan.valid[g])
        masks.append(jnp.broadcast_to(live.astype(jnp.float32)[:, None], (plan.sizes[g], 128)))
        live_pixels.append((live_counts[0, g] * (side * side)).astype(jnp.float32))
    x = jnp.concatenate(planes, axis=1)
    cot = jnp.concatenate(cotangents, axis=0)
    mask = jnp.concatenate(masks, axis=0)
    counts = jnp.pad(jnp.stack(live_pixels), (0, 125)).reshape(1, 128)

    def own_place(norms, width):
        rows = jnp.concatenate(norms, axis=0).astype(jnp.float32)
        rows = jnp.pad(rows, ((0, 8 - rows.shape[0]), (0, 0)))
        rows = jnp.where(lax.axis_index(REP) == 0, rows, 0.0)
        start = lax.axis_index(DP) * rows.shape[1]
        return lax.dynamic_update_slice(jnp.zeros((8, width), jnp.float32), rows, (0, start))

    mid_local, out_local = norm_a1.shape[1], norm_a3.shape[1]
    mid_width, out_width = mid_local * 2 * depth, out_local * 2 * depth
    norm_mid = own_place((norm_a1, norm_a2, norm_b1, norm_b2), mid_width)
    norm_out = own_place((norm_a3, norm_as, norm_b3), out_width)
    shifts = jnp.asarray(plan.shifts())

    out, *results = run_forward(plan, depth, x, shifts, mask, counts, norm_mid, norm_out, shards)
    small, fulls, saved = results[:5], results[5:12], results[12:]
    square_row = jnp.stack([jnp.sum(jnp.square(weight.astype(jnp.float32))) for weight in local_weights])
    square_row = jnp.pad(square_row.reshape(1, 7), ((0, 7), (0, 121)))
    dx, pgrad_mid, pgrad_b3, pgrad_j, squares, *totals = run_backward(
        plan, depth, x, shifts, cot, mask, square_row, small, saved, fulls
    )

    def spatial_out(total):
        return jnp.transpose(total, (0, 2, 1)).reshape(conv_a2.shape).astype(jnp.float32)

    gradients = (
        totals[0][0].T.astype(jnp.float32),
        spatial_out(totals[1]),
        totals[2].reshape(conv_a3.shape).astype(jnp.float32),
        totals[3].reshape(conv_as.shape).astype(jnp.float32),
        totals[4][0].T.astype(jnp.float32),
        spatial_out(totals[5]),
        totals[6].reshape(conv_b3.shape).astype(jnp.float32),
    )

    def norm_gradient(sums, local):
        both = jnp.stack([sums[3] + sums[4] + sums[5], sums[0] + sums[1] + sums[2]])
        return lax.dynamic_slice_in_dim(both, lax.axis_index(DP) * local, local, 1)

    norm_gradients = (
        norm_gradient(pgrad_mid[0], mid_local),
        norm_gradient(pgrad_mid[1], mid_local),
        norm_gradient(pgrad_j[:, :out_width], out_local),
        norm_gradient(pgrad_j[:, out_width:], out_local),
        norm_gradient(pgrad_mid[2], mid_local),
        norm_gradient(pgrad_mid[3], mid_local),
        norm_gradient(pgrad_b3, out_local),
    )
    weight_totals, grad_totals = squares[0, :7], squares[1, :7]
    weight_norm = jnp.sqrt(weight_totals)
    grad_norm = jnp.sqrt(grad_totals)
    trust_ratio = weight_norm / (grad_norm + DECAY_RATE * weight_norm)
    scaled = [
        trust_ratio[i] * (gradients[i] + DECAY_RATE * local_weights[i].astype(jnp.float32)) for i in range(7)
    ]
    outputs, grad_inputs = [], []
    for g in range(3):
        side, slots, start = plan.sides[g], plan.slots[g], plan.starts[g]
        rows = out[start : start + plan.valid[g]].reshape(side, side, slots, -1)
        outputs.append(jnp.transpose(rows, (2, 0, 1, 3)))
        split = dx[:, start : start + plan.valid[g]].reshape(2, 2, side, side, slots, -1)
        split = jnp.transpose(split, (2, 0, 3, 1, 4, 5)).reshape(2 * side, 2 * side, slots, -1)
        grad_inputs.append(jnp.transpose(split, (2, 0, 1, 3)))
    pairs = [piece for pair in zip(gradients, norm_gradients) for piece in pair]
    return (*outputs, *grad_inputs, *pairs, *scaled, jnp.stack([weight_totals, grad_totals]))


def solution(mesh):
    by_image, by_column = P((DP, REP), None, None, None), P(None, DP)
    by_channel = P(None, None, None, DP)
    weights = [by_column, by_column, by_channel] + [by_column] * 7 + [by_channel] + [by_column] * 3
    kernels = [by_column, by_channel] + [by_column] * 3 + [by_channel, by_column]
    return jax.shard_map(
        on_device,
        mesh=mesh,
        in_specs=(*[by_image] * 6, P((DP, REP), None), *weights),
        out_specs=(*[by_image] * 6, *weights, *kernels, P()),
        check_vma=False,
    )
```

```python
import functools

import jax
import jax.numpy as jnp
import numpy as np
from jax import lax
from jax.experimental import pallas as pl
from jax.experimental.pallas import tpu as pltpu
from jax.sharding import PartitionSpec as P

DP, REP = "dp", "rep"
EPSILON = 1e-05
DECAY_RATE = 5e-05


def silu_slope(values):
    sigmoid = jax.nn.sigmoid(values)
    return sigmoid * (1.0 + values * (1.0 - sigmoid))


def pointwise(inputs, weight):
    return jnp.tensordot(inputs, weight, 1, preferred_element_type=jnp.float32)


def pointwise_back(upstream, weight):
    return jnp.tensordot(upstream, weight, ((3,), (1,)), preferred_element_type=jnp.float32)


def weight_term(inputs, upstream):
    return jnp.tensordot(inputs, upstream, ((0, 1, 2),) * 2, preferred_element_type=jnp.float32)


def summed_terms(inputs, upstream):
    running = weight_term(inputs[0], upstream[0])
    for group_member in (1, 2):
        running = running + weight_term(inputs[group_member], upstream[group_member])
    return running


def patches(inputs, stride):
    padded = jnp.pad(inputs, ((0, 0), (1, 1), (1, 1), (0, 0)))
    extent = inputs.shape[1]
    pieces = []
    for offset_row in range(3):
        for offset_col in range(3):
            pieces.append(
                padded[
                    :,
                    offset_row : offset_row + extent : stride,
                    offset_col : offset_col + extent : stride,
                    :,
                ]
            )
    return jnp.concatenate(pieces, axis=3)


def fold_patches(upstream, stride, side_in):
    channels = upstream.shape[3] // 9
    padded = jnp.zeros((upstream.shape[0], side_in + 2, side_in + 2, channels), jnp.float32)
    for offset_row in range(3):
        for offset_col in range(3):
            start_at = (offset_row * 3 + offset_col) * channels
            padded = padded.at[
                :,
                offset_row : offset_row + side_in : stride,
                offset_col : offset_col + side_in : stride,
                :,
            ].add(upstream[..., start_at : start_at + channels])
    return padded[:, 1 : side_in + 1, 1 : side_in + 1, :]


def batch_norm(values, live_masks, norm_param, totals):
    gain_row = norm_param[0].astype(jnp.float32)
    shift_row = norm_param[1].astype(jnp.float32)
    firsts = []
    seconds = []
    for group_member in range(3):
        weighted = values[group_member] * live_masks[group_member]
        firsts.append(jnp.sum(weighted, axis=(0, 1, 2)))
        seconds.append(jnp.sum(weighted * values[group_member], axis=(0, 1, 2)))
    summed = lax.psum(
        (firsts[0], seconds[0], firsts[1], seconds[1], firsts[2], seconds[2]), (DP, REP)
    )
    normed = []
    means = []
    scales = []
    for group_member in range(3):
        pixel_count = (
            totals[group_member] * values[group_member].shape[1] * values[group_member].shape[2]
        )
        mean_value = summed[2 * group_member] / pixel_count
        inv_std = lax.rsqrt(
            summed[2 * group_member + 1] / pixel_count - mean_value * mean_value + EPSILON
        )
        normed.append((values[group_member] - mean_value) * inv_std * gain_row + shift_row)
        means.append(mean_value)
        scales.append(inv_std)
    return (normed, means, scales)


def norm_back(upstream, values, live_masks, norm_param, means, scales, totals):
    gain_row = norm_param[0].astype(jnp.float32)
    normals = []
    firsts = []
    seconds = []
    for group_member in range(3):
        normal = (values[group_member] - means[group_member]) * scales[group_member]
        weighted = upstream[group_member] * live_masks[group_member]
        normals.append(normal)
        firsts.append(jnp.sum(weighted, axis=(0, 1, 2)))
        seconds.append(jnp.sum(weighted * normal, axis=(0, 1, 2)))
    summed = lax.psum(
        (firsts[0], seconds[0], firsts[1], seconds[1], firsts[2], seconds[2]), (DP, REP)
    )
    results = []
    for group_member in range(3):
        pixel_count = (
            totals[group_member] * values[group_member].shape[1] * values[group_member].shape[2]
        )
        centered = (
            upstream[group_member]
            - summed[2 * group_member] / pixel_count
            - normals[group_member] * (summed[2 * group_member + 1] / pixel_count)
        )
        results.append(
            (live_masks[group_member] * gain_row * scales[group_member] * centered).astype(
                jnp.bfloat16
            )
        )
    param_grad = jnp.stack([summed[1] + summed[3] + summed[5], summed[0] + summed[2] + summed[4]])
    return (results, param_grad)


def own_columns(full, local_width):
    return lax.dynamic_slice_in_dim(full, lax.axis_index(DP) * local_width, local_width, 1)


def plain_on_device(
    input_160,
    input_224,
    input_288,
    cotangent_160,
    cotangent_224,
    cotangent_288,
    live_counts,
    conv_a1,
    norm_a1,
    conv_a2,
    norm_a2,
    conv_a3,
    norm_a3,
    conv_as,
    norm_as,
    conv_b1,
    norm_b1,
    conv_b2,
    norm_b2,
    conv_b3,
    norm_b3,
):
    inputs = (input_160, input_224, input_288)
    cotangents = (cotangent_160, cotangent_224, cotangent_288)
    live_masks = []
    masked = []
    for group_member in range(3):
        group_slot_count = inputs[group_member].shape[0]
        live_flags = (
            (jnp.arange(group_slot_count) < live_counts[0, group_member])
            .astype(jnp.float32)
            .reshape(group_slot_count, 1, 1, 1)
        )
        live_masks.append(live_flags)
        masked.append(inputs[group_member] * live_flags.astype(jnp.bfloat16))
    totals = lax.psum(live_counts[0].astype(jnp.float32), (DP, REP))
    local_weights = (conv_a1, conv_a2, conv_a3, conv_as, conv_b1, conv_b2, conv_b3)
    squares_list = []
    for weight in local_weights:
        squares_list.append(jnp.sum(jnp.square(weight.astype(jnp.float32))))
    weight_squares = jnp.stack(squares_list)
    gathered_a = (
        lax.all_gather(conv_a1, DP, axis=1, tiled=True),
        lax.all_gather(norm_a1, DP, axis=1, tiled=True),
        lax.all_gather(conv_a2, DP, axis=3, tiled=True),
        lax.all_gather(norm_a2, DP, axis=1, tiled=True),
        lax.all_gather(conv_a3, DP, axis=1, tiled=True),
        lax.all_gather(norm_a3, DP, axis=1, tiled=True),
        lax.all_gather(conv_as, DP, axis=1, tiled=True),
        lax.all_gather(norm_as, DP, axis=1, tiled=True),
    )
    full_a1, param_a1, full_a2, param_a2, full_a3, param_a3, full_as, param_as = gathered_a
    mid_width = full_a2.shape[3]
    out_width = full_a3.shape[1]
    hidden_a1 = [pointwise(masked[group_member], full_a1) for group_member in range(3)]
    normed_a1, means_a1, scales_a1 = batch_norm(hidden_a1, live_masks, param_a1, totals)
    act_a1 = [
        jax.nn.silu(normed_a1[group_member]).astype(jnp.bfloat16) for group_member in range(3)
    ]
    kernel_a2 = full_a2.reshape(9 * mid_width, mid_width)
    hidden_a2 = [
        pointwise(patches(act_a1[group_member], 2), kernel_a2) for group_member in range(3)
    ]
    normed_a2, means_a2, scales_a2 = batch_norm(hidden_a2, live_masks, param_a2, totals)
    act_a2 = [
        jax.nn.silu(normed_a2[group_member]).astype(jnp.bfloat16) for group_member in range(3)
    ]
    strided = [masked[group_member][:, ::2, ::2, :] for group_member in range(3)]
    joined = [
        jnp.concatenate(
            [pointwise(act_a2[group_member], full_a3), pointwise(strided[group_member], full_as)],
            axis=3,
        )
        for group_member in range(3)
    ]
    param_joined = jnp.concatenate([param_a3, param_as], axis=1)
    normed_j, means_j, scales_j = batch_norm(joined, live_masks, param_joined, totals)
    sum_a = [
        normed_j[group_member][..., :out_width] + normed_j[group_member][..., out_width:]
        for group_member in range(3)
    ]
    out_a = [
        (jax.nn.silu(sum_a[group_member]) * live_masks[group_member]).astype(jnp.bfloat16)
        for group_member in range(3)
    ]
    gathered_b = (
        lax.all_gather(conv_b1, DP, axis=1, tiled=True),
        lax.all_gather(norm_b1, DP, axis=1, tiled=True),
        lax.all_gather(conv_b2, DP, axis=3, tiled=True),
        lax.all_gather(norm_b2, DP, axis=1, tiled=True),
        lax.all_gather(conv_b3, DP, axis=1, tiled=True),
        lax.all_gather(norm_b3, DP, axis=1, tiled=True),
    )
    full_b1, param_b1, full_b2, param_b2, full_b3, param_b3 = gathered_b
    hidden_b1 = [pointwise(out_a[group_member], full_b1) for group_member in range(3)]
    normed_b1, means_b1, scales_b1 = batch_norm(hidden_b1, live_masks, param_b1, totals)
    act_b1 = [
        jax.nn.silu(normed_b1[group_member]).astype(jnp.bfloat16) for group_member in range(3)
    ]
    kernel_b2 = full_b2.reshape(9 * mid_width, mid_width)
    hidden_b2 = [
        pointwise(patches(act_b1[group_member], 1), kernel_b2) for group_member in range(3)
    ]
    normed_b2, means_b2, scales_b2 = batch_norm(hidden_b2, live_masks, param_b2, totals)
    act_b2 = [
        jax.nn.silu(normed_b2[group_member]).astype(jnp.bfloat16) for group_member in range(3)
    ]
    hidden_b3 = [pointwise(act_b2[group_member], full_b3) for group_member in range(3)]
    normed_b3, means_b3, scales_b3 = batch_norm(hidden_b3, live_masks, param_b3, totals)
    sum_b = [
        normed_b3[group_member] + out_a[group_member].astype(jnp.float32)
        for group_member in range(3)
    ]
    outputs = [
        (jax.nn.silu(sum_b[group_member]) * live_masks[group_member]).astype(jnp.bfloat16)
        for group_member in range(3)
    ]
    back_b = (
        lax.all_gather(conv_b1, DP, axis=1, tiled=True),
        lax.all_gather(norm_b1, DP, axis=1, tiled=True),
        lax.all_gather(conv_b2, DP, axis=3, tiled=True),
        lax.all_gather(norm_b2, DP, axis=1, tiled=True),
        lax.all_gather(conv_b3, DP, axis=1, tiled=True),
        lax.all_gather(norm_b3, DP, axis=1, tiled=True),
    )
    full_b1, param_b1, full_b2, param_b2, full_b3, param_b3 = back_b
    kernel_b2 = full_b2.reshape(9 * mid_width, mid_width)
    grad_sum_b = [
        cotangents[group_member].astype(jnp.float32)
        * live_masks[group_member]
        * silu_slope(sum_b[group_member])
        for group_member in range(3)
    ]
    grad_h_b3, pgrad_b3 = norm_back(
        grad_sum_b, hidden_b3, live_masks, param_b3, means_b3, scales_b3, totals
    )
    term_b3 = summed_terms(act_b2, grad_h_b3)
    grad_act = [
        pointwise_back(grad_h_b3[group_member], full_b3) * silu_slope(normed_b2[group_member])
        for group_member in range(3)
    ]
    grad_h_b2, pgrad_b2 = norm_back(
        grad_act, hidden_b2, live_masks, param_b2, means_b2, scales_b2, totals
    )
    term_b2 = summed_terms(
        [patches(act_b1[group_member], 1) for group_member in range(3)], grad_h_b2
    ).reshape(3, 3, mid_width, mid_width)
    grad_act = [
        fold_patches(
            pointwise_back(grad_h_b2[group_member], kernel_b2), 1, act_b1[group_member].shape[1]
        )
        * silu_slope(normed_b1[group_member])
        for group_member in range(3)
    ]
    grad_h_b1, pgrad_b1 = norm_back(
        grad_act, hidden_b1, live_masks, param_b1, means_b1, scales_b1, totals
    )
    term_b1 = summed_terms(out_a, grad_h_b1)
    grad_out_a = [
        grad_sum_b[group_member] + pointwise_back(grad_h_b1[group_member], full_b1)
        for group_member in range(3)
    ]
    shard_b = (
        lax.psum_scatter(term_b1, DP, scatter_dimension=1, tiled=True),
        lax.psum_scatter(term_b2, DP, scatter_dimension=3, tiled=True),
        lax.psum_scatter(term_b3, DP, scatter_dimension=1, tiled=True),
    )
    grads_b = (
        lax.psum(shard_b[0].astype(jnp.bfloat16), REP).astype(jnp.float32),
        lax.psum(shard_b[1].astype(jnp.bfloat16), REP).astype(jnp.float32),
        lax.psum(shard_b[2].astype(jnp.bfloat16), REP).astype(jnp.float32),
    )
    back_a = (
        lax.all_gather(conv_a1, DP, axis=1, tiled=True),
        lax.all_gather(norm_a1, DP, axis=1, tiled=True),
        lax.all_gather(conv_a2, DP, axis=3, tiled=True),
        lax.all_gather(norm_a2, DP, axis=1, tiled=True),
        lax.all_gather(conv_a3, DP, axis=1, tiled=True),
        lax.all_gather(norm_a3, DP, axis=1, tiled=True),
        lax.all_gather(conv_as, DP, axis=1, tiled=True),
        lax.all_gather(norm_as, DP, axis=1, tiled=True),
    )
    full_a1, param_a1, full_a2, param_a2, full_a3, param_a3, full_as, param_as = back_a
    kernel_a2 = full_a2.reshape(9 * mid_width, mid_width)
    param_joined = jnp.concatenate([param_a3, param_as], axis=1)
    grad_sum_a = [
        grad_out_a[group_member] * live_masks[group_member] * silu_slope(sum_a[group_member])
        for group_member in range(3)
    ]
    grad_joined = [
        jnp.concatenate([grad_sum_a[group_member], grad_sum_a[group_member]], axis=3)
        for group_member in range(3)
    ]
    grad_h_j, pgrad_j = norm_back(
        grad_joined, joined, live_masks, param_joined, means_j, scales_j, totals
    )
    grad_h_a3 = [grad_h_j[group_member][..., :out_width] for group_member in range(3)]
    grad_h_as = [grad_h_j[group_member][..., out_width:] for group_member in range(3)]
    term_a3 = summed_terms(act_a2, grad_h_a3)
    term_as = summed_terms(strided, grad_h_as)
    grad_act = [
        pointwise_back(grad_h_a3[group_member], full_a3) * silu_slope(normed_a2[group_member])
        for group_member in range(3)
    ]
    grad_h_a2, pgrad_a2 = norm_back(
        grad_act, hidden_a2, live_masks, param_a2, means_a2, scales_a2, totals
    )
    term_a2 = summed_terms(
        [patches(act_a1[group_member], 2) for group_member in range(3)], grad_h_a2
    ).reshape(3, 3, mid_width, mid_width)
    grad_act = [
        fold_patches(
            pointwise_back(grad_h_a2[group_member], kernel_a2), 2, act_a1[group_member].shape[1]
        )
        * silu_slope(normed_a1[group_member])
        for group_member in range(3)
    ]
    grad_h_a1, pgrad_a1 = norm_back(
        grad_act, hidden_a1, live_masks, param_a1, means_a1, scales_a1, totals
    )
    term_a1 = summed_terms(masked, grad_h_a1)
    grad_inputs = [
        pointwise_back(grad_h_a1[group_member], full_a1)
        .at[:, ::2, ::2, :]
        .add(pointwise_back(grad_h_as[group_member], full_as))
        .astype(jnp.bfloat16)
        for group_member in range(3)
    ]
    shard_a = (
        lax.psum_scatter(term_a1, DP, scatter_dimension=1, tiled=True),
        lax.psum_scatter(term_a2, DP, scatter_dimension=3, tiled=True),
        lax.psum_scatter(term_a3, DP, scatter_dimension=1, tiled=True),
        lax.psum_scatter(term_as, DP, scatter_dimension=1, tiled=True),
    )
    grads_a = (
        lax.psum(shard_a[0].astype(jnp.bfloat16), REP).astype(jnp.float32),
        lax.psum(shard_a[1].astype(jnp.bfloat16), REP).astype(jnp.float32),
        lax.psum(shard_a[2].astype(jnp.bfloat16), REP).astype(jnp.float32),
        lax.psum(shard_a[3].astype(jnp.bfloat16), REP).astype(jnp.float32),
    )
    mid_local = norm_a1.shape[1]
    out_local = norm_a3.shape[1]
    norm_grad_a1 = own_columns(pgrad_a1, mid_local)
    norm_grad_a2 = own_columns(pgrad_a2, mid_local)
    norm_grad_a3 = own_columns(pgrad_j[:, :out_width], out_local)
    norm_grad_as = own_columns(pgrad_j[:, out_width:], out_local)
    norm_grad_b1 = own_columns(pgrad_b1, mid_local)
    norm_grad_b2 = own_columns(pgrad_b2, mid_local)
    norm_grad_b3 = own_columns(pgrad_b3, out_local)
    gradients = (grads_a[0], grads_a[1], grads_a[2], grads_a[3], grads_b[0], grads_b[1], grads_b[2])
    grad_list = []
    for gradient in gradients:
        grad_list.append(jnp.sum(gradient * gradient))
    grad_squares = jnp.stack(grad_list)
    weight_totals, grad_totals = lax.psum((weight_squares, grad_squares), DP)
    weight_norm = jnp.sqrt(weight_totals)
    grad_norm = jnp.sqrt(grad_totals)
    trust_ratio = weight_norm / (grad_norm + DECAY_RATE * weight_norm)
    scaled = [
        trust_ratio[layer_id]
        * (gradients[layer_id] + DECAY_RATE * local_weights[layer_id].astype(jnp.float32))
        for layer_id in range(7)
    ]
    return (
        outputs[0],
        outputs[1],
        outputs[2],
        grad_inputs[0],
        grad_inputs[1],
        grad_inputs[2],
        gradients[0],
        norm_grad_a1,
        gradients[1],
        norm_grad_a2,
        gradients[2],
        norm_grad_a3,
        gradients[3],
        norm_grad_as,
        gradients[4],
        norm_grad_b1,
        gradients[5],
        norm_grad_b2,
        gradients[6],
        norm_grad_b3,
        scaled[0],
        scaled[1],
        scaled[2],
        scaled[3],
        scaled[4],
        scaled[5],
        scaled[6],
        jnp.stack([weight_totals, grad_totals]),
    )


MESH = pl.DeviceIdType.MESH
ANY = pl.BlockSpec(memory_space=pl.ANY)


def position():
    dp, rep = lax.axis_index(DP), lax.axis_index(REP)
    return dp // 2, lax.rem(dp, 2), rep // 2, lax.rem(rep, 2)


def device_at(z, x, y, core):
    return (z * 2 + x, y * 2 + core)


def greet(depth):
    z, x, y, core = position()
    barrier = pltpu.get_barrier_semaphore()
    peers = [(z, x, y, 1 - core), (z, x, 1 - y, core), (z, x, 1 - y, 1 - core)]
    peers += [(z, 1 - x, y, core), (z, 1 - x, y, 1 - core), (z, 1 - x, 1 - y, core), (z, 1 - x, 1 - y, 1 - core)]
    peers += [(lax.rem(z + step, depth), x, y, core) for step in range(1, depth)]
    for peer in peers:
        pl.semaphore_signal(barrier, inc=1, device_id=device_at(*peer), device_id_type=MESH)
    pl.semaphore_wait(barrier, len(peers))


def remote(src, dst, send, recv, peer):
    return pltpu.make_async_remote_copy(
        src_ref=src, dst_ref=dst, send_sem=send, recv_sem=recv, device_id=device_at(*peer), device_id_type=MESH
    )


def chunk_rows(rows, both, y, core):
    if both:
        return pl.ds(pl.multiple_of(core * (rows // 2), rows // 2), rows // 2)
    return pl.ds(pl.multiple_of(core * (rows // 2) + y * (rows // 4), rows // 4), rows // 4)


def core_rows(rows, core):
    return pl.ds(pl.multiple_of(core * (rows // 2), rows // 2), rows // 2)


class Gather:
    AHEAD = 4

    def __init__(self, shards, fulls, sems, depth):
        self.shards, self.fulls, self.depth = shards, fulls, depth
        (self.local_sem, self.z_send, self.z_recv, self.x_send, self.x_recv) = sems[:5]
        (self.y_send, self.y_recv, self.c_send, self.c_recv) = sems[5:]
        self.z, self.x, self.y, self.core = position()
        self.count = len(GATHER_CHUNKS)
        self.z_next = self.x_next = self.y_next = self.c_next = 0

    @staticmethod
    def scratch(depth):
        dma, count = pltpu.SemaphoreType.DMA, len(GATHER_CHUNKS)
        return [dma((count,))] + [dma((count, depth - 1))] * 2 + [dma((count,))] * 6

    def part(self, k):
        tensor, lead, leads, both, column, columns = GATHER_CHUNKS[k]
        rows = chunk_rows(self.shards[tensor].shape[1], both, self.y, self.core)
        return self.fulls[tensor], pl.ds(lead, leads), rows, pl.ds(column, columns)

    def place(self, k):
        full, lead, rows, cols = self.part(k)
        shard = self.shards[GATHER_CHUNKS[k][0]]
        return pltpu.make_async_copy(
            shard.at[lead, rows, cols], full.at[self.z, self.x, lead, rows, cols], self.local_sem.at[k]
        )

    def z_copies(self, k):
        full, lead, rows, cols = self.part(k)
        here = full.at[self.z, self.x, lead, rows, cols]
        return [
            remote(
                here,
                here,
                self.z_send.at[k, step - 1],
                self.z_recv.at[k, step - 1],
                (lax.rem(self.z + step, self.depth), self.x, self.y, self.core),
            )
            for step in range(1, self.depth)
        ]

    def x_copy(self, k):
        full, lead, rows, cols = self.part(k)
        here = full.at[:, self.x, lead, rows, cols]
        return remote(here, here, self.x_send.at[k], self.x_recv.at[k], (self.z, 1 - self.x, self.y, self.core))

    def y_copy(self, k):
        full, lead, rows, cols = self.part(k)
        here = full.at[:, :, lead, rows, cols]
        return remote(here, here, self.y_send.at[k], self.y_recv.at[k], (self.z, self.x, 1 - self.y, self.core))

    def c_copy(self, k):
        full, lead, _, cols = self.part(k)
        here = full.at[:, :, lead, core_rows(full.shape[3], self.core), cols]
        return remote(here, here, self.c_send.at[k], self.c_recv.at[k], (self.z, self.x, self.y, 1 - self.core))

    def place_all(self):
        for k in range(self.count):
            self.place(k).start()

    def launch(self, k):
        if k < self.count:
            self.place(k).wait()
            for copy in self.z_copies(k):
                copy.start()

    def begin(self):
        for k in range(self.AHEAD):
            self.launch(k)

    def z_step(self):
        k, self.z_next = self.z_next, self.z_next + 1
        for copy in self.z_copies(k):
            copy.wait_recv()
        self.x_copy(k).start()
        self.launch(k + self.AHEAD)

    def x_step(self):
        k, self.x_next = self.x_next, self.x_next + 1
        self.x_copy(k).wait_recv()
        (self.c_copy if GATHER_CHUNKS[k][3] else self.y_copy)(k).start()

    def y_step(self):
        k, self.y_next = self.y_next, self.y_next + 1
        if not GATHER_CHUNKS[k][3]:
            self.y_copy(k).wait_recv()
            self.c_copy(k).start()

    def c_step(self):
        k, self.c_next = self.c_next, self.c_next + 1
        self.c_copy(k).wait_recv()

    def tick(self, upto=-1):
        count = self.count
        if self.z_next < count:
            self.z_step()
        for before, after, step, lag in (
            (self.z_next, self.x_next, self.x_step, 2),
            (self.x_next, self.y_next, self.y_step, 2),
            (self.y_next, self.c_next, self.c_step, 1),
        ):
            if after < before and (before - after > lag or before == count or after <= upto):
                step()

    def pump(self, ticks=1):
        for _ in range(ticks):
            if self.c_next < self.count:
                self.tick()

    def ready(self, tensor):
        last = max(k for k, chunk in enumerate(GATHER_CHUNKS) if chunk[0] == tensor)
        while self.c_next <= last:
            self.tick(last)

    def close(self):
        for k in range(self.count):
            for copy in self.z_copies(k):
                copy.wait_send()
            self.x_copy(k).wait_send()
            if not GATHER_CHUNKS[k][3]:
                self.y_copy(k).wait_send()
            self.c_copy(k).wait_send()


def taps(tensor):
    pieces = []
    for lead in (0, 3, 6):
        pieces += [(tensor, lead, 1, True, 0, 512), (tensor, lead + 1, 2, False, 0, 512)]
    return pieces


CHUNKS = (
    [(0, 0, 1, False, column, 512) for column in (0, 512)],
    taps(1),
    [(2, lead, 1, False, 0, 256) for lead in (0, 1)],
    [(3, lead, 1, lead == 0, 0, 256) for lead in range(4)],
    [(4, 0, 1, column % 1024 == 0, column, 512) for column in (0, 512, 1024, 1536)],
    taps(5),
    [(6, lead, 1, False, 0, 256) for lead in (0, 1)],
)
GATHER_CHUNKS = [chunk for tensor in (0, 1, 3, 2, 4, 5, 6) for chunk in CHUNKS[tensor]]
REDUCE_CHUNKS = [chunk for tensor in (6, 5, 4, 2, 3, 1, 0) for chunk in CHUNKS[tensor]]


def add_blocks(extents, body):
    total = 1
    for extent in extents:
        total *= extent

    def step(flat, carry):
        index = []
        for extent in reversed(extents):
            index.append(lax.rem(flat, extent))
            flat = flat // extent
        body(*reversed(index))
        return carry

    lax.fori_loop(0, total, step, 0)


def add_to(target, source):
    target[...] = (target[...].astype(jnp.float32) + source[...].astype(jnp.float32)).astype(jnp.bfloat16)


class Reduce:
    def __init__(self, held, outs, c_hbm, y_hbm, refs, depth):
        self.held, self.outs, self.c_hbm, self.y_hbm, self.depth = held, outs, c_hbm, y_hbm, depth
        self.count = len(REDUCE_CHUNKS)
        refs = list(refs)

        def take(count):
            taken = refs[:count]
            del refs[:count]
            return taken

        self.from_x, self.from_z, self.swap = take(self.count), take(self.count), take(self.count)
        self.final = take(self.count)
        self.c_tall, self.c_wide, self.y_tall, self.y_wide, self.squares = take(5)
        self.c_sem, self.y_sem, self.x_sem, self.z_sem, self.s_sem, self.f_sem, self.q_sem, self.local_sem = take(8)
        self.z, self.x, self.y, self.core = position()
        self.enabled = 0
        self.next = [0] * len(self.LAGS)

    @staticmethod
    def sizes(shapes):
        for tensor, _, leads, both, _, columns in REDUCE_CHUNKS:
            rows = shapes[tensor][3]
            yield leads, rows, columns, rows // 2 if both else rows // 4, both

    @staticmethod
    def scratch(shapes, depth):
        dma, count = pltpu.SemaphoreType.DMA, len(REDUCE_CHUNKS)
        buffer = lambda *shape: pltpu.VMEM(shape, jnp.bfloat16)
        sizes = list(Reduce.sizes(shapes))
        return (
            [buffer(depth, leads, part, columns) for leads, _, columns, part, _ in sizes]
            + [buffer(depth - 1, leads, part, columns) for leads, _, columns, part, _ in sizes]
            + [buffer(leads, part, columns) if both else buffer(16, 128) for leads, _, columns, part, both in sizes]
            + [buffer(leads, rows, columns) for leads, rows, columns, _, _ in sizes]
            + [buffer(2, depth, 2, 1, shapes[2][3] // 2, shapes[2][4]), buffer(2, depth, 2, 2, shapes[0][3] // 2, 512)]
            + [buffer(2, depth, 2, 1, shapes[2][3] // 4, shapes[2][4]), buffer(2, depth, 2, 2, shapes[0][3] // 4, 512)]
            + [pltpu.VMEM((2 * depth + 3, 8, 128), jnp.float32)]
            + [dma((2, count))] * 3
            + [dma((2, count, depth - 1)), dma((2, count)), dma((2, count, 3)), dma((2, depth)), dma((3, count))]
        )

    def piece(self, k):
        tensor, lead, leads, both, column, columns = REDUCE_CHUNKS[k]
        held = self.held[tensor]
        rows = held.shape[3]
        return held, rows, pl.ds(lead, leads), pl.ds(column, columns), chunk_rows(rows, both, self.y, self.core)

    def extents(self, k):
        return REDUCE_CHUNKS[k][2], REDUCE_CHUNKS[k][1]

    def slot(self, k, tall, wide):
        tensor, _, leads = REDUCE_CHUNKS[k][:3]
        buffer = tall if tensor in (2, 3, 6) else wide
        return buffer.at[k % 2, :, :, pl.ds(0, leads)]

    def c_copy(self, k):
        held, rows, lead, cols, _ = self.piece(k)
        return remote(
            held.at[:, :, lead, core_rows(rows, 1 - self.core), cols],
            self.c_hbm[REDUCE_CHUNKS[k][0]].at[:, :, lead, :, cols],
            self.c_sem.at[0, k],
            self.c_sem.at[1, k],
            (self.z, self.x, self.y, 1 - self.core),
        )

    def c_load(self, k):
        _, _, lead, cols, _ = self.piece(k)
        return pltpu.make_async_copy(
            self.c_hbm[REDUCE_CHUNKS[k][0]].at[:, :, lead, :, cols],
            self.slot(k, self.c_tall, self.c_wide),
            self.local_sem.at[0, k],
        )

    def y_copy(self, k):
        held, rows, lead, cols, _ = self.piece(k)
        return remote(
            held.at[:, :, lead, chunk_rows(rows, False, 1 - self.y, self.core), cols],
            self.y_hbm[REDUCE_CHUNKS[k][0]].at[:, :, lead, :, cols],
            self.y_sem.at[0, k],
            self.y_sem.at[1, k],
            (self.z, self.x, 1 - self.y, self.core),
        )

    def y_load(self, k):
        _, _, lead, cols, _ = self.piece(k)
        return pltpu.make_async_copy(
            self.y_hbm[REDUCE_CHUNKS[k][0]].at[:, :, lead, :, cols],
            self.slot(k, self.y_tall, self.y_wide),
            self.local_sem.at[1, k],
        )

    def x_copy(self, k):
        held, _, lead, cols, rows = self.piece(k)
        return remote(
            held.at[:, 1 - self.x, lead, rows, cols],
            self.from_x[k],
            self.x_sem.at[0, k],
            self.x_sem.at[1, k],
            (self.z, 1 - self.x, self.y, self.core),
        )

    def z_copies(self, k):
        held, _, lead, cols, rows = self.piece(k)
        copies = []
        for step in range(1, self.depth):
            there = lax.rem(self.z + step, self.depth)
            copies.append(
                remote(
                    held.at[there, self.x, lead, rows, cols],
                    self.from_z[k].at[step - 1],
                    self.z_sem.at[0, k, step - 1],
                    self.z_sem.at[1, k, step - 1],
                    (there, self.x, self.y, self.core),
                )
            )
        return copies

    def s_copy(self, k):
        rows = self.piece(k)[4]
        return remote(
            self.final[k].at[:, rows],
            self.swap[k],
            self.s_sem.at[0, k],
            self.s_sem.at[1, k],
            (self.z, self.x, 1 - self.y, self.core),
        )

    def f_copies(self, k):
        here = self.final[k].at[:, self.piece(k)[4]]
        peers = [(self.z, self.x, self.y, 1 - self.core)]
        if not REDUCE_CHUNKS[k][3]:
            peers += [(self.z, self.x, 1 - self.y, self.core), (self.z, self.x, 1 - self.y, 1 - self.core)]
        return [
            remote(here, here, self.f_sem.at[0, k, i], self.f_sem.at[1, k, i], peer) for i, peer in enumerate(peers)
        ]

    def store(self, k):
        tensor = REDUCE_CHUNKS[k][0]
        _, _, lead, cols, _ = self.piece(k)
        return pltpu.make_async_copy(self.final[k], self.outs[tensor].at[lead, :, cols], self.local_sem.at[2, k])

    def add_c(self, k):
        held, rows, _, cols, _ = self.piece(k)
        leads, lead = self.extents(k)
        half, slot = core_rows(rows, self.core), self.slot(k, self.c_tall, self.c_wide)
        add_blocks(
            (self.depth, 2, leads), lambda z, x, i: add_to(held.at[z, x, lead + i, half, cols], slot.at[z, x, i])
        )

    def add_y(self, k):
        held, _, _, cols, rows = self.piece(k)
        leads, lead = self.extents(k)
        slot = self.slot(k, self.y_tall, self.y_wide)
        add_blocks(
            (self.depth, 2, leads), lambda z, x, i: add_to(held.at[z, x, lead + i, rows, cols], slot.at[z, x, i])
        )

    def add_x(self, k):
        held, _, _, cols, rows = self.piece(k)
        leads, lead = self.extents(k)
        add_blocks(
            (self.depth, leads), lambda z, i: add_to(held.at[z, self.x, lead + i, rows, cols], self.from_x[k].at[z, i])
        )

    def add_z(self, k):
        held, _, _, cols, rows = self.piece(k)
        leads, lead = self.extents(k)

        def body(i):
            total = held[self.z, self.x, lead + i, rows, cols].astype(jnp.float32)
            for step in range(1, self.depth):
                total = total + self.from_z[k][step - 1, i].astype(jnp.float32)
            self.final[k][i, rows] = total.astype(jnp.bfloat16)

        add_blocks((leads,), body)

    def add_s(self, k):
        rows = self.piece(k)[4]
        add_blocks((self.extents(k)[0],), lambda i: add_to(self.final[k].at[i, rows], self.swap[k].at[i]))

    def add_squares(self, k):
        leads = self.extents(k)[0]
        lanes = lax.broadcasted_iota(jnp.int32, (8, 128), 1)
        subs = lax.broadcasted_iota(jnp.int32, (8, 128), 0)
        where = (subs == 1) & (lanes == REDUCE_CHUNKS[k][0])

        def body(i):
            block = self.final[k][i].astype(jnp.float32)
            total = jnp.sum(jnp.sum(block * block, axis=0, keepdims=True), axis=1, keepdims=True)
            self.squares[2 * self.depth + 2] += jnp.where(where, total, 0.0)

        add_blocks((leads,), body)

    LAGS = (0, 2, 1, 2, 1, 2, 2, 1, 1)

    def stage(self, k, number):
        both = REDUCE_CHUNKS[k][3]
        if number == 0:
            self.c_copy(k).start()
        elif number == 1:
            self.c_copy(k).wait_recv()
            self.c_load(k).start()
        elif number == 2:
            self.c_load(k).wait()
            self.add_c(k)
            (self.x_copy if both else self.y_copy)(k).start()
        elif number == 3 and not both:
            self.y_copy(k).wait_recv()
            self.y_load(k).start()
        elif number == 4 and not both:
            self.y_load(k).wait()
            self.add_y(k)
            self.x_copy(k).start()
        elif number == 5:
            self.x_copy(k).wait_recv()
            self.add_x(k)
            for copy in self.z_copies(k):
                copy.start()
        elif number == 6:
            for copy in self.z_copies(k):
                copy.wait_recv()
            self.add_z(k)
            for copy in [self.s_copy(k)] if both else self.f_copies(k):
                copy.start()
        elif number == 7 and both:
            self.s_copy(k).wait_recv()
            self.s_copy(k).wait_send()
            self.add_s(k)
            for copy in self.f_copies(k):
                copy.start()
        elif number == 8:
            for copy in self.f_copies(k):
                copy.wait_recv()
            self.store(k).start()
            self.add_squares(k)

    def enable(self, tensor, leads_done=None):
        while self.enabled < self.count:
            chunk = REDUCE_CHUNKS[self.enabled]
            if chunk[0] != tensor or (leads_done is not None and chunk[1] + chunk[2] > leads_done):
                break
            self.enabled += 1

    def pump(self, ticks=1):
        for _ in range(ticks):
            for number in reversed(range(len(self.LAGS))):
                before = self.next[number - 1] if number else self.enabled
                behind = before - self.next[number]
                if behind > 0 and (behind > self.LAGS[number] or before == self.count):
                    self.stage(self.next[number], number)
                    self.next[number] += 1

    def finish(self, weight_squares, sums_out):
        while self.next[-1] < self.count:
            self.pump()
        squares, depth = self.squares, self.depth
        subs = lax.broadcasted_iota(jnp.int32, (8, 128), 0)
        mine = squares.at[self.z * 2 + self.x]
        mine[...] = squares[2 * depth + 2] + jnp.where(subs == 0, weight_squares[...], 0.0)
        copies = [
            remote(
                mine,
                mine,
                self.q_sem.at[0, step],
                self.q_sem.at[1, step],
                (lax.rem(self.z + step, depth), self.x, self.y, self.core),
            )
            for step in range(1, depth)
        ]
        for copy in copies:
            copy.start()
        for copy in copies:
            copy.wait_recv()
        own = squares[self.x]
        for deep in range(1, depth):
            own = own + squares[deep * 2 + self.x]
        column = squares.at[2 * depth + self.x]
        column[...] = own
        across = remote(
            column, column, self.q_sem.at[0, 0], self.q_sem.at[1, 0], (self.z, 1 - self.x, self.y, self.core)
        )
        across.start()
        across.wait_recv()
        sums_out[...] = squares[2 * depth] + squares[2 * depth + 1]
        across.wait_send()
        for copy in copies:
            copy.wait_send()
        for k in range(self.count):
            self.c_copy(k).wait_send()
            if not REDUCE_CHUNKS[k][3]:
                self.y_copy(k).wait_send()
            self.x_copy(k).wait_send()
            for copy in self.z_copies(k) + self.f_copies(k):
                copy.wait_send()
            self.store(k).wait()


class NearFar:
    def __init__(self, refs, depth):
        self.near, self.far, self.total, self.near_send, self.near_recv, self.far_send, self.far_recv = refs
        self.depth = depth
        self.z, self.x, self.y, self.core = position()
        self.mine = self.x * 4 + self.y * 2 + self.core
        self.pay = self.near.at[self.mine]
        self.sent = []

    @staticmethod
    def scratch(width, depth):
        dma = pltpu.SemaphoreType.DMA
        return [
            pltpu.VMEM((8, 8, width), jnp.float32),
            pltpu.VMEM((depth, 8, width), jnp.float32),
            pltpu.VMEM((8, width), jnp.float32),
            dma((7,)),
            dma((7,)),
            dma((depth - 1,)),
            dma((depth - 1,)),
        ]

    def near_copies(self):
        copies = []
        for offset in range(1, 8):
            x = 1 - self.x if offset & 4 else self.x
            y = 1 - self.y if offset & 2 else self.y
            core = 1 - self.core if offset & 1 else self.core
            here = self.near.at[self.mine]
            copies.append(
                remote(here, here, self.near_send.at[offset - 1], self.near_recv.at[offset - 1], (self.z, x, y, core))
            )
        return copies

    def far_copies(self):
        here = self.far.at[self.z]
        return [
            remote(
                here,
                here,
                self.far_send.at[step - 1],
                self.far_recv.at[step - 1],
                (lax.rem(self.z + step, self.depth), self.x, self.y, self.core),
            )
            for step in range(1, self.depth)
        ]

    def begin(self):
        for copy in self.near_copies():
            copy.start()

    def stages(self):
        def middle():
            for copy in self.near_copies():
                copy.wait_recv()
            total = self.near[0]
            for slot in range(1, 8):
                total = total + self.near[slot]
            self.far[self.z] = total
            for copy in self.far_copies():
                copy.start()

        def last():
            for copy in self.far_copies():
                copy.wait_recv()
            total = self.far[0]
            for slot in range(1, self.depth):
                total = total + self.far[slot]
            self.total[...] = total

        return [middle, last]

    def close(self):
        for copy in self.near_copies() + self.far_copies():
            copy.wait_send()


class Split:
    def __init__(self, refs, depth):
        (self.pay, self.half, self.quad, self.deep, self.total, self.c_send, self.c_recv) = refs[:7]
        (self.q_send, self.q_recv, self.z_send, self.z_recv, self.g_send, self.g_recv) = refs[7:]
        self.depth = depth
        self.z, self.x, self.y, self.core = position()
        self.width = self.pay.shape[1]
        self.mine = self.x * 2 + self.y

    @staticmethod
    def scratch(width, depth):
        dma = pltpu.SemaphoreType.DMA
        return [
            pltpu.VMEM((8, width), jnp.float32),
            pltpu.VMEM((8, width // 2), jnp.float32),
            pltpu.VMEM((4, 8, width // 8), jnp.float32),
            pltpu.VMEM((depth, 8, width // 8), jnp.float32),
            pltpu.VMEM((8, width), jnp.float32),
            dma((2,)),
            dma((2,)),
            dma((3,)),
            dma((3,)),
            dma((depth - 1,)),
            dma((depth - 1,)),
            dma((3,)),
            dma((3,)),
        ]

    def half_of(self, core):
        return pl.ds(pl.multiple_of(core * (self.width // 2), 128), self.width // 2)

    def eighth_of(self, slot):
        start = self.core * (self.width // 2) + slot * (self.width // 8)
        return pl.ds(pl.multiple_of(start, 128), self.width // 8)

    def core_copy(self):
        return remote(
            self.pay.at[:, self.half_of(1 - self.core)],
            self.half,
            self.c_send.at[0],
            self.c_recv.at[0],
            (self.z, self.x, self.y, 1 - self.core),
        )

    def around(self):
        for offset in range(1, 4):
            x = 1 - self.x if offset & 2 else self.x
            y = 1 - self.y if offset & 1 else self.y
            yield offset - 1, x, y

    def quad_copies(self):
        return [
            remote(
                self.pay.at[:, self.eighth_of(x * 2 + y)],
                self.quad.at[self.mine],
                self.q_send.at[i],
                self.q_recv.at[i],
                (self.z, x, y, self.core),
            )
            for i, x, y in self.around()
        ]

    def deep_copies(self):
        here = self.deep.at[self.z]
        return [
            remote(
                here,
                here,
                self.z_send.at[step - 1],
                self.z_recv.at[step - 1],
                (lax.rem(self.z + step, self.depth), self.x, self.y, self.core),
            )
            for step in range(1, self.depth)
        ]

    def gather_copies(self):
        here = self.total.at[:, self.eighth_of(self.mine)]
        return [
            remote(here, here, self.g_send.at[i], self.g_recv.at[i], (self.z, x, y, self.core))
            for i, x, y in self.around()
        ]

    def last_copy(self):
        here = self.total.at[:, self.half_of(self.core)]
        return remote(here, here, self.c_send.at[1], self.c_recv.at[1], (self.z, self.x, self.y, 1 - self.core))

    def begin(self):
        self.core_copy().start()

    def stages(self):
        def first():
            self.core_copy().wait_recv()
            half = self.half_of(self.core)
            self.pay[:, half] = self.pay[:, half] + self.half[...]
            for copy in self.quad_copies():
                copy.start()
            self.quad[self.mine] = self.pay[:, self.eighth_of(self.mine)]

        def second():
            for copy in self.quad_copies():
                copy.wait_recv()
            self.deep[self.z] = (self.quad[0] + self.quad[1]) + (self.quad[2] + self.quad[3])
            for copy in self.deep_copies():
                copy.start()

        def third():
            for copy in self.deep_copies():
                copy.wait_recv()
            total = self.deep[0]
            for slot in range(1, self.depth):
                total = total + self.deep[slot]
            self.total[:, self.eighth_of(self.mine)] = total
            for copy in self.gather_copies():
                copy.start()

        def fourth():
            for copy in self.gather_copies():
                copy.wait_recv()
            self.last_copy().start()

        def fifth():
            self.last_copy().wait_recv()
            for copy in self.gather_copies() + [self.last_copy()]:
                copy.wait_send()

        return [first, second, third, fourth, fifth]

    def close(self):
        self.core_copy().wait_send()
        for copy in self.quad_copies() + self.deep_copies():
            copy.wait_send()


def interleave(stages, works):
    done = 0
    for i, stage in enumerate(stages):
        upto = (len(works) * (i + 1)) // len(stages)
        for work in works[done:upto]:
            work()
        done = upto
        stage()


HAT_A1, HAT_A2, HAT_A3, HAT_AS, HAT_B1, HAT_B2, HAT_B3, PATCH_A, PATCH_B, ACT_A2, ACT_B2, OUT_A = SAVED = range(12)
NORMS_MID, NORMS_OUT, SUM_A1, SUM_A2, SUM_A3, SUM_AS, SUM_B1, SUM_B2, SUM_B3, SUM_J = range(10)


def paced(first, last, body, parts, pump):
    for part in range(parts):
        span = last - first
        lax.fori_loop(first + span * part // parts, first + span * (part + 1) // parts, body, 0)
        pump()


def columns(j):
    return pl.ds(pl.multiple_of(j * 128, 128), 128)


def dot(a, b):
    return lax.dot_general(a, b, (((1,), (0,)), ((), ())), preferred_element_type=jnp.float32)


def dot_nt(a, b):
    return lax.dot_general(a, b, (((1,), (1,)), ((), ())), preferred_element_type=jnp.float32)


def sigmoid(v):
    return 0.5 * jnp.tanh(0.5 * v) + 0.5


def slope(v):
    s = sigmoid(v)
    return s * (1.0 + v * (1.0 - s))


class Plan:
    def __init__(self, shapes):
        self.sides = [shape[1] // 2 for shape in shapes]
        self.slots = [shape[0] for shape in shapes]
        self.valid = [side * side * slots for side, slots in zip(self.sides, self.slots)]
        sizes = [-(-valid // 8) * 8 for valid in self.valid]
        sizes[2] += -sum(sizes) % 128
        self.starts = [0, sizes[0], sizes[0] + sizes[1]]
        self.sizes = sizes
        self.rows = sum(sizes)

    def spans(self):
        return [slice(start, start + size) for start, size in zip(self.starts, self.sizes)]

    def shifts(self):
        out = np.zeros((9, self.rows, self.rows), np.float32)
        for side, slots, start in zip(self.sides, self.slots, self.starts):
            at = lambda i, j, n: start + (i * side + j) * slots + n
            for di in (-1, 0, 1):
                for dj in (-1, 0, 1):
                    for i in range(max(0, -di), min(side, side - di)):
                        for j in range(max(0, -dj), min(side, side - dj)):
                            for n in range(slots):
                                out[(di + 1) * 3 + dj + 1, at(i, j, n), at(i + di, j + dj, n)] = 1.0
        return out.astype(jnp.bfloat16)


def put_sums(plan, pairs, mask, pay, base, width, pump=None):
    def body(j, carry):
        firsts, seconds = [0.0] * 3, [0.0] * 3
        for first, second in pairs(j):
            for g, span in enumerate(plan.spans()):
                live = first[span] * mask[span, :]
                firsts[g] = firsts[g] + jnp.sum(live, axis=0, keepdims=True)
                seconds[g] = seconds[g] + jnp.sum(live * second[span], axis=0, keepdims=True)
        zero = jnp.zeros((1, 128), jnp.float32)
        pay[:, columns(base + j)] = jnp.concatenate(firsts + seconds + [zero, zero], axis=0)
        return carry

    if pump is None:
        lax.fori_loop(0, width // 128, body, 0)
    else:
        paced(0, width // 128, body, 2, pump)


def put_scales(total, inverse, over, width, factor=1.0):
    def body(j, carry):
        at = columns(j)
        per = over[0:3, :] * factor
        means = total[0:3, at] * per
        variance = total[3:6, at] * per - means * means
        scales = lax.rsqrt(variance + EPSILON)
        zero = jnp.zeros((5, 128), jnp.float32)
        total[:, at] = jnp.concatenate([means, zero], axis=0)
        inverse[:, at] = jnp.concatenate([scales, zero], axis=0)
        return carry

    lax.fori_loop(0, width // 128, body, 0)


def by_group(plan, of):
    return jnp.concatenate([of(g, span) for g, span in enumerate(plan.spans())], axis=0)


def forward_names(depth):
    return (
        (NORMS_MID, NearFar.scratch(512, depth)),
        (NORMS_OUT, Split.scratch(2048, depth)),
        (SUM_A1, NearFar.scratch(512, depth)),
        (SUM_A2, NearFar.scratch(512, depth)),
        (SUM_AS, Split.scratch(2048, depth)),
        (SUM_A3, Split.scratch(2048, depth)),
        (SUM_B1, NearFar.scratch(512, depth)),
        (SUM_B2, NearFar.scratch(512, depth)),
        (SUM_B3, Split.scratch(2048, depth)),
    )


def forward_kernel(plan, depth, *refs):
    refs = list(refs)

    def take(count):
        taken = refs[:count]
        del refs[:count]
        return taken

    x_hbm, shift_hbm, mask, counts, norm_mid, norm_out = take(6)
    shards = take(7)
    out, inv_mid, inv_out, par_mid, par_out, over, weight_squares = take(7)
    weights_hbm = take(7)
    saved_hbm = dict(zip(SAVED, take(len(SAVED))))
    sums = {}
    for name, scratch in forward_names(depth):
        sums[name] = (NearFar if len(scratch) == 7 else Split)(take(len(scratch)), depth)
    x, shift = take(2)
    w_a1, w_a2, w_a3, w_as, w_b1, w_b2, w_b3 = weights = take(7)
    saved = dict(zip(SAVED, take(len(SAVED))))
    hid_a1, hid_mid, hid_out, hid_as, act = take(5)
    load_sem, save_sem, full_sem = take(3)
    gather = Gather(shards, weights, take(9), depth)

    loads = [
        pltpu.make_async_copy(src, dst, load_sem.at[i])
        for i, (src, dst) in enumerate(zip([x_hbm, shift_hbm], [x, shift]))
    ]
    gather.place_all()
    for copy in loads:
        copy.start()

    def keep(i):
        return pltpu.make_async_copy(weights[i], weights_hbm[i], full_sem.at[i])

    weight_squares[...] = jnp.zeros((8, 128), jnp.float32)

    def ready(i):
        gather.ready(i)
        keep(i).start()

    def add_square(i):
        at_row = lax.broadcasted_iota(jnp.int32, (8, 128), 0) == 0
        where = at_row & (lax.broadcasted_iota(jnp.int32, (8, 128), 1) == i)

        def body(lead, carry):
            block = weights[i][gather.z, gather.x, lead].astype(jnp.float32)
            total = jnp.sum(jnp.sum(block * block, axis=0, keepdims=True), axis=1, keepdims=True)
            weight_squares[...] += jnp.where(where, total, 0.0)
            return carry

        lax.fori_loop(0, weights[i].shape[2], body, 0)

    def pump():
        gather.pump()

    def save(name):
        pltpu.make_async_copy(saved[name], saved_hbm[name], save_sem.at[SAVED.index(name)]).start()

    greet(depth)
    gather.begin()
    sums[NORMS_MID].pay[...] = norm_mid[...]
    sums[NORMS_MID].begin()
    sums[NORMS_OUT].pay[...] = norm_out[...]
    sums[NORMS_OUT].begin()
    norms_mid_stages = sums[NORMS_MID].stages()
    norms_out_stages = sums[NORMS_OUT].stages()
    rows = plan.rows

    loads[0].wait()
    norms_mid_stages[0]()
    norms_out_stages[0]()
    ready(0)

    def conv_a1(p, carry):
        hid_a1[p] = dot_nt(x[p], w_a1[...].reshape(512, -1))
        return carry

    paced(0, 2, conv_a1, 2, pump)
    norms_mid_stages[1]()
    norms_out_stages[1]()
    paced(2, 4, conv_a1, 2, pump)
    par_mid[...] = sums[NORMS_MID].total[...]
    norms_out_stages[2]()

    total = sums[SUM_A1]
    put_sums(
        plan, lambda j: [(hid_a1[p, :, columns(j)],) * 2 for p in range(4)], mask, total.pay, 0, 512, pump
    )
    total.pay[6:7, 0:128] = counts[...]
    total.begin()
    add_square(0)
    pump()
    total.stages()[0]()
    norms_out_stages[3]()
    pump()
    total.stages()[1]()
    norms_out_stages[4]()
    par_out[...] = sums[NORMS_OUT].total[...]

    pixels = total.total[6:7, 0:128]
    lanes = lax.broadcasted_iota(jnp.int32, (1, 128), 1)
    inverse_counts = [
        jnp.broadcast_to(1.0 / jnp.sum(jnp.where(lanes == g, pixels, 0.0), axis=1, keepdims=True), (1, 128))
        for g in range(3)
    ]
    over[...] = jnp.concatenate(inverse_counts + [jnp.zeros((5, 128), jnp.float32)], axis=0)
    put_scales(total.total, inv_mid.at[0], over, 512, 0.25)

    def normalized(hidden, total, inverse, hat, params, row, j):
        at = columns(j)
        xhat = by_group(plan, lambda g, span: (hidden[span] - total[g : g + 1, at]) * inverse[g : g + 1, at])
        hat[:, at] = xhat.astype(jnp.bfloat16)
        return xhat * params[row : row + 1, at] + params[row + 1 : row + 2, at]

    def activate(hidden_of, total, inverse, hat, params, row, target):
        def body(j, carry):
            v = normalized(hidden_of(j), total, inverse, hat, params, row, j)
            target[:, columns(j)] = (v * sigmoid(v)).astype(jnp.bfloat16)
            return carry

        lax.fori_loop(0, 4, body, 0)

    def activate_a1(p, carry):
        activate(
            lambda j: hid_a1[p, :, columns(j)],
            total.total,
            inv_mid.at[0],
            saved[HAT_A1].at[p],
            par_mid,
            0,
            act.at[p],
        )
        return carry

    paced(0, 4, activate_a1, 4, pump)
    save(HAT_A1)

    loads[1].wait()
    patch = saved[PATCH_A]
    for tap in range(9):
        a, b = tap // 3, tap % 3
        plane = (0 if a == 1 else 2) + (0 if b == 1 else 1)
        matrix = (0 if a == 0 else 1) * 3 + (0 if b == 0 else 1)
        if matrix == 4:
            patch[tap] = act[plane]
        else:
            patch[tap] = dot(shift[matrix], act[plane]).astype(jnp.bfloat16)
        if tap in (2, 5):
            pump()
    save(PATCH_A)
    ready(1)

    def spatial(patch, weight):
        hid_mid[...] = dot_nt(patch[0], weight[:, :, 0].reshape(512, 512))

        def body(tap, carry):
            hid_mid[...] += dot_nt(patch[tap], weight[:, :, tap].reshape(512, 512))
            return carry

        paced(1, 9, body, 3, pump)

    spatial(patch, w_a2)

    def conv_as(d, carry):
        at = pl.ds(pl.multiple_of(d * 256, 256), 256)
        hid_as[:, at] = dot(x[0], w_as[d // 2, lax.rem(d, 2)].reshape(1024, 256))
        return carry

    def shortcut():
        ready(3)
        paced(0, 8, conv_as, 2, pump)
        put_sums(plan, lambda j: [(hid_as[:, columns(j)],) * 2], mask, sums[SUM_AS].pay, 0, 2048, pump)
        sums[SUM_AS].begin()

    as_stages = sums[SUM_AS].stages()

    def mid_sums(total, name_index, works):
        put_sums(plan, lambda j: [(hid_mid[:, columns(j)],) * 2], mask, total.pay, 0, 512)
        total.begin()
        interleave(total.stages(), works)
        put_scales(total.total, inv_mid.at[name_index], over, 512)

    mid_sums(sums[SUM_A2], 1, [pump, lambda: add_square(1), pump])
    activate(
        lambda j: hid_mid[:, columns(j)], sums[SUM_A2].total, inv_mid.at[1], saved[HAT_A2], par_mid, 2, saved[ACT_A2]
    )
    save(HAT_A2)
    save(ACT_A2)

    def expand(act_ref, weight):
        def body(d, carry):
            at = pl.ds(pl.multiple_of(d * 256, 256), 256)
            hid_out[:, at] = dot(act_ref[...], weight[d // 2, lax.rem(d, 2)].reshape(512, 256))
            return carry

        paced(0, 8, body, 2, pump)

    def out_sums(total, name_index, works):
        put_sums(plan, lambda j: [(hid_out[:, columns(j)],) * 2], mask, total.pay, 0, 2048, pump)
        total.begin()
        interleave(total.stages(), works)
        put_scales(total.total, inv_out.at[name_index], over, 2048)

    shortcut()
    as_stages[0]()
    ready(2)
    as_stages[1]()
    expand(saved[ACT_A2], w_a3)
    as_stages[2]()
    out_sums(sums[SUM_A3], 0, [as_stages[3], pump, as_stages[4], pump, lambda: add_square(2), lambda: add_square(3), pump])
    put_scales(sums[SUM_AS].total, inv_out.at[1], over, 2048)

    def join(j, carry):
        at = columns(j)
        v = normalized(hid_out[:, at], sums[SUM_A3].total, inv_out.at[0], saved[HAT_A3], par_out, 0, j)
        v = v + normalized(hid_as[:, at], sums[SUM_AS].total, inv_out.at[1], saved[HAT_AS], par_out, 2, j)
        saved[OUT_A][:, at] = (v * sigmoid(v) * mask[...]).astype(jnp.bfloat16)
        return carry

    paced(0, 16, join, 4, pump)
    for name in (HAT_A3, HAT_AS, OUT_A):
        save(name)

    ready(4)
    hid_mid[...] = dot_nt(saved[OUT_A][...], w_b1[...].reshape(512, -1))
    mid_sums(sums[SUM_B1], 2, [pump, lambda: add_square(4), pump])
    activate(
        lambda j: hid_mid[:, columns(j)], sums[SUM_B1].total, inv_mid.at[2], saved[HAT_B1], par_mid, 4, act.at[0]
    )
    save(HAT_B1)

    def patches(tap, carry):
        saved[PATCH_B][tap] = dot(shift[tap], act[0]).astype(jnp.bfloat16)
        return carry

    paced(0, 9, patches, 3, pump)
    save(PATCH_B)
    ready(5)
    spatial(saved[PATCH_B], w_b2)
    mid_sums(sums[SUM_B2], 3, [pump, lambda: add_square(5), pump])
    activate(
        lambda j: hid_mid[:, columns(j)], sums[SUM_B2].total, inv_mid.at[3], saved[HAT_B2], par_mid, 6, saved[ACT_B2]
    )
    save(HAT_B2)
    save(ACT_B2)
    ready(6)
    expand(saved[ACT_B2], w_b3)
    out_sums(sums[SUM_B3], 2, [lambda: add_square(6)])

    def finish(j, carry):
        at = columns(j)
        v = normalized(hid_out[:, at], sums[SUM_B3].total, inv_out.at[2], saved[HAT_B3], par_out, 4, j)
        v = v + saved[OUT_A][:, at].astype(jnp.float32)
        out[:, at] = (v * sigmoid(v) * mask[...]).astype(jnp.bfloat16)
        return carry

    lax.fori_loop(0, 16, finish, 0)
    save(HAT_B3)
    for total in sums.values():
        total.close()
    for i, name in enumerate(SAVED):
        pltpu.make_async_copy(saved[name], saved_hbm[name], save_sem.at[i]).wait()
    gather.close()
    for i in range(7):
        keep(i).wait()


def saved_shapes(rows):
    bf16 = jnp.bfloat16
    return (
        ((4, rows, 512), bf16),
        ((rows, 512), bf16),
        ((rows, 2048), bf16),
        ((rows, 2048), bf16),
        ((rows, 512), bf16),
        ((rows, 512), bf16),
        ((rows, 2048), bf16),
        ((9, rows, 512), bf16),
        ((9, rows, 512), bf16),
        ((rows, 512), bf16),
        ((rows, 512), bf16),
        ((rows, 2048), bf16),
    )


WHOLE = pl.BlockSpec(memory_space=pltpu.VMEM)
VMEM_LIMIT = 62 * 1024 * 1024


def run_forward(plan, depth, x, shifts, mask, counts, norm_mid, norm_out, shards):
    rows, f32, bf16 = plan.rows, jnp.float32, jnp.bfloat16
    dma = pltpu.SemaphoreType.DMA
    scratch = []
    for _, pieces in forward_names(depth):
        scratch += pieces
    scratch += [pltpu.VMEM(x.shape, bf16), pltpu.VMEM(shifts.shape, bf16)]
    fulls = [jax.ShapeDtypeStruct((depth, 2, *shard.shape), bf16) for shard in shards]
    scratch += [pltpu.VMEM(full.shape, bf16) for full in fulls]
    scratch += [pltpu.VMEM(shape, kind) for shape, kind in saved_shapes(rows)]
    scratch += [
        pltpu.VMEM((4, rows, 512), f32),
        pltpu.VMEM((rows, 512), f32),
        pltpu.VMEM((rows, 2048), f32),
        pltpu.VMEM((rows, 2048), f32),
        pltpu.VMEM((4, rows, 512), bf16),
        dma((2,)),
        dma((len(SAVED),)),
        dma((7,)),
    ]
    scratch += Gather.scratch(depth)
    small = [
        jax.ShapeDtypeStruct((rows, 2048), bf16),
        jax.ShapeDtypeStruct((4, 8, 512), f32),
        jax.ShapeDtypeStruct((3, 8, 2048), f32),
        jax.ShapeDtypeStruct((8, 512), f32),
        jax.ShapeDtypeStruct((8, 2048), f32),
        jax.ShapeDtypeStruct((8, 128), f32),
        jax.ShapeDtypeStruct((8, 128), f32),
    ]
    return pl.pallas_call(
        functools.partial(forward_kernel, plan, depth),
        out_shape=small + fulls + [jax.ShapeDtypeStruct(shape, kind) for shape, kind in saved_shapes(rows)],
        in_specs=[ANY, ANY] + [WHOLE] * 4 + [ANY] * 7,
        out_specs=[WHOLE] * 7 + [ANY] * 7 + [ANY] * len(SAVED),
        scratch_shapes=scratch,
        compiler_params=pltpu.CompilerParams(collective_id=0, has_side_effects=True, vmem_limit_bytes=VMEM_LIMIT),
    )(x, shifts, mask, counts, norm_mid, norm_out, *shards)


def backward_names(depth):
    return (
        (SUM_B3, Split.scratch(2048, depth)),
        (SUM_B2, NearFar.scratch(512, depth)),
        (SUM_B1, NearFar.scratch(512, depth)),
        (SUM_J, Split.scratch(4096, depth)),
        (SUM_A2, NearFar.scratch(512, depth)),
        (SUM_A1, NearFar.scratch(512, depth)),
    )


def backward_kernel(plan, depth, *refs):
    refs = list(refs)

    def take(count):
        taken = refs[:count]
        del refs[:count]
        return taken

    x_hbm, shift_hbm, cot_hbm, mask, weight_squares, inv_mid, inv_out, par_mid, par_out, over = take(10)
    saved_hbm = dict(zip(SAVED, take(len(SAVED))))
    weights_hbm = take(7)
    dx_hbm, pgrad_mid, pgrad_b3, pgrad_j, squares_out = take(5)
    gradients_hbm, c_hbm, y_hbm = take(7), take(7), take(7)
    sums = {}
    for name, scratch in backward_names(depth):
        sums[name] = (NearFar if len(scratch) == 7 else Split)(take(len(scratch)), depth)
    x, shift, cot = take(3)
    w_a1, w_a2, w_a3, w_as, w_b1, w_b2, w_b3 = weights = take(7)
    kept = [name for name in SAVED if name != PATCH_B]
    saved = dict(zip(kept, take(len(kept))))
    saved[PATCH_B] = saved[PATCH_A]
    dz, dact, dh_mid, flip = take(4)
    load_sem, saved_sem, dx_sem = take(3)
    dh_a, dh_b = cot, saved[HAT_B3]
    planes = [saved[HAT_AS].at[:, pl.ds(plane * 512, 512)] for plane in range(4)]
    reduce = Reduce(weights, gradients_hbm, c_hbm, y_hbm, refs, depth)
    reduce.squares[2 * depth + 2] = jnp.zeros((8, 128), jnp.float32)

    def pump():
        reduce.pump()

    def loading(name):
        return pltpu.make_async_copy(saved_hbm[name], saved[name], saved_sem.at[SAVED.index(name)])

    loads = [
        pltpu.make_async_copy(src, dst, load_sem.at[i])
        for i, (src, dst) in enumerate(zip([x_hbm, shift_hbm, cot_hbm, *weights_hbm], [x, shift, cot, *weights]))
    ]
    first = (HAT_B3, OUT_A)
    for name in first:
        loading(name).start()
    loads[2].start()
    order = (HAT_B2, ACT_B2, HAT_B1, PATCH_B, HAT_A3, HAT_AS, HAT_A2, ACT_A2, HAT_A1)
    loads[9].start()
    for name in order[:4]:
        loading(name).start()
    for i in (1, 8, 7):
        loads[i].start()
    for name in order[4:]:
        loading(name).start()
    for i in (5, 6, 4, 0, 3):
        loads[i].start()

    greet(depth)

    def quarter(d):
        return pl.ds(pl.multiple_of(d * 256, 256), 256)

    def affine(hat, params, row, at):
        return hat[:, at].astype(jnp.float32) * params[row : row + 1, at] + params[row + 1 : row + 2, at]

    def norm_back(dz_of, hat, total, base, inverse, params, row, target, blocks):
        def body(j, carry):
            at = columns(j)
            sums_at = columns(base + j)
            gain = params[row : row + 1, at]
            value, xhat = dz_of(j), hat[:, at].astype(jnp.float32)

            def of(g, span):
                first = total[g : g + 1, sums_at] * over_of(g)
                second = total[3 + g : 4 + g, sums_at] * over_of(g)
                return (gain * inverse[g : g + 1, at]) * (value[span] - first - xhat[span] * second)

            target[:, at] = (by_group(plan, of) * mask[...]).astype(jnp.bfloat16)
            return carry

        paced(0, blocks, body, 1 if blocks == 4 else 2, pump)

    scale = [1.0]

    def over_of(g):
        return over[g : g + 1, :] * scale[0]

    for name in first:
        loading(name).wait()
    loads[2].wait()

    def out_pairs(j):
        at = columns(j)
        v = affine(saved[HAT_B3], par_out, 4, at) + saved[OUT_A][:, at].astype(jnp.float32)
        value = cot[:, at].astype(jnp.float32) * mask[...] * slope(v)
        dz[:, at] = value
        return [(value, saved[HAT_B3][:, at].astype(jnp.float32))]

    total = sums[SUM_B3]
    put_sums(plan, out_pairs, mask, total.pay, 0, 2048)
    total.begin()
    for i in (9, 1, 8, 7):
        loads[i].wait()
    for name in order[:4]:
        loading(name).wait()
    flip[0:512] = saved[ACT_B2][...].T
    interleave(total.stages(), [])
    pgrad_b3[...] = total.total[...]
    norm_back(lambda j: dz[:, columns(j)], saved[HAT_B3], total.total, 0, inv_out.at[2], par_out, 4, dh_a, 16)

    def contract(dh, weight):
        dact[...] = dot_nt(dh[:, 0:256], weight[0, 0].reshape(512, 256))

        def body(d, carry):
            dact[...] += dot_nt(dh[:, quarter(d)], weight[d // 2, lax.rem(d, 2)].reshape(512, 256))
            return carry

        paced(1, 8, body, 2, pump)

    def expand_term(lhs, dh, weight, first_slot, last_slot):
        def body(d, carry):
            shape = weight.shape[2:]
            weight[d // 2, lax.rem(d, 2)] = dot(lhs, dh[:, quarter(d)]).astype(jnp.bfloat16).reshape(shape)
            return carry

        lax.fori_loop(first_slot, last_slot, body, 0)

    def mid_pairs(hat, row):
        def pairs(j):
            at = columns(j)
            value = dact[:, at] * slope(affine(saved[hat], par_mid, row, at))
            dact[:, at] = value
            return [(value, saved[hat][:, at].astype(jnp.float32))]

        return pairs

    def mid_norm(name, hat, index, row, works):
        total = sums[name]
        put_sums(plan, mid_pairs(hat, row), mask, total.pay, 0, 512, pump)
        total.begin()
        interleave(total.stages(), works)
        pgrad_mid[index] = total.total[...]
        norm_back(lambda j: dact[:, columns(j)], saved[hat], total.total, 0, inv_mid.at[index], par_mid, row, dh_mid, 4)

    contract(dh_a, w_b3)

    def third_term(part):
        def work():
            expand_term(flip[0:512, :], dh_a, w_b3, 4 * part, 4 * part + 4)
            if part:
                reduce.enable(6)
                pump()

        return work

    mid_norm(SUM_B2, HAT_B2, 3, 6, [third_term(0), third_term(1)])

    def spread(tap, carry):
        part = dot(
            dot(shift[8 - tap], dh_mid[...]).astype(jnp.bfloat16), w_b2[:, :, tap].reshape(512, 512)
        )
        dact[...] = part + jnp.where(tap == 0, 0.0, dact[...])
        return carry

    paced(0, 9, spread, 5, pump)
    flip[0:512] = dh_mid[...].T

    def spatial_term(weight, patch, first_tap, last_tap, tensor):
        def work():
            def body(tap, carry):
                weight[:, :, tap] = dot(flip[0:512, :], patch[tap]).astype(jnp.bfloat16).reshape(depth, 2, 64, 512)
                return carry

            lax.fori_loop(first_tap, last_tap, body, 0)
            reduce.enable(tensor, last_tap)
            pump()

        return work

    mid_norm(
        SUM_B1,
        HAT_B1,
        2,
        4,
        [spatial_term(w_b2, saved[PATCH_B], 0, 3, 5), spatial_term(w_b2, saved[PATCH_B], 3, 6, 5)],
    )
    spatial_term(w_b2, saved[PATCH_B], 6, 9, 5)()
    loading(PATCH_A).start()

    def residual(d, carry):
        at = quarter(d)
        dz[:, at] = dz[:, at] + dot(dh_mid[...], w_b1[:, :, 0, :, at].reshape(512, 256))
        return carry

    paced(0, 8, residual, 2, pump)
    for name in order[4:]:
        loading(name).wait()

    def join_pairs(j):
        at = columns(j)
        v = affine(saved[HAT_A3], par_out, 0, at) + affine(saved[HAT_AS], par_out, 2, at)
        value = dz[:, at] * mask[...] * slope(v)
        dz[:, at] = value
        return [(value, saved[HAT_A3][:, at].astype(jnp.float32))]

    total = sums[SUM_J]
    put_sums(plan, join_pairs, mask, total.pay, 0, 2048, pump)
    put_sums(
        plan, lambda j: [(dz[:, columns(j)], saved[HAT_AS][:, columns(j)].astype(jnp.float32))], mask, total.pay, 16, 2048, pump
    )
    total.begin()
    flip[0:512] = dh_mid[...].T

    def first_term(part):
        def work():
            def body(d, carry):
                at = quarter(d)
                value = dot(flip[0:512, :], saved[OUT_A][:, at]).astype(jnp.bfloat16)
                w_b1[:, :, 0, :, at] = value.reshape(depth, 2, 64, 256)
                return carry

            lax.fori_loop(2 * part, 2 * part + 2, body, 0)
            if part == 3:
                reduce.enable(4)
            pump()

        return work

    interleave(total.stages(), [first_term(part) for part in range(4)])
    pgrad_j[...] = total.total[...]
    norm_back(lambda j: dz[:, columns(j)], saved[HAT_A3], total.total, 0, inv_out.at[0], par_out, 0, dh_a, 16)
    pump()
    norm_back(lambda j: dz[:, columns(j)], saved[HAT_AS], total.total, 16, inv_out.at[1], par_out, 2, dh_b, 16)
    for i in (5, 6, 4, 0, 3):
        loads[i].wait()

    pump()
    contract(dh_a, w_a3)
    pump()
    flip[0:512] = saved[ACT_A2][...].T

    def third_term_a():
        expand_term(flip[0:512, :], dh_a, w_a3, 0, 4)
        pump()
        expand_term(flip[0:512, :], dh_a, w_a3, 4, 8)
        reduce.enable(2)
        pump()

    def shortcut():
        even = dz.at[:, 0:1024]
        even[...] = dot_nt(dh_b[:, 0:256], w_as[0, 0].reshape(1024, 256))

        def body(d, carry):
            even[...] += dot_nt(dh_b[:, quarter(d)], w_as[d // 2, lax.rem(d, 2)].reshape(1024, 256))
            return carry

        paced(1, 8, body, 3, pump)

        def keep(j, carry):
            value = even[:, columns(j)]
            high = value.astype(jnp.bfloat16)
            saved[OUT_A][:, columns(j)] = high
            saved[OUT_A][:, columns(8 + j)] = (value - high.astype(jnp.float32)).astype(jnp.bfloat16)
            return carry

        lax.fori_loop(0, 8, keep, 0)

    mid_norm(SUM_A2, HAT_A2, 1, 2, [third_term_a, shortcut])

    loading(PATCH_A).wait()
    flip[...] = x[0].T
    for part in range(4):
        expand_term(flip[...], dh_b, w_as, 2 * part, 2 * part + 2)
        pump()
    reduce.enable(3)
    for plane in range(4):
        at = slice(plane * 512, plane * 512 + 512)
        begun = False
        for tap in range(9):
            a, b = tap // 3, tap % 3
            if plane != (0 if a == 1 else 2) + (0 if b == 1 else 1):
                continue
            matrix = (2 if a == 0 else 1) * 3 + (2 if b == 0 else 1)
            moved = dh_mid[...] if matrix == 4 else dot(shift[matrix], dh_mid[...]).astype(jnp.bfloat16)
            part = dot(moved, w_a2[:, :, tap].reshape(512, 512))
            if begun:
                dz[:, at] += part
            else:
                dz[:, at] = part
            begun = True
        pump()

    def plane_pairs(j):
        at = columns(j)
        pairs = []
        for plane in range(4):
            wide = columns(4 * plane + j)
            xhat = saved[HAT_A1][plane, :, at].astype(jnp.float32)
            v = xhat * par_mid[0:1, at] + par_mid[1:2, at]
            value = dz[:, wide] * slope(v)
            dz[:, wide] = value
            pairs.append((value, xhat))
        return pairs

    total = sums[SUM_A1]
    put_sums(plan, plane_pairs, mask, total.pay, 0, 512, pump)
    total.begin()
    flip[0:512] = dh_mid[...].T
    stages = total.stages()
    spatial_term(w_a2, saved[PATCH_A], 0, 3, 1)()
    stages[0]()
    spatial_term(w_a2, saved[PATCH_A], 3, 6, 1)()
    stages[1]()
    spatial_term(w_a2, saved[PATCH_A], 6, 9, 1)()
    pgrad_mid[0] = total.total[...]
    scale[0] = 0.25
    for plane in range(4):
        norm_back(
            lambda j, plane=plane: dz[:, columns(4 * plane + j)],
            saved[HAT_A1].at[plane],
            total.total,
            0,
            inv_mid.at[0],
            par_mid,
            0,
            planes[plane],
            4,
        )

    def input_gradient(p):
        target = (dh_a if p < 2 else dh_b).at[:, pl.ds((p % 2) * 1024, 1024)]
        value = dot(planes[p][...], w_a1[...].reshape(512, -1))
        if p == 0:
            value = value + saved[OUT_A][:, 0:1024].astype(jnp.float32)
            value = value + saved[OUT_A][:, 1024:2048].astype(jnp.float32)
        target[...] = value.astype(jnp.bfloat16)
        copy = pltpu.make_async_copy(target, dx_hbm.at[p], dx_sem.at[p])
        copy.start()
        return copy

    copies = []
    for p in range(4):
        copies.append(input_gradient(p))
        pump()

    def last_term(c, carry):
        at = quarter(c)
        total = jnp.zeros((512, 256), jnp.float32)
        for p in range(4):
            total = total + lax.dot_general(
                planes[p][...], x[p, :, at], (((0,), (0,)), ((), ())), preferred_element_type=jnp.float32
            )
        w_a1[:, :, 0, :, at] = total.astype(jnp.bfloat16).reshape(depth, 2, 64, 256)
        return carry

    paced(0, 4, last_term, 2, pump)
    reduce.enable(0)
    reduce.finish(weight_squares, squares_out)
    for copy in copies:
        copy.wait()
    for total in sums.values():
        total.close()


def run_backward(plan, depth, x, shifts, cot, mask, weight_squares, small, saved, fulls):
    rows, f32, bf16 = plan.rows, jnp.float32, jnp.bfloat16
    dma = pltpu.SemaphoreType.DMA
    scratch = []
    for _, pieces in backward_names(depth):
        scratch += pieces
    scratch += [pltpu.VMEM(value.shape, bf16) for value in (x, shifts, cot)]
    scratch += [pltpu.VMEM(full.shape, bf16) for full in fulls]
    scratch += [pltpu.VMEM(shape, kind) for name, (shape, kind) in zip(SAVED, saved_shapes(rows)) if name != PATCH_B]
    scratch += [
        pltpu.VMEM((rows, 2048), f32),
        pltpu.VMEM((rows, 512), f32),
        pltpu.VMEM((rows, 512), bf16),
        pltpu.VMEM((1024, rows), bf16),
        dma((10,)),
        dma((len(SAVED),)),
        dma((4,)),
    ]
    shapes = [full.shape for full in fulls]
    scratch += Reduce.scratch(shapes, depth)

    def part(shape, over):
        return jax.ShapeDtypeStruct((*shape[:3], shape[3] // over, shape[4]), bf16)

    outs = pl.pallas_call(
        functools.partial(backward_kernel, plan, depth),
        out_shape=[
            jax.ShapeDtypeStruct(x.shape, bf16),
            jax.ShapeDtypeStruct((4, 8, 512), f32),
            jax.ShapeDtypeStruct((8, 2048), f32),
            jax.ShapeDtypeStruct((8, 4096), f32),
            jax.ShapeDtypeStruct((8, 128), f32),
        ]
        + [jax.ShapeDtypeStruct(shape[2:], bf16) for shape in shapes]
        + [part(shape, 2) for shape in shapes]
        + [part(shape, 4) for shape in shapes],
        in_specs=[ANY] * 3 + [WHOLE] * 7 + [ANY] * len(SAVED) + [ANY] * 7,
        out_specs=[ANY] + [WHOLE] * 4 + [ANY] * 21,
        scratch_shapes=scratch,
        compiler_params=pltpu.CompilerParams(collective_id=1, has_side_effects=True, vmem_limit_bytes=VMEM_LIMIT),
    )(x, shifts, cot, mask, weight_squares, *small, *saved, *fulls)
    return outs[:12]


def scale_kernel(squares, *refs):
    totals, weights, outs, rest = refs[:7], refs[7:14], refs[14:28], refs[28:]
    totals_in, weights_in, staged = rest[:7], rest[7:14], rest[14:28]
    in_sem, out_sem = rest[28:]

    def loads(i):
        return (
            pltpu.make_async_copy(totals[i], totals_in[i], in_sem.at[0, i]),
            pltpu.make_async_copy(weights[i], weights_in[i], in_sem.at[1, i]),
        )

    def stores(i):
        return [pltpu.make_async_copy(staged[2 * i + n], outs[2 * i + n], out_sem.at[n, i]) for n in (0, 1)]

    for i in range(7):
        for copy in loads(i):
            copy.start()
    weight_norm = jnp.sqrt(squares[0:1, :])
    trust = weight_norm / (jnp.sqrt(squares[1:2, :]) + DECAY_RATE * weight_norm)
    for i in range(7):
        for copy in loads(i):
            copy.wait()
        ratio = trust[0:1, i : i + 1]

        def body(lead, carry, i=i, ratio=ratio):
            gradient = totals_in[i][lead].astype(jnp.float32)
            staged[2 * i][lead] = gradient
            decayed = gradient + DECAY_RATE * weights_in[i][lead].astype(jnp.float32)
            staged[2 * i + 1][lead] = ratio * decayed
            return carry

        lax.fori_loop(0, totals_in[i].shape[0], body, 0)
        for copy in stores(i):
            copy.start()
    for i in range(7):
        for copy in stores(i):
            copy.wait()


def run_scale(squares, totals, shards):
    f32, bf16, dma = jnp.float32, jnp.bfloat16, pltpu.SemaphoreType.DMA
    shapes = [total.shape for total in totals]
    outs = pl.pallas_call(
        scale_kernel,
        out_shape=[jax.ShapeDtypeStruct(shape, f32) for shape in shapes for _ in (0, 1)],
        in_specs=[WHOLE] + [ANY] * 14,
        out_specs=[ANY] * 14,
        scratch_shapes=[pltpu.VMEM(shape, bf16) for shape in shapes * 2]
        + [pltpu.VMEM(shape, f32) for shape in shapes for _ in (0, 1)]
        + [dma((2, 7)), dma((2, 7))],
        compiler_params=pltpu.CompilerParams(vmem_limit_bytes=VMEM_LIMIT),
    )(squares, *totals, *shards)
    return outs[0::2], outs[1::2]


def on_device(
    input_160,
    input_224,
    input_288,
    cotangent_160,
    cotangent_224,
    cotangent_288,
    live_counts,
    conv_a1,
    norm_a1,
    conv_a2,
    norm_a2,
    conv_a3,
    norm_a3,
    conv_as,
    norm_as,
    conv_b1,
    norm_b1,
    conv_b2,
    norm_b2,
    conv_b3,
    norm_b3,
):
    if conv_a1.shape[1] % 64 or conv_a3.shape[1] % 128 or lax.axis_size(REP) != 4:
        return plain_on_device(
            input_160,
            input_224,
            input_288,
            cotangent_160,
            cotangent_224,
            cotangent_288,
            live_counts,
            conv_a1,
            norm_a1,
            conv_a2,
            norm_a2,
            conv_a3,
            norm_a3,
            conv_as,
            norm_as,
            conv_b1,
            norm_b1,
            conv_b2,
            norm_b2,
            conv_b3,
            norm_b3,
        )
    depth = lax.axis_size(DP) // 2
    inputs = (input_160, input_224, input_288)
    plan = Plan([value.shape for value in inputs])
    shards = (
        conv_a1.T[None],
        jnp.transpose(conv_a2, (0, 1, 3, 2)).reshape(9, conv_a2.shape[3], conv_a2.shape[2]),
        conv_a3.reshape(2, -1, conv_a3.shape[1]),
        conv_as.reshape(4, -1, conv_as.shape[1]),
        conv_b1.T[None],
        jnp.transpose(conv_b2, (0, 1, 3, 2)).reshape(9, conv_b2.shape[3], conv_b2.shape[2]),
        conv_b3.reshape(2, -1, conv_b3.shape[1]),
    )

    planes, cotangents, masks, live_pixels = [], [], [], []
    for g, (value, cotangent) in enumerate(
        zip(inputs, (cotangent_160, cotangent_224, cotangent_288))
    ):
        side, slots, fill = plan.sides[g], plan.slots[g], plan.sizes[g] - plan.valid[g]
        split = jnp.transpose(value, (1, 2, 0, 3)).reshape(side, 2, side, 2, slots, -1)
        split = jnp.transpose(split, (1, 3, 0, 2, 4, 5)).reshape(4, plan.valid[g], -1)
        planes.append(jnp.pad(split, ((0, 0), (0, fill), (0, 0))))
        cotangents.append(
            jnp.pad(jnp.transpose(cotangent, (1, 2, 0, 3)).reshape(plan.valid[g], -1), ((0, fill), (0, 0)))
        )
        row = jnp.arange(plan.sizes[g])
        live = (lax.rem(row, slots) < live_counts[0, g]) & (row < plan.valid[g])
        masks.append(jnp.broadcast_to(live.astype(jnp.float32)[:, None], (plan.sizes[g], 128)))
        live_pixels.append((live_counts[0, g] * (side * side)).astype(jnp.float32))
    x = jnp.concatenate(planes, axis=1)
    cot = jnp.concatenate(cotangents, axis=0)
    mask = jnp.concatenate(masks, axis=0)
    counts = jnp.pad(jnp.stack(live_pixels), (0, 125)).reshape(1, 128)

    def own_place(norms, width):
        rows = jnp.concatenate(norms, axis=0).astype(jnp.float32)
        rows = jnp.pad(rows, ((0, 8 - rows.shape[0]), (0, 0)))
        rows = jnp.where(lax.axis_index(REP) == 0, rows, 0.0)
        start = lax.axis_index(DP) * rows.shape[1]
        return lax.dynamic_update_slice(jnp.zeros((8, width), jnp.float32), rows, (0, start))

    mid_local, out_local = norm_a1.shape[1], norm_a3.shape[1]
    mid_width, out_width = mid_local * 2 * depth, out_local * 2 * depth
    norm_mid = own_place((norm_a1, norm_a2, norm_b1, norm_b2), mid_width)
    norm_out = own_place((norm_a3, norm_as, norm_b3), out_width)
    shifts = jnp.asarray(plan.shifts())

    out, *results = run_forward(plan, depth, x, shifts, mask, counts, norm_mid, norm_out, shards)
    small, square_row, fulls, saved = results[:5], results[5], results[6:13], results[13:]
    dx, pgrad_mid, pgrad_b3, pgrad_j, squares, *totals = run_backward(
        plan, depth, x, shifts, cot, mask, square_row, small, saved, fulls
    )

    def placed(values):
        return [
            values[0][0].T,
            jnp.transpose(values[1], (0, 2, 1)).reshape(conv_a2.shape),
            values[2].reshape(conv_a3.shape),
            values[3].reshape(conv_as.shape),
            values[4][0].T,
            jnp.transpose(values[5], (0, 2, 1)).reshape(conv_b2.shape),
            values[6].reshape(conv_b3.shape),
        ]

    gradients, scaled = run_scale(squares, totals, shards)
    gradients, scaled = placed(gradients), placed(scaled)

    def norm_gradient(sums, local):
        both = jnp.stack([sums[3] + sums[4] + sums[5], sums[0] + sums[1] + sums[2]])
        return lax.dynamic_slice_in_dim(both, lax.axis_index(DP) * local, local, 1)

    norm_gradients = (
        norm_gradient(pgrad_mid[0], mid_local),
        norm_gradient(pgrad_mid[1], mid_local),
        norm_gradient(pgrad_j[:, :out_width], out_local),
        norm_gradient(pgrad_j[:, out_width:], out_local),
        norm_gradient(pgrad_mid[2], mid_local),
        norm_gradient(pgrad_mid[3], mid_local),
        norm_gradient(pgrad_b3, out_local),
    )
    outputs, grad_inputs = [], []
    for g in range(3):
        side, slots, start = plan.sides[g], plan.slots[g], plan.starts[g]
        rows = out[start : start + plan.valid[g]].reshape(side, side, slots, -1)
        outputs.append(jnp.transpose(rows, (2, 0, 1, 3)))
        split = dx[:, start : start + plan.valid[g]].reshape(2, 2, side, side, slots, -1)
        split = jnp.transpose(split, (2, 0, 3, 1, 4, 5)).reshape(2 * side, 2 * side, slots, -1)
        grad_inputs.append(jnp.transpose(split, (2, 0, 1, 3)))
    pairs = [piece for pair in zip(gradients, norm_gradients) for piece in pair]
    return (*outputs, *grad_inputs, *pairs, *scaled, squares[0:2, 0:7])


def solution(mesh):
    by_image, by_column = P((DP, REP), None, None, None), P(None, DP)
    by_channel = P(None, None, None, DP)
    weights = [by_column, by_column, by_channel] + [by_column] * 7 + [by_channel] + [by_column] * 3
    kernels = [by_column, by_channel] + [by_column] * 3 + [by_channel, by_column]
    return jax.shard_map(
        on_device,
        mesh=mesh,
        in_specs=(*[by_image] * 6, P((DP, REP), None), *weights),
        out_specs=(*[by_image] * 6, *weights, *kernels, P()),
        check_vma=False,
    )
```

```python
import functools

import jax
import jax.numpy as jnp
import numpy as np
from jax import lax
from jax.experimental import pallas as pl
from jax.experimental.pallas import tpu as pltpu
from jax.sharding import PartitionSpec as P

DP, REP = "dp", "rep"
EPSILON = 1e-05
DECAY_RATE = 5e-05


def silu_slope(values):
    sigmoid = jax.nn.sigmoid(values)
    return sigmoid * (1.0 + values * (1.0 - sigmoid))


def pointwise(inputs, weight):
    return jnp.tensordot(inputs, weight, 1, preferred_element_type=jnp.float32)


def pointwise_back(upstream, weight):
    return jnp.tensordot(upstream, weight, ((3,), (1,)), preferred_element_type=jnp.float32)


def weight_term(inputs, upstream):
    return jnp.tensordot(inputs, upstream, ((0, 1, 2),) * 2, preferred_element_type=jnp.float32)


def summed_terms(inputs, upstream):
    running = weight_term(inputs[0], upstream[0])
    for group_member in (1, 2):
        running = running + weight_term(inputs[group_member], upstream[group_member])
    return running


def patches(inputs, stride):
    padded = jnp.pad(inputs, ((0, 0), (1, 1), (1, 1), (0, 0)))
    extent = inputs.shape[1]
    pieces = []
    for offset_row in range(3):
        for offset_col in range(3):
            pieces.append(
                padded[
                    :,
                    offset_row : offset_row + extent : stride,
                    offset_col : offset_col + extent : stride,
                    :,
                ]
            )
    return jnp.concatenate(pieces, axis=3)


def fold_patches(upstream, stride, side_in):
    channels = upstream.shape[3] // 9
    padded = jnp.zeros((upstream.shape[0], side_in + 2, side_in + 2, channels), jnp.float32)
    for offset_row in range(3):
        for offset_col in range(3):
            start_at = (offset_row * 3 + offset_col) * channels
            padded = padded.at[
                :,
                offset_row : offset_row + side_in : stride,
                offset_col : offset_col + side_in : stride,
                :,
            ].add(upstream[..., start_at : start_at + channels])
    return padded[:, 1 : side_in + 1, 1 : side_in + 1, :]


def batch_norm(values, live_masks, norm_param, totals):
    gain_row = norm_param[0].astype(jnp.float32)
    shift_row = norm_param[1].astype(jnp.float32)
    firsts = []
    seconds = []
    for group_member in range(3):
        weighted = values[group_member] * live_masks[group_member]
        firsts.append(jnp.sum(weighted, axis=(0, 1, 2)))
        seconds.append(jnp.sum(weighted * values[group_member], axis=(0, 1, 2)))
    summed = lax.psum(
        (firsts[0], seconds[0], firsts[1], seconds[1], firsts[2], seconds[2]), (DP, REP)
    )
    normed = []
    means = []
    scales = []
    for group_member in range(3):
        pixel_count = (
            totals[group_member] * values[group_member].shape[1] * values[group_member].shape[2]
        )
        mean_value = summed[2 * group_member] / pixel_count
        inv_std = lax.rsqrt(
            summed[2 * group_member + 1] / pixel_count - mean_value * mean_value + EPSILON
        )
        normed.append((values[group_member] - mean_value) * inv_std * gain_row + shift_row)
        means.append(mean_value)
        scales.append(inv_std)
    return (normed, means, scales)


def norm_back(upstream, values, live_masks, norm_param, means, scales, totals):
    gain_row = norm_param[0].astype(jnp.float32)
    normals = []
    firsts = []
    seconds = []
    for group_member in range(3):
        normal = (values[group_member] - means[group_member]) * scales[group_member]
        weighted = upstream[group_member] * live_masks[group_member]
        normals.append(normal)
        firsts.append(jnp.sum(weighted, axis=(0, 1, 2)))
        seconds.append(jnp.sum(weighted * normal, axis=(0, 1, 2)))
    summed = lax.psum(
        (firsts[0], seconds[0], firsts[1], seconds[1], firsts[2], seconds[2]), (DP, REP)
    )
    results = []
    for group_member in range(3):
        pixel_count = (
            totals[group_member] * values[group_member].shape[1] * values[group_member].shape[2]
        )
        centered = (
            upstream[group_member]
            - summed[2 * group_member] / pixel_count
            - normals[group_member] * (summed[2 * group_member + 1] / pixel_count)
        )
        results.append(
            (live_masks[group_member] * gain_row * scales[group_member] * centered).astype(
                jnp.bfloat16
            )
        )
    param_grad = jnp.stack([summed[1] + summed[3] + summed[5], summed[0] + summed[2] + summed[4]])
    return (results, param_grad)


def own_columns(full, local_width):
    return lax.dynamic_slice_in_dim(full, lax.axis_index(DP) * local_width, local_width, 1)


def plain_on_device(
    input_160,
    input_224,
    input_288,
    cotangent_160,
    cotangent_224,
    cotangent_288,
    live_counts,
    conv_a1,
    norm_a1,
    conv_a2,
    norm_a2,
    conv_a3,
    norm_a3,
    conv_as,
    norm_as,
    conv_b1,
    norm_b1,
    conv_b2,
    norm_b2,
    conv_b3,
    norm_b3,
):
    inputs = (input_160, input_224, input_288)
    cotangents = (cotangent_160, cotangent_224, cotangent_288)
    live_masks = []
    masked = []
    for group_member in range(3):
        group_slot_count = inputs[group_member].shape[0]
        live_flags = (
            (jnp.arange(group_slot_count) < live_counts[0, group_member])
            .astype(jnp.float32)
            .reshape(group_slot_count, 1, 1, 1)
        )
        live_masks.append(live_flags)
        masked.append(inputs[group_member] * live_flags.astype(jnp.bfloat16))
    totals = lax.psum(live_counts[0].astype(jnp.float32), (DP, REP))
    local_weights = (conv_a1, conv_a2, conv_a3, conv_as, conv_b1, conv_b2, conv_b3)
    squares_list = []
    for weight in local_weights:
        squares_list.append(jnp.sum(jnp.square(weight.astype(jnp.float32))))
    weight_squares = jnp.stack(squares_list)
    gathered_a = (
        lax.all_gather(conv_a1, DP, axis=1, tiled=True),
        lax.all_gather(norm_a1, DP, axis=1, tiled=True),
        lax.all_gather(conv_a2, DP, axis=3, tiled=True),
        lax.all_gather(norm_a2, DP, axis=1, tiled=True),
        lax.all_gather(conv_a3, DP, axis=1, tiled=True),
        lax.all_gather(norm_a3, DP, axis=1, tiled=True),
        lax.all_gather(conv_as, DP, axis=1, tiled=True),
        lax.all_gather(norm_as, DP, axis=1, tiled=True),
    )
    full_a1, param_a1, full_a2, param_a2, full_a3, param_a3, full_as, param_as = gathered_a
    mid_width = full_a2.shape[3]
    out_width = full_a3.shape[1]
    hidden_a1 = [pointwise(masked[group_member], full_a1) for group_member in range(3)]
    normed_a1, means_a1, scales_a1 = batch_norm(hidden_a1, live_masks, param_a1, totals)
    act_a1 = [
        jax.nn.silu(normed_a1[group_member]).astype(jnp.bfloat16) for group_member in range(3)
    ]
    kernel_a2 = full_a2.reshape(9 * mid_width, mid_width)
    hidden_a2 = [
        pointwise(patches(act_a1[group_member], 2), kernel_a2) for group_member in range(3)
    ]
    normed_a2, means_a2, scales_a2 = batch_norm(hidden_a2, live_masks, param_a2, totals)
    act_a2 = [
        jax.nn.silu(normed_a2[group_member]).astype(jnp.bfloat16) for group_member in range(3)
    ]
    strided = [masked[group_member][:, ::2, ::2, :] for group_member in range(3)]
    joined = [
        jnp.concatenate(
            [pointwise(act_a2[group_member], full_a3), pointwise(strided[group_member], full_as)],
            axis=3,
        )
        for group_member in range(3)
    ]
    param_joined = jnp.concatenate([param_a3, param_as], axis=1)
    normed_j, means_j, scales_j = batch_norm(joined, live_masks, param_joined, totals)
    sum_a = [
        normed_j[group_member][..., :out_width] + normed_j[group_member][..., out_width:]
        for group_member in range(3)
    ]
    out_a = [
        (jax.nn.silu(sum_a[group_member]) * live_masks[group_member]).astype(jnp.bfloat16)
        for group_member in range(3)
    ]
    gathered_b = (
        lax.all_gather(conv_b1, DP, axis=1, tiled=True),
        lax.all_gather(norm_b1, DP, axis=1, tiled=True),
        lax.all_gather(conv_b2, DP, axis=3, tiled=True),
        lax.all_gather(norm_b2, DP, axis=1, tiled=True),
        lax.all_gather(conv_b3, DP, axis=1, tiled=True),
        lax.all_gather(norm_b3, DP, axis=1, tiled=True),
    )
    full_b1, param_b1, full_b2, param_b2, full_b3, param_b3 = gathered_b
    hidden_b1 = [pointwise(out_a[group_member], full_b1) for group_member in range(3)]
    normed_b1, means_b1, scales_b1 = batch_norm(hidden_b1, live_masks, param_b1, totals)
    act_b1 = [
        jax.nn.silu(normed_b1[group_member]).astype(jnp.bfloat16) for group_member in range(3)
    ]
    kernel_b2 = full_b2.reshape(9 * mid_width, mid_width)
    hidden_b2 = [
        pointwise(patches(act_b1[group_member], 1), kernel_b2) for group_member in range(3)
    ]
    normed_b2, means_b2, scales_b2 = batch_norm(hidden_b2, live_masks, param_b2, totals)
    act_b2 = [
        jax.nn.silu(normed_b2[group_member]).astype(jnp.bfloat16) for group_member in range(3)
    ]
    hidden_b3 = [pointwise(act_b2[group_member], full_b3) for group_member in range(3)]
    normed_b3, means_b3, scales_b3 = batch_norm(hidden_b3, live_masks, param_b3, totals)
    sum_b = [
        normed_b3[group_member] + out_a[group_member].astype(jnp.float32)
        for group_member in range(3)
    ]
    outputs = [
        (jax.nn.silu(sum_b[group_member]) * live_masks[group_member]).astype(jnp.bfloat16)
        for group_member in range(3)
    ]
    back_b = (
        lax.all_gather(conv_b1, DP, axis=1, tiled=True),
        lax.all_gather(norm_b1, DP, axis=1, tiled=True),
        lax.all_gather(conv_b2, DP, axis=3, tiled=True),
        lax.all_gather(norm_b2, DP, axis=1, tiled=True),
        lax.all_gather(conv_b3, DP, axis=1, tiled=True),
        lax.all_gather(norm_b3, DP, axis=1, tiled=True),
    )
    full_b1, param_b1, full_b2, param_b2, full_b3, param_b3 = back_b
    kernel_b2 = full_b2.reshape(9 * mid_width, mid_width)
    grad_sum_b = [
        cotangents[group_member].astype(jnp.float32)
        * live_masks[group_member]
        * silu_slope(sum_b[group_member])
        for group_member in range(3)
    ]
    grad_h_b3, pgrad_b3 = norm_back(
        grad_sum_b, hidden_b3, live_masks, param_b3, means_b3, scales_b3, totals
    )
    term_b3 = summed_terms(act_b2, grad_h_b3)
    grad_act = [
        pointwise_back(grad_h_b3[group_member], full_b3) * silu_slope(normed_b2[group_member])
        for group_member in range(3)
    ]
    grad_h_b2, pgrad_b2 = norm_back(
        grad_act, hidden_b2, live_masks, param_b2, means_b2, scales_b2, totals
    )
    term_b2 = summed_terms(
        [patches(act_b1[group_member], 1) for group_member in range(3)], grad_h_b2
    ).reshape(3, 3, mid_width, mid_width)
    grad_act = [
        fold_patches(
            pointwise_back(grad_h_b2[group_member], kernel_b2), 1, act_b1[group_member].shape[1]
        )
        * silu_slope(normed_b1[group_member])
        for group_member in range(3)
    ]
    grad_h_b1, pgrad_b1 = norm_back(
        grad_act, hidden_b1, live_masks, param_b1, means_b1, scales_b1, totals
    )
    term_b1 = summed_terms(out_a, grad_h_b1)
    grad_out_a = [
        grad_sum_b[group_member] + pointwise_back(grad_h_b1[group_member], full_b1)
        for group_member in range(3)
    ]
    shard_b = (
        lax.psum_scatter(term_b1, DP, scatter_dimension=1, tiled=True),
        lax.psum_scatter(term_b2, DP, scatter_dimension=3, tiled=True),
        lax.psum_scatter(term_b3, DP, scatter_dimension=1, tiled=True),
    )
    grads_b = (
        lax.psum(shard_b[0].astype(jnp.bfloat16), REP).astype(jnp.float32),
        lax.psum(shard_b[1].astype(jnp.bfloat16), REP).astype(jnp.float32),
        lax.psum(shard_b[2].astype(jnp.bfloat16), REP).astype(jnp.float32),
    )
    back_a = (
        lax.all_gather(conv_a1, DP, axis=1, tiled=True),
        lax.all_gather(norm_a1, DP, axis=1, tiled=True),
        lax.all_gather(conv_a2, DP, axis=3, tiled=True),
        lax.all_gather(norm_a2, DP, axis=1, tiled=True),
        lax.all_gather(conv_a3, DP, axis=1, tiled=True),
        lax.all_gather(norm_a3, DP, axis=1, tiled=True),
        lax.all_gather(conv_as, DP, axis=1, tiled=True),
        lax.all_gather(norm_as, DP, axis=1, tiled=True),
    )
    full_a1, param_a1, full_a2, param_a2, full_a3, param_a3, full_as, param_as = back_a
    kernel_a2 = full_a2.reshape(9 * mid_width, mid_width)
    param_joined = jnp.concatenate([param_a3, param_as], axis=1)
    grad_sum_a = [
        grad_out_a[group_member] * live_masks[group_member] * silu_slope(sum_a[group_member])
        for group_member in range(3)
    ]
    grad_joined = [
        jnp.concatenate([grad_sum_a[group_member], grad_sum_a[group_member]], axis=3)
        for group_member in range(3)
    ]
    grad_h_j, pgrad_j = norm_back(
        grad_joined, joined, live_masks, param_joined, means_j, scales_j, totals
    )
    grad_h_a3 = [grad_h_j[group_member][..., :out_width] for group_member in range(3)]
    grad_h_as = [grad_h_j[group_member][..., out_width:] for group_member in range(3)]
    term_a3 = summed_terms(act_a2, grad_h_a3)
    term_as = summed_terms(strided, grad_h_as)
    grad_act = [
        pointwise_back(grad_h_a3[group_member], full_a3) * silu_slope(normed_a2[group_member])
        for group_member in range(3)
    ]
    grad_h_a2, pgrad_a2 = norm_back(
        grad_act, hidden_a2, live_masks, param_a2, means_a2, scales_a2, totals
    )
    term_a2 = summed_terms(
        [patches(act_a1[group_member], 2) for group_member in range(3)], grad_h_a2
    ).reshape(3, 3, mid_width, mid_width)
    grad_act = [
        fold_patches(
            pointwise_back(grad_h_a2[group_member], kernel_a2), 2, act_a1[group_member].shape[1]
        )
        * silu_slope(normed_a1[group_member])
        for group_member in range(3)
    ]
    grad_h_a1, pgrad_a1 = norm_back(
        grad_act, hidden_a1, live_masks, param_a1, means_a1, scales_a1, totals
    )
    term_a1 = summed_terms(masked, grad_h_a1)
    grad_inputs = [
        pointwise_back(grad_h_a1[group_member], full_a1)
        .at[:, ::2, ::2, :]
        .add(pointwise_back(grad_h_as[group_member], full_as))
        .astype(jnp.bfloat16)
        for group_member in range(3)
    ]
    shard_a = (
        lax.psum_scatter(term_a1, DP, scatter_dimension=1, tiled=True),
        lax.psum_scatter(term_a2, DP, scatter_dimension=3, tiled=True),
        lax.psum_scatter(term_a3, DP, scatter_dimension=1, tiled=True),
        lax.psum_scatter(term_as, DP, scatter_dimension=1, tiled=True),
    )
    grads_a = (
        lax.psum(shard_a[0].astype(jnp.bfloat16), REP).astype(jnp.float32),
        lax.psum(shard_a[1].astype(jnp.bfloat16), REP).astype(jnp.float32),
        lax.psum(shard_a[2].astype(jnp.bfloat16), REP).astype(jnp.float32),
        lax.psum(shard_a[3].astype(jnp.bfloat16), REP).astype(jnp.float32),
    )
    mid_local = norm_a1.shape[1]
    out_local = norm_a3.shape[1]
    norm_grad_a1 = own_columns(pgrad_a1, mid_local)
    norm_grad_a2 = own_columns(pgrad_a2, mid_local)
    norm_grad_a3 = own_columns(pgrad_j[:, :out_width], out_local)
    norm_grad_as = own_columns(pgrad_j[:, out_width:], out_local)
    norm_grad_b1 = own_columns(pgrad_b1, mid_local)
    norm_grad_b2 = own_columns(pgrad_b2, mid_local)
    norm_grad_b3 = own_columns(pgrad_b3, out_local)
    gradients = (grads_a[0], grads_a[1], grads_a[2], grads_a[3], grads_b[0], grads_b[1], grads_b[2])
    grad_list = []
    for gradient in gradients:
        grad_list.append(jnp.sum(gradient * gradient))
    grad_squares = jnp.stack(grad_list)
    weight_totals, grad_totals = lax.psum((weight_squares, grad_squares), DP)
    weight_norm = jnp.sqrt(weight_totals)
    grad_norm = jnp.sqrt(grad_totals)
    trust_ratio = weight_norm / (grad_norm + DECAY_RATE * weight_norm)
    scaled = [
        trust_ratio[layer_id]
        * (gradients[layer_id] + DECAY_RATE * local_weights[layer_id].astype(jnp.float32))
        for layer_id in range(7)
    ]
    return (
        outputs[0],
        outputs[1],
        outputs[2],
        grad_inputs[0],
        grad_inputs[1],
        grad_inputs[2],
        gradients[0],
        norm_grad_a1,
        gradients[1],
        norm_grad_a2,
        gradients[2],
        norm_grad_a3,
        gradients[3],
        norm_grad_as,
        gradients[4],
        norm_grad_b1,
        gradients[5],
        norm_grad_b2,
        gradients[6],
        norm_grad_b3,
        scaled[0],
        scaled[1],
        scaled[2],
        scaled[3],
        scaled[4],
        scaled[5],
        scaled[6],
        jnp.stack([weight_totals, grad_totals]),
    )


MESH = pl.DeviceIdType.MESH
ANY = pl.BlockSpec(memory_space=pl.ANY)


def position():
    dp, rep = lax.axis_index(DP), lax.axis_index(REP)
    return dp // 2, lax.rem(dp, 2), rep // 2, lax.rem(rep, 2)


def device_at(z, x, y, core):
    return (z * 2 + x, y * 2 + core)


def greet(depth, crosswise=False):
    z, x, y, core = position()
    barrier = pltpu.get_barrier_semaphore()
    peers = [(z, x, y, 1 - core), (z, x, 1 - y, core), (z, x, 1 - y, 1 - core)]
    peers += [(z, 1 - x, y, core), (z, 1 - x, y, 1 - core), (z, 1 - x, 1 - y, core), (z, 1 - x, 1 - y, 1 - core)]
    peers += [(lax.rem(z + step, depth), x, y, core) for step in range(1, depth)]
    if crosswise:
        peers += [(lax.rem(z + step, depth), 1 - x, y, core) for step in range(1, depth)]
    for peer in peers:
        pl.semaphore_signal(barrier, inc=1, device_id=device_at(*peer), device_id_type=MESH)
    pl.semaphore_wait(barrier, len(peers))


def remote(src, dst, send, recv, peer):
    return pltpu.make_async_remote_copy(
        src_ref=src, dst_ref=dst, send_sem=send, recv_sem=recv, device_id=device_at(*peer), device_id_type=MESH
    )


def chunk_rows(rows, both, y, core):
    if both:
        return pl.ds(pl.multiple_of(core * (rows // 2), rows // 2), rows // 2)
    return pl.ds(pl.multiple_of(core * (rows // 2) + y * (rows // 4), rows // 4), rows // 4)


def core_rows(rows, core):
    return pl.ds(pl.multiple_of(core * (rows // 2), rows // 2), rows // 2)


class Gather:
    AHEAD = 2

    def __init__(self, shards, fulls, sems, depth):
        self.shards, self.fulls, self.depth = shards, fulls, depth
        (self.local_sem, self.z_send, self.z_recv, self.x_send, self.x_recv) = sems[:5]
        (self.y_send, self.y_recv, self.c_send, self.c_recv) = sems[5:]
        self.z, self.x, self.y, self.core = position()
        self.count = len(GATHER_CHUNKS)
        self.z_next = self.x_next = self.y_next = self.c_next = 0

    @staticmethod
    def scratch(depth):
        dma, count = pltpu.SemaphoreType.DMA, len(GATHER_CHUNKS)
        return [dma((count,))] + [dma((count, depth - 1))] * 2 + [dma((count,))] * 6

    def part(self, k):
        tensor, lead, leads, both, column, columns = GATHER_CHUNKS[k]
        rows = chunk_rows(self.shards[tensor].shape[1], both, self.y, self.core)
        return self.fulls[tensor], pl.ds(lead, leads), rows, pl.ds(column, columns)

    def place(self, k):
        full, lead, rows, cols = self.part(k)
        shard = self.shards[GATHER_CHUNKS[k][0]]
        return pltpu.make_async_copy(
            shard.at[lead, rows, cols], full.at[self.z, self.x, lead, rows, cols], self.local_sem.at[k]
        )

    def z_copies(self, k):
        full, lead, rows, cols = self.part(k)
        here = full.at[self.z, self.x, lead, rows, cols]
        return [
            remote(
                here,
                here,
                self.z_send.at[k, step - 1],
                self.z_recv.at[k, step - 1],
                (lax.rem(self.z + step, self.depth), self.x, self.y, self.core),
            )
            for step in range(1, self.depth)
        ]

    def x_copy(self, k):
        full, lead, rows, cols = self.part(k)
        here = full.at[:, self.x, lead, rows, cols]
        return remote(here, here, self.x_send.at[k], self.x_recv.at[k], (self.z, 1 - self.x, self.y, self.core))

    def y_copy(self, k):
        full, lead, rows, cols = self.part(k)
        here = full.at[:, :, lead, rows, cols]
        return remote(here, here, self.y_send.at[k], self.y_recv.at[k], (self.z, self.x, 1 - self.y, self.core))

    def c_copy(self, k):
        full, lead, _, cols = self.part(k)
        here = full.at[:, :, lead, core_rows(full.shape[3], self.core), cols]
        return remote(here, here, self.c_send.at[k], self.c_recv.at[k], (self.z, self.x, self.y, 1 - self.core))

    def place_all(self):
        for k in range(self.count):
            self.place(k).start()

    def launch(self, k):
        if k < self.count:
            self.place(k).wait()
            for copy in self.z_copies(k):
                copy.start()

    def begin(self):
        for k in range(self.AHEAD):
            self.launch(k)

    def z_step(self):
        k, self.z_next = self.z_next, self.z_next + 1
        for copy in self.z_copies(k):
            copy.wait_recv()
        self.x_copy(k).start()
        self.launch(k + self.AHEAD)

    def x_step(self):
        k, self.x_next = self.x_next, self.x_next + 1
        self.x_copy(k).wait_recv()
        (self.c_copy if GATHER_CHUNKS[k][3] else self.y_copy)(k).start()

    def y_step(self):
        k, self.y_next = self.y_next, self.y_next + 1
        if not GATHER_CHUNKS[k][3]:
            self.y_copy(k).wait_recv()
            self.c_copy(k).start()

    def c_step(self):
        k, self.c_next = self.c_next, self.c_next + 1
        self.c_copy(k).wait_recv()

    def tick(self, upto=-1):
        count = self.count
        if self.z_next < count:
            self.z_step()
        for before, after, step, lag in (
            (self.z_next, self.x_next, self.x_step, 1),
            (self.x_next, self.y_next, self.y_step, 1),
            (self.y_next, self.c_next, self.c_step, 1),
        ):
            if after < before and (before - after > lag or before == count or after <= upto):
                step()

    def pump(self, ticks=1):
        for _ in range(ticks):
            if self.c_next < self.count:
                self.tick()

    def ready(self, tensor):
        last = max(k for k, chunk in enumerate(GATHER_CHUNKS) if chunk[0] == tensor)
        while self.c_next <= last:
            self.tick(last)

    def close(self):
        for k in range(self.count):
            for copy in self.z_copies(k):
                copy.wait_send()
            self.x_copy(k).wait_send()
            if not GATHER_CHUNKS[k][3]:
                self.y_copy(k).wait_send()
            self.c_copy(k).wait_send()


def taps(tensor):
    pieces = []
    for lead in (0, 3, 6):
        pieces += [(tensor, lead, 1, True, column, 256) for column in (0, 256)]
        pieces += [(tensor, lead + 1, 1, False, 0, 512), (tensor, lead + 2, 1, False, 0, 512)]
    return pieces


def blocks(tensor, leads, both):
    return [(tensor, lead, 1, lead in both, column, 128) for lead in leads for column in (0, 128)]


CHUNKS = (
    [(0, 0, 1, False, column, 512) for column in (0, 512)],
    taps(1),
    blocks(2, (0, 1), ()),
    blocks(3, (0, 1, 2, 3), (0,)),
    [
        (4, 0, 1, width == 256, column, width)
        for column, width in ((0, 256), (256, 256), (512, 512), (1024, 256), (1280, 256), (1536, 512))
    ],
    taps(5),
    blocks(6, (0, 1), ()),
)
GATHER_CHUNKS = [chunk for tensor in (0, 1, 3, 2, 4, 5, 6) for chunk in CHUNKS[tensor]]
REDUCE_CHUNKS = [chunk for tensor in (6, 5, 4, 2, 3, 1, 0) for chunk in CHUNKS[tensor]]


def add_blocks(extents, body):
    total = 1
    for extent in extents:
        total *= extent

    def step(flat, carry):
        index = []
        for extent in reversed(extents):
            index.append(lax.rem(flat, extent))
            flat = flat // extent
        body(*reversed(index))
        return carry

    lax.fori_loop(0, total, step, 0)


def add_to(target, source):
    target[...] = (target[...].astype(jnp.float32) + source[...].astype(jnp.float32)).astype(jnp.bfloat16)


class Reduce:
    def __init__(self, held, outs, c_hbm, y_hbm, refs, depth):
        self.held, self.outs, self.c_hbm, self.y_hbm, self.depth = held, outs, c_hbm, y_hbm, depth
        self.count = len(REDUCE_CHUNKS)
        refs = list(refs)

        def take(count):
            taken = refs[:count]
            del refs[:count]
            return taken

        self.from_x, self.from_z, self.swap = take(self.count), take(self.count), take(self.count)
        self.final = take(self.count)
        self.c_tall, self.c_wide, self.y_tall, self.y_wide, self.squares = take(5)
        self.c_sem, self.y_sem, self.x_sem, self.z_sem, self.s_sem, self.f_sem, self.q_sem, self.local_sem = take(8)
        self.z, self.x, self.y, self.core = position()
        self.enabled = 0
        self.next = [0] * len(self.LAGS)

    @staticmethod
    def sizes(shapes):
        for tensor, _, leads, both, _, columns in REDUCE_CHUNKS:
            rows = shapes[tensor][3]
            yield leads, rows, columns, rows // 2 if both else rows // 4, both

    @staticmethod
    def scratch(shapes, depth):
        dma, count = pltpu.SemaphoreType.DMA, len(REDUCE_CHUNKS)
        buffer = lambda *shape: pltpu.VMEM(shape, jnp.bfloat16)
        sizes = list(Reduce.sizes(shapes))
        return (
            [buffer(depth, leads, part, columns) for leads, _, columns, part, _ in sizes]
            + [buffer(depth - 1, leads, part, columns) for leads, _, columns, part, _ in sizes]
            + [buffer(leads, part, columns) if both else buffer(16, 128) for leads, _, columns, part, both in sizes]
            + [buffer(leads, rows, columns) for leads, rows, columns, _, _ in sizes]
            + [buffer(2, depth, 2, 1, shapes[2][3] // 2, 128), buffer(2, depth, 2, 1, shapes[0][3] // 2, 512)]
            + [buffer(2, depth, 2, 1, shapes[2][3] // 4, 128), buffer(2, depth, 2, 1, shapes[0][3] // 4, 512)]
            + [pltpu.VMEM((2 * depth + 3, 8, 128), jnp.float32)]
            + [dma((2, count))] * 3
            + [dma((2, count, depth - 1)), dma((2, count)), dma((2, count, 3)), dma((2, depth)), dma((3, count))]
        )

    def piece(self, k):
        tensor, lead, leads, both, column, columns = REDUCE_CHUNKS[k]
        held = self.held[tensor]
        rows = held.shape[3]
        return held, rows, pl.ds(lead, leads), pl.ds(column, columns), chunk_rows(rows, both, self.y, self.core)

    def extents(self, k):
        return REDUCE_CHUNKS[k][2], REDUCE_CHUNKS[k][1]

    def slot(self, k, tall, wide):
        tensor, columns = REDUCE_CHUNKS[k][0], REDUCE_CHUNKS[k][5]
        buffer = tall if tensor in (2, 3, 6) else wide
        return buffer.at[k % 2, :, :, :, :, pl.ds(0, columns)]

    def c_copy(self, k):
        held, rows, lead, cols, _ = self.piece(k)
        return remote(
            held.at[:, :, lead, core_rows(rows, 1 - self.core), cols],
            self.c_hbm[REDUCE_CHUNKS[k][0]].at[:, :, lead, :, cols],
            self.c_sem.at[0, k],
            self.c_sem.at[1, k],
            (self.z, self.x, self.y, 1 - self.core),
        )

    def c_load(self, k):
        _, _, lead, cols, _ = self.piece(k)
        return pltpu.make_async_copy(
            self.c_hbm[REDUCE_CHUNKS[k][0]].at[:, :, lead, :, cols],
            self.slot(k, self.c_tall, self.c_wide),
            self.local_sem.at[0, k],
        )

    def y_copy(self, k):
        held, rows, lead, cols, _ = self.piece(k)
        return remote(
            held.at[:, :, lead, chunk_rows(rows, False, 1 - self.y, self.core), cols],
            self.y_hbm[REDUCE_CHUNKS[k][0]].at[:, :, lead, :, cols],
            self.y_sem.at[0, k],
            self.y_sem.at[1, k],
            (self.z, self.x, 1 - self.y, self.core),
        )

    def y_load(self, k):
        _, _, lead, cols, _ = self.piece(k)
        return pltpu.make_async_copy(
            self.y_hbm[REDUCE_CHUNKS[k][0]].at[:, :, lead, :, cols],
            self.slot(k, self.y_tall, self.y_wide),
            self.local_sem.at[1, k],
        )

    def x_copy(self, k):
        held, _, lead, cols, rows = self.piece(k)
        return remote(
            held.at[:, 1 - self.x, lead, rows, cols],
            self.from_x[k],
            self.x_sem.at[0, k],
            self.x_sem.at[1, k],
            (self.z, 1 - self.x, self.y, self.core),
        )

    def z_copies(self, k):
        held, _, lead, cols, rows = self.piece(k)
        copies = []
        for step in range(1, self.depth):
            there = lax.rem(self.z + step, self.depth)
            copies.append(
                remote(
                    held.at[there, self.x, lead, rows, cols],
                    self.from_z[k].at[step - 1],
                    self.z_sem.at[0, k, step - 1],
                    self.z_sem.at[1, k, step - 1],
                    (there, self.x, self.y, self.core),
                )
            )
        return copies

    def s_copy(self, k):
        rows = self.piece(k)[4]
        return remote(
            self.final[k].at[:, rows],
            self.swap[k],
            self.s_sem.at[0, k],
            self.s_sem.at[1, k],
            (self.z, self.x, 1 - self.y, self.core),
        )

    def f_copies(self, k):
        here = self.final[k].at[:, self.piece(k)[4]]
        peers = [(self.z, self.x, self.y, 1 - self.core)]
        if not REDUCE_CHUNKS[k][3]:
            peers += [(self.z, self.x, 1 - self.y, self.core), (self.z, self.x, 1 - self.y, 1 - self.core)]
        return [
            remote(here, here, self.f_sem.at[0, k, i], self.f_sem.at[1, k, i], peer) for i, peer in enumerate(peers)
        ]

    def store(self, k):
        tensor = REDUCE_CHUNKS[k][0]
        _, _, lead, cols, _ = self.piece(k)
        return pltpu.make_async_copy(self.final[k], self.outs[tensor].at[lead, :, cols], self.local_sem.at[2, k])

    def add_c(self, k):
        held, rows, _, cols, _ = self.piece(k)
        leads, lead = self.extents(k)
        half, slot = core_rows(rows, self.core), self.slot(k, self.c_tall, self.c_wide)
        add_blocks(
            (self.depth, 2, leads), lambda z, x, i: add_to(held.at[z, x, lead + i, half, cols], slot.at[z, x, i])
        )

    def add_y(self, k):
        held, _, _, cols, rows = self.piece(k)
        leads, lead = self.extents(k)
        slot = self.slot(k, self.y_tall, self.y_wide)
        add_blocks(
            (self.depth, 2, leads), lambda z, x, i: add_to(held.at[z, x, lead + i, rows, cols], slot.at[z, x, i])
        )

    def add_x(self, k):
        held, _, _, cols, rows = self.piece(k)
        leads, lead = self.extents(k)
        add_blocks(
            (self.depth, leads), lambda z, i: add_to(held.at[z, self.x, lead + i, rows, cols], self.from_x[k].at[z, i])
        )

    def add_z(self, k):
        held, _, _, cols, rows = self.piece(k)
        leads, lead = self.extents(k)

        def body(i):
            total = held[self.z, self.x, lead + i, rows, cols].astype(jnp.float32)
            for step in range(1, self.depth):
                total = total + self.from_z[k][step - 1, i].astype(jnp.float32)
            self.final[k][i, rows] = total.astype(jnp.bfloat16)

        add_blocks((leads,), body)

    def add_s(self, k):
        rows = self.piece(k)[4]
        add_blocks((self.extents(k)[0],), lambda i: add_to(self.final[k].at[i, rows], self.swap[k].at[i]))

    def add_squares(self, k):
        leads = self.extents(k)[0]
        lanes = lax.broadcasted_iota(jnp.int32, (8, 128), 1)
        subs = lax.broadcasted_iota(jnp.int32, (8, 128), 0)
        where = (subs == 1) & (lanes == REDUCE_CHUNKS[k][0])

        def body(i):
            block = self.final[k][i].astype(jnp.float32)
            total = jnp.sum(jnp.sum(block * block, axis=0, keepdims=True), axis=1, keepdims=True)
            self.squares[2 * self.depth + 2] += jnp.where(where, total, 0.0)

        add_blocks((leads,), body)

    LAGS = (0, 1, 1, 1, 1, 1, 1, 1, 1)

    def stage(self, k, number):
        both = REDUCE_CHUNKS[k][3]
        if number == 0:
            self.c_copy(k).start()
        elif number == 1:
            self.c_copy(k).wait_recv()
            self.c_load(k).start()
        elif number == 2:
            self.c_load(k).wait()
            self.add_c(k)
            (self.x_copy if both else self.y_copy)(k).start()
        elif number == 3 and not both:
            self.y_copy(k).wait_recv()
            self.y_load(k).start()
        elif number == 4 and not both:
            self.y_load(k).wait()
            self.add_y(k)
            self.x_copy(k).start()
        elif number == 5:
            self.x_copy(k).wait_recv()
            self.add_x(k)
            for copy in self.z_copies(k):
                copy.start()
        elif number == 6:
            for copy in self.z_copies(k):
                copy.wait_recv()
            self.add_z(k)
            for copy in [self.s_copy(k)] if both else self.f_copies(k):
                copy.start()
        elif number == 7 and both:
            self.s_copy(k).wait_recv()
            self.s_copy(k).wait_send()
            self.add_s(k)
            for copy in self.f_copies(k):
                copy.start()
        elif number == 8:
            for copy in self.f_copies(k):
                copy.wait_recv()
            self.store(k).start()
            self.add_squares(k)

    def enable(self, tensor, leads_done=None):
        while self.enabled < self.count:
            chunk = REDUCE_CHUNKS[self.enabled]
            if chunk[0] != tensor or (leads_done is not None and chunk[1] + chunk[2] > leads_done):
                break
            self.enabled += 1

    def pump(self, ticks=1):
        for _ in range(ticks):
            for number in reversed(range(len(self.LAGS))):
                before = self.next[number - 1] if number else self.enabled
                behind = before - self.next[number]
                if behind > 0 and (behind > self.LAGS[number] or before == self.count):
                    self.stage(self.next[number], number)
                    self.next[number] += 1

    def finish(self, weight_squares, sums_out):
        while self.next[-1] < self.count:
            self.pump()
        squares, depth = self.squares, self.depth
        subs = lax.broadcasted_iota(jnp.int32, (8, 128), 0)
        mine = squares.at[self.z * 2 + self.x]
        mine[...] = squares[2 * depth + 2] + jnp.where(subs == 0, weight_squares[...], 0.0)
        copies = [
            remote(
                mine,
                mine,
                self.q_sem.at[0, step],
                self.q_sem.at[1, step],
                (lax.rem(self.z + step, depth), self.x, self.y, self.core),
            )
            for step in range(1, depth)
        ]
        for copy in copies:
            copy.start()
        for copy in copies:
            copy.wait_recv()
        own = squares[self.x]
        for deep in range(1, depth):
            own = own + squares[deep * 2 + self.x]
        column = squares.at[2 * depth + self.x]
        column[...] = own
        across = remote(
            column, column, self.q_sem.at[0, 0], self.q_sem.at[1, 0], (self.z, 1 - self.x, self.y, self.core)
        )
        across.start()
        across.wait_recv()
        sums_out[...] = squares[2 * depth] + squares[2 * depth + 1]
        across.wait_send()
        for copy in copies:
            copy.wait_send()
        for k in range(self.count):
            self.c_copy(k).wait_send()
            if not REDUCE_CHUNKS[k][3]:
                self.y_copy(k).wait_send()
            self.x_copy(k).wait_send()
            for copy in self.z_copies(k) + self.f_copies(k):
                copy.wait_send()
            self.store(k).wait()


class NearFar:
    def __init__(self, refs, depth):
        self.near, self.far, self.total, self.near_send, self.near_recv, self.far_send, self.far_recv = refs
        self.depth = depth
        self.z, self.x, self.y, self.core = position()
        self.mine = self.x * 4 + self.y * 2 + self.core
        self.pay = self.near.at[self.mine]
        self.sent = []

    @staticmethod
    def scratch(width, depth):
        dma = pltpu.SemaphoreType.DMA
        return [
            pltpu.VMEM((8, 8, width), jnp.float32),
            pltpu.VMEM((depth, 8, width), jnp.float32),
            pltpu.VMEM((8, width), jnp.float32),
            dma((7,)),
            dma((7,)),
            dma((depth - 1,)),
            dma((depth - 1,)),
        ]

    def near_copies(self):
        copies = []
        for offset in range(1, 8):
            x = 1 - self.x if offset & 4 else self.x
            y = 1 - self.y if offset & 2 else self.y
            core = 1 - self.core if offset & 1 else self.core
            here = self.near.at[self.mine]
            copies.append(
                remote(here, here, self.near_send.at[offset - 1], self.near_recv.at[offset - 1], (self.z, x, y, core))
            )
        return copies

    def far_copies(self):
        here = self.far.at[self.z]
        return [
            remote(
                here,
                here,
                self.far_send.at[step - 1],
                self.far_recv.at[step - 1],
                (lax.rem(self.z + step, self.depth), self.x, self.y, self.core),
            )
            for step in range(1, self.depth)
        ]

    def begin(self):
        for copy in self.near_copies():
            copy.start()

    def stages(self):
        def middle():
            for copy in self.near_copies():
                copy.wait_recv()
            total = self.near[0]
            for slot in range(1, 8):
                total = total + self.near[slot]
            self.far[self.z] = total
            for copy in self.far_copies():
                copy.start()

        def last():
            for copy in self.far_copies():
                copy.wait_recv()
            total = self.far[0]
            for slot in range(1, self.depth):
                total = total + self.far[slot]
            self.total[...] = total

        return [middle, last]

    def close(self):
        for copy in self.near_copies() + self.far_copies():
            copy.wait_send()


class Split:
    def __init__(self, refs, depth):
        (self.pay, self.half, self.quad, self.deep, self.total, self.c_send, self.c_recv) = refs[:7]
        (self.q_send, self.q_recv, self.z_send, self.z_recv, self.g_send, self.g_recv) = refs[7:]
        self.depth = depth
        self.z, self.x, self.y, self.core = position()
        self.width = self.pay.shape[1]
        self.mine = self.x * 2 + self.y

    @staticmethod
    def scratch(width, depth):
        dma = pltpu.SemaphoreType.DMA
        return [
            pltpu.VMEM((8, width), jnp.float32),
            pltpu.VMEM((8, width // 2), jnp.float32),
            pltpu.VMEM((4, 8, width // 8), jnp.float32),
            pltpu.VMEM((depth, 8, width // 8), jnp.float32),
            pltpu.VMEM((8, width), jnp.float32),
            dma((2,)),
            dma((2,)),
            dma((3,)),
            dma((3,)),
            dma((depth - 1,)),
            dma((depth - 1,)),
            dma((3,)),
            dma((3,)),
        ]

    def half_of(self, core):
        return pl.ds(pl.multiple_of(core * (self.width // 2), 128), self.width // 2)

    def eighth_of(self, slot):
        start = self.core * (self.width // 2) + slot * (self.width // 8)
        return pl.ds(pl.multiple_of(start, 128), self.width // 8)

    def core_copy(self):
        return remote(
            self.pay.at[:, self.half_of(1 - self.core)],
            self.half,
            self.c_send.at[0],
            self.c_recv.at[0],
            (self.z, self.x, self.y, 1 - self.core),
        )

    def around(self):
        for offset in range(1, 4):
            x = 1 - self.x if offset & 2 else self.x
            y = 1 - self.y if offset & 1 else self.y
            yield offset - 1, x, y

    def quad_copies(self):
        return [
            remote(
                self.pay.at[:, self.eighth_of(x * 2 + y)],
                self.quad.at[self.mine],
                self.q_send.at[i],
                self.q_recv.at[i],
                (self.z, x, y, self.core),
            )
            for i, x, y in self.around()
        ]

    def deep_copies(self):
        here = self.deep.at[self.z]
        return [
            remote(
                here,
                here,
                self.z_send.at[step - 1],
                self.z_recv.at[step - 1],
                (lax.rem(self.z + step, self.depth), self.x, self.y, self.core),
            )
            for step in range(1, self.depth)
        ]

    def gather_copies(self):
        here = self.total.at[:, self.eighth_of(self.mine)]
        return [
            remote(here, here, self.g_send.at[i], self.g_recv.at[i], (self.z, x, y, self.core))
            for i, x, y in self.around()
        ]

    def last_copy(self):
        here = self.total.at[:, self.half_of(self.core)]
        return remote(here, here, self.c_send.at[1], self.c_recv.at[1], (self.z, self.x, self.y, 1 - self.core))

    def begin(self):
        self.core_copy().start()

    def stages(self):
        def first():
            self.core_copy().wait_recv()
            half = self.half_of(self.core)
            self.pay[:, half] = self.pay[:, half] + self.half[...]
            for copy in self.quad_copies():
                copy.start()
            self.quad[self.mine] = self.pay[:, self.eighth_of(self.mine)]

        def second():
            for copy in self.quad_copies():
                copy.wait_recv()
            self.deep[self.z] = (self.quad[0] + self.quad[1]) + (self.quad[2] + self.quad[3])
            for copy in self.deep_copies():
                copy.start()

        def third():
            for copy in self.deep_copies():
                copy.wait_recv()
            total = self.deep[0]
            for slot in range(1, self.depth):
                total = total + self.deep[slot]
            self.total[:, self.eighth_of(self.mine)] = total
            for copy in self.gather_copies():
                copy.start()

        def fourth():
            for copy in self.gather_copies():
                copy.wait_recv()
            self.last_copy().start()

        def fifth():
            self.last_copy().wait_recv()
            for copy in self.gather_copies() + [self.last_copy()]:
                copy.wait_send()

        return [first, second, third, fourth, fifth]

    def close(self):
        self.core_copy().wait_send()
        for copy in self.quad_copies() + self.deep_copies():
            copy.wait_send()


def interleave(stages, works):
    done = 0
    for i, stage in enumerate(stages):
        upto = (len(works) * (i + 1)) // len(stages)
        for work in works[done:upto]:
            work()
        done = upto
        stage()


HAT_A1, HAT_A2, HAT_A3, HAT_AS, HAT_B1, HAT_B2, HAT_B3, PATCH_A, PATCH_B, ACT_A2, ACT_B2, OUT_A = SAVED = range(12)
SUM_A1, SUM_A2, SUM_A3, SUM_AS, SUM_B1, SUM_B2, SUM_B3, SUM_J = range(8)


def paced(first, last, body, parts, pump):
    for part in range(parts):
        span = last - first
        lax.fori_loop(first + span * part // parts, first + span * (part + 1) // parts, body, 0)
        pump()


def columns(j):
    return pl.ds(pl.multiple_of(j * 128, 128), 128)


def dot(a, b):
    return lax.dot_general(a, b, (((1,), (0,)), ((), ())), preferred_element_type=jnp.float32)


def dot_nt(a, b):
    return lax.dot_general(a, b, (((1,), (1,)), ((), ())), preferred_element_type=jnp.float32)


def sigmoid(v):
    return 0.5 * jnp.tanh(0.5 * v) + 0.5


def slope(v):
    s = sigmoid(v)
    return s * (1.0 + v * (1.0 - s))


class Plan:
    def __init__(self, shapes):
        self.sides = [shape[1] // 2 for shape in shapes]
        self.slots = [shape[0] for shape in shapes]
        self.valid = [side * side * slots for side, slots in zip(self.sides, self.slots)]
        sizes = [-(-valid // 8) * 8 for valid in self.valid]
        sizes[2] += -sum(sizes) % 128
        self.starts = [0, sizes[0], sizes[0] + sizes[1]]
        self.sizes = sizes
        self.rows = sum(sizes)

    def spans(self):
        return [slice(start, start + size) for start, size in zip(self.starts, self.sizes)]

    def shifts(self):
        out = np.zeros((9, self.rows, self.rows), np.float32)
        for side, slots, start in zip(self.sides, self.slots, self.starts):
            at = lambda i, j, n: start + (i * side + j) * slots + n
            for di in (-1, 0, 1):
                for dj in (-1, 0, 1):
                    for i in range(max(0, -di), min(side, side - di)):
                        for j in range(max(0, -dj), min(side, side - dj)):
                            for n in range(slots):
                                out[(di + 1) * 3 + dj + 1, at(i, j, n), at(i + di, j + dj, n)] = 1.0
        return out.astype(jnp.bfloat16)


def put_sums(plan, pairs, mask, pay, base, width, pump=None):
    def body(j, carry):
        firsts, seconds = [0.0] * 3, [0.0] * 3
        for first, second in pairs(j):
            for g, span in enumerate(plan.spans()):
                live = first[span] * mask[span, :]
                firsts[g] = firsts[g] + jnp.sum(live, axis=0, keepdims=True)
                seconds[g] = seconds[g] + jnp.sum(live * second[span], axis=0, keepdims=True)
        zero = jnp.zeros((1, 128), jnp.float32)
        pay[:, columns(base + j)] = jnp.concatenate(firsts + seconds + [zero, zero], axis=0)
        return carry

    if pump is None:
        lax.fori_loop(0, width // 128, body, 0)
    else:
        paced(0, width // 128, body, 2, pump)


def put_scales(total, inverse, over, width, factor=1.0):
    def body(j, carry):
        at = columns(j)
        per = over[0:3, :] * factor
        means = total[0:3, at] * per
        variance = total[3:6, at] * per - means * means
        scales = lax.rsqrt(variance + EPSILON)
        zero = jnp.zeros((5, 128), jnp.float32)
        total[:, at] = jnp.concatenate([means, zero], axis=0)
        inverse[:, at] = jnp.concatenate([scales, zero], axis=0)
        return carry

    lax.fori_loop(0, width // 128, body, 0)


def by_group(plan, of):
    return jnp.concatenate([of(g, span) for g, span in enumerate(plan.spans())], axis=0)


def forward_names(depth):
    return (
        (SUM_A1, NearFar.scratch(512, depth)),
        (SUM_A2, NearFar.scratch(512, depth)),
        (SUM_AS, Split.scratch(2048, depth)),
        (SUM_A3, Split.scratch(2048, depth)),
        (SUM_B1, NearFar.scratch(512, depth)),
        (SUM_B2, NearFar.scratch(512, depth)),
        (SUM_B3, Split.scratch(2048, depth)),
    )


def forward_kernel(plan, depth, *refs):
    refs = list(refs)

    def take(count):
        taken = refs[:count]
        del refs[:count]
        return taken

    x_hbm, shift_hbm, mask, counts, norm_mid, norm_out = take(6)
    shards = take(7)
    out, inv_mid, inv_out, par_mid, par_out, over, weight_squares = take(7)
    weights_hbm = take(7)
    saved_hbm = dict(zip(SAVED, take(len(SAVED))))
    sums = {}
    for name, scratch in forward_names(depth):
        sums[name] = (NearFar if len(scratch) == 7 else Split)(take(len(scratch)), depth)
    x, shift = take(2)
    w_a1, w_a2, w_a3, w_as, w_b1, w_b2, w_b3 = weights = take(7)
    saved = dict(zip(SAVED, take(len(SAVED))))
    hid_a1, hid_mid, hid_out, hid_as, act = take(5)
    load_sem, save_sem, full_sem, norms_mid, norms_out, norm_send, norm_recv = take(7)
    gather = Gather(shards, weights, take(9), depth)

    loads = [
        pltpu.make_async_copy(src, dst, load_sem.at[i])
        for i, (src, dst) in enumerate(zip([x_hbm, shift_hbm], [x, shift]))
    ]
    gather.place_all()
    for copy in loads:
        copy.start()

    def keep(i):
        return pltpu.make_async_copy(weights[i], weights_hbm[i], full_sem.at[i])

    weight_squares[...] = jnp.zeros((8, 128), jnp.float32)

    def ready(i):
        gather.ready(i)
        keep(i).start()

    def add_square(i):
        at_row = lax.broadcasted_iota(jnp.int32, (8, 128), 0) == 0
        where = at_row & (lax.broadcasted_iota(jnp.int32, (8, 128), 1) == i)

        def body(lead, carry):
            block = weights[i][gather.z, gather.x, lead].astype(jnp.float32)
            total = jnp.sum(jnp.sum(block * block, axis=0, keepdims=True), axis=1, keepdims=True)
            weight_squares[...] += jnp.where(where, total, 0.0)
            return carry

        lax.fori_loop(0, weights[i].shape[2], body, 0)

    def pump():
        gather.pump()

    def save(name):
        pltpu.make_async_copy(saved[name], saved_hbm[name], save_sem.at[SAVED.index(name)]).start()

    greet(depth, crosswise=True)
    place = gather.z * 2 + gather.x
    norms_mid[place] = norm_mid[...]
    own_lanes = pl.ds(pl.multiple_of(place * norm_out.shape[1], 128), norm_out.shape[1])
    norms_out[:, own_lanes] = norm_out[...]

    def norm_copies(kind):
        here = norms_out.at[:, own_lanes] if kind else norms_mid.at[place]
        copies = []
        for i in range(1, 2 * depth):
            peer = (lax.rem(gather.z + i // 2, depth), 1 - gather.x if i % 2 else gather.x, gather.y, gather.core)
            copies.append(remote(here, here, norm_send.at[kind, i], norm_recv.at[kind, i], peer))
        return copies

    for copy in norm_copies(0) + norm_copies(1):
        copy.start()
    gather.begin()
    rows = plan.rows

    loads[0].wait()
    ready(0)

    def conv_a1(p, carry):
        hid_a1[p] = dot_nt(x[p], w_a1[...].reshape(512, -1))
        return carry

    paced(0, 2, conv_a1, 2, pump)
    paced(2, 4, conv_a1, 2, pump)

    total = sums[SUM_A1]
    put_sums(
        plan, lambda j: [(hid_a1[p, :, columns(j)],) * 2 for p in range(4)], mask, total.pay, 0, 512, pump
    )
    total.pay[6:7, 0:128] = counts[...]
    total.begin()
    add_square(0)
    pump()
    total.stages()[0]()
    pump()
    total.stages()[1]()
    for copy in norm_copies(0):
        copy.wait_recv()
    own_norms = norms_mid[0]
    for slot in range(1, 2 * depth):
        own_norms = own_norms + norms_mid[slot]
    par_mid[...] = own_norms

    pixels = total.total[6:7, 0:128]
    lanes = lax.broadcasted_iota(jnp.int32, (1, 128), 1)
    inverse_counts = [
        jnp.broadcast_to(1.0 / jnp.sum(jnp.where(lanes == g, pixels, 0.0), axis=1, keepdims=True), (1, 128))
        for g in range(3)
    ]
    over[...] = jnp.concatenate(inverse_counts + [jnp.zeros((5, 128), jnp.float32)], axis=0)
    put_scales(total.total, inv_mid.at[0], over, 512, 0.25)

    def normalized(hidden, total, inverse, hat, params, row, j):
        at = columns(j)
        xhat = by_group(plan, lambda g, span: (hidden[span] - total[g : g + 1, at]) * inverse[g : g + 1, at])
        hat[:, at] = xhat.astype(jnp.bfloat16)
        return xhat * params[row : row + 1, at] + params[row + 1 : row + 2, at]

    def activate(hidden_of, total, inverse, hat, params, row, target):
        def body(j, carry):
            v = normalized(hidden_of(j), total, inverse, hat, params, row, j)
            target[:, columns(j)] = (v * sigmoid(v)).astype(jnp.bfloat16)
            return carry

        lax.fori_loop(0, 4, body, 0)

    def activate_a1(p, carry):
        activate(
            lambda j: hid_a1[p, :, columns(j)],
            total.total,
            inv_mid.at[0],
            saved[HAT_A1].at[p],
            par_mid,
            0,
            act.at[p],
        )
        return carry

    paced(0, 4, activate_a1, 4, pump)
    save(HAT_A1)

    loads[1].wait()
    patch = saved[PATCH_A]
    for tap in range(9):
        a, b = tap // 3, tap % 3
        plane = (0 if a == 1 else 2) + (0 if b == 1 else 1)
        matrix = (0 if a == 0 else 1) * 3 + (0 if b == 0 else 1)
        if matrix == 4:
            patch[tap] = act[plane]
        else:
            patch[tap] = dot(shift[matrix], act[plane]).astype(jnp.bfloat16)
        if tap in (2, 5):
            pump()
    save(PATCH_A)
    ready(1)

    def spatial(patch, weight):
        hid_mid[...] = dot_nt(patch[0], weight[:, :, 0].reshape(512, 512))

        def body(tap, carry):
            hid_mid[...] += dot_nt(patch[tap], weight[:, :, tap].reshape(512, 512))
            return carry

        paced(1, 9, body, 3, pump)

    spatial(patch, w_a2)

    def conv_as(d, carry):
        at = pl.ds(pl.multiple_of(d * 256, 256), 256)
        hid_as[:, at] = dot(x[0], w_as[d // 2, lax.rem(d, 2)].reshape(1024, 256))
        return carry

    def shortcut():
        ready(3)
        paced(0, 8, conv_as, 2, pump)
        put_sums(plan, lambda j: [(hid_as[:, columns(j)],) * 2], mask, sums[SUM_AS].pay, 0, 2048, pump)
        sums[SUM_AS].begin()

    as_stages = sums[SUM_AS].stages()

    def mid_sums(total, name_index, works):
        put_sums(plan, lambda j: [(hid_mid[:, columns(j)],) * 2], mask, total.pay, 0, 512)
        total.begin()
        interleave(total.stages(), works)
        put_scales(total.total, inv_mid.at[name_index], over, 512)

    mid_sums(sums[SUM_A2], 1, [pump, lambda: add_square(1), pump])
    activate(
        lambda j: hid_mid[:, columns(j)], sums[SUM_A2].total, inv_mid.at[1], saved[HAT_A2], par_mid, 2, saved[ACT_A2]
    )
    save(HAT_A2)
    save(ACT_A2)

    def expand(act_ref, weight):
        def body(d, carry):
            at = pl.ds(pl.multiple_of(d * 256, 256), 256)
            hid_out[:, at] = dot(act_ref[...], weight[d // 2, lax.rem(d, 2)].reshape(512, 256))
            return carry

        paced(0, 8, body, 2, pump)

    def out_sums(total, name_index, works):
        put_sums(plan, lambda j: [(hid_out[:, columns(j)],) * 2], mask, total.pay, 0, 2048, pump)
        total.begin()
        interleave(total.stages(), works)
        put_scales(total.total, inv_out.at[name_index], over, 2048)

    shortcut()
    as_stages[0]()
    ready(2)
    as_stages[1]()
    expand(saved[ACT_A2], w_a3)
    as_stages[2]()
    out_sums(sums[SUM_A3], 0, [as_stages[3], pump, as_stages[4], pump, lambda: add_square(2), lambda: add_square(3), pump])
    put_scales(sums[SUM_AS].total, inv_out.at[1], over, 2048)

    for copy in norm_copies(1):
        copy.wait_recv()
    par_out[...] = norms_out[...]

    def join(j, carry):
        at = columns(j)
        v = normalized(hid_out[:, at], sums[SUM_A3].total, inv_out.at[0], saved[HAT_A3], par_out, 0, j)
        v = v + normalized(hid_as[:, at], sums[SUM_AS].total, inv_out.at[1], saved[HAT_AS], par_out, 2, j)
        saved[OUT_A][:, at] = (v * sigmoid(v) * mask[...]).astype(jnp.bfloat16)
        return carry

    paced(0, 16, join, 4, pump)
    for name in (HAT_A3, HAT_AS, OUT_A):
        save(name)

    ready(4)
    hid_mid[...] = dot_nt(saved[OUT_A][...], w_b1[...].reshape(512, -1))
    mid_sums(sums[SUM_B1], 2, [pump, lambda: add_square(4), pump])
    activate(
        lambda j: hid_mid[:, columns(j)], sums[SUM_B1].total, inv_mid.at[2], saved[HAT_B1], par_mid, 4, act.at[0]
    )
    save(HAT_B1)

    def patches(tap, carry):
        saved[PATCH_B][tap] = dot(shift[tap], act[0]).astype(jnp.bfloat16)
        return carry

    paced(0, 9, patches, 3, pump)
    save(PATCH_B)
    ready(5)
    spatial(saved[PATCH_B], w_b2)
    mid_sums(sums[SUM_B2], 3, [pump, lambda: add_square(5), pump])
    activate(
        lambda j: hid_mid[:, columns(j)], sums[SUM_B2].total, inv_mid.at[3], saved[HAT_B2], par_mid, 6, saved[ACT_B2]
    )
    save(HAT_B2)
    save(ACT_B2)
    ready(6)
    expand(saved[ACT_B2], w_b3)
    out_sums(sums[SUM_B3], 2, [lambda: add_square(6)])

    def finish(j, carry):
        at = columns(j)
        v = normalized(hid_out[:, at], sums[SUM_B3].total, inv_out.at[2], saved[HAT_B3], par_out, 4, j)
        v = v + saved[OUT_A][:, at].astype(jnp.float32)
        out[:, at] = (v * sigmoid(v) * mask[...]).astype(jnp.bfloat16)
        return carry

    lax.fori_loop(0, 16, finish, 0)
    save(HAT_B3)
    for total in sums.values():
        total.close()
    for i, name in enumerate(SAVED):
        pltpu.make_async_copy(saved[name], saved_hbm[name], save_sem.at[i]).wait()
    gather.close()
    for copy in norm_copies(0) + norm_copies(1):
        copy.wait_send()
    for i in range(7):
        keep(i).wait()


def saved_shapes(rows):
    bf16 = jnp.bfloat16
    return (
        ((4, rows, 512), bf16),
        ((rows, 512), bf16),
        ((rows, 2048), bf16),
        ((rows, 2048), bf16),
        ((rows, 512), bf16),
        ((rows, 512), bf16),
        ((rows, 2048), bf16),
        ((9, rows, 512), bf16),
        ((9, rows, 512), bf16),
        ((rows, 512), bf16),
        ((rows, 512), bf16),
        ((rows, 2048), bf16),
    )


WHOLE = pl.BlockSpec(memory_space=pltpu.VMEM)
VMEM_LIMIT = 62 * 1024 * 1024


def run_forward(plan, depth, x, shifts, mask, counts, norm_mid, norm_out, shards):
    rows, f32, bf16 = plan.rows, jnp.float32, jnp.bfloat16
    dma = pltpu.SemaphoreType.DMA
    scratch = []
    for _, pieces in forward_names(depth):
        scratch += pieces
    scratch += [pltpu.VMEM(x.shape, bf16), pltpu.VMEM(shifts.shape, bf16)]
    fulls = [jax.ShapeDtypeStruct((depth, 2, *shard.shape), bf16) for shard in shards]
    scratch += [pltpu.VMEM(full.shape, bf16) for full in fulls]
    scratch += [pltpu.VMEM(shape, kind) for shape, kind in saved_shapes(rows)]
    scratch += [
        pltpu.VMEM((4, rows, 512), f32),
        pltpu.VMEM((rows, 512), f32),
        pltpu.VMEM((rows, 2048), f32),
        pltpu.VMEM((rows, 2048), f32),
        pltpu.VMEM((4, rows, 512), bf16),
        dma((2,)),
        dma((len(SAVED),)),
        dma((7,)),
        pltpu.VMEM((2 * depth, 8, 512), f32),
        pltpu.VMEM((8, 2048), f32),
        dma((2, 2 * depth)),
        dma((2, 2 * depth)),
    ]
    scratch += Gather.scratch(depth)
    small = [
        jax.ShapeDtypeStruct((rows, 2048), bf16),
        jax.ShapeDtypeStruct((4, 8, 512), f32),
        jax.ShapeDtypeStruct((3, 8, 2048), f32),
        jax.ShapeDtypeStruct((8, 512), f32),
        jax.ShapeDtypeStruct((8, 2048), f32),
        jax.ShapeDtypeStruct((8, 128), f32),
        jax.ShapeDtypeStruct((8, 128), f32),
    ]
    return pl.pallas_call(
        functools.partial(forward_kernel, plan, depth),
        out_shape=small + fulls + [jax.ShapeDtypeStruct(shape, kind) for shape, kind in saved_shapes(rows)],
        in_specs=[ANY, ANY] + [WHOLE] * 4 + [ANY] * 7,
        out_specs=[WHOLE] * 7 + [ANY] * 7 + [ANY] * len(SAVED),
        scratch_shapes=scratch,
        compiler_params=pltpu.CompilerParams(collective_id=0, has_side_effects=True, vmem_limit_bytes=VMEM_LIMIT),
    )(x, shifts, mask, counts, norm_mid, norm_out, *shards)


def backward_names(depth):
    return (
        (SUM_B3, Split.scratch(2048, depth)),
        (SUM_B2, NearFar.scratch(512, depth)),
        (SUM_B1, NearFar.scratch(512, depth)),
        (SUM_J, Split.scratch(4096, depth)),
        (SUM_A2, NearFar.scratch(512, depth)),
        (SUM_A1, NearFar.scratch(512, depth)),
    )


def backward_kernel(plan, depth, *refs):
    refs = list(refs)

    def take(count):
        taken = refs[:count]
        del refs[:count]
        return taken

    x_hbm, shift_hbm, cot_hbm, mask, weight_squares, inv_mid, inv_out, par_mid, par_out, over = take(10)
    saved_hbm = dict(zip(SAVED, take(len(SAVED))))
    weights_hbm = take(7)
    dx_hbm, pgrad_mid, pgrad_b3, pgrad_j, squares_out = take(5)
    gradients_hbm, c_hbm, y_hbm = take(7), take(7), take(7)
    sums = {}
    for name, scratch in backward_names(depth):
        sums[name] = (NearFar if len(scratch) == 7 else Split)(take(len(scratch)), depth)
    x, shift, cot = take(3)
    w_a1, w_a2, w_a3, w_as, w_b1, w_b2, w_b3 = weights = take(7)
    kept = [name for name in SAVED if name != PATCH_B]
    saved = dict(zip(kept, take(len(kept))))
    saved[PATCH_B] = saved[PATCH_A]
    dz, dact, dh_mid, flip = take(4)
    load_sem, saved_sem, dx_sem = take(3)
    dh_a, dh_b = cot, saved[HAT_B3]
    planes = [saved[HAT_AS].at[:, pl.ds(plane * 512, 512)] for plane in range(4)]
    reduce = Reduce(weights, gradients_hbm, c_hbm, y_hbm, refs, depth)
    reduce.squares[2 * depth + 2] = jnp.zeros((8, 128), jnp.float32)

    def pump():
        reduce.pump()

    def loading(name):
        return pltpu.make_async_copy(saved_hbm[name], saved[name], saved_sem.at[SAVED.index(name)])

    loads = [
        pltpu.make_async_copy(src, dst, load_sem.at[i])
        for i, (src, dst) in enumerate(zip([x_hbm, shift_hbm, cot_hbm, *weights_hbm], [x, shift, cot, *weights]))
    ]
    first = (HAT_B3, OUT_A)
    for name in first:
        loading(name).start()
    loads[2].start()
    order = (HAT_B2, ACT_B2, HAT_B1, PATCH_B, HAT_A3, HAT_AS, HAT_A2, ACT_A2, HAT_A1)
    loads[9].start()
    for name in order[:4]:
        loading(name).start()
    for i in (1, 8, 7):
        loads[i].start()
    for name in order[4:]:
        loading(name).start()
    for i in (5, 6, 4, 0, 3):
        loads[i].start()

    greet(depth)

    def quarter(d):
        return pl.ds(pl.multiple_of(d * 256, 256), 256)

    def affine(hat, params, row, at):
        return hat[:, at].astype(jnp.float32) * params[row : row + 1, at] + params[row + 1 : row + 2, at]

    def norm_back(dz_of, hat, total, base, inverse, params, row, target, blocks):
        def body(j, carry):
            at = columns(j)
            sums_at = columns(base + j)
            gain = params[row : row + 1, at]
            value, xhat = dz_of(j), hat[:, at].astype(jnp.float32)

            def of(g, span):
                first = total[g : g + 1, sums_at] * over_of(g)
                second = total[3 + g : 4 + g, sums_at] * over_of(g)
                return (gain * inverse[g : g + 1, at]) * (value[span] - first - xhat[span] * second)

            target[:, at] = (by_group(plan, of) * mask[...]).astype(jnp.bfloat16)
            return carry

        paced(0, blocks, body, 1 if blocks == 4 else 2, pump)

    scale = [1.0]

    def over_of(g):
        return over[g : g + 1, :] * scale[0]

    for name in first:
        loading(name).wait()
    loads[2].wait()

    def out_pairs(j):
        at = columns(j)
        v = affine(saved[HAT_B3], par_out, 4, at) + saved[OUT_A][:, at].astype(jnp.float32)
        value = cot[:, at].astype(jnp.float32) * mask[...] * slope(v)
        dz[:, at] = value
        return [(value, saved[HAT_B3][:, at].astype(jnp.float32))]

    total = sums[SUM_B3]
    put_sums(plan, out_pairs, mask, total.pay, 0, 2048)
    total.begin()
    for i in (9, 1, 8, 7):
        loads[i].wait()
    for name in order[:4]:
        loading(name).wait()
    flip[0:512] = saved[ACT_B2][...].T
    interleave(total.stages(), [])
    pgrad_b3[...] = total.total[...]
    norm_back(lambda j: dz[:, columns(j)], saved[HAT_B3], total.total, 0, inv_out.at[2], par_out, 4, dh_a, 16)

    def contract(dh, weight):
        dact[...] = dot_nt(dh[:, 0:256], weight[0, 0].reshape(512, 256))

        def body(d, carry):
            dact[...] += dot_nt(dh[:, quarter(d)], weight[d // 2, lax.rem(d, 2)].reshape(512, 256))
            return carry

        paced(1, 8, body, 2, pump)

    def expand_term(lhs, dh, weight, first_slot, last_slot):
        def body(d, carry):
            shape = weight.shape[2:]
            weight[d // 2, lax.rem(d, 2)] = dot(lhs, dh[:, quarter(d)]).astype(jnp.bfloat16).reshape(shape)
            return carry

        lax.fori_loop(first_slot, last_slot, body, 0)

    def mid_pairs(hat, row):
        def pairs(j):
            at = columns(j)
            value = dact[:, at] * slope(affine(saved[hat], par_mid, row, at))
            dact[:, at] = value
            return [(value, saved[hat][:, at].astype(jnp.float32))]

        return pairs

    def mid_norm(name, hat, index, row, works):
        total = sums[name]
        put_sums(plan, mid_pairs(hat, row), mask, total.pay, 0, 512, pump)
        total.begin()
        interleave(total.stages(), works)
        pgrad_mid[index] = total.total[...]
        norm_back(lambda j: dact[:, columns(j)], saved[hat], total.total, 0, inv_mid.at[index], par_mid, row, dh_mid, 4)

    contract(dh_a, w_b3)

    def third_term(part):
        def work():
            expand_term(flip[0:512, :], dh_a, w_b3, 4 * part, 4 * part + 4)
            if part:
                reduce.enable(6)
                pump()

        return work

    mid_norm(SUM_B2, HAT_B2, 3, 6, [third_term(0), third_term(1)])

    def spread(tap, carry):
        part = dot(
            dot(shift[8 - tap], dh_mid[...]).astype(jnp.bfloat16), w_b2[:, :, tap].reshape(512, 512)
        )
        dact[...] = part + jnp.where(tap == 0, 0.0, dact[...])
        return carry

    paced(0, 9, spread, 5, pump)
    flip[0:512] = dh_mid[...].T

    def spatial_term(weight, patch, first_tap, last_tap, tensor):
        def work():
            def body(tap, carry):
                weight[:, :, tap] = dot(flip[0:512, :], patch[tap]).astype(jnp.bfloat16).reshape(depth, 2, 64, 512)
                return carry

            lax.fori_loop(first_tap, last_tap, body, 0)
            reduce.enable(tensor, last_tap)
            pump()

        return work

    mid_norm(
        SUM_B1,
        HAT_B1,
        2,
        4,
        [spatial_term(w_b2, saved[PATCH_B], 0, 3, 5), spatial_term(w_b2, saved[PATCH_B], 3, 6, 5)],
    )
    spatial_term(w_b2, saved[PATCH_B], 6, 9, 5)()
    loading(PATCH_A).start()

    def residual(d, carry):
        at = quarter(d)
        dz[:, at] = dz[:, at] + dot(dh_mid[...], w_b1[:, :, 0, :, at].reshape(512, 256))
        return carry

    paced(0, 8, residual, 2, pump)
    for name in order[4:]:
        loading(name).wait()

    def join_pairs(j):
        at = columns(j)
        v = affine(saved[HAT_A3], par_out, 0, at) + affine(saved[HAT_AS], par_out, 2, at)
        value = dz[:, at] * mask[...] * slope(v)
        dz[:, at] = value
        return [(value, saved[HAT_A3][:, at].astype(jnp.float32))]

    total = sums[SUM_J]
    put_sums(plan, join_pairs, mask, total.pay, 0, 2048, pump)
    put_sums(
        plan, lambda j: [(dz[:, columns(j)], saved[HAT_AS][:, columns(j)].astype(jnp.float32))], mask, total.pay, 16, 2048, pump
    )
    total.begin()
    flip[0:512] = dh_mid[...].T

    def first_term(part):
        def work():
            def body(d, carry):
                at = quarter(d)
                value = dot(flip[0:512, :], saved[OUT_A][:, at]).astype(jnp.bfloat16)
                w_b1[:, :, 0, :, at] = value.reshape(depth, 2, 64, 256)
                return carry

            lax.fori_loop(2 * part, 2 * part + 2, body, 0)
            if part == 3:
                reduce.enable(4)
            pump()

        return work

    interleave(total.stages(), [first_term(part) for part in range(4)])
    pgrad_j[...] = total.total[...]
    norm_back(lambda j: dz[:, columns(j)], saved[HAT_A3], total.total, 0, inv_out.at[0], par_out, 0, dh_a, 16)
    pump()
    norm_back(lambda j: dz[:, columns(j)], saved[HAT_AS], total.total, 16, inv_out.at[1], par_out, 2, dh_b, 16)
    for i in (5, 6, 4, 0, 3):
        loads[i].wait()

    pump()
    contract(dh_a, w_a3)
    pump()
    flip[0:512] = saved[ACT_A2][...].T

    def third_term_a():
        expand_term(flip[0:512, :], dh_a, w_a3, 0, 4)
        pump()
        expand_term(flip[0:512, :], dh_a, w_a3, 4, 8)
        reduce.enable(2)
        pump()

    def shortcut():
        even = dz.at[:, 0:1024]
        even[...] = dot_nt(dh_b[:, 0:256], w_as[0, 0].reshape(1024, 256))

        def body(d, carry):
            even[...] += dot_nt(dh_b[:, quarter(d)], w_as[d // 2, lax.rem(d, 2)].reshape(1024, 256))
            return carry

        paced(1, 8, body, 3, pump)

        def keep(j, carry):
            value = even[:, columns(j)]
            high = value.astype(jnp.bfloat16)
            saved[OUT_A][:, columns(j)] = high
            saved[OUT_A][:, columns(8 + j)] = (value - high.astype(jnp.float32)).astype(jnp.bfloat16)
            return carry

        lax.fori_loop(0, 8, keep, 0)

    mid_norm(SUM_A2, HAT_A2, 1, 2, [third_term_a, shortcut])

    loading(PATCH_A).wait()
    flip[...] = x[0].T
    for part in range(4):
        expand_term(flip[...], dh_b, w_as, 2 * part, 2 * part + 2)
        pump()
    reduce.enable(3)
    for plane in range(4):
        at = slice(plane * 512, plane * 512 + 512)
        begun = False
        for tap in range(9):
            a, b = tap // 3, tap % 3
            if plane != (0 if a == 1 else 2) + (0 if b == 1 else 1):
                continue
            matrix = (2 if a == 0 else 1) * 3 + (2 if b == 0 else 1)
            moved = dh_mid[...] if matrix == 4 else dot(shift[matrix], dh_mid[...]).astype(jnp.bfloat16)
            part = dot(moved, w_a2[:, :, tap].reshape(512, 512))
            if begun:
                dz[:, at] += part
            else:
                dz[:, at] = part
            begun = True
        pump()

    def plane_pairs(j):
        at = columns(j)
        pairs = []
        for plane in range(4):
            wide = columns(4 * plane + j)
            xhat = saved[HAT_A1][plane, :, at].astype(jnp.float32)
            v = xhat * par_mid[0:1, at] + par_mid[1:2, at]
            value = dz[:, wide] * slope(v)
            dz[:, wide] = value
            pairs.append((value, xhat))
        return pairs

    total = sums[SUM_A1]
    put_sums(plan, plane_pairs, mask, total.pay, 0, 512, pump)
    total.begin()
    flip[0:512] = dh_mid[...].T
    stages = total.stages()
    spatial_term(w_a2, saved[PATCH_A], 0, 3, 1)()
    stages[0]()
    spatial_term(w_a2, saved[PATCH_A], 3, 6, 1)()
    stages[1]()
    spatial_term(w_a2, saved[PATCH_A], 6, 9, 1)()
    pgrad_mid[0] = total.total[...]
    scale[0] = 0.25
    for plane in range(4):
        norm_back(
            lambda j, plane=plane: dz[:, columns(4 * plane + j)],
            saved[HAT_A1].at[plane],
            total.total,
            0,
            inv_mid.at[0],
            par_mid,
            0,
            planes[plane],
            4,
        )

    def input_gradient(p):
        target = (dh_a if p < 2 else dh_b).at[:, pl.ds((p % 2) * 1024, 1024)]
        value = dot(planes[p][...], w_a1[...].reshape(512, -1))
        if p == 0:
            value = value + saved[OUT_A][:, 0:1024].astype(jnp.float32)
            value = value + saved[OUT_A][:, 1024:2048].astype(jnp.float32)
        target[...] = value.astype(jnp.bfloat16)
        copy = pltpu.make_async_copy(target, dx_hbm.at[p], dx_sem.at[p])
        copy.start()
        return copy

    copies = []
    for p in range(4):
        copies.append(input_gradient(p))
        pump()

    def last_term(c, carry):
        at = quarter(c)
        total = jnp.zeros((512, 256), jnp.float32)
        for p in range(4):
            total = total + lax.dot_general(
                planes[p][...], x[p, :, at], (((0,), (0,)), ((), ())), preferred_element_type=jnp.float32
            )
        w_a1[:, :, 0, :, at] = total.astype(jnp.bfloat16).reshape(depth, 2, 64, 256)
        return carry

    paced(0, 4, last_term, 2, pump)
    reduce.enable(0)
    reduce.finish(weight_squares, squares_out)
    for copy in copies:
        copy.wait()
    for total in sums.values():
        total.close()


def run_backward(plan, depth, x, shifts, cot, mask, weight_squares, small, saved, fulls):
    rows, f32, bf16 = plan.rows, jnp.float32, jnp.bfloat16
    dma = pltpu.SemaphoreType.DMA
    scratch = []
    for _, pieces in backward_names(depth):
        scratch += pieces
    scratch += [pltpu.VMEM(value.shape, bf16) for value in (x, shifts, cot)]
    scratch += [pltpu.VMEM(full.shape, bf16) for full in fulls]
    scratch += [pltpu.VMEM(shape, kind) for name, (shape, kind) in zip(SAVED, saved_shapes(rows)) if name != PATCH_B]
    scratch += [
        pltpu.VMEM((rows, 2048), f32),
        pltpu.VMEM((rows, 512), f32),
        pltpu.VMEM((rows, 512), bf16),
        pltpu.VMEM((1024, rows), bf16),
        dma((10,)),
        dma((len(SAVED),)),
        dma((4,)),
    ]
    shapes = [full.shape for full in fulls]
    scratch += Reduce.scratch(shapes, depth)

    def part(shape, over):
        return jax.ShapeDtypeStruct((*shape[:3], shape[3] // over, shape[4]), bf16)

    outs = pl.pallas_call(
        functools.partial(backward_kernel, plan, depth),
        out_shape=[
            jax.ShapeDtypeStruct(x.shape, bf16),
            jax.ShapeDtypeStruct((4, 8, 512), f32),
            jax.ShapeDtypeStruct((8, 2048), f32),
            jax.ShapeDtypeStruct((8, 4096), f32),
            jax.ShapeDtypeStruct((8, 128), f32),
        ]
        + [jax.ShapeDtypeStruct(shape[2:], bf16) for shape in shapes]
        + [part(shape, 2) for shape in shapes]
        + [part(shape, 4) for shape in shapes],
        in_specs=[ANY] * 3 + [WHOLE] * 7 + [ANY] * len(SAVED) + [ANY] * 7,
        out_specs=[ANY] + [WHOLE] * 4 + [ANY] * 21,
        scratch_shapes=scratch,
        compiler_params=pltpu.CompilerParams(collective_id=1, has_side_effects=True, vmem_limit_bytes=VMEM_LIMIT),
    )(x, shifts, cot, mask, weight_squares, *small, *saved, *fulls)
    return outs[:12]


def scale_kernel(squares, *refs):
    totals, weights, outs, rest = refs[:7], refs[7:14], refs[14:28], refs[28:]
    totals_in, weights_in, staged = rest[:7], rest[7:14], rest[14:28]
    in_sem, out_sem = rest[28:]

    def loads(i):
        return (
            pltpu.make_async_copy(totals[i], totals_in[i], in_sem.at[0, i]),
            pltpu.make_async_copy(weights[i], weights_in[i], in_sem.at[1, i]),
        )

    def stores(i):
        return [pltpu.make_async_copy(staged[2 * i + n], outs[2 * i + n], out_sem.at[n, i]) for n in (0, 1)]

    for i in range(7):
        for copy in loads(i):
            copy.start()
    weight_norm = jnp.sqrt(squares[0:1, :])
    trust = weight_norm / (jnp.sqrt(squares[1:2, :]) + DECAY_RATE * weight_norm)
    for i in range(7):
        for copy in loads(i):
            copy.wait()
        ratio = trust[0:1, i : i + 1]

        def body(lead, carry, i=i, ratio=ratio):
            gradient = totals_in[i][lead].astype(jnp.float32)
            staged[2 * i][lead] = gradient
            decayed = gradient + DECAY_RATE * weights_in[i][lead].astype(jnp.float32)
            staged[2 * i + 1][lead] = ratio * decayed
            return carry

        lax.fori_loop(0, totals_in[i].shape[0], body, 0)
        for copy in stores(i):
            copy.start()
    for i in range(7):
        for copy in stores(i):
            copy.wait()


def run_scale(squares, totals, shards):
    f32, bf16, dma = jnp.float32, jnp.bfloat16, pltpu.SemaphoreType.DMA
    shapes = [total.shape for total in totals]
    outs = pl.pallas_call(
        scale_kernel,
        out_shape=[jax.ShapeDtypeStruct(shape, f32) for shape in shapes for _ in (0, 1)],
        in_specs=[WHOLE] + [ANY] * 14,
        out_specs=[ANY] * 14,
        scratch_shapes=[pltpu.VMEM(shape, bf16) for shape in shapes * 2]
        + [pltpu.VMEM(shape, f32) for shape in shapes for _ in (0, 1)]
        + [dma((2, 7)), dma((2, 7))],
        compiler_params=pltpu.CompilerParams(vmem_limit_bytes=VMEM_LIMIT),
    )(squares, *totals, *shards)
    return outs[0::2], outs[1::2]


def on_device(
    input_160,
    input_224,
    input_288,
    cotangent_160,
    cotangent_224,
    cotangent_288,
    live_counts,
    conv_a1,
    norm_a1,
    conv_a2,
    norm_a2,
    conv_a3,
    norm_a3,
    conv_as,
    norm_as,
    conv_b1,
    norm_b1,
    conv_b2,
    norm_b2,
    conv_b3,
    norm_b3,
):
    if conv_a1.shape[1] % 64 or conv_a3.shape[1] % 128 or lax.axis_size(REP) != 4:
        return plain_on_device(
            input_160,
            input_224,
            input_288,
            cotangent_160,
            cotangent_224,
            cotangent_288,
            live_counts,
            conv_a1,
            norm_a1,
            conv_a2,
            norm_a2,
            conv_a3,
            norm_a3,
            conv_as,
            norm_as,
            conv_b1,
            norm_b1,
            conv_b2,
            norm_b2,
            conv_b3,
            norm_b3,
        )
    depth = lax.axis_size(DP) // 2
    inputs = (input_160, input_224, input_288)
    plan = Plan([value.shape for value in inputs])
    shards = (
        conv_a1.T[None],
        jnp.transpose(conv_a2, (0, 1, 3, 2)).reshape(9, conv_a2.shape[3], conv_a2.shape[2]),
        conv_a3.reshape(2, -1, conv_a3.shape[1]),
        conv_as.reshape(4, -1, conv_as.shape[1]),
        conv_b1.T[None],
        jnp.transpose(conv_b2, (0, 1, 3, 2)).reshape(9, conv_b2.shape[3], conv_b2.shape[2]),
        conv_b3.reshape(2, -1, conv_b3.shape[1]),
    )

    planes, cotangents, masks, live_pixels = [], [], [], []
    for g, (value, cotangent) in enumerate(
        zip(inputs, (cotangent_160, cotangent_224, cotangent_288))
    ):
        side, slots, fill = plan.sides[g], plan.slots[g], plan.sizes[g] - plan.valid[g]
        split = jnp.transpose(value, (1, 2, 0, 3)).reshape(side, 2, side, 2, slots, -1)
        split = jnp.transpose(split, (1, 3, 0, 2, 4, 5)).reshape(4, plan.valid[g], -1)
        planes.append(jnp.pad(split, ((0, 0), (0, fill), (0, 0))))
        cotangents.append(
            jnp.pad(jnp.transpose(cotangent, (1, 2, 0, 3)).reshape(plan.valid[g], -1), ((0, fill), (0, 0)))
        )
        row = jnp.arange(plan.sizes[g])
        live = (lax.rem(row, slots) < live_counts[0, g]) & (row < plan.valid[g])
        masks.append(jnp.broadcast_to(live.astype(jnp.float32)[:, None], (plan.sizes[g], 128)))
        live_pixels.append((live_counts[0, g] * (side * side)).astype(jnp.float32))
    x = jnp.concatenate(planes, axis=1)
    cot = jnp.concatenate(cotangents, axis=0)
    mask = jnp.concatenate(masks, axis=0)
    counts = jnp.pad(jnp.stack(live_pixels), (0, 125)).reshape(1, 128)

    def stacked(norms):
        rows = jnp.concatenate(norms, axis=0).astype(jnp.float32)
        return jnp.pad(rows, ((0, 8 - rows.shape[0]), (0, 0)))

    mid_local, out_local = norm_a1.shape[1], norm_a3.shape[1]
    mid_width, out_width = mid_local * 2 * depth, out_local * 2 * depth
    norm_mid = lax.dynamic_update_slice(
        jnp.zeros((8, mid_width), jnp.float32),
        stacked((norm_a1, norm_a2, norm_b1, norm_b2)),
        (0, lax.axis_index(DP) * mid_local),
    )
    norm_out = stacked((norm_a3, norm_as, norm_b3))
    shifts = jnp.asarray(plan.shifts())

    out, *results = run_forward(plan, depth, x, shifts, mask, counts, norm_mid, norm_out, shards)
    small, square_row, fulls, saved = results[:5], results[5], results[6:13], results[13:]
    dx, pgrad_mid, pgrad_b3, pgrad_j, squares, *totals = run_backward(
        plan, depth, x, shifts, cot, mask, square_row, small, saved, fulls
    )

    def placed(values):
        return [
            values[0][0].T,
            jnp.transpose(values[1], (0, 2, 1)).reshape(conv_a2.shape),
            values[2].reshape(conv_a3.shape),
            values[3].reshape(conv_as.shape),
            values[4][0].T,
            jnp.transpose(values[5], (0, 2, 1)).reshape(conv_b2.shape),
            values[6].reshape(conv_b3.shape),
        ]

    gradients, scaled = run_scale(squares, totals, shards)
    gradients, scaled = placed(gradients), placed(scaled)

    def norm_gradient(sums, local):
        both = jnp.stack([sums[3] + sums[4] + sums[5], sums[0] + sums[1] + sums[2]])
        return lax.dynamic_slice_in_dim(both, lax.axis_index(DP) * local, local, 1)

    norm_gradients = (
        norm_gradient(pgrad_mid[0], mid_local),
        norm_gradient(pgrad_mid[1], mid_local),
        norm_gradient(pgrad_j[:, :out_width], out_local),
        norm_gradient(pgrad_j[:, out_width:], out_local),
        norm_gradient(pgrad_mid[2], mid_local),
        norm_gradient(pgrad_mid[3], mid_local),
        norm_gradient(pgrad_b3, out_local),
    )
    outputs, grad_inputs = [], []
    for g in range(3):
        side, slots, start = plan.sides[g], plan.slots[g], plan.starts[g]
        rows = out[start : start + plan.valid[g]].reshape(side, side, slots, -1)
        outputs.append(jnp.transpose(rows, (2, 0, 1, 3)))
        split = dx[:, start : start + plan.valid[g]].reshape(2, 2, side, side, slots, -1)
        split = jnp.transpose(split, (2, 0, 3, 1, 4, 5)).reshape(2 * side, 2 * side, slots, -1)
        grad_inputs.append(jnp.transpose(split, (2, 0, 1, 3)))
    pairs = [piece for pair in zip(gradients, norm_gradients) for piece in pair]
    return (*outputs, *grad_inputs, *pairs, *scaled, squares[0:2, 0:7])


def solution(mesh):
    by_image, by_column = P((DP, REP), None, None, None), P(None, DP)
    by_channel = P(None, None, None, DP)
    weights = [by_column, by_column, by_channel] + [by_column] * 7 + [by_channel] + [by_column] * 3
    kernels = [by_column, by_channel] + [by_column] * 3 + [by_channel, by_column]
    return jax.shard_map(
        on_device,
        mesh=mesh,
        in_specs=(*[by_image] * 6, P((DP, REP), None), *weights),
        out_specs=(*[by_image] * 6, *weights, *kernels, P()),
        check_vma=False,
    )
```

```python
import functools

import jax
import jax.numpy as jnp
import numpy as np
from jax import lax
from jax.experimental import pallas as pl
from jax.experimental.pallas import tpu as pltpu
from jax.sharding import PartitionSpec as P

DP, REP = "dp", "rep"
EPSILON = 1e-05
DECAY_RATE = 5e-05


def silu_slope(values):
    sigmoid = jax.nn.sigmoid(values)
    return sigmoid * (1.0 + values * (1.0 - sigmoid))


def pointwise(inputs, weight):
    return jnp.tensordot(inputs, weight, 1, preferred_element_type=jnp.float32)


def pointwise_back(upstream, weight):
    return jnp.tensordot(upstream, weight, ((3,), (1,)), preferred_element_type=jnp.float32)


def weight_term(inputs, upstream):
    return jnp.tensordot(inputs, upstream, ((0, 1, 2),) * 2, preferred_element_type=jnp.float32)


def summed_terms(inputs, upstream):
    running = weight_term(inputs[0], upstream[0])
    for group_member in (1, 2):
        running = running + weight_term(inputs[group_member], upstream[group_member])
    return running


def patches(inputs, stride):
    padded = jnp.pad(inputs, ((0, 0), (1, 1), (1, 1), (0, 0)))
    extent = inputs.shape[1]
    pieces = []
    for offset_row in range(3):
        for offset_col in range(3):
            pieces.append(
                padded[
                    :,
                    offset_row : offset_row + extent : stride,
                    offset_col : offset_col + extent : stride,
                    :,
                ]
            )
    return jnp.concatenate(pieces, axis=3)


def fold_patches(upstream, stride, side_in):
    channels = upstream.shape[3] // 9
    padded = jnp.zeros((upstream.shape[0], side_in + 2, side_in + 2, channels), jnp.float32)
    for offset_row in range(3):
        for offset_col in range(3):
            start_at = (offset_row * 3 + offset_col) * channels
            padded = padded.at[
                :,
                offset_row : offset_row + side_in : stride,
                offset_col : offset_col + side_in : stride,
                :,
            ].add(upstream[..., start_at : start_at + channels])
    return padded[:, 1 : side_in + 1, 1 : side_in + 1, :]


def batch_norm(values, live_masks, norm_param, totals):
    gain_row = norm_param[0].astype(jnp.float32)
    shift_row = norm_param[1].astype(jnp.float32)
    firsts = []
    seconds = []
    for group_member in range(3):
        weighted = values[group_member] * live_masks[group_member]
        firsts.append(jnp.sum(weighted, axis=(0, 1, 2)))
        seconds.append(jnp.sum(weighted * values[group_member], axis=(0, 1, 2)))
    summed = lax.psum(
        (firsts[0], seconds[0], firsts[1], seconds[1], firsts[2], seconds[2]), (DP, REP)
    )
    normed = []
    means = []
    scales = []
    for group_member in range(3):
        pixel_count = (
            totals[group_member] * values[group_member].shape[1] * values[group_member].shape[2]
        )
        mean_value = summed[2 * group_member] / pixel_count
        inv_std = lax.rsqrt(
            summed[2 * group_member + 1] / pixel_count - mean_value * mean_value + EPSILON
        )
        normed.append((values[group_member] - mean_value) * inv_std * gain_row + shift_row)
        means.append(mean_value)
        scales.append(inv_std)
    return (normed, means, scales)


def norm_back(upstream, values, live_masks, norm_param, means, scales, totals):
    gain_row = norm_param[0].astype(jnp.float32)
    normals = []
    firsts = []
    seconds = []
    for group_member in range(3):
        normal = (values[group_member] - means[group_member]) * scales[group_member]
        weighted = upstream[group_member] * live_masks[group_member]
        normals.append(normal)
        firsts.append(jnp.sum(weighted, axis=(0, 1, 2)))
        seconds.append(jnp.sum(weighted * normal, axis=(0, 1, 2)))
    summed = lax.psum(
        (firsts[0], seconds[0], firsts[1], seconds[1], firsts[2], seconds[2]), (DP, REP)
    )
    results = []
    for group_member in range(3):
        pixel_count = (
            totals[group_member] * values[group_member].shape[1] * values[group_member].shape[2]
        )
        centered = (
            upstream[group_member]
            - summed[2 * group_member] / pixel_count
            - normals[group_member] * (summed[2 * group_member + 1] / pixel_count)
        )
        results.append(
            (live_masks[group_member] * gain_row * scales[group_member] * centered).astype(
                jnp.bfloat16
            )
        )
    param_grad = jnp.stack([summed[1] + summed[3] + summed[5], summed[0] + summed[2] + summed[4]])
    return (results, param_grad)


def own_columns(full, local_width):
    return lax.dynamic_slice_in_dim(full, lax.axis_index(DP) * local_width, local_width, 1)


def plain_on_device(
    input_160,
    input_224,
    input_288,
    cotangent_160,
    cotangent_224,
    cotangent_288,
    live_counts,
    conv_a1,
    norm_a1,
    conv_a2,
    norm_a2,
    conv_a3,
    norm_a3,
    conv_as,
    norm_as,
    conv_b1,
    norm_b1,
    conv_b2,
    norm_b2,
    conv_b3,
    norm_b3,
):
    inputs = (input_160, input_224, input_288)
    cotangents = (cotangent_160, cotangent_224, cotangent_288)
    live_masks = []
    masked = []
    for group_member in range(3):
        group_slot_count = inputs[group_member].shape[0]
        live_flags = (
            (jnp.arange(group_slot_count) < live_counts[0, group_member])
            .astype(jnp.float32)
            .reshape(group_slot_count, 1, 1, 1)
        )
        live_masks.append(live_flags)
        masked.append(inputs[group_member] * live_flags.astype(jnp.bfloat16))
    totals = lax.psum(live_counts[0].astype(jnp.float32), (DP, REP))
    local_weights = (conv_a1, conv_a2, conv_a3, conv_as, conv_b1, conv_b2, conv_b3)
    squares_list = []
    for weight in local_weights:
        squares_list.append(jnp.sum(jnp.square(weight.astype(jnp.float32))))
    weight_squares = jnp.stack(squares_list)
    gathered_a = (
        lax.all_gather(conv_a1, DP, axis=1, tiled=True),
        lax.all_gather(norm_a1, DP, axis=1, tiled=True),
        lax.all_gather(conv_a2, DP, axis=3, tiled=True),
        lax.all_gather(norm_a2, DP, axis=1, tiled=True),
        lax.all_gather(conv_a3, DP, axis=1, tiled=True),
        lax.all_gather(norm_a3, DP, axis=1, tiled=True),
        lax.all_gather(conv_as, DP, axis=1, tiled=True),
        lax.all_gather(norm_as, DP, axis=1, tiled=True),
    )
    full_a1, param_a1, full_a2, param_a2, full_a3, param_a3, full_as, param_as = gathered_a
    mid_width = full_a2.shape[3]
    out_width = full_a3.shape[1]
    hidden_a1 = [pointwise(masked[group_member], full_a1) for group_member in range(3)]
    normed_a1, means_a1, scales_a1 = batch_norm(hidden_a1, live_masks, param_a1, totals)
    act_a1 = [
        jax.nn.silu(normed_a1[group_member]).astype(jnp.bfloat16) for group_member in range(3)
    ]
    kernel_a2 = full_a2.reshape(9 * mid_width, mid_width)
    hidden_a2 = [
        pointwise(patches(act_a1[group_member], 2), kernel_a2) for group_member in range(3)
    ]
    normed_a2, means_a2, scales_a2 = batch_norm(hidden_a2, live_masks, param_a2, totals)
    act_a2 = [
        jax.nn.silu(normed_a2[group_member]).astype(jnp.bfloat16) for group_member in range(3)
    ]
    strided = [masked[group_member][:, ::2, ::2, :] for group_member in range(3)]
    joined = [
        jnp.concatenate(
            [pointwise(act_a2[group_member], full_a3), pointwise(strided[group_member], full_as)],
            axis=3,
        )
        for group_member in range(3)
    ]
    param_joined = jnp.concatenate([param_a3, param_as], axis=1)
    normed_j, means_j, scales_j = batch_norm(joined, live_masks, param_joined, totals)
    sum_a = [
        normed_j[group_member][..., :out_width] + normed_j[group_member][..., out_width:]
        for group_member in range(3)
    ]
    out_a = [
        (jax.nn.silu(sum_a[group_member]) * live_masks[group_member]).astype(jnp.bfloat16)
        for group_member in range(3)
    ]
    gathered_b = (
        lax.all_gather(conv_b1, DP, axis=1, tiled=True),
        lax.all_gather(norm_b1, DP, axis=1, tiled=True),
        lax.all_gather(conv_b2, DP, axis=3, tiled=True),
        lax.all_gather(norm_b2, DP, axis=1, tiled=True),
        lax.all_gather(conv_b3, DP, axis=1, tiled=True),
        lax.all_gather(norm_b3, DP, axis=1, tiled=True),
    )
    full_b1, param_b1, full_b2, param_b2, full_b3, param_b3 = gathered_b
    hidden_b1 = [pointwise(out_a[group_member], full_b1) for group_member in range(3)]
    normed_b1, means_b1, scales_b1 = batch_norm(hidden_b1, live_masks, param_b1, totals)
    act_b1 = [
        jax.nn.silu(normed_b1[group_member]).astype(jnp.bfloat16) for group_member in range(3)
    ]
    kernel_b2 = full_b2.reshape(9 * mid_width, mid_width)
    hidden_b2 = [
        pointwise(patches(act_b1[group_member], 1), kernel_b2) for group_member in range(3)
    ]
    normed_b2, means_b2, scales_b2 = batch_norm(hidden_b2, live_masks, param_b2, totals)
    act_b2 = [
        jax.nn.silu(normed_b2[group_member]).astype(jnp.bfloat16) for group_member in range(3)
    ]
    hidden_b3 = [pointwise(act_b2[group_member], full_b3) for group_member in range(3)]
    normed_b3, means_b3, scales_b3 = batch_norm(hidden_b3, live_masks, param_b3, totals)
    sum_b = [
        normed_b3[group_member] + out_a[group_member].astype(jnp.float32)
        for group_member in range(3)
    ]
    outputs = [
        (jax.nn.silu(sum_b[group_member]) * live_masks[group_member]).astype(jnp.bfloat16)
        for group_member in range(3)
    ]
    back_b = (
        lax.all_gather(conv_b1, DP, axis=1, tiled=True),
        lax.all_gather(norm_b1, DP, axis=1, tiled=True),
        lax.all_gather(conv_b2, DP, axis=3, tiled=True),
        lax.all_gather(norm_b2, DP, axis=1, tiled=True),
        lax.all_gather(conv_b3, DP, axis=1, tiled=True),
        lax.all_gather(norm_b3, DP, axis=1, tiled=True),
    )
    full_b1, param_b1, full_b2, param_b2, full_b3, param_b3 = back_b
    kernel_b2 = full_b2.reshape(9 * mid_width, mid_width)
    grad_sum_b = [
        cotangents[group_member].astype(jnp.float32)
        * live_masks[group_member]
        * silu_slope(sum_b[group_member])
        for group_member in range(3)
    ]
    grad_h_b3, pgrad_b3 = norm_back(
        grad_sum_b, hidden_b3, live_masks, param_b3, means_b3, scales_b3, totals
    )
    term_b3 = summed_terms(act_b2, grad_h_b3)
    grad_act = [
        pointwise_back(grad_h_b3[group_member], full_b3) * silu_slope(normed_b2[group_member])
        for group_member in range(3)
    ]
    grad_h_b2, pgrad_b2 = norm_back(
        grad_act, hidden_b2, live_masks, param_b2, means_b2, scales_b2, totals
    )
    term_b2 = summed_terms(
        [patches(act_b1[group_member], 1) for group_member in range(3)], grad_h_b2
    ).reshape(3, 3, mid_width, mid_width)
    grad_act = [
        fold_patches(
            pointwise_back(grad_h_b2[group_member], kernel_b2), 1, act_b1[group_member].shape[1]
        )
        * silu_slope(normed_b1[group_member])
        for group_member in range(3)
    ]
    grad_h_b1, pgrad_b1 = norm_back(
        grad_act, hidden_b1, live_masks, param_b1, means_b1, scales_b1, totals
    )
    term_b1 = summed_terms(out_a, grad_h_b1)
    grad_out_a = [
        grad_sum_b[group_member] + pointwise_back(grad_h_b1[group_member], full_b1)
        for group_member in range(3)
    ]
    shard_b = (
        lax.psum_scatter(term_b1, DP, scatter_dimension=1, tiled=True),
        lax.psum_scatter(term_b2, DP, scatter_dimension=3, tiled=True),
        lax.psum_scatter(term_b3, DP, scatter_dimension=1, tiled=True),
    )
    grads_b = (
        lax.psum(shard_b[0].astype(jnp.bfloat16), REP).astype(jnp.float32),
        lax.psum(shard_b[1].astype(jnp.bfloat16), REP).astype(jnp.float32),
        lax.psum(shard_b[2].astype(jnp.bfloat16), REP).astype(jnp.float32),
    )
    back_a = (
        lax.all_gather(conv_a1, DP, axis=1, tiled=True),
        lax.all_gather(norm_a1, DP, axis=1, tiled=True),
        lax.all_gather(conv_a2, DP, axis=3, tiled=True),
        lax.all_gather(norm_a2, DP, axis=1, tiled=True),
        lax.all_gather(conv_a3, DP, axis=1, tiled=True),
        lax.all_gather(norm_a3, DP, axis=1, tiled=True),
        lax.all_gather(conv_as, DP, axis=1, tiled=True),
        lax.all_gather(norm_as, DP, axis=1, tiled=True),
    )
    full_a1, param_a1, full_a2, param_a2, full_a3, param_a3, full_as, param_as = back_a
    kernel_a2 = full_a2.reshape(9 * mid_width, mid_width)
    param_joined = jnp.concatenate([param_a3, param_as], axis=1)
    grad_sum_a = [
        grad_out_a[group_member] * live_masks[group_member] * silu_slope(sum_a[group_member])
        for group_member in range(3)
    ]
    grad_joined = [
        jnp.concatenate([grad_sum_a[group_member], grad_sum_a[group_member]], axis=3)
        for group_member in range(3)
    ]
    grad_h_j, pgrad_j = norm_back(
        grad_joined, joined, live_masks, param_joined, means_j, scales_j, totals
    )
    grad_h_a3 = [grad_h_j[group_member][..., :out_width] for group_member in range(3)]
    grad_h_as = [grad_h_j[group_member][..., out_width:] for group_member in range(3)]
    term_a3 = summed_terms(act_a2, grad_h_a3)
    term_as = summed_terms(strided, grad_h_as)
    grad_act = [
        pointwise_back(grad_h_a3[group_member], full_a3) * silu_slope(normed_a2[group_member])
        for group_member in range(3)
    ]
    grad_h_a2, pgrad_a2 = norm_back(
        grad_act, hidden_a2, live_masks, param_a2, means_a2, scales_a2, totals
    )
    term_a2 = summed_terms(
        [patches(act_a1[group_member], 2) for group_member in range(3)], grad_h_a2
    ).reshape(3, 3, mid_width, mid_width)
    grad_act = [
        fold_patches(
            pointwise_back(grad_h_a2[group_member], kernel_a2), 2, act_a1[group_member].shape[1]
        )
        * silu_slope(normed_a1[group_member])
        for group_member in range(3)
    ]
    grad_h_a1, pgrad_a1 = norm_back(
        grad_act, hidden_a1, live_masks, param_a1, means_a1, scales_a1, totals
    )
    term_a1 = summed_terms(masked, grad_h_a1)
    grad_inputs = [
        pointwise_back(grad_h_a1[group_member], full_a1)
        .at[:, ::2, ::2, :]
        .add(pointwise_back(grad_h_as[group_member], full_as))
        .astype(jnp.bfloat16)
        for group_member in range(3)
    ]
    shard_a = (
        lax.psum_scatter(term_a1, DP, scatter_dimension=1, tiled=True),
        lax.psum_scatter(term_a2, DP, scatter_dimension=3, tiled=True),
        lax.psum_scatter(term_a3, DP, scatter_dimension=1, tiled=True),
        lax.psum_scatter(term_as, DP, scatter_dimension=1, tiled=True),
    )
    grads_a = (
        lax.psum(shard_a[0].astype(jnp.bfloat16), REP).astype(jnp.float32),
        lax.psum(shard_a[1].astype(jnp.bfloat16), REP).astype(jnp.float32),
        lax.psum(shard_a[2].astype(jnp.bfloat16), REP).astype(jnp.float32),
        lax.psum(shard_a[3].astype(jnp.bfloat16), REP).astype(jnp.float32),
    )
    mid_local = norm_a1.shape[1]
    out_local = norm_a3.shape[1]
    norm_grad_a1 = own_columns(pgrad_a1, mid_local)
    norm_grad_a2 = own_columns(pgrad_a2, mid_local)
    norm_grad_a3 = own_columns(pgrad_j[:, :out_width], out_local)
    norm_grad_as = own_columns(pgrad_j[:, out_width:], out_local)
    norm_grad_b1 = own_columns(pgrad_b1, mid_local)
    norm_grad_b2 = own_columns(pgrad_b2, mid_local)
    norm_grad_b3 = own_columns(pgrad_b3, out_local)
    gradients = (grads_a[0], grads_a[1], grads_a[2], grads_a[3], grads_b[0], grads_b[1], grads_b[2])
    grad_list = []
    for gradient in gradients:
        grad_list.append(jnp.sum(gradient * gradient))
    grad_squares = jnp.stack(grad_list)
    weight_totals, grad_totals = lax.psum((weight_squares, grad_squares), DP)
    weight_norm = jnp.sqrt(weight_totals)
    grad_norm = jnp.sqrt(grad_totals)
    trust_ratio = weight_norm / (grad_norm + DECAY_RATE * weight_norm)
    scaled = [
        trust_ratio[layer_id]
        * (gradients[layer_id] + DECAY_RATE * local_weights[layer_id].astype(jnp.float32))
        for layer_id in range(7)
    ]
    return (
        outputs[0],
        outputs[1],
        outputs[2],
        grad_inputs[0],
        grad_inputs[1],
        grad_inputs[2],
        gradients[0],
        norm_grad_a1,
        gradients[1],
        norm_grad_a2,
        gradients[2],
        norm_grad_a3,
        gradients[3],
        norm_grad_as,
        gradients[4],
        norm_grad_b1,
        gradients[5],
        norm_grad_b2,
        gradients[6],
        norm_grad_b3,
        scaled[0],
        scaled[1],
        scaled[2],
        scaled[3],
        scaled[4],
        scaled[5],
        scaled[6],
        jnp.stack([weight_totals, grad_totals]),
    )


MESH = pl.DeviceIdType.MESH
ANY = pl.BlockSpec(memory_space=pl.ANY)


def position():
    dp, rep = lax.axis_index(DP), lax.axis_index(REP)
    return dp // 2, lax.rem(dp, 2), rep // 2, lax.rem(rep, 2)


def device_at(z, x, y, core):
    return (z * 2 + x, y * 2 + core)


def greet(depth, crosswise=False):
    z, x, y, core = position()
    barrier = pltpu.get_barrier_semaphore()
    peers = [(z, x, y, 1 - core), (z, x, 1 - y, core), (z, x, 1 - y, 1 - core)]
    peers += [(z, 1 - x, y, core), (z, 1 - x, y, 1 - core), (z, 1 - x, 1 - y, core), (z, 1 - x, 1 - y, 1 - core)]
    peers += [(lax.rem(z + step, depth), x, y, core) for step in range(1, depth)]
    if crosswise:
        peers += [(lax.rem(z + step, depth), 1 - x, y, core) for step in range(1, depth)]
    for peer in peers:
        pl.semaphore_signal(barrier, inc=1, device_id=device_at(*peer), device_id_type=MESH)
    pl.semaphore_wait(barrier, len(peers))


def remote(src, dst, send, recv, peer):
    return pltpu.make_async_remote_copy(
        src_ref=src, dst_ref=dst, send_sem=send, recv_sem=recv, device_id=device_at(*peer), device_id_type=MESH
    )


def chunk_rows(rows, both, y, core):
    if both:
        return pl.ds(pl.multiple_of(core * (rows // 2), rows // 2), rows // 2)
    return pl.ds(pl.multiple_of(core * (rows // 2) + y * (rows // 4), rows // 4), rows // 4)


def core_rows(rows, core):
    return pl.ds(pl.multiple_of(core * (rows // 2), rows // 2), rows // 2)


class Gather:
    AHEAD = 3

    def __init__(self, shards, fulls, sems, depth):
        self.shards, self.fulls, self.depth = shards, fulls, depth
        (self.local_sem, self.z_send, self.z_recv, self.x_send, self.x_recv) = sems[:5]
        (self.y_send, self.y_recv, self.c_send, self.c_recv) = sems[5:]
        self.z, self.x, self.y, self.core = position()
        self.count = len(GATHER_CHUNKS)
        self.z_next = self.x_next = self.y_next = self.c_next = 0

    @staticmethod
    def scratch(depth):
        dma, count = pltpu.SemaphoreType.DMA, len(GATHER_CHUNKS)
        return [dma((count,))] + [dma((count, depth - 1))] * 2 + [dma((count,))] * 6

    def part(self, k):
        tensor, lead, leads, both, column, columns = GATHER_CHUNKS[k]
        rows = chunk_rows(self.shards[tensor].shape[1], both, self.y, self.core)
        return self.fulls[tensor], pl.ds(lead, leads), rows, pl.ds(column, columns)

    def place(self, k):
        full, lead, rows, cols = self.part(k)
        shard = self.shards[GATHER_CHUNKS[k][0]]
        return pltpu.make_async_copy(
            shard.at[lead, rows, cols], full.at[self.z, self.x, lead, rows, cols], self.local_sem.at[k]
        )

    def z_copies(self, k):
        full, lead, rows, cols = self.part(k)
        here = full.at[self.z, self.x, lead, rows, cols]
        return [
            remote(
                here,
                here,
                self.z_send.at[k, step - 1],
                self.z_recv.at[k, step - 1],
                (lax.rem(self.z + step, self.depth), self.x, self.y, self.core),
            )
            for step in range(1, self.depth)
        ]

    def x_copy(self, k):
        full, lead, rows, cols = self.part(k)
        here = full.at[:, self.x, lead, rows, cols]
        return remote(here, here, self.x_send.at[k], self.x_recv.at[k], (self.z, 1 - self.x, self.y, self.core))

    def y_copy(self, k):
        full, lead, rows, cols = self.part(k)
        here = full.at[:, :, lead, rows, cols]
        return remote(here, here, self.y_send.at[k], self.y_recv.at[k], (self.z, self.x, 1 - self.y, self.core))

    def c_copy(self, k):
        full, lead, _, cols = self.part(k)
        here = full.at[:, :, lead, core_rows(full.shape[3], self.core), cols]
        return remote(here, here, self.c_send.at[k], self.c_recv.at[k], (self.z, self.x, self.y, 1 - self.core))

    def place_all(self):
        for k in range(self.count):
            self.place(k).start()

    def launch(self, k):
        if k < self.count:
            self.place(k).wait()
            for copy in self.z_copies(k):
                copy.start()

    def begin(self):
        for k in range(self.AHEAD):
            self.launch(k)

    def z_step(self):
        k, self.z_next = self.z_next, self.z_next + 1
        for copy in self.z_copies(k):
            copy.wait_recv()
        self.x_copy(k).start()
        self.launch(k + self.AHEAD)

    def x_step(self):
        k, self.x_next = self.x_next, self.x_next + 1
        self.x_copy(k).wait_recv()
        (self.c_copy if GATHER_CHUNKS[k][3] else self.y_copy)(k).start()

    def y_step(self):
        k, self.y_next = self.y_next, self.y_next + 1
        if not GATHER_CHUNKS[k][3]:
            self.y_copy(k).wait_recv()
            self.c_copy(k).start()

    def c_step(self):
        k, self.c_next = self.c_next, self.c_next + 1
        self.c_copy(k).wait_recv()

    def tick(self, upto=-1):
        count = self.count
        if self.z_next < count:
            self.z_step()
        for before, after, step, lag in (
            (self.z_next, self.x_next, self.x_step, 1),
            (self.x_next, self.y_next, self.y_step, 1),
            (self.y_next, self.c_next, self.c_step, 1),
        ):
            if after < before and (before - after > lag or before == count or after <= upto):
                step()

    def pump(self, ticks=1):
        for _ in range(ticks):
            if self.c_next < self.count:
                self.tick()

    def ready(self, tensor):
        last = max(k for k, chunk in enumerate(GATHER_CHUNKS) if chunk[0] == tensor)
        while self.c_next <= last:
            self.tick(last)

    def close(self):
        for k in range(self.count):
            for copy in self.z_copies(k):
                copy.wait_send()
            self.x_copy(k).wait_send()
            if not GATHER_CHUNKS[k][3]:
                self.y_copy(k).wait_send()
            self.c_copy(k).wait_send()


def taps(tensor):
    pieces = []
    for lead in (0, 3, 6):
        pieces += [(tensor, lead, 1, True, 0, 512), (tensor, lead + 1, 2, False, 0, 512)]
    return pieces


CHUNKS = (
    [(0, 0, 1, False, column, 512) for column in (0, 512)],
    taps(1),
    [(2, lead, 1, False, 0, 256) for lead in (0, 1)],
    [(3, lead, 1, lead == 0, 0, 256) for lead in range(4)],
    [(4, 0, 1, column % 1024 == 0, column, 512) for column in (0, 512, 1024, 1536)],
    taps(5),
    [(6, lead, 1, False, 0, 256) for lead in (0, 1)],
)
GATHER_CHUNKS = [chunk for tensor in (0, 1, 3, 2, 4, 5, 6) for chunk in CHUNKS[tensor]]
REDUCE_CHUNKS = [chunk for tensor in (6, 5, 4, 2, 3, 1, 0) for chunk in CHUNKS[tensor]]


def add_blocks(extents, body):
    total = 1
    for extent in extents:
        total *= extent

    def step(flat, carry):
        index = []
        for extent in reversed(extents):
            index.append(lax.rem(flat, extent))
            flat = flat // extent
        body(*reversed(index))
        return carry

    lax.fori_loop(0, total, step, 0)


def add_to(target, source):
    target[...] = (target[...].astype(jnp.float32) + source[...].astype(jnp.float32)).astype(jnp.bfloat16)


class Reduce:
    def __init__(self, held, outs, c_hbm, y_hbm, refs, depth):
        self.held, self.outs, self.c_hbm, self.y_hbm, self.depth = held, outs, c_hbm, y_hbm, depth
        self.count = len(REDUCE_CHUNKS)
        refs = list(refs)

        def take(count):
            taken = refs[:count]
            del refs[:count]
            return taken

        self.from_x, self.from_z, self.swap = take(self.count), take(self.count), take(self.count)
        self.final = take(self.count)
        self.c_tall, self.c_wide, self.y_tall, self.y_wide, self.squares = take(5)
        self.c_sem, self.y_sem, self.x_sem, self.z_sem, self.s_sem, self.f_sem, self.q_sem, self.local_sem = take(8)
        self.z, self.x, self.y, self.core = position()
        self.enabled = 0
        self.next = [0] * len(self.LAGS)

    @staticmethod
    def sizes(shapes):
        for tensor, _, leads, both, _, columns in REDUCE_CHUNKS:
            rows = shapes[tensor][3]
            yield leads, rows, columns, rows // 2 if both else rows // 4, both

    @staticmethod
    def scratch(shapes, depth):
        dma, count = pltpu.SemaphoreType.DMA, len(REDUCE_CHUNKS)
        buffer = lambda *shape: pltpu.VMEM(shape, jnp.bfloat16)
        sizes = list(Reduce.sizes(shapes))
        return (
            [buffer(depth, leads, part, columns) for leads, _, columns, part, _ in sizes]
            + [buffer(depth - 1, leads, part, columns) for leads, _, columns, part, _ in sizes]
            + [buffer(leads, part, columns) if both else buffer(16, 128) for leads, _, columns, part, both in sizes]
            + [buffer(leads, rows, columns) for leads, rows, columns, _, _ in sizes]
            + [buffer(2, depth, 2, 1, shapes[2][3] // 2, shapes[2][4]), buffer(2, depth, 2, 2, shapes[0][3] // 2, 512)]
            + [buffer(2, depth, 2, 1, shapes[2][3] // 4, shapes[2][4]), buffer(2, depth, 2, 2, shapes[0][3] // 4, 512)]
            + [pltpu.VMEM((2 * depth + 3, 8, 128), jnp.float32)]
            + [dma((2, count))] * 3
            + [dma((2, count, depth - 1)), dma((2, count)), dma((2, count, 3)), dma((2, depth)), dma((3, count))]
        )

    def piece(self, k):
        tensor, lead, leads, both, column, columns = REDUCE_CHUNKS[k]
        held = self.held[tensor]
        rows = held.shape[3]
        return held, rows, pl.ds(lead, leads), pl.ds(column, columns), chunk_rows(rows, both, self.y, self.core)

    def extents(self, k):
        return REDUCE_CHUNKS[k][2], REDUCE_CHUNKS[k][1]

    def slot(self, k, tall, wide):
        tensor, _, leads = REDUCE_CHUNKS[k][:3]
        buffer = tall if tensor in (2, 3, 6) else wide
        return buffer.at[k % 2, :, :, pl.ds(0, leads)]

    def c_copy(self, k):
        held, rows, lead, cols, _ = self.piece(k)
        return remote(
            held.at[:, :, lead, core_rows(rows, 1 - self.core), cols],
            self.c_hbm[REDUCE_CHUNKS[k][0]].at[:, :, lead, :, cols],
            self.c_sem.at[0, k],
            self.c_sem.at[1, k],
            (self.z, self.x, self.y, 1 - self.core),
        )

    def c_load(self, k):
        _, _, lead, cols, _ = self.piece(k)
        return pltpu.make_async_copy(
            self.c_hbm[REDUCE_CHUNKS[k][0]].at[:, :, lead, :, cols],
            self.slot(k, self.c_tall, self.c_wide),
            self.local_sem.at[0, k],
        )

    def y_copy(self, k):
        held, rows, lead, cols, _ = self.piece(k)
        return remote(
            held.at[:, :, lead, chunk_rows(rows, False, 1 - self.y, self.core), cols],
            self.y_hbm[REDUCE_CHUNKS[k][0]].at[:, :, lead, :, cols],
            self.y_sem.at[0, k],
            self.y_sem.at[1, k],
            (self.z, self.x, 1 - self.y, self.core),
        )

    def y_load(self, k):
        _, _, lead, cols, _ = self.piece(k)
        return pltpu.make_async_copy(
            self.y_hbm[REDUCE_CHUNKS[k][0]].at[:, :, lead, :, cols],
            self.slot(k, self.y_tall, self.y_wide),
            self.local_sem.at[1, k],
        )

    def x_copy(self, k):
        held, _, lead, cols, rows = self.piece(k)
        return remote(
            held.at[:, 1 - self.x, lead, rows, cols],
            self.from_x[k],
            self.x_sem.at[0, k],
            self.x_sem.at[1, k],
            (self.z, 1 - self.x, self.y, self.core),
        )

    def z_copies(self, k):
        held, _, lead, cols, rows = self.piece(k)
        copies = []
        for step in range(1, self.depth):
            there = lax.rem(self.z + step, self.depth)
            copies.append(
                remote(
                    held.at[there, self.x, lead, rows, cols],
                    self.from_z[k].at[step - 1],
                    self.z_sem.at[0, k, step - 1],
                    self.z_sem.at[1, k, step - 1],
                    (there, self.x, self.y, self.core),
                )
            )
        return copies

    def s_copy(self, k):
        rows = self.piece(k)[4]
        return remote(
            self.final[k].at[:, rows],
            self.swap[k],
            self.s_sem.at[0, k],
            self.s_sem.at[1, k],
            (self.z, self.x, 1 - self.y, self.core),
        )

    def f_copies(self, k):
        here = self.final[k].at[:, self.piece(k)[4]]
        peers = [(self.z, self.x, self.y, 1 - self.core)]
        if not REDUCE_CHUNKS[k][3]:
            peers += [(self.z, self.x, 1 - self.y, self.core), (self.z, self.x, 1 - self.y, 1 - self.core)]
        return [
            remote(here, here, self.f_sem.at[0, k, i], self.f_sem.at[1, k, i], peer) for i, peer in enumerate(peers)
        ]

    def store(self, k):
        tensor = REDUCE_CHUNKS[k][0]
        _, _, lead, cols, _ = self.piece(k)
        return pltpu.make_async_copy(self.final[k], self.outs[tensor].at[lead, :, cols], self.local_sem.at[2, k])

    def add_c(self, k):
        held, rows, _, cols, _ = self.piece(k)
        leads, lead = self.extents(k)
        half, slot = core_rows(rows, self.core), self.slot(k, self.c_tall, self.c_wide)
        add_blocks(
            (self.depth, 2, leads), lambda z, x, i: add_to(held.at[z, x, lead + i, half, cols], slot.at[z, x, i])
        )

    def add_y(self, k):
        held, _, _, cols, rows = self.piece(k)
        leads, lead = self.extents(k)
        slot = self.slot(k, self.y_tall, self.y_wide)
        add_blocks(
            (self.depth, 2, leads), lambda z, x, i: add_to(held.at[z, x, lead + i, rows, cols], slot.at[z, x, i])
        )

    def add_x(self, k):
        held, _, _, cols, rows = self.piece(k)
        leads, lead = self.extents(k)
        add_blocks(
            (self.depth, leads), lambda z, i: add_to(held.at[z, self.x, lead + i, rows, cols], self.from_x[k].at[z, i])
        )

    def add_z(self, k):
        held, _, _, cols, rows = self.piece(k)
        leads, lead = self.extents(k)

        def body(i):
            total = held[self.z, self.x, lead + i, rows, cols].astype(jnp.float32)
            for step in range(1, self.depth):
                total = total + self.from_z[k][step - 1, i].astype(jnp.float32)
            self.final[k][i, rows] = total.astype(jnp.bfloat16)

        add_blocks((leads,), body)

    def add_s(self, k):
        rows = self.piece(k)[4]
        add_blocks((self.extents(k)[0],), lambda i: add_to(self.final[k].at[i, rows], self.swap[k].at[i]))

    def add_squares(self, k):
        leads = self.extents(k)[0]
        lanes = lax.broadcasted_iota(jnp.int32, (8, 128), 1)
        subs = lax.broadcasted_iota(jnp.int32, (8, 128), 0)
        where = (subs == 1) & (lanes == REDUCE_CHUNKS[k][0])

        def body(i):
            block = self.final[k][i].astype(jnp.float32)
            total = jnp.sum(jnp.sum(block * block, axis=0, keepdims=True), axis=1, keepdims=True)
            self.squares[2 * self.depth + 2] += jnp.where(where, total, 0.0)

        add_blocks((leads,), body)

    LAGS = (0, 1, 1, 1, 1, 1, 1, 1, 1)

    def stage(self, k, number):
        both = REDUCE_CHUNKS[k][3]
        if number == 0:
            self.c_copy(k).start()
        elif number == 1:
            self.c_copy(k).wait_recv()
            self.c_load(k).start()
        elif number == 2:
            self.c_load(k).wait()
            self.add_c(k)
            (self.x_copy if both else self.y_copy)(k).start()
        elif number == 3 and not both:
            self.y_copy(k).wait_recv()
            self.y_load(k).start()
        elif number == 4 and not both:
            self.y_load(k).wait()
            self.add_y(k)
            self.x_copy(k).start()
        elif number == 5:
            self.x_copy(k).wait_recv()
            self.add_x(k)
            for copy in self.z_copies(k):
                copy.start()
        elif number == 6:
            for copy in self.z_copies(k):
                copy.wait_recv()
            self.add_z(k)
            for copy in [self.s_copy(k)] if both else self.f_copies(k):
                copy.start()
        elif number == 7 and both:
            self.s_copy(k).wait_recv()
            self.s_copy(k).wait_send()
            self.add_s(k)
            for copy in self.f_copies(k):
                copy.start()
        elif number == 8:
            for copy in self.f_copies(k):
                copy.wait_recv()
            self.store(k).start()
            self.add_squares(k)

    def enable(self, tensor, leads_done=None):
        while self.enabled < self.count:
            chunk = REDUCE_CHUNKS[self.enabled]
            if chunk[0] != tensor or (leads_done is not None and chunk[1] + chunk[2] > leads_done):
                break
            self.enabled += 1

    def pump(self, ticks=1):
        for _ in range(ticks):
            for number in reversed(range(len(self.LAGS))):
                before = self.next[number - 1] if number else self.enabled
                behind = before - self.next[number]
                if behind > 0 and (behind > self.LAGS[number] or before == self.count):
                    self.stage(self.next[number], number)
                    self.next[number] += 1

    def finish(self, weight_squares, sums_out):
        while self.next[-1] < self.count:
            self.pump()
        squares, depth = self.squares, self.depth
        subs = lax.broadcasted_iota(jnp.int32, (8, 128), 0)
        mine = squares.at[self.z * 2 + self.x]
        mine[...] = squares[2 * depth + 2] + jnp.where(subs == 0, weight_squares[...], 0.0)
        copies = [
            remote(
                mine,
                mine,
                self.q_sem.at[0, step],
                self.q_sem.at[1, step],
                (lax.rem(self.z + step, depth), self.x, self.y, self.core),
            )
            for step in range(1, depth)
        ]
        for copy in copies:
            copy.start()
        for copy in copies:
            copy.wait_recv()
        own = squares[self.x]
        for deep in range(1, depth):
            own = own + squares[deep * 2 + self.x]
        column = squares.at[2 * depth + self.x]
        column[...] = own
        across = remote(
            column, column, self.q_sem.at[0, 0], self.q_sem.at[1, 0], (self.z, 1 - self.x, self.y, self.core)
        )
        across.start()
        across.wait_recv()
        sums_out[...] = squares[2 * depth] + squares[2 * depth + 1]
        across.wait_send()
        for copy in copies:
            copy.wait_send()
        for k in range(self.count):
            self.c_copy(k).wait_send()
            if not REDUCE_CHUNKS[k][3]:
                self.y_copy(k).wait_send()
            self.x_copy(k).wait_send()
            for copy in self.z_copies(k) + self.f_copies(k):
                copy.wait_send()
            self.store(k).wait()


class NearFar:
    def __init__(self, refs, depth):
        self.near, self.far, self.total, self.near_send, self.near_recv, self.far_send, self.far_recv = refs
        self.depth = depth
        self.z, self.x, self.y, self.core = position()
        self.mine = self.x * 4 + self.y * 2 + self.core
        self.pay = self.near.at[self.mine]
        self.sent = []

    @staticmethod
    def scratch(width, depth):
        dma = pltpu.SemaphoreType.DMA
        return [
            pltpu.VMEM((8, 8, width), jnp.float32),
            pltpu.VMEM((depth, 8, width), jnp.float32),
            pltpu.VMEM((8, width), jnp.float32),
            dma((7,)),
            dma((7,)),
            dma((depth - 1,)),
            dma((depth - 1,)),
        ]

    def near_copies(self):
        copies = []
        for offset in range(1, 8):
            x = 1 - self.x if offset & 4 else self.x
            y = 1 - self.y if offset & 2 else self.y
            core = 1 - self.core if offset & 1 else self.core
            here = self.near.at[self.mine]
            copies.append(
                remote(here, here, self.near_send.at[offset - 1], self.near_recv.at[offset - 1], (self.z, x, y, core))
            )
        return copies

    def far_copies(self):
        here = self.far.at[self.z]
        return [
            remote(
                here,
                here,
                self.far_send.at[step - 1],
                self.far_recv.at[step - 1],
                (lax.rem(self.z + step, self.depth), self.x, self.y, self.core),
            )
            for step in range(1, self.depth)
        ]

    def begin(self):
        for copy in self.near_copies():
            copy.start()

    def stages(self):
        def middle():
            for copy in self.near_copies():
                copy.wait_recv()
            total = self.near[0]
            for slot in range(1, 8):
                total = total + self.near[slot]
            self.far[self.z] = total
            for copy in self.far_copies():
                copy.start()

        def last():
            for copy in self.far_copies():
                copy.wait_recv()
            total = self.far[0]
            for slot in range(1, self.depth):
                total = total + self.far[slot]
            self.total[...] = total

        return [middle, last]

    def close(self):
        for copy in self.near_copies() + self.far_copies():
            copy.wait_send()


class Split:
    def __init__(self, refs, depth):
        (self.pay, self.near, self.deep, self.total, self.n_send, self.n_recv) = refs[:6]
        (self.z_send, self.z_recv, self.g_send, self.g_recv) = refs[6:]
        self.depth = depth
        self.z, self.x, self.y, self.core = position()
        self.width = self.pay.shape[1]
        self.mine = self.x * 4 + self.y * 2 + self.core

    @staticmethod
    def scratch(width, depth):
        dma = pltpu.SemaphoreType.DMA
        return [
            pltpu.VMEM((8, width), jnp.float32),
            pltpu.VMEM((8, 8, width // 8), jnp.float32),
            pltpu.VMEM((depth, 8, width // 8), jnp.float32),
            pltpu.VMEM((8, width), jnp.float32),
            dma((7,)),
            dma((7,)),
            dma((depth - 1,)),
            dma((depth - 1,)),
            dma((7,)),
            dma((7,)),
        ]

    def eighth_of(self, slot):
        return pl.ds(pl.multiple_of(slot * (self.width // 8), 128), self.width // 8)

    def around(self):
        for offset in range(1, 8):
            x = 1 - self.x if offset & 4 else self.x
            y = 1 - self.y if offset & 2 else self.y
            core = 1 - self.core if offset & 1 else self.core
            yield offset - 1, x, y, core

    def near_copies(self):
        return [
            remote(
                self.pay.at[:, self.eighth_of(x * 4 + y * 2 + core)],
                self.near.at[self.mine],
                self.n_send.at[i],
                self.n_recv.at[i],
                (self.z, x, y, core),
            )
            for i, x, y, core in self.around()
        ]

    def deep_copies(self):
        here = self.deep.at[self.z]
        return [
            remote(
                here,
                here,
                self.z_send.at[step - 1],
                self.z_recv.at[step - 1],
                (lax.rem(self.z + step, self.depth), self.x, self.y, self.core),
            )
            for step in range(1, self.depth)
        ]

    def gather_copies(self):
        here = self.total.at[:, self.eighth_of(self.mine)]
        return [
            remote(here, here, self.g_send.at[i], self.g_recv.at[i], (self.z, x, y, core))
            for i, x, y, core in self.around()
        ]

    def begin(self):
        for copy in self.near_copies():
            copy.start()
        self.near[self.mine] = self.pay[:, self.eighth_of(self.mine)]

    def stages(self):
        def first():
            for copy in self.near_copies():
                copy.wait_recv()
            total = self.near[0]
            for slot in range(1, 8):
                total = total + self.near[slot]
            self.deep[self.z] = total
            for copy in self.deep_copies():
                copy.start()

        def second():
            for copy in self.deep_copies():
                copy.wait_recv()
            total = self.deep[0]
            for slot in range(1, self.depth):
                total = total + self.deep[slot]
            self.total[:, self.eighth_of(self.mine)] = total
            for copy in self.gather_copies():
                copy.start()

        def third():
            for copy in self.gather_copies():
                copy.wait_recv()
            for copy in self.gather_copies():
                copy.wait_send()

        return [first, second, third]

    def close(self):
        for copy in self.near_copies() + self.deep_copies():
            copy.wait_send()


def interleave(stages, works):
    done = 0
    for i, stage in enumerate(stages):
        upto = (len(works) * (i + 1)) // len(stages)
        for work in works[done:upto]:
            work()
        done = upto
        stage()


HAT_A1, HAT_A2, HAT_A3, HAT_AS, HAT_B1, HAT_B2, HAT_B3, PATCH_A, PATCH_B, ACT_A2, ACT_B2, OUT_A = SAVED = range(12)
SUM_A1, SUM_A2, SUM_B1, SUM_B2, SUM_B3, SUM_J = range(6)


def paced(first, last, body, parts, pump):
    for part in range(parts):
        span = last - first
        lax.fori_loop(first + span * part // parts, first + span * (part + 1) // parts, body, 0)
        pump()


def columns(j):
    return pl.ds(pl.multiple_of(j * 128, 128), 128)


def dot(a, b):
    return lax.dot_general(a, b, (((1,), (0,)), ((), ())), preferred_element_type=jnp.float32)


def dot_nt(a, b):
    return lax.dot_general(a, b, (((1,), (1,)), ((), ())), preferred_element_type=jnp.float32)


def sigmoid(v):
    return 0.5 * jnp.tanh(0.5 * v) + 0.5


def slope(v):
    s = sigmoid(v)
    return s * (1.0 + v * (1.0 - s))


class Plan:
    def __init__(self, shapes):
        self.sides = [shape[1] // 2 for shape in shapes]
        self.slots = [shape[0] for shape in shapes]
        self.valid = [side * side * slots for side, slots in zip(self.sides, self.slots)]
        sizes = [-(-valid // 8) * 8 for valid in self.valid]
        sizes[2] += -sum(sizes) % 128
        self.starts = [0, sizes[0], sizes[0] + sizes[1]]
        self.sizes = sizes
        self.rows = sum(sizes)

    def spans(self):
        return [slice(start, start + size) for start, size in zip(self.starts, self.sizes)]

    def slot_rows(self):
        out = np.full((self.rows, 128), 1e6, np.float32)
        for start, valid, slots in zip(self.starts, self.valid, self.slots):
            out[start : start + valid] = (np.arange(valid) % slots)[:, None]
        return out

    def shifts(self):
        out = np.zeros((9, self.rows, self.rows), np.float32)
        for side, slots, start in zip(self.sides, self.slots, self.starts):
            at = lambda i, j, n: start + (i * side + j) * slots + n
            for di in (-1, 0, 1):
                for dj in (-1, 0, 1):
                    for i in range(max(0, -di), min(side, side - di)):
                        for j in range(max(0, -dj), min(side, side - dj)):
                            for n in range(slots):
                                out[(di + 1) * 3 + dj + 1, at(i, j, n), at(i + di, j + dj, n)] = 1.0
        return out.astype(jnp.bfloat16)


def put_sums(plan, pairs, mask, pay, base, width, pump=None):
    def body(j, carry):
        firsts, seconds = [0.0] * 3, [0.0] * 3
        for first, second in pairs(j):
            for g, span in enumerate(plan.spans()):
                live = first[span] * mask[span, :]
                firsts[g] = firsts[g] + jnp.sum(live, axis=0, keepdims=True)
                seconds[g] = seconds[g] + jnp.sum(live * second[span], axis=0, keepdims=True)
        zero = jnp.zeros((1, 128), jnp.float32)
        pay[:, columns(base + j)] = jnp.concatenate(firsts + seconds + [zero, zero], axis=0)
        return carry

    if pump is None:
        lax.fori_loop(0, width // 128, body, 0)
    else:
        paced(0, width // 128, body, 2, pump)


def put_scales(total, inverse, over, width, factor=1.0, base=0):
    def body(j, carry):
        at, to = columns(base + j), columns(j)
        per = over[0:3, :] * factor
        means = total[0:3, at] * per
        variance = total[3:6, at] * per - means * means
        scales = lax.rsqrt(variance + EPSILON)
        zero = jnp.zeros((5, 128), jnp.float32)
        total[:, at] = jnp.concatenate([means, zero], axis=0)
        inverse[:, to] = jnp.concatenate([scales, zero], axis=0)
        return carry

    lax.fori_loop(0, width // 128, body, 0)


def by_group(plan, of):
    return jnp.concatenate([of(g, span) for g, span in enumerate(plan.spans())], axis=0)


def forward_names(depth):
    return (
        (SUM_A1, NearFar.scratch(512, depth)),
        (SUM_A2, NearFar.scratch(512, depth)),
        (SUM_J, Split.scratch(4096, depth)),
        (SUM_B1, NearFar.scratch(512, depth)),
        (SUM_B2, NearFar.scratch(512, depth)),
        (SUM_B3, Split.scratch(2048, depth)),
    )


def forward_kernel(plan, depth, *refs):
    refs = list(refs)

    def take(count):
        taken = refs[:count]
        del refs[:count]
        return taken

    x_hbm, shift_hbm, slot_rows, live, norm_mid, norm_out = take(6)
    shards = take(7)
    outs = take(3)
    mask, inv_mid, inv_out, par_mid, par_out, over, weight_squares = take(7)
    weights_hbm = take(7)
    saved_hbm = dict(zip(SAVED, take(len(SAVED))))
    sums = {}
    for name, scratch in forward_names(depth):
        sums[name] = (NearFar if len(scratch) == 7 else Split)(take(len(scratch)), depth)
    x, shift = take(2)
    w_a1, w_a2, w_a3, w_as, w_b1, w_b2, w_b3 = weights = take(7)
    saved = dict(zip(SAVED, take(len(SAVED))))
    hid_a1, hid_mid, hid_out, hid_as, act = take(5)
    load_sem, save_sem, full_sem, norms_mid, norms_out, norm_send, norm_recv = take(7)
    gather = Gather(shards, weights, take(9), depth)

    loads = [
        pltpu.make_async_copy(src, dst, load_sem.at[i])
        for i, (src, dst) in enumerate(zip([x_hbm, shift_hbm], [x, shift]))
    ]
    gather.place_all()
    for copy in loads:
        copy.start()

    def keep(i):
        return pltpu.make_async_copy(weights[i], weights_hbm[i], full_sem.at[i])

    weight_squares[...] = jnp.zeros((8, 128), jnp.float32)

    def ready(i):
        gather.ready(i)
        keep(i).start()

    def add_square(i):
        at_row = lax.broadcasted_iota(jnp.int32, (8, 128), 0) == 0
        where = at_row & (lax.broadcasted_iota(jnp.int32, (8, 128), 1) == i)

        def body(lead, carry):
            block = weights[i][gather.z, gather.x, lead].astype(jnp.float32)
            total = jnp.sum(jnp.sum(block * block, axis=0, keepdims=True), axis=1, keepdims=True)
            weight_squares[...] += jnp.where(where, total, 0.0)
            return carry

        lax.fori_loop(0, weights[i].shape[2], body, 0)

    def pump():
        gather.pump()

    def save(name):
        pltpu.make_async_copy(saved[name], saved_hbm[name], save_sem.at[SAVED.index(name)]).start()

    greet(depth, crosswise=True)
    place = gather.z * 2 + gather.x
    norms_mid[place] = norm_mid[...]
    own_lanes = pl.ds(pl.multiple_of(place * norm_out.shape[1], 128), norm_out.shape[1])
    norms_out[:, own_lanes] = norm_out[...]

    def norm_copies(kind):
        here = norms_out.at[:, own_lanes] if kind else norms_mid.at[place]
        copies = []
        for i in range(1, 2 * depth):
            peer = (lax.rem(gather.z + i // 2, depth), 1 - gather.x if i % 2 else gather.x, gather.y, gather.core)
            copies.append(remote(here, here, norm_send.at[kind, i], norm_recv.at[kind, i], peer))
        return copies

    for copy in norm_copies(0) + norm_copies(1):
        copy.start()
    gather.begin()
    lanes = lax.broadcasted_iota(jnp.int32, (1, 128), 1)

    def live_of(g):
        return jnp.sum(jnp.where(lanes == g, live[...], 0.0), axis=1, keepdims=True)

    for g, span in enumerate(plan.spans()):
        mask[span, :] = jnp.where(slot_rows[span, :] < live_of(g), 1.0, 0.0)
    counts = jnp.zeros((1, 128), jnp.float32)
    for g, side in enumerate(plan.sides):
        counts = counts + jnp.where(lanes == g, live[...] * float(side * side), 0.0)

    loads[0].wait()
    ready(0)

    def conv_a1(p, carry):
        hid_a1[p] = dot_nt(x[p], w_a1[...].reshape(512, -1))
        return carry

    paced(0, 4, conv_a1, 2, pump)

    total = sums[SUM_A1]
    put_sums(
        plan, lambda j: [(hid_a1[p, :, columns(j)],) * 2 for p in range(4)], mask, total.pay, 0, 512
    )
    total.pay[6:7, 0:128] = counts
    total.begin()
    add_square(0)
    total.stages()[0]()
    total.stages()[1]()
    pump()
    for copy in norm_copies(0):
        copy.wait_recv()
    own_norms = norms_mid[0]
    for slot in range(1, 2 * depth):
        own_norms = own_norms + norms_mid[slot]
    par_mid[...] = own_norms

    pixels = total.total[6:7, 0:128]
    inverse_counts = [
        jnp.broadcast_to(1.0 / jnp.sum(jnp.where(lanes == g, pixels, 0.0), axis=1, keepdims=True), (1, 128))
        for g in range(3)
    ]
    over[...] = jnp.concatenate(inverse_counts + [jnp.zeros((5, 128), jnp.float32)], axis=0)
    put_scales(total.total, inv_mid.at[0], over, 512, 0.25)

    def normalized(hidden, total, inverse, hat, params, row, j, base=0):
        at, sums_at = columns(j), columns(base + j)
        xhat = by_group(plan, lambda g, span: (hidden[span] - total[g : g + 1, sums_at]) * inverse[g : g + 1, at])
        hat[:, at] = xhat.astype(jnp.bfloat16)
        return xhat * params[row : row + 1, at] + params[row + 1 : row + 2, at]

    def activate(hidden_of, total, inverse, hat, params, row, target):
        def body(j, carry):
            v = normalized(hidden_of(j), total, inverse, hat, params, row, j)
            target[:, columns(j)] = (v * sigmoid(v)).astype(jnp.bfloat16)
            return carry

        lax.fori_loop(0, 4, body, 0)

    def activate_a1(p, carry):
        activate(
            lambda j: hid_a1[p, :, columns(j)],
            total.total,
            inv_mid.at[0],
            saved[HAT_A1].at[p],
            par_mid,
            0,
            act.at[p],
        )
        return carry

    paced(0, 4, activate_a1, 2, pump)
    save(HAT_A1)

    loads[1].wait()
    patch = saved[PATCH_A]
    for tap in range(9):
        a, b = tap // 3, tap % 3
        plane = (0 if a == 1 else 2) + (0 if b == 1 else 1)
        matrix = (0 if a == 0 else 1) * 3 + (0 if b == 0 else 1)
        if matrix == 4:
            patch[tap] = act[plane]
        else:
            patch[tap] = dot(shift[matrix], act[plane]).astype(jnp.bfloat16)
        if tap == 4:
            pump()
    save(PATCH_A)
    ready(1)

    def spatial(patch, weight):
        hid_mid[...] = dot_nt(patch[0], weight[:, :, 0].reshape(512, 512))

        def body(tap, carry):
            hid_mid[...] += dot_nt(patch[tap], weight[:, :, tap].reshape(512, 512))
            return carry

        paced(1, 9, body, 2, pump)

    spatial(patch, w_a2)

    def conv_as(d, carry):
        at = pl.ds(pl.multiple_of(d * 256, 256), 256)
        hid_as[:, at] = dot(x[0], w_as[d // 2, lax.rem(d, 2)].reshape(1024, 256))
        return carry

    def shortcut():
        ready(3)
        paced(0, 8, conv_as, 2, pump)
        put_sums(plan, lambda j: [(hid_as[:, columns(j)],) * 2], mask, sums[SUM_J].pay, 16, 2048)

    def mid_sums(total, name_index, works):
        put_sums(plan, lambda j: [(hid_mid[:, columns(j)],) * 2], mask, total.pay, 0, 512)
        total.begin()
        interleave(total.stages(), works)
        put_scales(total.total, inv_mid.at[name_index], over, 512)

    mid_sums(sums[SUM_A2], 1, [lambda: add_square(1)])
    pump()
    activate(
        lambda j: hid_mid[:, columns(j)], sums[SUM_A2].total, inv_mid.at[1], saved[HAT_A2], par_mid, 2, saved[ACT_A2]
    )
    save(HAT_A2)
    save(ACT_A2)

    def expand(act_ref, weight):
        def body(d, carry):
            at = pl.ds(pl.multiple_of(d * 256, 256), 256)
            hid_out[:, at] = dot(act_ref[...], weight[d // 2, lax.rem(d, 2)].reshape(512, 256))
            return carry

        paced(0, 8, body, 2, pump)

    shortcut()
    pump()
    ready(2)
    expand(saved[ACT_A2], w_a3)
    total = sums[SUM_J]
    put_sums(plan, lambda j: [(hid_out[:, columns(j)],) * 2], mask, total.pay, 0, 2048)
    total.begin()
    interleave(total.stages(), [lambda: add_square(2), lambda: add_square(3)])
    pump()
    put_scales(total.total, inv_out.at[0], over, 2048)
    put_scales(total.total, inv_out.at[1], over, 2048, base=16)
    for copy in norm_copies(1):
        copy.wait_recv()
    par_out[...] = norms_out[...]

    def join(j, carry):
        at = columns(j)
        v = normalized(hid_out[:, at], total.total, inv_out.at[0], saved[HAT_A3], par_out, 0, j)
        v = v + normalized(hid_as[:, at], total.total, inv_out.at[1], saved[HAT_AS], par_out, 2, j, 16)
        saved[OUT_A][:, at] = (v * sigmoid(v) * mask[...]).astype(jnp.bfloat16)
        return carry

    paced(0, 16, join, 3, pump)
    for name in (HAT_A3, HAT_AS, OUT_A):
        save(name)

    ready(4)
    hid_mid[...] = dot_nt(saved[OUT_A][...], w_b1[...].reshape(512, -1))
    mid_sums(sums[SUM_B1], 2, [lambda: add_square(4)])
    pump()
    activate(
        lambda j: hid_mid[:, columns(j)], sums[SUM_B1].total, inv_mid.at[2], saved[HAT_B1], par_mid, 4, act.at[0]
    )
    save(HAT_B1)

    def patches(tap, carry):
        saved[PATCH_B][tap] = dot(shift[tap], act[0]).astype(jnp.bfloat16)
        return carry

    paced(0, 9, patches, 2, pump)
    save(PATCH_B)
    ready(5)
    spatial(saved[PATCH_B], w_b2)
    mid_sums(sums[SUM_B2], 3, [lambda: add_square(5)])
    pump()
    activate(
        lambda j: hid_mid[:, columns(j)], sums[SUM_B2].total, inv_mid.at[3], saved[HAT_B2], par_mid, 6, saved[ACT_B2]
    )
    save(HAT_B2)
    save(ACT_B2)
    ready(6)
    expand(saved[ACT_B2], w_b3)
    total_b = sums[SUM_B3]
    put_sums(plan, lambda j: [(hid_out[:, columns(j)],) * 2], mask, total_b.pay, 0, 2048)
    total_b.begin()
    interleave(total_b.stages(), [lambda: add_square(6)])
    put_scales(total_b.total, inv_out.at[2], over, 2048)

    def finish(j, carry):
        at = columns(j)
        v = normalized(hid_out[:, at], total_b.total, inv_out.at[2], saved[HAT_B3], par_out, 4, j)
        v = v + saved[OUT_A][:, at].astype(jnp.float32)
        v = v * sigmoid(v) * mask[...]
        for g, target in enumerate(outs):
            start = plan.starts[g]
            target[:, at] = v[start : start + plan.valid[g]].astype(jnp.bfloat16)
        return carry

    lax.fori_loop(0, 16, finish, 0)
    save(HAT_B3)
    for total in sums.values():
        total.close()
    for i, name in enumerate(SAVED):
        pltpu.make_async_copy(saved[name], saved_hbm[name], save_sem.at[i]).wait()
    gather.close()
    for copy in norm_copies(0) + norm_copies(1):
        copy.wait_send()
    for i in range(7):
        keep(i).wait()


def saved_shapes(rows):
    bf16 = jnp.bfloat16
    return (
        ((4, rows, 512), bf16),
        ((rows, 512), bf16),
        ((rows, 2048), bf16),
        ((rows, 2048), bf16),
        ((rows, 512), bf16),
        ((rows, 512), bf16),
        ((rows, 2048), bf16),
        ((9, rows, 512), bf16),
        ((9, rows, 512), bf16),
        ((rows, 512), bf16),
        ((rows, 512), bf16),
        ((rows, 2048), bf16),
    )


WHOLE = pl.BlockSpec(memory_space=pltpu.VMEM)
VMEM_LIMIT = 62 * 1024 * 1024


def run_forward(plan, depth, x, shifts, slot_rows, live, norm_mid, norm_out, shards):
    rows, f32, bf16 = plan.rows, jnp.float32, jnp.bfloat16
    dma = pltpu.SemaphoreType.DMA
    scratch = []
    for _, pieces in forward_names(depth):
        scratch += pieces
    scratch += [pltpu.VMEM(x.shape, bf16), pltpu.VMEM(shifts.shape, bf16)]
    fulls = [jax.ShapeDtypeStruct((depth, 2, *shard.shape), bf16) for shard in shards]
    scratch += [pltpu.VMEM(full.shape, bf16) for full in fulls]
    scratch += [pltpu.VMEM(shape, kind) for shape, kind in saved_shapes(rows)]
    scratch += [
        pltpu.VMEM((4, rows, 512), f32),
        pltpu.VMEM((rows, 512), f32),
        pltpu.VMEM((rows, 2048), f32),
        pltpu.VMEM((rows, 2048), f32),
        pltpu.VMEM((4, rows, 512), bf16),
        dma((2,)),
        dma((len(SAVED),)),
        dma((7,)),
        pltpu.VMEM((2 * depth, 8, 512), f32),
        pltpu.VMEM((8, 2048), f32),
        dma((2, 2 * depth)),
        dma((2, 2 * depth)),
    ]
    scratch += Gather.scratch(depth)
    small = [jax.ShapeDtypeStruct((valid, 2048), bf16) for valid in plan.valid]
    small += [
        jax.ShapeDtypeStruct((rows, 128), f32),
        jax.ShapeDtypeStruct((4, 8, 512), f32),
        jax.ShapeDtypeStruct((3, 8, 2048), f32),
        jax.ShapeDtypeStruct((8, 512), f32),
        jax.ShapeDtypeStruct((8, 2048), f32),
        jax.ShapeDtypeStruct((8, 128), f32),
        jax.ShapeDtypeStruct((8, 128), f32),
    ]
    return pl.pallas_call(
        functools.partial(forward_kernel, plan, depth),
        out_shape=small + fulls + [jax.ShapeDtypeStruct(shape, kind) for shape, kind in saved_shapes(rows)],
        in_specs=[ANY, ANY] + [WHOLE] * 4 + [ANY] * 7,
        out_specs=[WHOLE] * 10 + [ANY] * 7 + [ANY] * len(SAVED),
        scratch_shapes=scratch,
        compiler_params=pltpu.CompilerParams(collective_id=0, has_side_effects=True, vmem_limit_bytes=VMEM_LIMIT),
    )(x, shifts, slot_rows, live, norm_mid, norm_out, *shards)


def backward_names(depth):
    return (
        (SUM_B3, Split.scratch(2048, depth)),
        (SUM_B2, NearFar.scratch(512, depth)),
        (SUM_B1, NearFar.scratch(512, depth)),
        (SUM_J, Split.scratch(4096, depth)),
        (SUM_A2, NearFar.scratch(512, depth)),
        (SUM_A1, NearFar.scratch(512, depth)),
    )


def backward_kernel(plan, depth, *refs):
    refs = list(refs)

    def take(count):
        taken = refs[:count]
        del refs[:count]
        return taken

    x_hbm, shift_hbm, cot_hbm, mask, weight_squares, inv_mid, inv_out, par_mid, par_out, over = take(10)
    saved_hbm = dict(zip(SAVED, take(len(SAVED))))
    weights_hbm = take(7)
    dx_hbm, pgrad_mid, pgrad_b3, pgrad_j, squares_out = take(5)
    gradients_hbm, c_hbm, y_hbm = take(7), take(7), take(7)
    sums = {}
    for name, scratch in backward_names(depth):
        sums[name] = (NearFar if len(scratch) == 7 else Split)(take(len(scratch)), depth)
    x, shift, cot = take(3)
    w_a1, w_a2, w_a3, w_as, w_b1, w_b2, w_b3 = weights = take(7)
    kept = [name for name in SAVED if name != PATCH_B]
    saved = dict(zip(kept, take(len(kept))))
    saved[PATCH_B] = saved[PATCH_A]
    dz, dact, dh_mid, flip = take(4)
    load_sem, saved_sem, dx_sem = take(3)
    dh_a, dh_b = cot, saved[HAT_B3]
    planes = [saved[HAT_AS].at[:, pl.ds(plane * 512, 512)] for plane in range(4)]
    reduce = Reduce(weights, gradients_hbm, c_hbm, y_hbm, refs, depth)
    reduce.squares[2 * depth + 2] = jnp.zeros((8, 128), jnp.float32)

    def pump():
        reduce.pump()

    def loading(name):
        return pltpu.make_async_copy(saved_hbm[name], saved[name], saved_sem.at[SAVED.index(name)])

    loads = [
        pltpu.make_async_copy(src, dst, load_sem.at[i])
        for i, (src, dst) in enumerate(zip([x_hbm, shift_hbm, cot_hbm, *weights_hbm], [x, shift, cot, *weights]))
    ]
    first = (HAT_B3, OUT_A)
    for name in first:
        loading(name).start()
    loads[2].start()
    order = (HAT_B2, ACT_B2, HAT_B1, PATCH_B, HAT_A3, HAT_AS, HAT_A2, ACT_A2, HAT_A1)
    loads[9].start()
    for name in order[:4]:
        loading(name).start()
    for i in (1, 8, 7):
        loads[i].start()
    for name in order[4:]:
        loading(name).start()
    for i in (5, 6, 4, 0, 3):
        loads[i].start()

    greet(depth)

    def quarter(d):
        return pl.ds(pl.multiple_of(d * 256, 256), 256)

    def affine(hat, params, row, at):
        return hat[:, at].astype(jnp.float32) * params[row : row + 1, at] + params[row + 1 : row + 2, at]

    def norm_back(dz_of, hat, total, base, inverse, params, row, target, blocks):
        def body(j, carry):
            at = columns(j)
            sums_at = columns(base + j)
            gain = params[row : row + 1, at]
            value, xhat = dz_of(j), hat[:, at].astype(jnp.float32)

            def of(g, span):
                first = total[g : g + 1, sums_at] * over_of(g)
                second = total[3 + g : 4 + g, sums_at] * over_of(g)
                return (gain * inverse[g : g + 1, at]) * (value[span] - first - xhat[span] * second)

            target[:, at] = (by_group(plan, of) * mask[...]).astype(jnp.bfloat16)
            return carry

        paced(0, blocks, body, 1 if blocks == 4 else 2, pump)

    scale = [1.0]

    def over_of(g):
        return over[g : g + 1, :] * scale[0]

    for name in first:
        loading(name).wait()
    loads[2].wait()

    def out_pairs(j):
        at = columns(j)
        v = affine(saved[HAT_B3], par_out, 4, at) + saved[OUT_A][:, at].astype(jnp.float32)
        value = cot[:, at].astype(jnp.float32) * mask[...] * slope(v)
        dz[:, at] = value
        return [(value, saved[HAT_B3][:, at].astype(jnp.float32))]

    total = sums[SUM_B3]
    put_sums(plan, out_pairs, mask, total.pay, 0, 2048)
    total.begin()
    for i in (9, 1, 8, 7):
        loads[i].wait()
    for name in order[:4]:
        loading(name).wait()
    flip[0:512] = saved[ACT_B2][...].T
    interleave(total.stages(), [])
    pgrad_b3[...] = total.total[...]
    norm_back(lambda j: dz[:, columns(j)], saved[HAT_B3], total.total, 0, inv_out.at[2], par_out, 4, dh_a, 16)

    def contract(dh, weight):
        dact[...] = dot_nt(dh[:, 0:256], weight[0, 0].reshape(512, 256))

        def body(d, carry):
            dact[...] += dot_nt(dh[:, quarter(d)], weight[d // 2, lax.rem(d, 2)].reshape(512, 256))
            return carry

        lax.fori_loop(1, 8, body, 0)

    def expand_term(lhs, dh, weight, first_slot, last_slot):
        def body(d, carry):
            shape = weight.shape[2:]
            weight[d // 2, lax.rem(d, 2)] = dot(lhs, dh[:, quarter(d)]).astype(jnp.bfloat16).reshape(shape)
            return carry

        lax.fori_loop(first_slot, last_slot, body, 0)

    def mid_pairs(hat, row):
        def pairs(j):
            at = columns(j)
            value = dact[:, at] * slope(affine(saved[hat], par_mid, row, at))
            dact[:, at] = value
            return [(value, saved[hat][:, at].astype(jnp.float32))]

        return pairs

    def mid_norm(name, hat, index, row, works):
        total = sums[name]
        put_sums(plan, mid_pairs(hat, row), mask, total.pay, 0, 512)
        total.begin()
        interleave(total.stages(), works)
        pgrad_mid[index] = total.total[...]
        norm_back(lambda j: dact[:, columns(j)], saved[hat], total.total, 0, inv_mid.at[index], par_mid, row, dh_mid, 4)

    contract(dh_a, w_b3)
    expand_term(flip[0:512, :], dh_a, w_b3, 0, 8)
    reduce.enable(6)
    pump()
    mid_norm(SUM_B2, HAT_B2, 3, 6, [])
    pump()

    def spread(tap, carry):
        part = dot(
            dot(shift[8 - tap], dh_mid[...]).astype(jnp.bfloat16), w_b2[:, :, tap].reshape(512, 512)
        )
        dact[...] = part + jnp.where(tap == 0, 0.0, dact[...])
        return carry

    paced(0, 9, spread, 2, pump)
    flip[0:512] = dh_mid[...].T

    def spatial_term(weight, patch, first_tap, last_tap, tensor):
        def work():
            def body(tap, carry):
                weight[:, :, tap] = dot(flip[0:512, :], patch[tap]).astype(jnp.bfloat16).reshape(depth, 2, 64, 512)
                return carry

            lax.fori_loop(first_tap, last_tap, body, 0)
            reduce.enable(tensor, last_tap)

        return work

    mid_norm(
        SUM_B1,
        HAT_B1,
        2,
        4,
        [spatial_term(w_b2, saved[PATCH_B], 0, 3, 5), spatial_term(w_b2, saved[PATCH_B], 3, 6, 5)],
    )
    pump()
    spatial_term(w_b2, saved[PATCH_B], 6, 9, 5)()
    pump()
    loading(PATCH_A).start()

    def residual(d, carry):
        at = quarter(d)
        dz[:, at] = dz[:, at] + dot(dh_mid[...], w_b1[:, :, 0, :, at].reshape(512, 256))
        return carry

    paced(0, 8, residual, 2, pump)
    for name in order[4:]:
        loading(name).wait()

    def join_pairs(j):
        at = columns(j)
        v = affine(saved[HAT_A3], par_out, 0, at) + affine(saved[HAT_AS], par_out, 2, at)
        value = dz[:, at] * mask[...] * slope(v)
        dz[:, at] = value
        return [(value, saved[HAT_A3][:, at].astype(jnp.float32))]

    total = sums[SUM_J]
    put_sums(plan, join_pairs, mask, total.pay, 0, 2048, pump)
    put_sums(
        plan, lambda j: [(dz[:, columns(j)], saved[HAT_AS][:, columns(j)].astype(jnp.float32))], mask, total.pay, 16, 2048
    )
    total.begin()
    flip[0:512] = dh_mid[...].T

    def first_term(part):
        def work():
            def body(d, carry):
                at = quarter(d)
                value = dot(flip[0:512, :], saved[OUT_A][:, at]).astype(jnp.bfloat16)
                w_b1[:, :, 0, :, at] = value.reshape(depth, 2, 64, 256)
                return carry

            lax.fori_loop(2 * part, 2 * part + 2, body, 0)
            if part == 3:
                reduce.enable(4)

        return work

    interleave(total.stages(), [first_term(part) for part in range(4)])
    pgrad_j[...] = total.total[...]
    norm_back(lambda j: dz[:, columns(j)], saved[HAT_A3], total.total, 0, inv_out.at[0], par_out, 0, dh_a, 16)
    pump()
    norm_back(lambda j: dz[:, columns(j)], saved[HAT_AS], total.total, 16, inv_out.at[1], par_out, 2, dh_b, 16)
    for i in (5, 6, 4, 0, 3):
        loads[i].wait()

    pump()
    contract(dh_a, w_a3)
    pump()
    flip[0:512] = saved[ACT_A2][...].T

    def third_term_a():
        expand_term(flip[0:512, :], dh_a, w_a3, 0, 8)
        reduce.enable(2)

    def shortcut():
        even = dz.at[:, 0:1024]
        even[...] = dot_nt(dh_b[:, 0:256], w_as[0, 0].reshape(1024, 256))

        def body(d, carry):
            even[...] += dot_nt(dh_b[:, quarter(d)], w_as[d // 2, lax.rem(d, 2)].reshape(1024, 256))
            return carry

        lax.fori_loop(1, 8, body, 0)

        def keep(j, carry):
            value = even[:, columns(j)]
            high = value.astype(jnp.bfloat16)
            saved[OUT_A][:, columns(j)] = high
            saved[OUT_A][:, columns(8 + j)] = (value - high.astype(jnp.float32)).astype(jnp.bfloat16)
            return carry

        lax.fori_loop(0, 8, keep, 0)

    mid_norm(SUM_A2, HAT_A2, 1, 2, [third_term_a, shortcut])

    loading(PATCH_A).wait()
    flip[...] = x[0].T
    for part in range(4):
        expand_term(flip[...], dh_b, w_as, 2 * part, 2 * part + 2)
        pump()
    reduce.enable(3)
    for plane in range(4):
        at = slice(plane * 512, plane * 512 + 512)
        begun = False
        if plane == 2:
            pump()
        for tap in range(9):
            a, b = tap // 3, tap % 3
            if plane != (0 if a == 1 else 2) + (0 if b == 1 else 1):
                continue
            matrix = (2 if a == 0 else 1) * 3 + (2 if b == 0 else 1)
            moved = dh_mid[...] if matrix == 4 else dot(shift[matrix], dh_mid[...]).astype(jnp.bfloat16)
            part = dot(moved, w_a2[:, :, tap].reshape(512, 512))
            if begun:
                dz[:, at] += part
            else:
                dz[:, at] = part
            begun = True
    pump()

    def plane_pairs(j):
        at = columns(j)
        pairs = []
        for plane in range(4):
            wide = columns(4 * plane + j)
            xhat = saved[HAT_A1][plane, :, at].astype(jnp.float32)
            v = xhat * par_mid[0:1, at] + par_mid[1:2, at]
            value = dz[:, wide] * slope(v)
            dz[:, wide] = value
            pairs.append((value, xhat))
        return pairs

    total = sums[SUM_A1]
    put_sums(plan, plane_pairs, mask, total.pay, 0, 512)
    total.begin()
    flip[0:512] = dh_mid[...].T
    stages = total.stages()
    spatial_term(w_a2, saved[PATCH_A], 0, 3, 1)()
    stages[0]()
    spatial_term(w_a2, saved[PATCH_A], 3, 6, 1)()
    stages[1]()
    pump()
    spatial_term(w_a2, saved[PATCH_A], 6, 9, 1)()
    pump()
    pgrad_mid[0] = total.total[...]
    scale[0] = 0.25
    for plane in range(4):
        norm_back(
            lambda j, plane=plane: dz[:, columns(4 * plane + j)],
            saved[HAT_A1].at[plane],
            total.total,
            0,
            inv_mid.at[0],
            par_mid,
            0,
            planes[plane],
            4,
        )

    def input_gradient(p):
        target = (dh_a if p < 2 else dh_b).at[:, pl.ds((p % 2) * 1024, 1024)]
        value = dot(planes[p][...], w_a1[...].reshape(512, -1))
        if p == 0:
            value = value + saved[OUT_A][:, 0:1024].astype(jnp.float32)
            value = value + saved[OUT_A][:, 1024:2048].astype(jnp.float32)
        target[...] = value.astype(jnp.bfloat16)
        copy = pltpu.make_async_copy(target, dx_hbm.at[p], dx_sem.at[p])
        copy.start()
        return copy

    copies = []
    for p in range(4):
        copies.append(input_gradient(p))
        pump()

    def last_term(c, carry):
        at = quarter(c)
        total = jnp.zeros((512, 256), jnp.float32)
        for p in range(4):
            total = total + lax.dot_general(
                planes[p][...], x[p, :, at], (((0,), (0,)), ((), ())), preferred_element_type=jnp.float32
            )
        w_a1[:, :, 0, :, at] = total.astype(jnp.bfloat16).reshape(depth, 2, 64, 256)
        return carry

    paced(0, 4, last_term, 2, pump)
    reduce.enable(0)
    reduce.finish(weight_squares, squares_out)
    for copy in copies:
        copy.wait()
    for total in sums.values():
        total.close()


def run_backward(plan, depth, x, shifts, cot, mask, weight_squares, small, saved, fulls):
    rows, f32, bf16 = plan.rows, jnp.float32, jnp.bfloat16
    dma = pltpu.SemaphoreType.DMA
    scratch = []
    for _, pieces in backward_names(depth):
        scratch += pieces
    scratch += [pltpu.VMEM(value.shape, bf16) for value in (x, shifts, cot)]
    scratch += [pltpu.VMEM(full.shape, bf16) for full in fulls]
    scratch += [pltpu.VMEM(shape, kind) for name, (shape, kind) in zip(SAVED, saved_shapes(rows)) if name != PATCH_B]
    scratch += [
        pltpu.VMEM((rows, 2048), f32),
        pltpu.VMEM((rows, 512), f32),
        pltpu.VMEM((rows, 512), bf16),
        pltpu.VMEM((1024, rows), bf16),
        dma((10,)),
        dma((len(SAVED),)),
        dma((4,)),
    ]
    shapes = [full.shape for full in fulls]
    scratch += Reduce.scratch(shapes, depth)

    def part(shape, over):
        return jax.ShapeDtypeStruct((*shape[:3], shape[3] // over, shape[4]), bf16)

    outs = pl.pallas_call(
        functools.partial(backward_kernel, plan, depth),
        out_shape=[
            jax.ShapeDtypeStruct(x.shape, bf16),
            jax.ShapeDtypeStruct((4, 8, 512), f32),
            jax.ShapeDtypeStruct((8, 2048), f32),
            jax.ShapeDtypeStruct((8, 4096), f32),
            jax.ShapeDtypeStruct((8, 128), f32),
        ]
        + [jax.ShapeDtypeStruct(shape[2:], bf16) for shape in shapes]
        + [part(shape, 2) for shape in shapes]
        + [part(shape, 4) for shape in shapes],
        in_specs=[ANY] * 3 + [WHOLE] * 7 + [ANY] * len(SAVED) + [ANY] * 7,
        out_specs=[ANY] + [WHOLE] * 4 + [ANY] * 21,
        scratch_shapes=scratch,
        compiler_params=pltpu.CompilerParams(collective_id=1, has_side_effects=True, vmem_limit_bytes=VMEM_LIMIT),
    )(x, shifts, cot, mask, weight_squares, *small, *saved, *fulls)
    return outs[:12]


def scale_kernel(depth, squares, sums_mid, sums_b3, sums_j, *refs):
    refs = list(refs)

    def take(count):
        taken = refs[:count]
        del refs[:count]
        return taken

    totals, weights, outs, norm_outs = take(7), take(7), take(14), take(7)
    squares_out, totals_in, weights_in, staged = take(1)[0], take(7), take(7), take(14)
    in_sem, out_sem = refs

    def loads(i):
        return (
            pltpu.make_async_copy(totals[i], totals_in[i], in_sem.at[0, i]),
            pltpu.make_async_copy(weights[i], weights_in[i], in_sem.at[1, i]),
        )

    def stores(i):
        return [pltpu.make_async_copy(staged[2 * i + n], outs[2 * i + n], out_sem.at[n, i]) for n in (0, 1)]

    for i in range(7):
        for copy in loads(i):
            copy.start()

    squares_out[...] = squares[0:2, 0:7]
    place = lax.axis_index(DP)

    def both(sums):
        seconds = sums[3:4] + sums[4:5] + sums[5:6]
        return jnp.concatenate([seconds, sums[0:1] + sums[1:2] + sums[2:3]], axis=0)

    def put(target, sums, base):
        width = target.shape[1]
        span = max(width, 128)
        start = (place * width) // span * span + base
        block = both(sums[:, pl.ds(pl.multiple_of(start, 128), span)])
        for piece in range(span // width):
            part = block[:, piece * width : (piece + 1) * width]

            @pl.when(lax.rem(place, span // width) == piece)
            def _(part=part):
                target[...] = part

    for i, (sums, base) in enumerate(
        (
            (sums_mid.at[0], 0),
            (sums_mid.at[1], 0),
            (sums_j, 0),
            (sums_j, sums_j.shape[1] // 2),
            (sums_mid.at[2], 0),
            (sums_mid.at[3], 0),
            (sums_b3, 0),
        )
    ):
        put(norm_outs[i], sums, base)

    weight_norm = jnp.sqrt(squares[0:1, :])
    trust = weight_norm / (jnp.sqrt(squares[1:2, :]) + DECAY_RATE * weight_norm)
    for i in range(7):
        for copy in loads(i):
            copy.wait()
        ratio = trust[0:1, i : i + 1]

        def body(lead, carry, i=i, ratio=ratio):
            gradient = totals_in[i][lead].astype(jnp.float32)
            staged[2 * i][lead] = gradient
            decayed = gradient + DECAY_RATE * weights_in[i][lead].astype(jnp.float32)
            staged[2 * i + 1][lead] = ratio * decayed
            return carry

        lax.fori_loop(0, totals_in[i].shape[0], body, 0)
        for copy in stores(i):
            copy.start()
    for i in range(7):
        for copy in stores(i):
            copy.wait()


def run_scale(depth, squares, sums, totals, shards, widths):
    f32, bf16, dma = jnp.float32, jnp.bfloat16, pltpu.SemaphoreType.DMA
    shapes = [total.shape for total in totals]
    outs = pl.pallas_call(
        functools.partial(scale_kernel, depth),
        out_shape=[jax.ShapeDtypeStruct(shape, f32) for shape in shapes for _ in (0, 1)]
        + [jax.ShapeDtypeStruct((2, width), f32) for width in widths]
        + [jax.ShapeDtypeStruct((2, 7), f32)],
        in_specs=[WHOLE] * 4 + [ANY] * 14,
        out_specs=[ANY] * 14 + [WHOLE] * 8,
        scratch_shapes=[pltpu.VMEM(shape, bf16) for shape in shapes * 2]
        + [pltpu.VMEM(shape, f32) for shape in shapes for _ in (0, 1)]
        + [dma((2, 7)), dma((2, 7))],
        compiler_params=pltpu.CompilerParams(vmem_limit_bytes=VMEM_LIMIT),
    )(squares, *sums, *totals, *shards)
    return outs[0:14:2], outs[1:14:2], outs[14:21], outs[21]


def on_device(
    input_160,
    input_224,
    input_288,
    cotangent_160,
    cotangent_224,
    cotangent_288,
    live_counts,
    conv_a1,
    norm_a1,
    conv_a2,
    norm_a2,
    conv_a3,
    norm_a3,
    conv_as,
    norm_as,
    conv_b1,
    norm_b1,
    conv_b2,
    norm_b2,
    conv_b3,
    norm_b3,
):
    if conv_a1.shape[1] % 64 or conv_a3.shape[1] % 128 or lax.axis_size(REP) != 4:
        return plain_on_device(
            input_160,
            input_224,
            input_288,
            cotangent_160,
            cotangent_224,
            cotangent_288,
            live_counts,
            conv_a1,
            norm_a1,
            conv_a2,
            norm_a2,
            conv_a3,
            norm_a3,
            conv_as,
            norm_as,
            conv_b1,
            norm_b1,
            conv_b2,
            norm_b2,
            conv_b3,
            norm_b3,
        )
    depth = lax.axis_size(DP) // 2
    inputs = (input_160, input_224, input_288)
    plan = Plan([value.shape for value in inputs])
    shards = (
        conv_a1.T[None],
        jnp.transpose(conv_a2, (0, 1, 3, 2)).reshape(9, conv_a2.shape[3], conv_a2.shape[2]),
        conv_a3.reshape(2, -1, conv_a3.shape[1]),
        conv_as.reshape(4, -1, conv_as.shape[1]),
        conv_b1.T[None],
        jnp.transpose(conv_b2, (0, 1, 3, 2)).reshape(9, conv_b2.shape[3], conv_b2.shape[2]),
        conv_b3.reshape(2, -1, conv_b3.shape[1]),
    )

    planes, cotangents = [], []
    for g, (value, cotangent) in enumerate(
        zip(inputs, (cotangent_160, cotangent_224, cotangent_288))
    ):
        side, slots, fill = plan.sides[g], plan.slots[g], plan.sizes[g] - plan.valid[g]
        split = jnp.transpose(value, (1, 2, 0, 3)).reshape(side, 2, side, 2, slots, -1)
        split = jnp.transpose(split, (1, 3, 0, 2, 4, 5)).reshape(4, plan.valid[g], -1)
        planes.append(jnp.pad(split, ((0, 0), (0, fill), (0, 0))))
        cotangents.append(
            jnp.pad(jnp.transpose(cotangent, (1, 2, 0, 3)).reshape(plan.valid[g], -1), ((0, fill), (0, 0)))
        )
    x = jnp.concatenate(planes, axis=1)
    cot = jnp.concatenate(cotangents, axis=0)
    live = jnp.pad(live_counts.astype(jnp.float32), ((0, 0), (0, 128 - live_counts.shape[1])))

    def stacked(norms):
        rows = jnp.concatenate(norms, axis=0).astype(jnp.float32)
        return jnp.pad(rows, ((0, 8 - rows.shape[0]), (0, 0)))

    mid_local = norm_a1.shape[1]
    mid_width = mid_local * 2 * depth
    norm_mid = lax.dynamic_update_slice(
        jnp.zeros((8, mid_width), jnp.float32),
        stacked((norm_a1, norm_a2, norm_b1, norm_b2)),
        (0, lax.axis_index(DP) * mid_local),
    )
    norm_out = stacked((norm_a3, norm_as, norm_b3))
    shifts = jnp.asarray(plan.shifts())

    results = run_forward(
        plan, depth, x, shifts, jnp.asarray(plan.slot_rows()), live, norm_mid, norm_out, shards
    )
    outs, mask, small, square_row = results[:3], results[3], results[4:9], results[9]
    fulls, saved = results[10:17], results[17:]
    dx, pgrad_mid, pgrad_b3, pgrad_j, squares, *totals = run_backward(
        plan, depth, x, shifts, cot, mask, square_row, small, saved, fulls
    )

    def placed(values):
        return [
            values[0][0].T,
            jnp.transpose(values[1], (0, 2, 1)).reshape(conv_a2.shape),
            values[2].reshape(conv_a3.shape),
            values[3].reshape(conv_as.shape),
            values[4][0].T,
            jnp.transpose(values[5], (0, 2, 1)).reshape(conv_b2.shape),
            values[6].reshape(conv_b3.shape),
        ]

    widths = [norm.shape[1] for norm in (norm_a1, norm_a2, norm_a3, norm_as, norm_b1, norm_b2, norm_b3)]
    gradients, scaled, norm_gradients, squares = run_scale(
        depth, squares, (pgrad_mid, pgrad_b3, pgrad_j), totals, shards, widths
    )
    gradients, scaled = placed(gradients), placed(scaled)

    outputs, grad_inputs = [], []
    for g in range(3):
        side, slots, start = plan.sides[g], plan.slots[g], plan.starts[g]
        rows = outs[g].reshape(side, side, slots, -1)
        outputs.append(jnp.transpose(rows, (2, 0, 1, 3)))
        split = dx[:, start : start + plan.valid[g]].reshape(2, 2, side, side, slots, -1)
        split = jnp.transpose(split, (2, 0, 3, 1, 4, 5)).reshape(2 * side, 2 * side, slots, -1)
        grad_inputs.append(jnp.transpose(split, (2, 0, 1, 3)))
    pairs = [piece for pair in zip(gradients, norm_gradients) for piece in pair]
    return (*outputs, *grad_inputs, *pairs, *scaled, squares)


def solution(mesh):
    by_image, by_column = P((DP, REP), None, None, None), P(None, DP)
    by_channel = P(None, None, None, DP)
    weights = [by_column, by_column, by_channel] + [by_column] * 7 + [by_channel] + [by_column] * 3
    kernels = [by_column, by_channel] + [by_column] * 3 + [by_channel, by_column]
    return jax.shard_map(
        on_device,
        mesh=mesh,
        in_specs=(*[by_image] * 6, P((DP, REP), None), *weights),
        out_specs=(*[by_image] * 6, *weights, *kernels, P()),
        check_vma=False,
    )
```

```python
import functools

import jax
import jax.numpy as jnp
import numpy as np
from jax import lax
from jax.experimental import pallas as pl
from jax.experimental.pallas import tpu as pltpu
from jax.sharding import PartitionSpec as P

DP, REP = "dp", "rep"
EPSILON = 1e-05
DECAY_RATE = 5e-05


def silu_slope(values):
    sigmoid = jax.nn.sigmoid(values)
    return sigmoid * (1.0 + values * (1.0 - sigmoid))


def pointwise(inputs, weight):
    return jnp.tensordot(inputs, weight, 1, preferred_element_type=jnp.float32)


def pointwise_back(upstream, weight):
    return jnp.tensordot(upstream, weight, ((3,), (1,)), preferred_element_type=jnp.float32)


def weight_term(inputs, upstream):
    return jnp.tensordot(inputs, upstream, ((0, 1, 2),) * 2, preferred_element_type=jnp.float32)


def summed_terms(inputs, upstream):
    running = weight_term(inputs[0], upstream[0])
    for group_member in (1, 2):
        running = running + weight_term(inputs[group_member], upstream[group_member])
    return running


def patches(inputs, stride):
    padded = jnp.pad(inputs, ((0, 0), (1, 1), (1, 1), (0, 0)))
    extent = inputs.shape[1]
    pieces = []
    for offset_row in range(3):
        for offset_col in range(3):
            pieces.append(
                padded[
                    :,
                    offset_row : offset_row + extent : stride,
                    offset_col : offset_col + extent : stride,
                    :,
                ]
            )
    return jnp.concatenate(pieces, axis=3)


def fold_patches(upstream, stride, side_in):
    channels = upstream.shape[3] // 9
    padded = jnp.zeros((upstream.shape[0], side_in + 2, side_in + 2, channels), jnp.float32)
    for offset_row in range(3):
        for offset_col in range(3):
            start_at = (offset_row * 3 + offset_col) * channels
            padded = padded.at[
                :,
                offset_row : offset_row + side_in : stride,
                offset_col : offset_col + side_in : stride,
                :,
            ].add(upstream[..., start_at : start_at + channels])
    return padded[:, 1 : side_in + 1, 1 : side_in + 1, :]


def batch_norm(values, live_masks, norm_param, totals):
    gain_row = norm_param[0].astype(jnp.float32)
    shift_row = norm_param[1].astype(jnp.float32)
    firsts = []
    seconds = []
    for group_member in range(3):
        weighted = values[group_member] * live_masks[group_member]
        firsts.append(jnp.sum(weighted, axis=(0, 1, 2)))
        seconds.append(jnp.sum(weighted * values[group_member], axis=(0, 1, 2)))
    summed = lax.psum(
        (firsts[0], seconds[0], firsts[1], seconds[1], firsts[2], seconds[2]), (DP, REP)
    )
    normed = []
    means = []
    scales = []
    for group_member in range(3):
        pixel_count = (
            totals[group_member] * values[group_member].shape[1] * values[group_member].shape[2]
        )
        mean_value = summed[2 * group_member] / pixel_count
        inv_std = lax.rsqrt(
            summed[2 * group_member + 1] / pixel_count - mean_value * mean_value + EPSILON
        )
        normed.append((values[group_member] - mean_value) * inv_std * gain_row + shift_row)
        means.append(mean_value)
        scales.append(inv_std)
    return (normed, means, scales)


def norm_back(upstream, values, live_masks, norm_param, means, scales, totals):
    gain_row = norm_param[0].astype(jnp.float32)
    normals = []
    firsts = []
    seconds = []
    for group_member in range(3):
        normal = (values[group_member] - means[group_member]) * scales[group_member]
        weighted = upstream[group_member] * live_masks[group_member]
        normals.append(normal)
        firsts.append(jnp.sum(weighted, axis=(0, 1, 2)))
        seconds.append(jnp.sum(weighted * normal, axis=(0, 1, 2)))
    summed = lax.psum(
        (firsts[0], seconds[0], firsts[1], seconds[1], firsts[2], seconds[2]), (DP, REP)
    )
    results = []
    for group_member in range(3):
        pixel_count = (
            totals[group_member] * values[group_member].shape[1] * values[group_member].shape[2]
        )
        centered = (
            upstream[group_member]
            - summed[2 * group_member] / pixel_count
            - normals[group_member] * (summed[2 * group_member + 1] / pixel_count)
        )
        results.append(
            (live_masks[group_member] * gain_row * scales[group_member] * centered).astype(
                jnp.bfloat16
            )
        )
    param_grad = jnp.stack([summed[1] + summed[3] + summed[5], summed[0] + summed[2] + summed[4]])
    return (results, param_grad)


def own_columns(full, local_width):
    return lax.dynamic_slice_in_dim(full, lax.axis_index(DP) * local_width, local_width, 1)


def plain_on_device(
    input_160,
    input_224,
    input_288,
    cotangent_160,
    cotangent_224,
    cotangent_288,
    live_counts,
    conv_a1,
    norm_a1,
    conv_a2,
    norm_a2,
    conv_a3,
    norm_a3,
    conv_as,
    norm_as,
    conv_b1,
    norm_b1,
    conv_b2,
    norm_b2,
    conv_b3,
    norm_b3,
):
    inputs = (input_160, input_224, input_288)
    cotangents = (cotangent_160, cotangent_224, cotangent_288)
    live_masks = []
    masked = []
    for group_member in range(3):
        group_slot_count = inputs[group_member].shape[0]
        live_flags = (
            (jnp.arange(group_slot_count) < live_counts[0, group_member])
            .astype(jnp.float32)
            .reshape(group_slot_count, 1, 1, 1)
        )
        live_masks.append(live_flags)
        masked.append(inputs[group_member] * live_flags.astype(jnp.bfloat16))
    totals = lax.psum(live_counts[0].astype(jnp.float32), (DP, REP))
    local_weights = (conv_a1, conv_a2, conv_a3, conv_as, conv_b1, conv_b2, conv_b3)
    squares_list = []
    for weight in local_weights:
        squares_list.append(jnp.sum(jnp.square(weight.astype(jnp.float32))))
    weight_squares = jnp.stack(squares_list)
    gathered_a = (
        lax.all_gather(conv_a1, DP, axis=1, tiled=True),
        lax.all_gather(norm_a1, DP, axis=1, tiled=True),
        lax.all_gather(conv_a2, DP, axis=3, tiled=True),
        lax.all_gather(norm_a2, DP, axis=1, tiled=True),
        lax.all_gather(conv_a3, DP, axis=1, tiled=True),
        lax.all_gather(norm_a3, DP, axis=1, tiled=True),
        lax.all_gather(conv_as, DP, axis=1, tiled=True),
        lax.all_gather(norm_as, DP, axis=1, tiled=True),
    )
    full_a1, param_a1, full_a2, param_a2, full_a3, param_a3, full_as, param_as = gathered_a
    mid_width = full_a2.shape[3]
    out_width = full_a3.shape[1]
    hidden_a1 = [pointwise(masked[group_member], full_a1) for group_member in range(3)]
    normed_a1, means_a1, scales_a1 = batch_norm(hidden_a1, live_masks, param_a1, totals)
    act_a1 = [
        jax.nn.silu(normed_a1[group_member]).astype(jnp.bfloat16) for group_member in range(3)
    ]
    kernel_a2 = full_a2.reshape(9 * mid_width, mid_width)
    hidden_a2 = [
        pointwise(patches(act_a1[group_member], 2), kernel_a2) for group_member in range(3)
    ]
    normed_a2, means_a2, scales_a2 = batch_norm(hidden_a2, live_masks, param_a2, totals)
    act_a2 = [
        jax.nn.silu(normed_a2[group_member]).astype(jnp.bfloat16) for group_member in range(3)
    ]
    strided = [masked[group_member][:, ::2, ::2, :] for group_member in range(3)]
    joined = [
        jnp.concatenate(
            [pointwise(act_a2[group_member], full_a3), pointwise(strided[group_member], full_as)],
            axis=3,
        )
        for group_member in range(3)
    ]
    param_joined = jnp.concatenate([param_a3, param_as], axis=1)
    normed_j, means_j, scales_j = batch_norm(joined, live_masks, param_joined, totals)
    sum_a = [
        normed_j[group_member][..., :out_width] + normed_j[group_member][..., out_width:]
        for group_member in range(3)
    ]
    out_a = [
        (jax.nn.silu(sum_a[group_member]) * live_masks[group_member]).astype(jnp.bfloat16)
        for group_member in range(3)
    ]
    gathered_b = (
        lax.all_gather(conv_b1, DP, axis=1, tiled=True),
        lax.all_gather(norm_b1, DP, axis=1, tiled=True),
        lax.all_gather(conv_b2, DP, axis=3, tiled=True),
        lax.all_gather(norm_b2, DP, axis=1, tiled=True),
        lax.all_gather(conv_b3, DP, axis=1, tiled=True),
        lax.all_gather(norm_b3, DP, axis=1, tiled=True),
    )
    full_b1, param_b1, full_b2, param_b2, full_b3, param_b3 = gathered_b
    hidden_b1 = [pointwise(out_a[group_member], full_b1) for group_member in range(3)]
    normed_b1, means_b1, scales_b1 = batch_norm(hidden_b1, live_masks, param_b1, totals)
    act_b1 = [
        jax.nn.silu(normed_b1[group_member]).astype(jnp.bfloat16) for group_member in range(3)
    ]
    kernel_b2 = full_b2.reshape(9 * mid_width, mid_width)
    hidden_b2 = [
        pointwise(patches(act_b1[group_member], 1), kernel_b2) for group_member in range(3)
    ]
    normed_b2, means_b2, scales_b2 = batch_norm(hidden_b2, live_masks, param_b2, totals)
    act_b2 = [
        jax.nn.silu(normed_b2[group_member]).astype(jnp.bfloat16) for group_member in range(3)
    ]
    hidden_b3 = [pointwise(act_b2[group_member], full_b3) for group_member in range(3)]
    normed_b3, means_b3, scales_b3 = batch_norm(hidden_b3, live_masks, param_b3, totals)
    sum_b = [
        normed_b3[group_member] + out_a[group_member].astype(jnp.float32)
        for group_member in range(3)
    ]
    outputs = [
        (jax.nn.silu(sum_b[group_member]) * live_masks[group_member]).astype(jnp.bfloat16)
        for group_member in range(3)
    ]
    back_b = (
        lax.all_gather(conv_b1, DP, axis=1, tiled=True),
        lax.all_gather(norm_b1, DP, axis=1, tiled=True),
        lax.all_gather(conv_b2, DP, axis=3, tiled=True),
        lax.all_gather(norm_b2, DP, axis=1, tiled=True),
        lax.all_gather(conv_b3, DP, axis=1, tiled=True),
        lax.all_gather(norm_b3, DP, axis=1, tiled=True),
    )
    full_b1, param_b1, full_b2, param_b2, full_b3, param_b3 = back_b
    kernel_b2 = full_b2.reshape(9 * mid_width, mid_width)
    grad_sum_b = [
        cotangents[group_member].astype(jnp.float32)
        * live_masks[group_member]
        * silu_slope(sum_b[group_member])
        for group_member in range(3)
    ]
    grad_h_b3, pgrad_b3 = norm_back(
        grad_sum_b, hidden_b3, live_masks, param_b3, means_b3, scales_b3, totals
    )
    term_b3 = summed_terms(act_b2, grad_h_b3)
    grad_act = [
        pointwise_back(grad_h_b3[group_member], full_b3) * silu_slope(normed_b2[group_member])
        for group_member in range(3)
    ]
    grad_h_b2, pgrad_b2 = norm_back(
        grad_act, hidden_b2, live_masks, param_b2, means_b2, scales_b2, totals
    )
    term_b2 = summed_terms(
        [patches(act_b1[group_member], 1) for group_member in range(3)], grad_h_b2
    ).reshape(3, 3, mid_width, mid_width)
    grad_act = [
        fold_patches(
            pointwise_back(grad_h_b2[group_member], kernel_b2), 1, act_b1[group_member].shape[1]
        )
        * silu_slope(normed_b1[group_member])
        for group_member in range(3)
    ]
    grad_h_b1, pgrad_b1 = norm_back(
        grad_act, hidden_b1, live_masks, param_b1, means_b1, scales_b1, totals
    )
    term_b1 = summed_terms(out_a, grad_h_b1)
    grad_out_a = [
        grad_sum_b[group_member] + pointwise_back(grad_h_b1[group_member], full_b1)
        for group_member in range(3)
    ]
    shard_b = (
        lax.psum_scatter(term_b1, DP, scatter_dimension=1, tiled=True),
        lax.psum_scatter(term_b2, DP, scatter_dimension=3, tiled=True),
        lax.psum_scatter(term_b3, DP, scatter_dimension=1, tiled=True),
    )
    grads_b = (
        lax.psum(shard_b[0].astype(jnp.bfloat16), REP).astype(jnp.float32),
        lax.psum(shard_b[1].astype(jnp.bfloat16), REP).astype(jnp.float32),
        lax.psum(shard_b[2].astype(jnp.bfloat16), REP).astype(jnp.float32),
    )
    back_a = (
        lax.all_gather(conv_a1, DP, axis=1, tiled=True),
        lax.all_gather(norm_a1, DP, axis=1, tiled=True),
        lax.all_gather(conv_a2, DP, axis=3, tiled=True),
        lax.all_gather(norm_a2, DP, axis=1, tiled=True),
        lax.all_gather(conv_a3, DP, axis=1, tiled=True),
        lax.all_gather(norm_a3, DP, axis=1, tiled=True),
        lax.all_gather(conv_as, DP, axis=1, tiled=True),
        lax.all_gather(norm_as, DP, axis=1, tiled=True),
    )
    full_a1, param_a1, full_a2, param_a2, full_a3, param_a3, full_as, param_as = back_a
    kernel_a2 = full_a2.reshape(9 * mid_width, mid_width)
    param_joined = jnp.concatenate([param_a3, param_as], axis=1)
    grad_sum_a = [
        grad_out_a[group_member] * live_masks[group_member] * silu_slope(sum_a[group_member])
        for group_member in range(3)
    ]
    grad_joined = [
        jnp.concatenate([grad_sum_a[group_member], grad_sum_a[group_member]], axis=3)
        for group_member in range(3)
    ]
    grad_h_j, pgrad_j = norm_back(
        grad_joined, joined, live_masks, param_joined, means_j, scales_j, totals
    )
    grad_h_a3 = [grad_h_j[group_member][..., :out_width] for group_member in range(3)]
    grad_h_as = [grad_h_j[group_member][..., out_width:] for group_member in range(3)]
    term_a3 = summed_terms(act_a2, grad_h_a3)
    term_as = summed_terms(strided, grad_h_as)
    grad_act = [
        pointwise_back(grad_h_a3[group_member], full_a3) * silu_slope(normed_a2[group_member])
        for group_member in range(3)
    ]
    grad_h_a2, pgrad_a2 = norm_back(
        grad_act, hidden_a2, live_masks, param_a2, means_a2, scales_a2, totals
    )
    term_a2 = summed_terms(
        [patches(act_a1[group_member], 2) for group_member in range(3)], grad_h_a2
    ).reshape(3, 3, mid_width, mid_width)
    grad_act = [
        fold_patches(
            pointwise_back(grad_h_a2[group_member], kernel_a2), 2, act_a1[group_member].shape[1]
        )
        * silu_slope(normed_a1[group_member])
        for group_member in range(3)
    ]
    grad_h_a1, pgrad_a1 = norm_back(
        grad_act, hidden_a1, live_masks, param_a1, means_a1, scales_a1, totals
    )
    term_a1 = summed_terms(masked, grad_h_a1)
    grad_inputs = [
        pointwise_back(grad_h_a1[group_member], full_a1)
        .at[:, ::2, ::2, :]
        .add(pointwise_back(grad_h_as[group_member], full_as))
        .astype(jnp.bfloat16)
        for group_member in range(3)
    ]
    shard_a = (
        lax.psum_scatter(term_a1, DP, scatter_dimension=1, tiled=True),
        lax.psum_scatter(term_a2, DP, scatter_dimension=3, tiled=True),
        lax.psum_scatter(term_a3, DP, scatter_dimension=1, tiled=True),
        lax.psum_scatter(term_as, DP, scatter_dimension=1, tiled=True),
    )
    grads_a = (
        lax.psum(shard_a[0].astype(jnp.bfloat16), REP).astype(jnp.float32),
        lax.psum(shard_a[1].astype(jnp.bfloat16), REP).astype(jnp.float32),
        lax.psum(shard_a[2].astype(jnp.bfloat16), REP).astype(jnp.float32),
        lax.psum(shard_a[3].astype(jnp.bfloat16), REP).astype(jnp.float32),
    )
    mid_local = norm_a1.shape[1]
    out_local = norm_a3.shape[1]
    norm_grad_a1 = own_columns(pgrad_a1, mid_local)
    norm_grad_a2 = own_columns(pgrad_a2, mid_local)
    norm_grad_a3 = own_columns(pgrad_j[:, :out_width], out_local)
    norm_grad_as = own_columns(pgrad_j[:, out_width:], out_local)
    norm_grad_b1 = own_columns(pgrad_b1, mid_local)
    norm_grad_b2 = own_columns(pgrad_b2, mid_local)
    norm_grad_b3 = own_columns(pgrad_b3, out_local)
    gradients = (grads_a[0], grads_a[1], grads_a[2], grads_a[3], grads_b[0], grads_b[1], grads_b[2])
    grad_list = []
    for gradient in gradients:
        grad_list.append(jnp.sum(gradient * gradient))
    grad_squares = jnp.stack(grad_list)
    weight_totals, grad_totals = lax.psum((weight_squares, grad_squares), DP)
    weight_norm = jnp.sqrt(weight_totals)
    grad_norm = jnp.sqrt(grad_totals)
    trust_ratio = weight_norm / (grad_norm + DECAY_RATE * weight_norm)
    scaled = [
        trust_ratio[layer_id]
        * (gradients[layer_id] + DECAY_RATE * local_weights[layer_id].astype(jnp.float32))
        for layer_id in range(7)
    ]
    return (
        outputs[0],
        outputs[1],
        outputs[2],
        grad_inputs[0],
        grad_inputs[1],
        grad_inputs[2],
        gradients[0],
        norm_grad_a1,
        gradients[1],
        norm_grad_a2,
        gradients[2],
        norm_grad_a3,
        gradients[3],
        norm_grad_as,
        gradients[4],
        norm_grad_b1,
        gradients[5],
        norm_grad_b2,
        gradients[6],
        norm_grad_b3,
        scaled[0],
        scaled[1],
        scaled[2],
        scaled[3],
        scaled[4],
        scaled[5],
        scaled[6],
        jnp.stack([weight_totals, grad_totals]),
    )


MESH = pl.DeviceIdType.MESH
ANY = pl.BlockSpec(memory_space=pl.ANY)


def position():
    dp, rep = lax.axis_index(DP), lax.axis_index(REP)
    return dp // 2, lax.rem(dp, 2), rep // 2, lax.rem(rep, 2)


def device_at(z, x, y, core):
    return (z * 2 + x, y * 2 + core)


def greet(depth, crosswise=False):
    z, x, y, core = position()
    barrier = pltpu.get_barrier_semaphore()
    peers = [(z, x, y, 1 - core), (z, x, 1 - y, core), (z, x, 1 - y, 1 - core)]
    peers += [(z, 1 - x, y, core), (z, 1 - x, y, 1 - core), (z, 1 - x, 1 - y, core), (z, 1 - x, 1 - y, 1 - core)]
    peers += [(lax.rem(z + step, depth), x, y, core) for step in range(1, depth)]
    if crosswise:
        peers += [(lax.rem(z + step, depth), 1 - x, y, core) for step in range(1, depth)]
    for peer in peers:
        pl.semaphore_signal(barrier, inc=1, device_id=device_at(*peer), device_id_type=MESH)
    pl.semaphore_wait(barrier, len(peers))


def remote(src, dst, send, recv, peer):
    return pltpu.make_async_remote_copy(
        src_ref=src, dst_ref=dst, send_sem=send, recv_sem=recv, device_id=device_at(*peer), device_id_type=MESH
    )


def chunk_rows(rows, both, y, core):
    if both:
        return pl.ds(pl.multiple_of(core * (rows // 2), rows // 2), rows // 2)
    return pl.ds(pl.multiple_of(core * (rows // 2) + y * (rows // 4), rows // 4), rows // 4)


def core_rows(rows, core):
    return pl.ds(pl.multiple_of(core * (rows // 2), rows // 2), rows // 2)


class Gather:
    AHEAD = 3

    def __init__(self, shards, fulls, sems, depth):
        self.shards, self.fulls, self.depth = shards, fulls, depth
        (self.local_sem, self.z_send, self.z_recv, self.x_send, self.x_recv) = sems[:5]
        (self.y_send, self.y_recv, self.c_send, self.c_recv) = sems[5:]
        self.z, self.x, self.y, self.core = position()
        self.count = len(GATHER_CHUNKS)
        self.z_next = self.x_next = self.y_next = self.c_next = 0

    @staticmethod
    def scratch(depth):
        dma, count = pltpu.SemaphoreType.DMA, len(GATHER_CHUNKS)
        return [dma((count,))] + [dma((count, depth - 1))] * 2 + [dma((count,))] * 6

    def part(self, k):
        tensor, lead, leads, both, column, columns = GATHER_CHUNKS[k]
        rows = chunk_rows(self.shards[tensor].shape[1], both, self.y, self.core)
        return self.fulls[tensor], pl.ds(lead, leads), rows, pl.ds(column, columns)

    def place(self, k):
        full, lead, rows, cols = self.part(k)
        shard = self.shards[GATHER_CHUNKS[k][0]]
        return pltpu.make_async_copy(
            shard.at[lead, rows, cols], full.at[self.z, self.x, lead, rows, cols], self.local_sem.at[k]
        )

    def z_copies(self, k):
        full, lead, rows, cols = self.part(k)
        here = full.at[self.z, self.x, lead, rows, cols]
        return [
            remote(
                here,
                here,
                self.z_send.at[k, step - 1],
                self.z_recv.at[k, step - 1],
                (lax.rem(self.z + step, self.depth), self.x, self.y, self.core),
            )
            for step in range(1, self.depth)
        ]

    def x_copy(self, k):
        full, lead, rows, cols = self.part(k)
        here = full.at[:, self.x, lead, rows, cols]
        return remote(here, here, self.x_send.at[k], self.x_recv.at[k], (self.z, 1 - self.x, self.y, self.core))

    def y_copy(self, k):
        full, lead, rows, cols = self.part(k)
        here = full.at[:, :, lead, rows, cols]
        return remote(here, here, self.y_send.at[k], self.y_recv.at[k], (self.z, self.x, 1 - self.y, self.core))

    def c_copy(self, k):
        full, lead, _, cols = self.part(k)
        here = full.at[:, :, lead, core_rows(full.shape[3], self.core), cols]
        return remote(here, here, self.c_send.at[k], self.c_recv.at[k], (self.z, self.x, self.y, 1 - self.core))

    def place_all(self):
        for k in range(self.count):
            self.place(k).start()

    def launch(self, k):
        if k < self.count:
            self.place(k).wait()
            for copy in self.z_copies(k):
                copy.start()

    def begin(self):
        for k in range(self.AHEAD):
            self.launch(k)

    def z_step(self):
        k, self.z_next = self.z_next, self.z_next + 1
        for copy in self.z_copies(k):
            copy.wait_recv()
        self.x_copy(k).start()
        self.launch(k + self.AHEAD)

    def x_step(self):
        k, self.x_next = self.x_next, self.x_next + 1
        self.x_copy(k).wait_recv()
        (self.c_copy if GATHER_CHUNKS[k][3] else self.y_copy)(k).start()

    def y_step(self):
        k, self.y_next = self.y_next, self.y_next + 1
        if not GATHER_CHUNKS[k][3]:
            self.y_copy(k).wait_recv()
            self.c_copy(k).start()

    def c_step(self):
        k, self.c_next = self.c_next, self.c_next + 1
        self.c_copy(k).wait_recv()

    def tick(self, upto=-1):
        count = self.count
        if self.z_next < count:
            self.z_step()
        for before, after, step, lag in (
            (self.z_next, self.x_next, self.x_step, 1),
            (self.x_next, self.y_next, self.y_step, 1),
            (self.y_next, self.c_next, self.c_step, 1),
        ):
            if after < before and (before - after > lag or before == count or after <= upto):
                step()

    def pump(self, ticks=1):
        for _ in range(ticks):
            if self.c_next < self.count:
                self.tick()

    def ready(self, tensor):
        last = max(k for k, chunk in enumerate(GATHER_CHUNKS) if chunk[0] == tensor)
        while self.c_next <= last:
            self.tick(last)

    def close(self):
        for k in range(self.count):
            for copy in self.z_copies(k):
                copy.wait_send()
            self.x_copy(k).wait_send()
            if not GATHER_CHUNKS[k][3]:
                self.y_copy(k).wait_send()
            self.c_copy(k).wait_send()


def taps(tensor):
    pieces = []
    for lead in (0, 3, 6):
        pieces += [(tensor, lead, 1, True, 0, 512), (tensor, lead + 1, 2, False, 0, 512)]
    return pieces


CHUNKS = (
    [(0, 0, 1, False, column, 512) for column in (0, 512)],
    taps(1),
    [(2, lead, 1, False, 0, 256) for lead in (0, 1)],
    [(3, lead, 1, lead == 0, 0, 256) for lead in range(4)],
    [(4, 0, 1, column % 1024 == 0, column, 512) for column in (0, 512, 1024, 1536)],
    taps(5),
    [(6, lead, 1, False, 0, 256) for lead in (0, 1)],
)
GATHER_CHUNKS = [chunk for tensor in (0, 1, 3, 2, 4, 5, 6) for chunk in CHUNKS[tensor]]
REDUCE_CHUNKS = [chunk for tensor in (6, 5, 4, 2, 3, 1, 0) for chunk in CHUNKS[tensor]]


def add_blocks(extents, body):
    total = 1
    for extent in extents:
        total *= extent

    def step(flat, carry):
        index = []
        for extent in reversed(extents):
            index.append(lax.rem(flat, extent))
            flat = flat // extent
        body(*reversed(index))
        return carry

    lax.fori_loop(0, total, step, 0)


def add_to(target, source):
    target[...] = (target[...].astype(jnp.float32) + source[...].astype(jnp.float32)).astype(jnp.bfloat16)


class Reduce:
    def __init__(self, held, outs, c_hbm, y_hbm, refs, depth):
        self.held, self.outs, self.c_hbm, self.y_hbm, self.depth = held, outs, c_hbm, y_hbm, depth
        self.count = len(REDUCE_CHUNKS)
        refs = list(refs)

        def take(count):
            taken = refs[:count]
            del refs[:count]
            return taken

        self.from_x, self.from_z, self.swap = take(self.count), take(self.count), take(self.count)
        self.final = take(self.count)
        self.c_tall, self.c_wide, self.y_tall, self.y_wide, self.squares = take(5)
        self.c_sem, self.y_sem, self.x_sem, self.z_sem, self.s_sem, self.f_sem, self.q_sem, self.local_sem = take(8)
        self.z, self.x, self.y, self.core = position()
        self.enabled = 0
        self.next = [0] * len(self.LAGS)

    @staticmethod
    def sizes(shapes):
        for tensor, _, leads, both, _, columns in REDUCE_CHUNKS:
            rows = shapes[tensor][3]
            yield leads, rows, columns, rows // 2 if both else rows // 4, both

    @staticmethod
    def scratch(shapes, depth):
        dma, count = pltpu.SemaphoreType.DMA, len(REDUCE_CHUNKS)
        buffer = lambda *shape: pltpu.VMEM(shape, jnp.bfloat16)
        sizes = list(Reduce.sizes(shapes))
        return (
            [buffer(depth, leads, part, columns) for leads, _, columns, part, _ in sizes]
            + [buffer(depth - 1, leads, part, columns) for leads, _, columns, part, _ in sizes]
            + [buffer(leads, part, columns) if both else buffer(16, 128) for leads, _, columns, part, both in sizes]
            + [buffer(leads, rows, columns) for leads, rows, columns, _, _ in sizes]
            + [buffer(2, depth, 2, 1, shapes[2][3] // 2, shapes[2][4]), buffer(2, depth, 2, 2, shapes[0][3] // 2, 512)]
            + [buffer(2, depth, 2, 1, shapes[2][3] // 4, shapes[2][4]), buffer(2, depth, 2, 2, shapes[0][3] // 4, 512)]
            + [pltpu.VMEM((2 * depth + 3, 8, 128), jnp.float32)]
            + [dma((2, count))] * 3
            + [dma((2, count, depth - 1)), dma((2, count)), dma((2, count, 3)), dma((2, depth)), dma((3, count))]
        )

    def piece(self, k):
        tensor, lead, leads, both, column, columns = REDUCE_CHUNKS[k]
        held = self.held[tensor]
        rows = held.shape[3]
        return held, rows, pl.ds(lead, leads), pl.ds(column, columns), chunk_rows(rows, both, self.y, self.core)

    def extents(self, k):
        return REDUCE_CHUNKS[k][2], REDUCE_CHUNKS[k][1]

    def slot(self, k, tall, wide):
        tensor, _, leads = REDUCE_CHUNKS[k][:3]
        buffer = tall if tensor in (2, 3, 6) else wide
        return buffer.at[k % 2, :, :, pl.ds(0, leads)]

    def c_copy(self, k):
        held, rows, lead, cols, _ = self.piece(k)
        return remote(
            held.at[:, :, lead, core_rows(rows, 1 - self.core), cols],
            self.c_hbm[REDUCE_CHUNKS[k][0]].at[:, :, lead, :, cols],
            self.c_sem.at[0, k],
            self.c_sem.at[1, k],
            (self.z, self.x, self.y, 1 - self.core),
        )

    def c_load(self, k):
        _, _, lead, cols, _ = self.piece(k)
        return pltpu.make_async_copy(
            self.c_hbm[REDUCE_CHUNKS[k][0]].at[:, :, lead, :, cols],
            self.slot(k, self.c_tall, self.c_wide),
            self.local_sem.at[0, k],
        )

    def y_copy(self, k):
        held, rows, lead, cols, _ = self.piece(k)
        return remote(
            held.at[:, :, lead, chunk_rows(rows, False, 1 - self.y, self.core), cols],
            self.y_hbm[REDUCE_CHUNKS[k][0]].at[:, :, lead, :, cols],
            self.y_sem.at[0, k],
            self.y_sem.at[1, k],
            (self.z, self.x, 1 - self.y, self.core),
        )

    def y_load(self, k):
        _, _, lead, cols, _ = self.piece(k)
        return pltpu.make_async_copy(
            self.y_hbm[REDUCE_CHUNKS[k][0]].at[:, :, lead, :, cols],
            self.slot(k, self.y_tall, self.y_wide),
            self.local_sem.at[1, k],
        )

    def x_copy(self, k):
        held, _, lead, cols, rows = self.piece(k)
        return remote(
            held.at[:, 1 - self.x, lead, rows, cols],
            self.from_x[k],
            self.x_sem.at[0, k],
            self.x_sem.at[1, k],
            (self.z, 1 - self.x, self.y, self.core),
        )

    def z_copies(self, k):
        held, _, lead, cols, rows = self.piece(k)
        copies = []
        for step in range(1, self.depth):
            there = lax.rem(self.z + step, self.depth)
            copies.append(
                remote(
                    held.at[there, self.x, lead, rows, cols],
                    self.from_z[k].at[step - 1],
                    self.z_sem.at[0, k, step - 1],
                    self.z_sem.at[1, k, step - 1],
                    (there, self.x, self.y, self.core),
                )
            )
        return copies

    def s_copy(self, k):
        rows = self.piece(k)[4]
        return remote(
            self.final[k].at[:, rows],
            self.swap[k],
            self.s_sem.at[0, k],
            self.s_sem.at[1, k],
            (self.z, self.x, 1 - self.y, self.core),
        )

    def f_copies(self, k):
        here = self.final[k].at[:, self.piece(k)[4]]
        peers = [(self.z, self.x, self.y, 1 - self.core)]
        if not REDUCE_CHUNKS[k][3]:
            peers += [(self.z, self.x, 1 - self.y, self.core), (self.z, self.x, 1 - self.y, 1 - self.core)]
        return [
            remote(here, here, self.f_sem.at[0, k, i], self.f_sem.at[1, k, i], peer) for i, peer in enumerate(peers)
        ]

    def store(self, k):
        tensor = REDUCE_CHUNKS[k][0]
        _, _, lead, cols, _ = self.piece(k)
        return pltpu.make_async_copy(self.final[k], self.outs[tensor].at[lead, :, cols], self.local_sem.at[2, k])

    def add_c(self, k):
        held, rows, _, cols, _ = self.piece(k)
        leads, lead = self.extents(k)
        half, slot = core_rows(rows, self.core), self.slot(k, self.c_tall, self.c_wide)
        add_blocks(
            (self.depth, 2, leads), lambda z, x, i: add_to(held.at[z, x, lead + i, half, cols], slot.at[z, x, i])
        )

    def add_y(self, k):
        held, _, _, cols, rows = self.piece(k)
        leads, lead = self.extents(k)
        slot = self.slot(k, self.y_tall, self.y_wide)
        add_blocks(
            (self.depth, 2, leads), lambda z, x, i: add_to(held.at[z, x, lead + i, rows, cols], slot.at[z, x, i])
        )

    def add_x(self, k):
        held, _, _, cols, rows = self.piece(k)
        leads, lead = self.extents(k)
        add_blocks(
            (self.depth, leads), lambda z, i: add_to(held.at[z, self.x, lead + i, rows, cols], self.from_x[k].at[z, i])
        )

    def add_z(self, k):
        held, _, _, cols, rows = self.piece(k)
        leads, lead = self.extents(k)

        def body(i):
            total = held[self.z, self.x, lead + i, rows, cols].astype(jnp.float32)
            for step in range(1, self.depth):
                total = total + self.from_z[k][step - 1, i].astype(jnp.float32)
            self.final[k][i, rows] = total.astype(jnp.bfloat16)

        add_blocks((leads,), body)

    def add_s(self, k):
        rows = self.piece(k)[4]
        add_blocks((self.extents(k)[0],), lambda i: add_to(self.final[k].at[i, rows], self.swap[k].at[i]))

    def add_squares(self, k):
        leads = self.extents(k)[0]
        lanes = lax.broadcasted_iota(jnp.int32, (8, 128), 1)
        subs = lax.broadcasted_iota(jnp.int32, (8, 128), 0)
        where = (subs == 1) & (lanes == REDUCE_CHUNKS[k][0])

        def body(i):
            block = self.final[k][i].astype(jnp.float32)
            total = jnp.sum(jnp.sum(block * block, axis=0, keepdims=True), axis=1, keepdims=True)
            self.squares[2 * self.depth + 2] += jnp.where(where, total, 0.0)

        add_blocks((leads,), body)

    LAGS = (0, 1, 1, 1, 1, 1, 1, 1, 1)

    def stage(self, k, number):
        both = REDUCE_CHUNKS[k][3]
        if number == 0:
            self.c_copy(k).start()
        elif number == 1:
            self.c_copy(k).wait_recv()
            self.c_load(k).start()
        elif number == 2:
            self.c_load(k).wait()
            self.add_c(k)
            (self.x_copy if both else self.y_copy)(k).start()
        elif number == 3 and not both:
            self.y_copy(k).wait_recv()
            self.y_load(k).start()
        elif number == 4 and not both:
            self.y_load(k).wait()
            self.add_y(k)
            self.x_copy(k).start()
        elif number == 5:
            self.x_copy(k).wait_recv()
            self.add_x(k)
            for copy in self.z_copies(k):
                copy.start()
        elif number == 6:
            for copy in self.z_copies(k):
                copy.wait_recv()
            self.add_z(k)
            for copy in [self.s_copy(k)] if both else self.f_copies(k):
                copy.start()
        elif number == 7 and both:
            self.s_copy(k).wait_recv()
            self.s_copy(k).wait_send()
            self.add_s(k)
            for copy in self.f_copies(k):
                copy.start()
        elif number == 8:
            for copy in self.f_copies(k):
                copy.wait_recv()
            self.store(k).start()
            self.add_squares(k)

    def enable(self, tensor, leads_done=None):
        while self.enabled < self.count:
            chunk = REDUCE_CHUNKS[self.enabled]
            if chunk[0] != tensor or (leads_done is not None and chunk[1] + chunk[2] > leads_done):
                break
            self.enabled += 1

    def pump(self, ticks=1):
        for _ in range(ticks):
            for number in reversed(range(len(self.LAGS))):
                before = self.next[number - 1] if number else self.enabled
                behind = before - self.next[number]
                if behind > 0 and (behind > self.LAGS[number] or before == self.count):
                    self.stage(self.next[number], number)
                    self.next[number] += 1

    def finish(self, weight_squares, sums_out):
        while self.next[-1] < self.count:
            self.pump()
        squares, depth = self.squares, self.depth
        subs = lax.broadcasted_iota(jnp.int32, (8, 128), 0)
        mine = squares.at[self.z * 2 + self.x]
        mine[...] = squares[2 * depth + 2] + jnp.where(subs == 0, weight_squares[...], 0.0)
        copies = [
            remote(
                mine,
                mine,
                self.q_sem.at[0, step],
                self.q_sem.at[1, step],
                (lax.rem(self.z + step, depth), self.x, self.y, self.core),
            )
            for step in range(1, depth)
        ]
        for copy in copies:
            copy.start()
        for copy in copies:
            copy.wait_recv()
        own = squares[self.x]
        for deep in range(1, depth):
            own = own + squares[deep * 2 + self.x]
        column = squares.at[2 * depth + self.x]
        column[...] = own
        across = remote(
            column, column, self.q_sem.at[0, 0], self.q_sem.at[1, 0], (self.z, 1 - self.x, self.y, self.core)
        )
        across.start()
        across.wait_recv()
        sums_out[...] = squares[2 * depth] + squares[2 * depth + 1]
        across.wait_send()
        for copy in copies:
            copy.wait_send()
        for k in range(self.count):
            self.c_copy(k).wait_send()
            if not REDUCE_CHUNKS[k][3]:
                self.y_copy(k).wait_send()
            self.x_copy(k).wait_send()
            for copy in self.z_copies(k) + self.f_copies(k):
                copy.wait_send()
            self.store(k).wait()


class NearFar:
    def __init__(self, refs, depth):
        self.near, self.far, self.total, self.near_send, self.near_recv, self.far_send, self.far_recv = refs
        self.depth = depth
        self.z, self.x, self.y, self.core = position()
        self.mine = self.x * 4 + self.y * 2 + self.core
        self.pay = self.near.at[self.mine]
        self.sent = []

    @staticmethod
    def scratch(width, depth):
        dma = pltpu.SemaphoreType.DMA
        return [
            pltpu.VMEM((8, 8, width), jnp.float32),
            pltpu.VMEM((depth, 8, width), jnp.float32),
            pltpu.VMEM((8, width), jnp.float32),
            dma((7,)),
            dma((7,)),
            dma((depth - 1,)),
            dma((depth - 1,)),
        ]

    def near_copies(self):
        copies = []
        for offset in range(1, 8):
            x = 1 - self.x if offset & 4 else self.x
            y = 1 - self.y if offset & 2 else self.y
            core = 1 - self.core if offset & 1 else self.core
            here = self.near.at[self.mine]
            copies.append(
                remote(here, here, self.near_send.at[offset - 1], self.near_recv.at[offset - 1], (self.z, x, y, core))
            )
        return copies

    def far_copies(self):
        here = self.far.at[self.z]
        return [
            remote(
                here,
                here,
                self.far_send.at[step - 1],
                self.far_recv.at[step - 1],
                (lax.rem(self.z + step, self.depth), self.x, self.y, self.core),
            )
            for step in range(1, self.depth)
        ]

    def begin(self):
        for copy in self.near_copies():
            copy.start()

    def stages(self):
        def middle():
            for copy in self.near_copies():
                copy.wait_recv()
            total = self.near[0]
            for slot in range(1, 8):
                total = total + self.near[slot]
            self.far[self.z] = total
            for copy in self.far_copies():
                copy.start()

        def last():
            for copy in self.far_copies():
                copy.wait_recv()
            total = self.far[0]
            for slot in range(1, self.depth):
                total = total + self.far[slot]
            self.total[...] = total

        return [middle, last]

    def close(self):
        for copy in self.near_copies() + self.far_copies():
            copy.wait_send()


class Split:
    def __init__(self, refs, depth):
        (self.pay, self.near, self.deep, self.total, self.n_send, self.n_recv) = refs[:6]
        (self.z_send, self.z_recv, self.g_send, self.g_recv) = refs[6:]
        self.depth = depth
        self.z, self.x, self.y, self.core = position()
        self.width = self.pay.shape[1]
        self.mine = self.x * 4 + self.y * 2 + self.core

    @staticmethod
    def scratch(width, depth):
        dma = pltpu.SemaphoreType.DMA
        return [
            pltpu.VMEM((8, width), jnp.float32),
            pltpu.VMEM((8, 8, width // 8), jnp.float32),
            pltpu.VMEM((depth, 8, width // 8), jnp.float32),
            pltpu.VMEM((8, width), jnp.float32),
            dma((7,)),
            dma((7,)),
            dma((depth - 1,)),
            dma((depth - 1,)),
            dma((7,)),
            dma((7,)),
        ]

    def eighth_of(self, slot):
        return pl.ds(pl.multiple_of(slot * (self.width // 8), 128), self.width // 8)

    def around(self):
        for offset in range(1, 8):
            x = 1 - self.x if offset & 4 else self.x
            y = 1 - self.y if offset & 2 else self.y
            core = 1 - self.core if offset & 1 else self.core
            yield offset - 1, x, y, core

    def near_copies(self):
        return [
            remote(
                self.pay.at[:, self.eighth_of(x * 4 + y * 2 + core)],
                self.near.at[self.mine],
                self.n_send.at[i],
                self.n_recv.at[i],
                (self.z, x, y, core),
            )
            for i, x, y, core in self.around()
        ]

    def deep_copies(self):
        here = self.deep.at[self.z]
        return [
            remote(
                here,
                here,
                self.z_send.at[step - 1],
                self.z_recv.at[step - 1],
                (lax.rem(self.z + step, self.depth), self.x, self.y, self.core),
            )
            for step in range(1, self.depth)
        ]

    def gather_copies(self):
        here = self.total.at[:, self.eighth_of(self.mine)]
        return [
            remote(here, here, self.g_send.at[i], self.g_recv.at[i], (self.z, x, y, core))
            for i, x, y, core in self.around()
        ]

    def begin(self):
        for copy in self.near_copies():
            copy.start()
        self.near[self.mine] = self.pay[:, self.eighth_of(self.mine)]

    def stages(self):
        def first():
            for copy in self.near_copies():
                copy.wait_recv()
            total = self.near[0]
            for slot in range(1, 8):
                total = total + self.near[slot]
            self.deep[self.z] = total
            for copy in self.deep_copies():
                copy.start()

        def second():
            for copy in self.deep_copies():
                copy.wait_recv()
            total = self.deep[0]
            for slot in range(1, self.depth):
                total = total + self.deep[slot]
            self.total[:, self.eighth_of(self.mine)] = total
            for copy in self.gather_copies():
                copy.start()

        def third():
            for copy in self.gather_copies():
                copy.wait_recv()
            for copy in self.gather_copies():
                copy.wait_send()

        return [first, second, third]

    def close(self):
        for copy in self.near_copies() + self.deep_copies():
            copy.wait_send()


def interleave(stages, works):
    done = 0
    for i, stage in enumerate(stages):
        upto = (len(works) * (i + 1)) // len(stages)
        for work in works[done:upto]:
            work()
        done = upto
        stage()


HAT_A1, HAT_A2, HAT_A3, HAT_AS, HAT_B1, HAT_B2, HAT_B3, PATCH_A, PATCH_B, ACT_A2, ACT_B2, OUT_A = SAVED = range(12)
SUM_A1, SUM_A2, SUM_B1, SUM_B2, SUM_B3, SUM_J = range(6)


def paced(first, last, body, parts, pump):
    for part in range(parts):
        span = last - first
        lax.fori_loop(first + span * part // parts, first + span * (part + 1) // parts, body, 0)
        pump()


def columns(j):
    return pl.ds(pl.multiple_of(j * 128, 128), 128)


def dot(a, b):
    return lax.dot_general(a, b, (((1,), (0,)), ((), ())), preferred_element_type=jnp.float32)


def dot_nt(a, b):
    return lax.dot_general(a, b, (((1,), (1,)), ((), ())), preferred_element_type=jnp.float32)


def sigmoid(v):
    return 0.5 * jnp.tanh(0.5 * v) + 0.5


def slope(v):
    s = sigmoid(v)
    return s * (1.0 + v * (1.0 - s))


class Plan:
    def __init__(self, shapes):
        self.sides = [shape[1] // 2 for shape in shapes]
        self.slots = [shape[0] for shape in shapes]
        self.valid = [side * side * slots for side, slots in zip(self.sides, self.slots)]
        sizes = [-(-valid // 8) * 8 for valid in self.valid]
        sizes[2] += -sum(sizes) % 128
        self.starts = [0, sizes[0], sizes[0] + sizes[1]]
        self.sizes = sizes
        self.rows = sum(sizes)

    def spans(self):
        return [slice(start, start + size) for start, size in zip(self.starts, self.sizes)]

    def slot_rows(self):
        out = np.full((self.rows, 128), 1e6, np.float32)
        for start, valid, slots in zip(self.starts, self.valid, self.slots):
            out[start : start + valid] = (np.arange(valid) % slots)[:, None]
        return out

    def shifts(self):
        out = np.zeros((9, self.rows, self.rows), np.float32)
        for side, slots, start in zip(self.sides, self.slots, self.starts):
            at = lambda i, j, n: start + (i * side + j) * slots + n
            for di in (-1, 0, 1):
                for dj in (-1, 0, 1):
                    for i in range(max(0, -di), min(side, side - di)):
                        for j in range(max(0, -dj), min(side, side - dj)):
                            for n in range(slots):
                                out[(di + 1) * 3 + dj + 1, at(i, j, n), at(i + di, j + dj, n)] = 1.0
        return out.astype(jnp.bfloat16)


def put_sums(plan, pairs, mask, pay, base, width, pump=None):
    def body(j, carry):
        firsts, seconds = [0.0] * 3, [0.0] * 3
        for first, second in pairs(j):
            for g, span in enumerate(plan.spans()):
                live = first[span] * mask[span, :]
                firsts[g] = firsts[g] + jnp.sum(live, axis=0, keepdims=True)
                seconds[g] = seconds[g] + jnp.sum(live * second[span], axis=0, keepdims=True)
        zero = jnp.zeros((1, 128), jnp.float32)
        pay[:, columns(base + j)] = jnp.concatenate(firsts + seconds + [zero, zero], axis=0)
        return carry

    if pump is None:
        lax.fori_loop(0, width // 128, body, 0)
    else:
        paced(0, width // 128, body, 2, pump)


def put_scales(total, inverse, over, width, factor=1.0, base=0):
    def body(j, carry):
        at, to = columns(base + j), columns(j)
        per = over[0:3, :] * factor
        means = total[0:3, at] * per
        variance = total[3:6, at] * per - means * means
        scales = lax.rsqrt(variance + EPSILON)
        zero = jnp.zeros((5, 128), jnp.float32)
        total[:, at] = jnp.concatenate([means, zero], axis=0)
        inverse[:, to] = jnp.concatenate([scales, zero], axis=0)
        return carry

    lax.fori_loop(0, width // 128, body, 0)


def by_group(plan, of):
    return jnp.concatenate([of(g, span) for g, span in enumerate(plan.spans())], axis=0)


def forward_names(depth):
    return (
        (SUM_A1, NearFar.scratch(512, depth)),
        (SUM_A2, NearFar.scratch(512, depth)),
        (SUM_J, Split.scratch(4096, depth)),
        (SUM_B1, NearFar.scratch(512, depth)),
        (SUM_B2, NearFar.scratch(512, depth)),
        (SUM_B3, Split.scratch(2048, depth)),
    )


def forward_kernel(plan, depth, *refs):
    refs = list(refs)

    def take(count):
        taken = refs[:count]
        del refs[:count]
        return taken

    x_hbm, shift_hbm, slot_rows, live, norm_mid, norm_out = take(6)
    shards = take(7)
    outs = take(3)
    mask, inv_mid, inv_out, par_mid, par_out, over, weight_squares = take(7)
    weights_hbm = take(7)
    saved_hbm = dict(zip(SAVED, take(len(SAVED))))
    sums = {}
    for name, scratch in forward_names(depth):
        sums[name] = (NearFar if len(scratch) == 7 else Split)(take(len(scratch)), depth)
    x, shift = take(2)
    w_a1, w_a2, w_a3, w_as, w_b1, w_b2, w_b3 = weights = take(7)
    saved = dict(zip(SAVED, take(len(SAVED))))
    hid_a1, hid_mid, hid_out, hid_as, act = take(5)
    load_sem, save_sem, full_sem, norms_mid, norms_out, norm_send, norm_recv = take(7)
    gather = Gather(shards, weights, take(9), depth)

    loads = [
        pltpu.make_async_copy(src, dst, load_sem.at[i])
        for i, (src, dst) in enumerate(zip([x_hbm, shift_hbm], [x, shift]))
    ]
    gather.place_all()
    for copy in loads:
        copy.start()

    def keep(i):
        return pltpu.make_async_copy(weights[i], weights_hbm[i], full_sem.at[i])

    weight_squares[...] = jnp.zeros((8, 128), jnp.float32)

    def ready(i):
        gather.ready(i)
        keep(i).start()

    def add_square(i):
        at_row = lax.broadcasted_iota(jnp.int32, (8, 128), 0) == 0
        where = at_row & (lax.broadcasted_iota(jnp.int32, (8, 128), 1) == i)

        def body(lead, carry):
            block = weights[i][gather.z, gather.x, lead].astype(jnp.float32)
            total = jnp.sum(jnp.sum(block * block, axis=0, keepdims=True), axis=1, keepdims=True)
            weight_squares[...] += jnp.where(where, total, 0.0)
            return carry

        lax.fori_loop(0, weights[i].shape[2], body, 0)

    def pump():
        gather.pump()

    def save(name):
        pltpu.make_async_copy(saved[name], saved_hbm[name], save_sem.at[SAVED.index(name)]).start()

    greet(depth, crosswise=True)
    place = gather.z * 2 + gather.x
    norms_mid[place] = norm_mid[...]
    own_lanes = pl.ds(pl.multiple_of(place * norm_out.shape[1], 128), norm_out.shape[1])
    norms_out[:, own_lanes] = norm_out[...]

    def norm_copies(kind):
        here = norms_out.at[:, own_lanes] if kind else norms_mid.at[place]
        copies = []
        for i in range(1, 2 * depth):
            peer = (lax.rem(gather.z + i // 2, depth), 1 - gather.x if i % 2 else gather.x, gather.y, gather.core)
            copies.append(remote(here, here, norm_send.at[kind, i], norm_recv.at[kind, i], peer))
        return copies

    for copy in norm_copies(0) + norm_copies(1):
        copy.start()
    gather.begin()
    lanes = lax.broadcasted_iota(jnp.int32, (1, 128), 1)

    def live_of(g):
        return jnp.sum(jnp.where(lanes == g, live[...], 0.0), axis=1, keepdims=True)

    for g, span in enumerate(plan.spans()):
        mask[span, :] = jnp.where(slot_rows[span, :] < live_of(g), 1.0, 0.0)
    counts = jnp.zeros((1, 128), jnp.float32)
    for g, side in enumerate(plan.sides):
        counts = counts + jnp.where(lanes == g, live[...] * float(side * side), 0.0)

    loads[0].wait()
    ready(0)

    def conv_a1(p, carry):
        hid_a1[p] = dot_nt(x[p], w_a1[...].reshape(512, -1))
        return carry

    lax.fori_loop(0, 2, conv_a1, 0)
    pump()
    lax.fori_loop(2, 4, conv_a1, 0)

    total = sums[SUM_A1]
    put_sums(
        plan, lambda j: [(hid_a1[p, :, columns(j)],) * 2 for p in range(4)], mask, total.pay, 0, 512
    )
    total.pay[6:7, 0:128] = counts
    total.begin()
    add_square(0)
    pump()
    total.stages()[0]()
    pump()
    total.stages()[1]()
    for copy in norm_copies(0):
        copy.wait_recv()
    own_norms = norms_mid[0]
    for slot in range(1, 2 * depth):
        own_norms = own_norms + norms_mid[slot]
    par_mid[...] = own_norms

    pixels = total.total[6:7, 0:128]
    inverse_counts = [
        jnp.broadcast_to(1.0 / jnp.sum(jnp.where(lanes == g, pixels, 0.0), axis=1, keepdims=True), (1, 128))
        for g in range(3)
    ]
    over[...] = jnp.concatenate(inverse_counts + [jnp.zeros((5, 128), jnp.float32)], axis=0)
    put_scales(total.total, inv_mid.at[0], over, 512, 0.25)

    def normalized(hidden, total, inverse, hat, params, row, j, base=0):
        at, sums_at = columns(j), columns(base + j)
        xhat = by_group(plan, lambda g, span: (hidden[span] - total[g : g + 1, sums_at]) * inverse[g : g + 1, at])
        hat[:, at] = xhat.astype(jnp.bfloat16)
        return xhat * params[row : row + 1, at] + params[row + 1 : row + 2, at]

    def activate(hidden_of, total, inverse, hat, params, row, target):
        def body(j, carry):
            v = normalized(hidden_of(j), total, inverse, hat, params, row, j)
            target[:, columns(j)] = (v * sigmoid(v)).astype(jnp.bfloat16)
            return carry

        lax.fori_loop(0, 4, body, 0)

    def activate_a1(p, carry):
        activate(
            lambda j: hid_a1[p, :, columns(j)],
            total.total,
            inv_mid.at[0],
            saved[HAT_A1].at[p],
            par_mid,
            0,
            act.at[p],
        )
        return carry

    lax.fori_loop(0, 2, activate_a1, 0)
    pump()
    lax.fori_loop(2, 4, activate_a1, 0)
    save(HAT_A1)

    loads[1].wait()
    patch = saved[PATCH_A]
    for tap in range(9):
        a, b = tap // 3, tap % 3
        plane = (0 if a == 1 else 2) + (0 if b == 1 else 1)
        matrix = (0 if a == 0 else 1) * 3 + (0 if b == 0 else 1)
        if matrix == 4:
            patch[tap] = act[plane]
        else:
            patch[tap] = dot(shift[matrix], act[plane]).astype(jnp.bfloat16)
        if tap == 4:
            pump()
    save(PATCH_A)
    ready(1)

    def spatial(patch, weight):
        hid_mid[...] = dot_nt(patch[0], weight[:, :, 0].reshape(512, 512))

        def body(tap, carry):
            hid_mid[...] += dot_nt(patch[tap], weight[:, :, tap].reshape(512, 512))
            return carry

        lax.fori_loop(1, 9, body, 0)

    spatial(patch, w_a2)

    def conv_as(d, carry):
        at = pl.ds(pl.multiple_of(d * 256, 256), 256)
        hid_as[:, at] = dot(x[0], w_as[d // 2, lax.rem(d, 2)].reshape(1024, 256))
        return carry

    def shortcut():
        ready(3)
        lax.fori_loop(0, 8, conv_as, 0)
        put_sums(plan, lambda j: [(hid_as[:, columns(j)],) * 2], mask, sums[SUM_J].pay, 16, 2048)

    def mid_sums(total, name_index, works):
        put_sums(plan, lambda j: [(hid_mid[:, columns(j)],) * 2], mask, total.pay, 0, 512)
        total.begin()
        interleave(total.stages(), works)
        put_scales(total.total, inv_mid.at[name_index], over, 512)

    mid_sums(sums[SUM_A2], 1, [pump, lambda: add_square(1), pump])
    activate(
        lambda j: hid_mid[:, columns(j)], sums[SUM_A2].total, inv_mid.at[1], saved[HAT_A2], par_mid, 2, saved[ACT_A2]
    )
    save(HAT_A2)
    save(ACT_A2)

    def expand(act_ref, weight):
        def body(d, carry):
            at = pl.ds(pl.multiple_of(d * 256, 256), 256)
            hid_out[:, at] = dot(act_ref[...], weight[d // 2, lax.rem(d, 2)].reshape(512, 256))
            return carry

        lax.fori_loop(0, 8, body, 0)

    shortcut()
    ready(2)
    expand(saved[ACT_A2], w_a3)
    total = sums[SUM_J]
    put_sums(plan, lambda j: [(hid_out[:, columns(j)],) * 2], mask, total.pay, 0, 2048)
    total.begin()
    interleave(total.stages(), [pump, lambda: add_square(2), pump, lambda: add_square(3), pump])
    put_scales(total.total, inv_out.at[0], over, 2048)
    put_scales(total.total, inv_out.at[1], over, 2048, base=16)
    for copy in norm_copies(1):
        copy.wait_recv()
    par_out[...] = norms_out[...]

    def join(j, carry):
        at = columns(j)
        v = normalized(hid_out[:, at], total.total, inv_out.at[0], saved[HAT_A3], par_out, 0, j)
        v = v + normalized(hid_as[:, at], total.total, inv_out.at[1], saved[HAT_AS], par_out, 2, j, 16)
        saved[OUT_A][:, at] = (v * sigmoid(v) * mask[...]).astype(jnp.bfloat16)
        return carry

    lax.fori_loop(0, 16, join, 0)
    for name in (HAT_A3, HAT_AS, OUT_A):
        save(name)

    ready(4)
    hid_mid[...] = dot_nt(saved[OUT_A][...], w_b1[...].reshape(512, -1))
    mid_sums(sums[SUM_B1], 2, [pump, lambda: add_square(4), pump])
    activate(
        lambda j: hid_mid[:, columns(j)], sums[SUM_B1].total, inv_mid.at[2], saved[HAT_B1], par_mid, 4, act.at[0]
    )
    save(HAT_B1)

    def patches(tap, carry):
        saved[PATCH_B][tap] = dot(shift[tap], act[0]).astype(jnp.bfloat16)
        return carry

    lax.fori_loop(0, 9, patches, 0)
    save(PATCH_B)
    ready(5)
    spatial(saved[PATCH_B], w_b2)
    mid_sums(sums[SUM_B2], 3, [pump, lambda: add_square(5), pump])
    activate(
        lambda j: hid_mid[:, columns(j)], sums[SUM_B2].total, inv_mid.at[3], saved[HAT_B2], par_mid, 6, saved[ACT_B2]
    )
    save(HAT_B2)
    save(ACT_B2)
    ready(6)
    expand(saved[ACT_B2], w_b3)
    total_b = sums[SUM_B3]
    put_sums(plan, lambda j: [(hid_out[:, columns(j)],) * 2], mask, total_b.pay, 0, 2048)
    total_b.begin()
    interleave(total_b.stages(), [lambda: add_square(6)])
    put_scales(total_b.total, inv_out.at[2], over, 2048)

    def finish(j, carry):
        at = columns(j)
        v = normalized(hid_out[:, at], total_b.total, inv_out.at[2], saved[HAT_B3], par_out, 4, j)
        v = v + saved[OUT_A][:, at].astype(jnp.float32)
        v = v * sigmoid(v) * mask[...]
        for g, target in enumerate(outs):
            start = plan.starts[g]
            target[:, at] = v[start : start + plan.valid[g]].astype(jnp.bfloat16)
        return carry

    lax.fori_loop(0, 16, finish, 0)
    save(HAT_B3)
    for total in sums.values():
        total.close()
    for i, name in enumerate(SAVED):
        pltpu.make_async_copy(saved[name], saved_hbm[name], save_sem.at[i]).wait()
    gather.close()
    for copy in norm_copies(0) + norm_copies(1):
        copy.wait_send()
    for i in range(7):
        keep(i).wait()


def saved_shapes(rows):
    bf16 = jnp.bfloat16
    return (
        ((4, rows, 512), bf16),
        ((rows, 512), bf16),
        ((rows, 2048), bf16),
        ((rows, 2048), bf16),
        ((rows, 512), bf16),
        ((rows, 512), bf16),
        ((rows, 2048), bf16),
        ((9, rows, 512), bf16),
        ((9, rows, 512), bf16),
        ((rows, 512), bf16),
        ((rows, 512), bf16),
        ((rows, 2048), bf16),
    )


WHOLE = pl.BlockSpec(memory_space=pltpu.VMEM)
VMEM_LIMIT = 62 * 1024 * 1024


def run_forward(plan, depth, x, shifts, slot_rows, live, norm_mid, norm_out, shards):
    rows, f32, bf16 = plan.rows, jnp.float32, jnp.bfloat16
    dma = pltpu.SemaphoreType.DMA
    scratch = []
    for _, pieces in forward_names(depth):
        scratch += pieces
    scratch += [pltpu.VMEM(x.shape, bf16), pltpu.VMEM(shifts.shape, bf16)]
    fulls = [jax.ShapeDtypeStruct((depth, 2, *shard.shape), bf16) for shard in shards]
    scratch += [pltpu.VMEM(full.shape, bf16) for full in fulls]
    scratch += [pltpu.VMEM(shape, kind) for shape, kind in saved_shapes(rows)]
    scratch += [
        pltpu.VMEM((4, rows, 512), f32),
        pltpu.VMEM((rows, 512), f32),
        pltpu.VMEM((rows, 2048), f32),
        pltpu.VMEM((rows, 2048), f32),
        pltpu.VMEM((4, rows, 512), bf16),
        dma((2,)),
        dma((len(SAVED),)),
        dma((7,)),
        pltpu.VMEM((2 * depth, 8, 512), f32),
        pltpu.VMEM((8, 2048), f32),
        dma((2, 2 * depth)),
        dma((2, 2 * depth)),
    ]
    scratch += Gather.scratch(depth)
    small = [jax.ShapeDtypeStruct((valid, 2048), bf16) for valid in plan.valid]
    small += [
        jax.ShapeDtypeStruct((rows, 128), f32),
        jax.ShapeDtypeStruct((4, 8, 512), f32),
        jax.ShapeDtypeStruct((3, 8, 2048), f32),
        jax.ShapeDtypeStruct((8, 512), f32),
        jax.ShapeDtypeStruct((8, 2048), f32),
        jax.ShapeDtypeStruct((8, 128), f32),
        jax.ShapeDtypeStruct((8, 128), f32),
    ]
    return pl.pallas_call(
        functools.partial(forward_kernel, plan, depth),
        out_shape=small + fulls + [jax.ShapeDtypeStruct(shape, kind) for shape, kind in saved_shapes(rows)],
        in_specs=[ANY, ANY] + [WHOLE] * 4 + [ANY] * 7,
        out_specs=[WHOLE] * 10 + [ANY] * 7 + [ANY] * len(SAVED),
        scratch_shapes=scratch,
        compiler_params=pltpu.CompilerParams(collective_id=0, has_side_effects=True, vmem_limit_bytes=VMEM_LIMIT),
    )(x, shifts, slot_rows, live, norm_mid, norm_out, *shards)


def backward_names(depth):
    return (
        (SUM_B3, Split.scratch(2048, depth)),
        (SUM_B2, NearFar.scratch(512, depth)),
        (SUM_B1, NearFar.scratch(512, depth)),
        (SUM_J, Split.scratch(4096, depth)),
        (SUM_A2, NearFar.scratch(512, depth)),
        (SUM_A1, NearFar.scratch(512, depth)),
    )


def backward_kernel(plan, depth, *refs):
    refs = list(refs)

    def take(count):
        taken = refs[:count]
        del refs[:count]
        return taken

    x_hbm, shift_hbm, cot_hbm, mask, weight_squares, inv_mid, inv_out, par_mid, par_out, over = take(10)
    saved_hbm = dict(zip(SAVED, take(len(SAVED))))
    weights_hbm = take(7)
    dx_hbm, pgrad_mid, pgrad_b3, pgrad_j, squares_out = take(5)
    gradients_hbm, c_hbm, y_hbm = take(7), take(7), take(7)
    sums = {}
    for name, scratch in backward_names(depth):
        sums[name] = (NearFar if len(scratch) == 7 else Split)(take(len(scratch)), depth)
    x, shift, cot = take(3)
    w_a1, w_a2, w_a3, w_as, w_b1, w_b2, w_b3 = weights = take(7)
    kept = [name for name in SAVED if name != PATCH_B]
    saved = dict(zip(kept, take(len(kept))))
    saved[PATCH_B] = saved[PATCH_A]
    dz, dact, dh_mid, flip = take(4)
    load_sem, saved_sem, dx_sem = take(3)
    dh_a, dh_b = cot, saved[HAT_B3]
    planes = [saved[HAT_AS].at[:, pl.ds(plane * 512, 512)] for plane in range(4)]
    reduce = Reduce(weights, gradients_hbm, c_hbm, y_hbm, refs, depth)
    reduce.squares[2 * depth + 2] = jnp.zeros((8, 128), jnp.float32)

    def pump():
        reduce.pump()

    def loading(name):
        return pltpu.make_async_copy(saved_hbm[name], saved[name], saved_sem.at[SAVED.index(name)])

    loads = [
        pltpu.make_async_copy(src, dst, load_sem.at[i])
        for i, (src, dst) in enumerate(zip([x_hbm, shift_hbm, cot_hbm, *weights_hbm], [x, shift, cot, *weights]))
    ]
    first = (HAT_B3, OUT_A)
    for name in first:
        loading(name).start()
    loads[2].start()
    order = (HAT_B2, ACT_B2, HAT_B1, PATCH_B, HAT_A3, HAT_AS, HAT_A2, ACT_A2, HAT_A1)
    loads[9].start()
    for name in order[:4]:
        loading(name).start()
    for i in (1, 8, 7):
        loads[i].start()
    for name in order[4:]:
        loading(name).start()
    for i in (5, 6, 4, 0, 3):
        loads[i].start()

    greet(depth)

    def quarter(d):
        return pl.ds(pl.multiple_of(d * 256, 256), 256)

    def affine(hat, params, row, at):
        return hat[:, at].astype(jnp.float32) * params[row : row + 1, at] + params[row + 1 : row + 2, at]

    def norm_back(dz_of, hat, total, base, inverse, params, row, target, blocks):
        def body(j, carry):
            at = columns(j)
            sums_at = columns(base + j)
            gain = params[row : row + 1, at]
            value, xhat = dz_of(j), hat[:, at].astype(jnp.float32)

            def of(g, span):
                first = total[g : g + 1, sums_at] * over_of(g)
                second = total[3 + g : 4 + g, sums_at] * over_of(g)
                return (gain * inverse[g : g + 1, at]) * (value[span] - first - xhat[span] * second)

            target[:, at] = (by_group(plan, of) * mask[...]).astype(jnp.bfloat16)
            return carry

        lax.fori_loop(0, blocks, body, 0)

    scale = [1.0]

    def over_of(g):
        return over[g : g + 1, :] * scale[0]

    for name in first:
        loading(name).wait()
    loads[2].wait()

    def out_pairs(j):
        at = columns(j)
        v = affine(saved[HAT_B3], par_out, 4, at) + saved[OUT_A][:, at].astype(jnp.float32)
        value = cot[:, at].astype(jnp.float32) * mask[...] * slope(v)
        dz[:, at] = value
        return [(value, saved[HAT_B3][:, at].astype(jnp.float32))]

    total = sums[SUM_B3]
    put_sums(plan, out_pairs, mask, total.pay, 0, 2048)
    total.begin()
    for i in (9, 1, 8, 7):
        loads[i].wait()
    for name in order[:4]:
        loading(name).wait()
    flip[0:512] = saved[ACT_B2][...].T
    interleave(total.stages(), [])
    pgrad_b3[...] = total.total[...]
    norm_back(lambda j: dz[:, columns(j)], saved[HAT_B3], total.total, 0, inv_out.at[2], par_out, 4, dh_a, 16)

    def contract(dh, weight):
        dact[...] = dot_nt(dh[:, 0:256], weight[0, 0].reshape(512, 256))

        def body(d, carry):
            dact[...] += dot_nt(dh[:, quarter(d)], weight[d // 2, lax.rem(d, 2)].reshape(512, 256))
            return carry

        lax.fori_loop(1, 8, body, 0)

    def expand_term(lhs, dh, weight, first_slot, last_slot):
        def body(d, carry):
            shape = weight.shape[2:]
            weight[d // 2, lax.rem(d, 2)] = dot(lhs, dh[:, quarter(d)]).astype(jnp.bfloat16).reshape(shape)
            return carry

        lax.fori_loop(first_slot, last_slot, body, 0)

    def mid_pairs(hat, row):
        def pairs(j):
            at = columns(j)
            value = dact[:, at] * slope(affine(saved[hat], par_mid, row, at))
            dact[:, at] = value
            return [(value, saved[hat][:, at].astype(jnp.float32))]

        return pairs

    def mid_norm(name, hat, index, row, works):
        total = sums[name]
        put_sums(plan, mid_pairs(hat, row), mask, total.pay, 0, 512)
        total.begin()
        interleave(total.stages(), works)
        pgrad_mid[index] = total.total[...]
        norm_back(lambda j: dact[:, columns(j)], saved[hat], total.total, 0, inv_mid.at[index], par_mid, row, dh_mid, 4)

    contract(dh_a, w_b3)
    expand_term(flip[0:512, :], dh_a, w_b3, 0, 8)
    reduce.enable(6)
    pump()
    mid_norm(SUM_B2, HAT_B2, 3, 6, [pump, pump])

    def spread(tap, carry):
        part = dot(
            dot(shift[8 - tap], dh_mid[...]).astype(jnp.bfloat16), w_b2[:, :, tap].reshape(512, 512)
        )
        dact[...] = part + jnp.where(tap == 0, 0.0, dact[...])
        return carry

    lax.fori_loop(0, 9, spread, 0)
    flip[0:512] = dh_mid[...].T

    def spatial_term(weight, patch, first_tap, last_tap, tensor):
        def work():
            def body(tap, carry):
                weight[:, :, tap] = dot(flip[0:512, :], patch[tap]).astype(jnp.bfloat16).reshape(depth, 2, 64, 512)
                return carry

            lax.fori_loop(first_tap, last_tap, body, 0)
            reduce.enable(tensor, last_tap)

        return work

    mid_norm(
        SUM_B1,
        HAT_B1,
        2,
        4,
        [spatial_term(w_b2, saved[PATCH_B], 0, 3, 5), pump, spatial_term(w_b2, saved[PATCH_B], 3, 6, 5), pump],
    )
    spatial_term(w_b2, saved[PATCH_B], 6, 9, 5)()
    pump()
    loading(PATCH_A).start()

    def residual(d, carry):
        at = quarter(d)
        dz[:, at] = dz[:, at] + dot(dh_mid[...], w_b1[:, :, 0, :, at].reshape(512, 256))
        return carry

    lax.fori_loop(0, 8, residual, 0)
    pump()
    for name in order[4:]:
        loading(name).wait()

    def join_pairs(j):
        at = columns(j)
        v = affine(saved[HAT_A3], par_out, 0, at) + affine(saved[HAT_AS], par_out, 2, at)
        value = dz[:, at] * mask[...] * slope(v)
        dz[:, at] = value
        return [(value, saved[HAT_A3][:, at].astype(jnp.float32))]

    total = sums[SUM_J]
    put_sums(plan, join_pairs, mask, total.pay, 0, 2048)
    put_sums(
        plan, lambda j: [(dz[:, columns(j)], saved[HAT_AS][:, columns(j)].astype(jnp.float32))], mask, total.pay, 16, 2048
    )
    total.begin()
    flip[0:512] = dh_mid[...].T

    def first_term(part):
        def work():
            def body(d, carry):
                at = quarter(d)
                value = dot(flip[0:512, :], saved[OUT_A][:, at]).astype(jnp.bfloat16)
                w_b1[:, :, 0, :, at] = value.reshape(depth, 2, 64, 256)
                return carry

            lax.fori_loop(2 * part, 2 * part + 2, body, 0)
            if part == 3:
                reduce.enable(4)
            pump()

        return work

    interleave(total.stages(), [first_term(part) for part in range(4)])
    pgrad_j[...] = total.total[...]
    norm_back(lambda j: dz[:, columns(j)], saved[HAT_A3], total.total, 0, inv_out.at[0], par_out, 0, dh_a, 16)
    pump()
    norm_back(lambda j: dz[:, columns(j)], saved[HAT_AS], total.total, 16, inv_out.at[1], par_out, 2, dh_b, 16)
    for i in (5, 6, 4, 0, 3):
        loads[i].wait()

    pump()
    contract(dh_a, w_a3)
    pump()
    flip[0:512] = saved[ACT_A2][...].T

    def third_term_a():
        expand_term(flip[0:512, :], dh_a, w_a3, 0, 8)
        reduce.enable(2)
        pump()

    def shortcut():
        even = dz.at[:, 0:1024]
        even[...] = dot_nt(dh_b[:, 0:256], w_as[0, 0].reshape(1024, 256))

        def body(d, carry):
            even[...] += dot_nt(dh_b[:, quarter(d)], w_as[d // 2, lax.rem(d, 2)].reshape(1024, 256))
            return carry

        lax.fori_loop(1, 8, body, 0)

        def keep(j, carry):
            value = even[:, columns(j)]
            high = value.astype(jnp.bfloat16)
            saved[OUT_A][:, columns(j)] = high
            saved[OUT_A][:, columns(8 + j)] = (value - high.astype(jnp.float32)).astype(jnp.bfloat16)
            return carry

        lax.fori_loop(0, 8, keep, 0)

    mid_norm(SUM_A2, HAT_A2, 1, 2, [third_term_a, shortcut, pump])

    loading(PATCH_A).wait()
    flip[...] = x[0].T
    for part in range(4):
        expand_term(flip[...], dh_b, w_as, 2 * part, 2 * part + 2)
        pump()
    reduce.enable(3)
    for plane in range(4):
        at = slice(plane * 512, plane * 512 + 512)
        begun = False
        if plane == 2:
            pump()
        for tap in range(9):
            a, b = tap // 3, tap % 3
            if plane != (0 if a == 1 else 2) + (0 if b == 1 else 1):
                continue
            matrix = (2 if a == 0 else 1) * 3 + (2 if b == 0 else 1)
            moved = dh_mid[...] if matrix == 4 else dot(shift[matrix], dh_mid[...]).astype(jnp.bfloat16)
            part = dot(moved, w_a2[:, :, tap].reshape(512, 512))
            if begun:
                dz[:, at] += part
            else:
                dz[:, at] = part
            begun = True
    pump()

    def plane_pairs(j):
        at = columns(j)
        pairs = []
        for plane in range(4):
            wide = columns(4 * plane + j)
            xhat = saved[HAT_A1][plane, :, at].astype(jnp.float32)
            v = xhat * par_mid[0:1, at] + par_mid[1:2, at]
            value = dz[:, wide] * slope(v)
            dz[:, wide] = value
            pairs.append((value, xhat))
        return pairs

    total = sums[SUM_A1]
    put_sums(plan, plane_pairs, mask, total.pay, 0, 512)
    total.begin()
    flip[0:512] = dh_mid[...].T
    stages = total.stages()
    spatial_term(w_a2, saved[PATCH_A], 0, 3, 1)()
    pump()
    stages[0]()
    spatial_term(w_a2, saved[PATCH_A], 3, 6, 1)()
    pump()
    stages[1]()
    pump()
    spatial_term(w_a2, saved[PATCH_A], 6, 9, 1)()
    pump()
    pgrad_mid[0] = total.total[...]
    scale[0] = 0.25
    for plane in range(4):
        norm_back(
            lambda j, plane=plane: dz[:, columns(4 * plane + j)],
            saved[HAT_A1].at[plane],
            total.total,
            0,
            inv_mid.at[0],
            par_mid,
            0,
            planes[plane],
            4,
        )

    def input_gradient(p):
        target = (dh_a if p < 2 else dh_b).at[:, pl.ds((p % 2) * 1024, 1024)]
        value = dot(planes[p][...], w_a1[...].reshape(512, -1))
        if p == 0:
            value = value + saved[OUT_A][:, 0:1024].astype(jnp.float32)
            value = value + saved[OUT_A][:, 1024:2048].astype(jnp.float32)
        target[...] = value.astype(jnp.bfloat16)
        copy = pltpu.make_async_copy(target, dx_hbm.at[p], dx_sem.at[p])
        copy.start()
        return copy

    copies = []
    for p in range(4):
        copies.append(input_gradient(p))
        pump()

    def last_term(c, carry):
        at = quarter(c)
        total = jnp.zeros((512, 256), jnp.float32)
        for p in range(4):
            total = total + lax.dot_general(
                planes[p][...], x[p, :, at], (((0,), (0,)), ((), ())), preferred_element_type=jnp.float32
            )
        w_a1[:, :, 0, :, at] = total.astype(jnp.bfloat16).reshape(depth, 2, 64, 256)
        return carry

    paced(0, 4, last_term, 2, pump)
    reduce.enable(0)
    reduce.finish(weight_squares, squares_out)
    for copy in copies:
        copy.wait()
    for total in sums.values():
        total.close()


def run_backward(plan, depth, x, shifts, cot, mask, weight_squares, small, saved, fulls):
    rows, f32, bf16 = plan.rows, jnp.float32, jnp.bfloat16
    dma = pltpu.SemaphoreType.DMA
    scratch = []
    for _, pieces in backward_names(depth):
        scratch += pieces
    scratch += [pltpu.VMEM(value.shape, bf16) for value in (x, shifts, cot)]
    scratch += [pltpu.VMEM(full.shape, bf16) for full in fulls]
    scratch += [pltpu.VMEM(shape, kind) for name, (shape, kind) in zip(SAVED, saved_shapes(rows)) if name != PATCH_B]
    scratch += [
        pltpu.VMEM((rows, 2048), f32),
        pltpu.VMEM((rows, 512), f32),
        pltpu.VMEM((rows, 512), bf16),
        pltpu.VMEM((1024, rows), bf16),
        dma((10,)),
        dma((len(SAVED),)),
        dma((4,)),
    ]
    shapes = [full.shape for full in fulls]
    scratch += Reduce.scratch(shapes, depth)

    def part(shape, over):
        return jax.ShapeDtypeStruct((*shape[:3], shape[3] // over, shape[4]), bf16)

    outs = pl.pallas_call(
        functools.partial(backward_kernel, plan, depth),
        out_shape=[
            jax.ShapeDtypeStruct(x.shape, bf16),
            jax.ShapeDtypeStruct((4, 8, 512), f32),
            jax.ShapeDtypeStruct((8, 2048), f32),
            jax.ShapeDtypeStruct((8, 4096), f32),
            jax.ShapeDtypeStruct((8, 128), f32),
        ]
        + [jax.ShapeDtypeStruct(shape[2:], bf16) for shape in shapes]
        + [part(shape, 2) for shape in shapes]
        + [part(shape, 4) for shape in shapes],
        in_specs=[ANY] * 3 + [WHOLE] * 7 + [ANY] * len(SAVED) + [ANY] * 7,
        out_specs=[ANY] + [WHOLE] * 4 + [ANY] * 21,
        scratch_shapes=scratch,
        compiler_params=pltpu.CompilerParams(collective_id=1, has_side_effects=True, vmem_limit_bytes=VMEM_LIMIT),
    )(x, shifts, cot, mask, weight_squares, *small, *saved, *fulls)
    return outs[:12]


def scale_kernel(depth, squares, sums_mid, sums_b3, sums_j, *refs):
    refs = list(refs)

    def take(count):
        taken = refs[:count]
        del refs[:count]
        return taken

    totals, weights, outs, norm_outs = take(7), take(7), take(14), take(7)
    squares_out, totals_in, weights_in, staged = take(1)[0], take(7), take(7), take(14)
    in_sem, out_sem = refs

    def loads(i):
        return (
            pltpu.make_async_copy(totals[i], totals_in[i], in_sem.at[0, i]),
            pltpu.make_async_copy(weights[i], weights_in[i], in_sem.at[1, i]),
        )

    def stores(i):
        return [pltpu.make_async_copy(staged[2 * i + n], outs[2 * i + n], out_sem.at[n, i]) for n in (0, 1)]

    for i in range(7):
        for copy in loads(i):
            copy.start()

    squares_out[...] = squares[0:2, 0:7]
    place = lax.axis_index(DP)

    def both(sums):
        seconds = sums[3:4] + sums[4:5] + sums[5:6]
        return jnp.concatenate([seconds, sums[0:1] + sums[1:2] + sums[2:3]], axis=0)

    def put(target, sums, base):
        width = target.shape[1]
        span = max(width, 128)
        start = (place * width) // span * span + base
        block = both(sums[:, pl.ds(pl.multiple_of(start, 128), span)])
        for piece in range(span // width):
            part = block[:, piece * width : (piece + 1) * width]

            @pl.when(lax.rem(place, span // width) == piece)
            def _(part=part):
                target[...] = part

    for i, (sums, base) in enumerate(
        (
            (sums_mid.at[0], 0),
            (sums_mid.at[1], 0),
            (sums_j, 0),
            (sums_j, sums_j.shape[1] // 2),
            (sums_mid.at[2], 0),
            (sums_mid.at[3], 0),
            (sums_b3, 0),
        )
    ):
        put(norm_outs[i], sums, base)

    weight_norm = jnp.sqrt(squares[0:1, :])
    trust = weight_norm / (jnp.sqrt(squares[1:2, :]) + DECAY_RATE * weight_norm)
    for i in range(7):
        for copy in loads(i):
            copy.wait()
        ratio = trust[0:1, i : i + 1]

        def body(lead, carry, i=i, ratio=ratio):
            gradient = totals_in[i][lead].astype(jnp.float32)
            staged[2 * i][lead] = gradient
            decayed = gradient + DECAY_RATE * weights_in[i][lead].astype(jnp.float32)
            staged[2 * i + 1][lead] = ratio * decayed
            return carry

        lax.fori_loop(0, totals_in[i].shape[0], body, 0)
        for copy in stores(i):
            copy.start()
    for i in range(7):
        for copy in stores(i):
            copy.wait()


def run_scale(depth, squares, sums, totals, shards, widths):
    f32, bf16, dma = jnp.float32, jnp.bfloat16, pltpu.SemaphoreType.DMA
    shapes = [total.shape for total in totals]
    outs = pl.pallas_call(
        functools.partial(scale_kernel, depth),
        out_shape=[jax.ShapeDtypeStruct(shape, f32) for shape in shapes for _ in (0, 1)]
        + [jax.ShapeDtypeStruct((2, width), f32) for width in widths]
        + [jax.ShapeDtypeStruct((2, 7), f32)],
        in_specs=[WHOLE] * 4 + [ANY] * 14,
        out_specs=[ANY] * 14 + [WHOLE] * 8,
        scratch_shapes=[pltpu.VMEM(shape, bf16) for shape in shapes * 2]
        + [pltpu.VMEM(shape, f32) for shape in shapes for _ in (0, 1)]
        + [dma((2, 7)), dma((2, 7))],
        compiler_params=pltpu.CompilerParams(vmem_limit_bytes=VMEM_LIMIT),
    )(squares, *sums, *totals, *shards)
    return outs[0:14:2], outs[1:14:2], outs[14:21], outs[21]


def on_device(
    input_160,
    input_224,
    input_288,
    cotangent_160,
    cotangent_224,
    cotangent_288,
    live_counts,
    conv_a1,
    norm_a1,
    conv_a2,
    norm_a2,
    conv_a3,
    norm_a3,
    conv_as,
    norm_as,
    conv_b1,
    norm_b1,
    conv_b2,
    norm_b2,
    conv_b3,
    norm_b3,
):
    if conv_a1.shape[1] % 64 or conv_a3.shape[1] % 128 or lax.axis_size(REP) != 4:
        return plain_on_device(
            input_160,
            input_224,
            input_288,
            cotangent_160,
            cotangent_224,
            cotangent_288,
            live_counts,
            conv_a1,
            norm_a1,
            conv_a2,
            norm_a2,
            conv_a3,
            norm_a3,
            conv_as,
            norm_as,
            conv_b1,
            norm_b1,
            conv_b2,
            norm_b2,
            conv_b3,
            norm_b3,
        )
    depth = lax.axis_size(DP) // 2
    inputs = (input_160, input_224, input_288)
    plan = Plan([value.shape for value in inputs])
    shards = (
        conv_a1.T[None],
        jnp.transpose(conv_a2, (0, 1, 3, 2)).reshape(9, conv_a2.shape[3], conv_a2.shape[2]),
        conv_a3.reshape(2, -1, conv_a3.shape[1]),
        conv_as.reshape(4, -1, conv_as.shape[1]),
        conv_b1.T[None],
        jnp.transpose(conv_b2, (0, 1, 3, 2)).reshape(9, conv_b2.shape[3], conv_b2.shape[2]),
        conv_b3.reshape(2, -1, conv_b3.shape[1]),
    )

    planes, cotangents = [], []
    for g, (value, cotangent) in enumerate(
        zip(inputs, (cotangent_160, cotangent_224, cotangent_288))
    ):
        side, slots, fill = plan.sides[g], plan.slots[g], plan.sizes[g] - plan.valid[g]
        split = jnp.transpose(value, (1, 2, 0, 3)).reshape(side, 2, side, 2, slots, -1)
        split = jnp.transpose(split, (1, 3, 0, 2, 4, 5)).reshape(4, plan.valid[g], -1)
        planes.append(jnp.pad(split, ((0, 0), (0, fill), (0, 0))))
        cotangents.append(
            jnp.pad(jnp.transpose(cotangent, (1, 2, 0, 3)).reshape(plan.valid[g], -1), ((0, fill), (0, 0)))
        )
    x = jnp.concatenate(planes, axis=1)
    cot = jnp.concatenate(cotangents, axis=0)
    live = jnp.pad(live_counts.astype(jnp.float32), ((0, 0), (0, 128 - live_counts.shape[1])))

    def stacked(norms):
        rows = jnp.concatenate(norms, axis=0).astype(jnp.float32)
        return jnp.pad(rows, ((0, 8 - rows.shape[0]), (0, 0)))

    mid_local = norm_a1.shape[1]
    mid_width = mid_local * 2 * depth
    norm_mid = lax.dynamic_update_slice(
        jnp.zeros((8, mid_width), jnp.float32),
        stacked((norm_a1, norm_a2, norm_b1, norm_b2)),
        (0, lax.axis_index(DP) * mid_local),
    )
    norm_out = stacked((norm_a3, norm_as, norm_b3))
    shifts = jnp.asarray(plan.shifts())

    results = run_forward(
        plan, depth, x, shifts, jnp.asarray(plan.slot_rows()), live, norm_mid, norm_out, shards
    )
    outs, mask, small, square_row = results[:3], results[3], results[4:9], results[9]
    fulls, saved = results[10:17], results[17:]
    dx, pgrad_mid, pgrad_b3, pgrad_j, squares, *totals = run_backward(
        plan, depth, x, shifts, cot, mask, square_row, small, saved, fulls
    )

    def placed(values):
        return [
            values[0][0].T,
            jnp.transpose(values[1], (0, 2, 1)).reshape(conv_a2.shape),
            values[2].reshape(conv_a3.shape),
            values[3].reshape(conv_as.shape),
            values[4][0].T,
            jnp.transpose(values[5], (0, 2, 1)).reshape(conv_b2.shape),
            values[6].reshape(conv_b3.shape),
        ]

    widths = [norm.shape[1] for norm in (norm_a1, norm_a2, norm_a3, norm_as, norm_b1, norm_b2, norm_b3)]
    gradients, scaled, norm_gradients, squares = run_scale(
        depth, squares, (pgrad_mid, pgrad_b3, pgrad_j), totals, shards, widths
    )
    gradients, scaled = placed(gradients), placed(scaled)

    outputs, grad_inputs = [], []
    for g in range(3):
        side, slots, start = plan.sides[g], plan.slots[g], plan.starts[g]
        rows = outs[g].reshape(side, side, slots, -1)
        outputs.append(jnp.transpose(rows, (2, 0, 1, 3)))
        split = dx[:, start : start + plan.valid[g]].reshape(2, 2, side, side, slots, -1)
        split = jnp.transpose(split, (2, 0, 3, 1, 4, 5)).reshape(2 * side, 2 * side, slots, -1)
        grad_inputs.append(jnp.transpose(split, (2, 0, 1, 3)))
    pairs = [piece for pair in zip(gradients, norm_gradients) for piece in pair]
    return (*outputs, *grad_inputs, *pairs, *scaled, squares)


def solution(mesh):
    by_image, by_column = P((DP, REP), None, None, None), P(None, DP)
    by_channel = P(None, None, None, DP)
    weights = [by_column, by_column, by_channel] + [by_column] * 7 + [by_channel] + [by_column] * 3
    kernels = [by_column, by_channel] + [by_column] * 3 + [by_channel, by_column]
    return jax.shard_map(
        on_device,
        mesh=mesh,
        in_specs=(*[by_image] * 6, P((DP, REP), None), *weights),
        out_specs=(*[by_image] * 6, *weights, *kernels, P()),
        check_vma=False,
    )
```
